32 devices in a mesh: group: 4 (over z), ghost: 8 (over y, x, core).
Axes of the slice: x: 2, y: 2, z: 4, core: 2. Of those that a mesh axis runs over, the one named last changes fastest.
Arguments:
- inputs: bfloat16 [25088, 1024], P(('group', 'ghost')), may hold values from -6 to 6
- out_grad: bfloat16 [25088, 1024], P(('group', 'ghost')), may hold values from -6 to 6
- conv_first: bfloat16 [1024, 256], replicated, may hold values from -0.25 to 0.25
- conv_middle: bfloat16 [2304, 256], replicated, may hold values from -0.1875 to 0.1875
- conv_last: bfloat16 [256, 1024], replicated, may hold values from -0.375 to 0.375
- gain: float32 [1024], replicated, may hold values from 0.5 to 1.5
Outputs:
- input_grad: bfloat16 [25088, 1024], P(('group', 'ghost'))
- first_grad: float32 [262144], P(('group', 'ghost'))
- middle_grad: float32 [589824], P(('group', 'ghost'))
- last_grad: float32 [262144], P(('group', 'ghost'))
- gain_grad: float32 [1024], P(('group', 'ghost'))
The draws below stay inside these ranges and needn't reach their ends.
All inputs are finite; a program needn't handle non-finite values.
Results may differ from the reference program's by a relative error of at most 0.0071.
Values sent between devices are 32-bit elements; how exact they have to be, the bound alone decides.
No kernel may reach another device: no remote copies, remote signals or barrier semaphores. Data moves between devices by JAX's collectives and lax.ppermute only.
A program may use at most 128 MiB of HBM per device.

```python
import jax
import jax.numpy as jnp
from jax import lax

WIDE = 1024
MID = 256
GROUP = 64
NEWTON = 5
SIDE = 14
GHOST_ROWS = 6272
CELLS = 25088


def raised(array, rng, source, target, blocks, factor):
    def block_of(axis_at):
        return (jnp.arange(array.shape[axis_at]) // (array.shape[axis_at] // blocks)).reshape((-1,) + (1,) * (array.ndim - 1 - axis_at))

    first = jax.random.permutation(rng, blocks)[block_of(target)]
    far = (block_of(target) + blocks // 2) % blocks
    return jnp.where((block_of(source) == first) | (block_of(source) == far), factor * array, array)


def shard_levels(stream_key, extent, shards, smallest, top_value):
    def one(position, blocks):
        draws = jax.random.uniform(jax.random.fold_in(jax.random.fold_in(stream_key, 6), position), (blocks,), jnp.float32, smallest / len(shards), top_value / len(shards))
        return jnp.repeat(jnp.exp(draws), extent[position] // blocks).reshape((-1,) + (1,) * (len(extent) - position - 1))

    loudness = one(*shards[0])
    for cut in shards[1:]:
        loudness = loudness * one(*cut)
    return loudness


def normal_values(rng, dims, width, bound, cuts=(), held_as=jnp.bfloat16):
    loudness = shard_levels(rng, dims, cuts, -0.22, 0.18) if cuts else 1.0
    drawn = jax.random.normal(rng, dims, jnp.float32) * width * loudness
    return jnp.minimum(jnp.maximum(drawn, -bound), bound).astype(held_as)


def heavy_noise(stream_key, dims, scale, most, cuts, heavy, kind=jnp.bfloat16):
    entries = scale * jax.random.normal(stream_key, dims, jnp.float32)
    if cuts:
        entries = entries * shard_levels(stream_key, dims, cuts, -0.22, 0.18)
    return jnp.clip(raised(entries, jax.random.fold_in(stream_key, 3), *heavy), -most, most).astype(kind)


def setup_inputs(seed: int = 0) -> dict:
    streams_of = jax.random.split(jax.random.key(seed), 7)
    inputs = heavy_noise(streams_of[0], (CELLS, WIDE), 1.0, 6.0, ((0, 32),), (0, 1, 32, 2.75))
    out_grad = normal_values(streams_of[1], (CELLS, WIDE), 1.0, 6.0, ((0, 32),))
    conv_first = normal_values(streams_of[2], (WIDE, MID), (WIDE / 2) ** -0.5, 0.25)
    conv_middle = normal_values(streams_of[3], (9 * MID, MID), (9 * MID / 2) ** -0.5, 0.1875)
    conv_last = normal_values(streams_of[4], (MID, WIDE), MID ** -0.5, 0.375)
    gain = jnp.clip(1.0 + 0.1 * jax.random.normal(streams_of[5], (WIDE,), jnp.float32), 0.5, 1.5)
    return dict(inputs=inputs, out_grad=out_grad, conv_first=conv_first, conv_middle=conv_middle, conv_last=conv_last, gain=gain)


epsilon = 1e-05

def silu_slope(value):
    sig = jax.nn.sigmoid(value)
    return sig * (1.0 + value * (1.0 - sig))

def patches(act, side):
    channels = act.shape[-1]
    images = act.reshape(-1, side, side, channels)
    padded = jnp.pad(images, ((0, 0), (1, 1), (1, 1), (0, 0)))
    pieces = [padded[:, row_off:row_off + side, col_off:col_off + side, :] for row_off in range(3) for col_off in range(3)]
    return jnp.concatenate(pieces, axis=-1).reshape(-1, 9 * channels)

def unpatch(dcolumns, side):
    channels = dcolumns.shape[-1] // 9
    images = dcolumns.reshape(-1, side, side, 9, channels)
    padded = jnp.pad(images, ((0, 0), (1, 1), (1, 1), (0, 0), (0, 0)))
    summed = jnp.zeros((images.shape[0], side, side, channels), jnp.float32)
    for row_off in range(3):
        for col_off in range(3):
            summed = summed + padded[:, 2 - row_off:2 - row_off + side, 2 - col_off:2 - col_off + side, 3 * row_off + col_off, :]
    return summed.reshape(-1, channels)

def batched(left, right):
    return jnp.einsum('gij,gjk->gik', left, right, precision=lax.Precision.HIGHEST)

def gram(left, right):
    return jnp.einsum('rgi,rgj->gij', left, right, precision=lax.Precision.HIGHEST)

def whitener(covariance):
    traces = jnp.trace(covariance, axis1=1, axis2=2)
    normed = covariance / traces[:, None, None]
    identity = jnp.broadcast_to(jnp.eye(covariance.shape[1], dtype=jnp.float32), covariance.shape)
    project = identity
    for sweep in range(NEWTON):
        cubed = batched(batched(project, project), project)
        project = 1.5 * project - 0.5 * batched(cubed, normed)
    return project / jnp.sqrt(traces)[:, None, None]

def contract(left, right):
    return lax.dot_general(left, right, (((0,), (0,)), ((), ())), preferred_element_type=jnp.float32)

def ghost_pass(inputs, out_grad, conv_first, conv_middle, conv_last, gain):
    rows = inputs.shape[0]
    blocks = WIDE // GROUP
    act1 = jnp.dot(inputs, conv_first, preferred_element_type=jnp.float32)
    hidden1 = jax.nn.silu(act1).astype(jnp.bfloat16)
    columns = patches(hidden1, SIDE)
    act2 = jnp.dot(columns, conv_middle, preferred_element_type=jnp.float32)
    hidden2 = jax.nn.silu(act2).astype(jnp.bfloat16)
    branch = jnp.dot(hidden2, conv_last, preferred_element_type=jnp.float32)
    mean = lax.optimization_barrier(jnp.sum(branch, 0)) / rows
    centered = branch - mean
    grouped = centered.reshape(rows, blocks, GROUP)
    identity = jnp.broadcast_to(jnp.eye(GROUP, dtype=jnp.float32), (blocks, GROUP, GROUP))
    covariance = gram(grouped, grouped) / rows + epsilon * identity
    whiten, pullback = jax.vjp(whitener, covariance)
    white = jnp.einsum('rgi,gij->rgj', grouped, whiten, precision=lax.Precision.HIGHEST).reshape(rows, WIDE)
    pre = inputs.astype(jnp.float32) + gain * white
    dpre = out_grad.astype(jnp.float32) * silu_slope(pre)
    dwhite = (dpre * gain).reshape(rows, blocks, GROUP)
    gain_part = lax.optimization_barrier(jnp.sum(dpre * white, 0))
    colsum = lax.optimization_barrier(jnp.sum(dwhite, 0))
    cross = gram(grouped, dwhite)
    dcov = pullback(cross)[0]
    sym_cov = dcov + jnp.swapaxes(dcov, 1, 2)
    dbranch = jnp.einsum('rgj,gij->rgi', dwhite - colsum / rows, whiten, precision=lax.Precision.HIGHEST)
    dbranch = dbranch + jnp.einsum('rgi,gij->rgj', grouped, sym_cov, precision=lax.Precision.HIGHEST) / rows
    dbranch = dbranch.reshape(rows, WIDE).astype(jnp.bfloat16)
    last_part = contract(hidden2, dbranch)
    dmid2 = (lax.dot_general(dbranch, conv_last, (((1,), (1,)), ((), ())), preferred_element_type=jnp.float32) * silu_slope(act2)).astype(jnp.bfloat16)
    middle_part = contract(columns, dmid2)
    dcolumns = lax.dot_general(dmid2, conv_middle, (((1,), (1,)), ((), ())), preferred_element_type=jnp.float32)
    dhid1 = unpatch(dcolumns, SIDE)
    dmid1 = (dhid1 * silu_slope(act1)).astype(jnp.bfloat16)
    first_part = contract(inputs, dmid1)
    input_grad = (lax.dot_general(dmid1, conv_first, (((1,), (1,)), ((), ())), preferred_element_type=jnp.float32) + dpre).astype(jnp.bfloat16)
    return (input_grad, (first_part, middle_part, last_part, gain_part))

def reference(inputs, out_grad, conv_first, conv_middle, conv_last, gain):
    count = CELLS // GHOST_ROWS
    xs_in = inputs.reshape(count, GHOST_ROWS, WIDE)
    xs_grad = out_grad.reshape(count, GHOST_ROWS, WIDE)
    start = (jnp.zeros((WIDE, MID), jnp.float32), jnp.zeros((9 * MID, MID), jnp.float32), jnp.zeros((MID, WIDE), jnp.float32), jnp.zeros((WIDE,), jnp.float32))

    def step_fn(carry, pieces):
        result, parts = ghost_pass(pieces[0], pieces[1], conv_first, conv_middle, conv_last, gain)
        return (jax.tree.map(lambda left, right: left + right, carry, parts), result)
    sums, grads = lax.scan(step_fn, start, (xs_in, xs_grad))
    scale = CELLS ** (-0.5)
    return (grads.reshape(CELLS, WIDE), (sums[0] * scale).reshape(-1), (sums[1] * scale).reshape(-1), (sums[2] * scale).reshape(-1), sums[3] * scale)
```

```python
import functools

import jax
import jax.numpy as jnp
from jax import lax
from jax.experimental import pallas as pl
from jax.experimental.pallas import tpu as pltpu
from jax.sharding import PartitionSpec as P

GROUP = 64
NEWTON = 5
SIDE = 14
LINE = 16
PAIR = 2 * GROUP
TALL = GROUP + 8
epsilon = 1e-05

F32 = jnp.float32
BF16 = jnp.bfloat16


def dot(left, right):
    return jnp.dot(left, right, preferred_element_type=F32)


def dot_t(left, right):
    return lax.dot_general(left, right, (((0,), (0,)), ((), ())), preferred_element_type=F32)


def dot_nt(left, right):
    return lax.dot_general(left, right, (((1,), (1,)), ((), ())), preferred_element_type=F32)


def exact(left, right):
    return jnp.dot(left, right, preferred_element_type=F32, precision=lax.Precision.HIGHEST)


def sigmoid(value):
    return 1.0 / (1.0 + jnp.exp(-value))


def chunk_of(rows, most):
    best = 16
    for size in range(16, most + 1, 16):
        if rows % size == 0:
            best = size
    return best


def left_half(shape):
    return lax.broadcasted_iota(jnp.int32, shape, 1) < GROUP


def spread(packed):
    left = left_half(packed.shape)
    zero = jnp.zeros_like(packed)
    return jnp.concatenate([jnp.where(left, packed, zero), jnp.where(left, zero, packed)], axis=0)


def pack(square):
    top, bottom = square[:GROUP], square[GROUP:]
    return jnp.where(left_half(top.shape), top, bottom)


def vectors(*rows):
    at = lax.broadcasted_iota(jnp.int32, (8, PAIR), 0)
    tile = jnp.zeros((8, PAIR), F32)
    for place, row in enumerate(rows):
        tile = jnp.where(at == place, row, tile)
    return tile


def fold(value):
    rows, lanes = value.shape
    return jnp.sum(value.reshape(rows // 8, 8, lanes), axis=0)


def pad_lines(source, ext, rows):
    for line in range(rows // SIDE):
        place = 24 + LINE * (line + line // SIDE)
        ext[place : place + SIDE, :] = source[SIDE * line : SIDE * (line + 1), :]


def unpad_lines(source, target, rows):
    for line in range(rows // SIDE):
        place = LINE * (line + line // SIDE)
        target[SIDE * line : SIDE * (line + 1), :] = source[place : place + SIDE, :]


def padded_rows(rows):
    return rows // (SIDE * SIDE) * (SIDE + 1) * LINE


def shifted(ext, cols):
    length = cols.shape[1]
    for col in range(3):
        cols[col] = ext[7 + col : 7 + col + length, :].astype(BF16)


def emit_split(source, keep, send, core, piece):
    def step(at, carry):
        here = pl.ds(pl.multiple_of(at * piece, 8), piece)
        mine = pl.ds(pl.multiple_of((2 * at + core) * piece, 8), piece)
        other = pl.ds(pl.multiple_of((2 * at + 1 - core) * piece, 8), piece)
        keep[here, :] = source[mine, :]
        send[here, :] = source[other, :]
        return carry

    lax.fori_loop(0, keep.shape[0] // piece, step, 0)


def forward_kernel(spot, x, w1, wm, w3, h1pad, s1, h2, s2, *rest, split):
    rows = x.shape[0]
    outs, (ext, cols, flat, branch, stats) = rest[:-5], rest[-5:]
    chunk = chunk_of(rows, 128)
    ext[...] = jnp.zeros_like(ext)

    def first(at, carry):
        here = pl.ds(pl.multiple_of(at * chunk, 16), chunk)
        act = dot(x[here, :], w1[...])
        sig = sigmoid(act)
        flat[here, :] = act * sig
        s1[here, :] = sig * (1.0 + act * (1.0 - sig))
        return carry

    lax.fori_loop(0, rows // chunk, first, 0)
    pad_lines(flat, ext, rows)
    shifted(ext, cols)
    padded = padded_rows(rows)
    h1pad[...] = cols[1, LINE : LINE + padded, :]
    big = chunk_of(padded, 256)

    def middle(at, carry):
        base = pl.multiple_of(at * big, 16)
        total = jnp.zeros((big, wm.shape[1]), F32)
        for row in range(3):
            for col in range(3):
                left = cols[col, pl.ds(base + LINE * row, big), :]
                k = 3 * row + col
                depth = left.shape[1]
                total = total + dot(left, wm[k * depth : (k + 1) * depth, :])
        ext[pl.ds(base, big), :] = total
        return carry

    lax.fori_loop(0, padded // big, middle, 0)
    unpad_lines(ext, flat, rows)
    width = w3.shape[1]

    def last(at, total):
        here = pl.ds(pl.multiple_of(at * chunk, 16), chunk)
        act = flat[here, :]
        sig = sigmoid(act)
        hidden = (act * sig).astype(BF16)
        h2[here, :] = hidden
        s2[here, :] = sig * (1.0 + act * (1.0 - sig))
        out = dot(hidden, w3[...])
        branch[here, :] = out
        return total + fold(out)

    total = lax.fori_loop(0, rows // chunk, last, jnp.zeros((8, width), F32))
    total = jnp.sum(total, axis=0, keepdims=True)
    mean = total / rows
    for quad in range(width // 256):
        lanes = slice(256 * quad, 256 * (quad + 1))
        centered = (branch[:, lanes] - mean[:, lanes]).astype(BF16)
        square = dot_t(centered, centered)
        for half in range(2):
            pair = 2 * quad + half
            ch = slice(PAIR * pair, PAIR * (pair + 1))
            row = mean[:, ch]
            tile = vectors(row)
            outer = lax.dot_general(
                tile, tile, (((0,), (0,)), ((), ())), preferred_element_type=F32,
                precision=lax.Precision.HIGHEST,
            )
            inner = square[PAIR * half : PAIR * (half + 1), PAIR * half : PAIR * (half + 1)]
            place = jnp.bitwise_xor(pair, spot[0]) if split else pair
            stats[place, :GROUP, :] = pack(inner + outer * rows)
            stats[place, GROUP:, :] = vectors(total[:, ch])
    if split:
        for at, out in enumerate(outs):
            out[...] = stats[at]
    else:
        outs[0][...] = stats[...]


def identity():
    shape = (PAIR, PAIR)
    return jnp.where(
        lax.broadcasted_iota(jnp.int32, shape, 0) == lax.broadcasted_iota(jnp.int32, shape, 1),
        1.0, 0.0,
    ).astype(F32)


def per_block(square):
    row_sums = jnp.sum(square, axis=1, keepdims=True)
    top = jnp.sum(row_sums[:GROUP], axis=0, keepdims=True)
    bottom = jnp.sum(row_sums[GROUP:], axis=0, keepdims=True)
    upper = lax.broadcasted_iota(jnp.int32, (PAIR, 1), 0) < GROUP
    return jnp.where(upper, top, bottom)


def whiten_one(total, span, keep, at):
    mean = total[GROUP : GROUP + 1, :] / span
    tile = vectors(mean)
    outer = lax.dot_general(
        tile, tile, (((0,), (0,)), ((), ())), preferred_element_type=F32,
        precision=lax.Precision.HIGHEST,
    )
    eye = identity()
    blocks = spread(jnp.ones((GROUP, PAIR), F32))
    cov = spread(total[:GROUP, :]) / span - outer * blocks + epsilon * eye
    trace = per_block(cov * eye)
    normed = cov / trace
    keep[at, 0] = normed
    keep[at, 1] = eye / trace
    power = 1.5 * eye - 0.5 * normed
    for sweep in range(NEWTON - 1):
        square = exact(power, power)
        side = exact(power, normed)
        keep[at, 2 + 2 * sweep] = power
        keep[at, 3 + 2 * sweep] = exact(square, power)
        power = 1.5 * power - 0.5 * exact(square, side)
    keep[at, 2 * NEWTON] = power
    return jnp.concatenate([pack(power / jnp.sqrt(trace)), vectors(mean)], axis=0)


def pull_one(total, span, keep, at):
    eye = identity()
    normed = keep[at, 0]
    inverse = per_block(keep[at, 1]) / GROUP
    cross = spread(total[:GROUP, :])
    cross = cross + cross.T
    root = jnp.sqrt(inverse)
    power = keep[at, 2 * NEWTON]
    grad = cross * root
    trace_grad = -0.5 * inverse * root * per_block(cross * power)
    normed_grad = jnp.zeros_like(grad)
    for sweep in reversed(range(NEWTON - 1)):
        power_k = keep[at, 2 + 2 * sweep]
        cubed = keep[at, 3 + 2 * sweep]
        product = exact(cubed, grad)
        normed_grad = normed_grad - 0.25 * (product + product.T)
        turned = exact(grad, normed)
        turned = exact(turned + turned.T, power_k)
        outer = exact(turned, power_k)
        inner = exact(power_k, turned)
        grad = 1.5 * grad - 0.25 * (outer + outer.T + inner)
    normed_grad = normed_grad - 0.5 * grad
    trace_grad = trace_grad - inverse * per_block(normed_grad * normed)
    both = normed_grad * inverse + eye * trace_grad
    whiten = power * root
    bias = -exact(vectors(total[GROUP : GROUP + 1, :] / span), whiten.T)
    return jnp.concatenate(
        [pack(both / span), vectors(bias[0:1, :], total[GROUP + 1 : GROUP + 2, :])], axis=0
    )


def whiten_kernel(*refs, span, pieces):
    terms, (out, keep) = refs[:pieces], refs[pieces:]
    for at in range(out.shape[0]):
        total = terms[0][at]
        for term in terms[1:]:
            total = total + term[at]
        out[at] = whiten_one(total, span, keep, at)


def pull_kernel(total_ref, keep, out, *, span):
    own = keep.shape[0]
    for at in range(own):
        if total_ref.shape[0] == own:
            total = total_ref[at]
        else:
            total = total_ref[0]
            for term in range(1, total_ref.shape[0]):
                total = total + total_ref[term]
        result = pull_one(total, span, keep, at)
        if out.shape[0] == own:
            out[at] = result
        else:
            for copy in range(out.shape[0]):
                out[copy] = result


def place_pairs(spot, shares, pairs, split):
    if split:
        for at, share in enumerate(shares):
            pairs[jnp.bitwise_xor(at, spot[0])] = share[0]
    else:
        pairs[...] = shares[0][...]


def quad_matrix(pairs, quad):
    zero = jnp.zeros((PAIR, PAIR), F32)
    first = spread(pairs[2 * quad, :GROUP, :])
    second = spread(pairs[2 * quad + 1, :GROUP, :])
    top = jnp.concatenate([first, zero], axis=1)
    bottom = jnp.concatenate([zero, second], axis=1)
    return jnp.concatenate([top, bottom], axis=0).astype(BF16)


def row_of(pairs, quad, place):
    at = GROUP + place
    return jnp.concatenate(
        [pairs[2 * quad, at : at + 1, :], pairs[2 * quad + 1, at : at + 1, :]], axis=1
    )


def backward_kernel(spot, x, og, h2, w3, gain, *rest, split, shares):
    given, (cen, dwb, dpre_out, w_out, stats, pairs) = rest[:shares], rest[shares:]
    rows, width = x.shape
    place_pairs(spot, given, pairs, split)
    w_out[...] = pairs[...]
    chunk = chunk_of(rows, 128)
    for quad in range(width // 256):
        lanes = slice(256 * quad, 256 * (quad + 1))
        whiten = quad_matrix(pairs, quad)
        mean = row_of(pairs, quad, 0)
        scale = gain[:, lanes]

        def step(at, carry, lanes=lanes, whiten=whiten, mean=mean, scale=scale):
            col_sum, gain_sum = carry
            here = pl.ds(pl.multiple_of(at * chunk, 16), chunk)
            centered = (dot(h2[here, :], w3[:, lanes]) - mean).astype(BF16)
            cen[here, lanes] = centered
            white = dot(centered, whiten)
            pre = x[here, lanes].astype(F32) + scale * white
            sig = sigmoid(pre)
            dpre = og[here, lanes].astype(F32) * (sig * (1.0 + pre * (1.0 - sig)))
            dpre_out[here, lanes] = dpre
            dwhite = scale * dpre
            dwb[here, lanes] = dwhite.astype(BF16)
            return col_sum + fold(dwhite), gain_sum + fold(dpre * white)

        zero = jnp.zeros((8, 256), F32)
        col_sum, gain_sum = lax.fori_loop(0, rows // chunk, step, (zero, zero))
        col_sum = jnp.sum(col_sum, axis=0, keepdims=True)
        gain_sum = jnp.sum(gain_sum, axis=0, keepdims=True)
        square = dot_t(cen[:, lanes], dwb[:, lanes])
        for half in range(2):
            ch = slice(PAIR * half, PAIR * (half + 1))
            stats[2 * quad + half, :GROUP, :] = pack(square[ch, ch])
            stats[2 * quad + half, GROUP:, :] = vectors(col_sum[:, ch], gain_sum[:, ch])


def last_kernel(spot, dwb, cen, h2, s2, w3, wpairs, spairs, cols, *rest, piece):
    outs, (ext, flat, dbranch, part) = rest[:-4], rest[-4:]
    rows, width = dwb.shape
    chunk = chunk_of(rows, 128)
    ext[...] = jnp.zeros_like(ext)
    for quad in range(width // 256):
        lanes = slice(256 * quad, 256 * (quad + 1))
        whiten = quad_matrix(wpairs, quad)
        sym = quad_matrix(spairs, quad)
        bias = row_of(spairs, quad, 0)

        def step(at, carry, lanes=lanes, whiten=whiten, sym=sym, bias=bias):
            here = pl.ds(pl.multiple_of(at * chunk, 16), chunk)
            value = dot_nt(dwb[here, lanes], whiten) + dot(cen[here, lanes], sym) + bias
            dbranch[here, lanes] = value.astype(BF16)
            return carry

        lax.fori_loop(0, rows // chunk, step, 0)

    def middle(at, carry):
        here = pl.ds(pl.multiple_of(at * chunk, 16), chunk)
        flat[here, :] = dot_nt(dbranch[here, :], w3[...]) * s2[here, :]
        return carry

    lax.fori_loop(0, rows // chunk, middle, 0)
    pad_lines(flat, ext, rows)
    shifted(ext, cols)
    for quad in range(width // 256):
        lanes = slice(256 * quad, 256 * (quad + 1))
        part[:, lanes] = dot_t(h2[...], dbranch[:, lanes])
    finish(part, outs, spot, piece)


def finish(part, outs, spot, piece):
    if piece:
        emit_split(part, outs[0], outs[1], spot[1], piece)
    else:
        outs[0][...] = part[...]


def middle_kernel(spot, cols, h1pad, wm, s1, dmid1, *rest, piece):
    outs, (ext, flat, part) = rest[:-3], rest[-3:]
    padded, depth = h1pad.shape
    rows = s1.shape[0]
    for row in range(3):
        for col in range(3):
            k = 3 * row + col
            near = cols[2 - col, LINE * (2 - row) : LINE * (2 - row) + padded, :]
            part[k * depth : (k + 1) * depth, :] = dot_t(h1pad[...], near)
    big = chunk_of(padded, 256)

    def step(at, carry):
        base = pl.multiple_of(at * big, 16)
        total = jnp.zeros((big, depth), F32)
        for row in range(3):
            for col in range(3):
                near = cols[2 - col, pl.ds(base + LINE * (2 - row), big), :]
                k = 3 * row + col
                total = total + dot_nt(near, wm[k * depth : (k + 1) * depth, :])
        ext[pl.ds(base, big), :] = total
        return carry

    lax.fori_loop(0, padded // big, step, 0)
    unpad_lines(ext, flat, rows)
    dmid1[...] = (flat[...] * s1[...]).astype(BF16)
    finish(part, outs, spot, piece)


def first_kernel(spot, x, dmid1, *rest, piece):
    outs, part = rest[:-1], rest[-1]
    for quad in range(x.shape[1] // 256):
        lanes = slice(256 * quad, 256 * (quad + 1))
        part[lanes, :] = dot_t(x[:, lanes], dmid1[...])
    finish(part, outs, spot, piece)


def input_kernel(dmid1, w1, dpre, out):
    rows = dpre.shape[0]
    chunk = chunk_of(rows, 128)

    def step(at, carry):
        here = pl.ds(pl.multiple_of(at * chunk, 16), chunk)
        out[here, :] = (dot_nt(dmid1[here, :], w1[...]) + dpre[here, :]).astype(BF16)
        return carry

    lax.fori_loop(0, rows // chunk, step, 0)


def call(kernel, outs, args, scratch=(), scalars=0, flops=0):
    specs = [pl.BlockSpec(memory_space=pltpu.SMEM)] * scalars
    specs += [pl.BlockSpec(memory_space=pltpu.VMEM)] * (len(args) - scalars)
    size = sum(a.size * a.dtype.itemsize for a in args)
    size += sum(o.size * o.dtype.itemsize for o in outs)
    return pl.pallas_call(
        kernel,
        out_shape=tuple(outs),
        in_specs=specs,
        out_specs=tuple(pl.BlockSpec(memory_space=pltpu.VMEM) for _ in outs),
        scratch_shapes=list(scratch),
        cost_estimate=pl.CostEstimate(flops=flops, bytes_accessed=size, transcendentals=0),
        compiler_params=pltpu.CompilerParams(vmem_limit_bytes=40 * 2**20),
    )(*args)


def shape(dims, dtype=F32):
    return jax.ShapeDtypeStruct(dims, dtype)


def swap(value, axis, size, flip):
    return lax.ppermute(value, axis, [(at, at ^ flip) for at in range(size)])


def halve(value, dim, mine, axis, size, flip):
    keep = lax.dynamic_index_in_dim(value, mine, dim, keepdims=False)
    send = lax.dynamic_index_in_dim(value, 1 - mine, dim, keepdims=False)
    return keep + swap(send, axis, size, flip)


def scatter_sum(keep, send, sizes, lead):
    groups, ghosts = sizes
    value = keep + swap(send, "ghost", ghosts, 1)
    names = []
    for bit in reversed(range(groups.bit_length() - 1)):
        names.append(("group", groups, bit))
    for bit in reversed(range(1, ghosts.bit_length() - 1)):
        names.append(("ghost", ghosts, bit))
    order = [n for n in names if n[0] == "ghost"]
    if lead:
        order = order[::-1]
    order = order + [n for n in names if n[0] == "group"][::-1]
    rows, lanes = value.shape
    value = value.reshape((2,) * len(names) + (rows >> len(names), lanes))
    for axis, size, bit in order:
        dim = names.index((axis, size, bit))
        mine = (lax.axis_index(axis) >> bit) & 1
        value = halve(value, dim, mine, axis, size, 1 << bit)
        names.pop(dim)
    return value


def power_of_two(value):
    return value & (value - 1) == 0


def shards(inputs, out_grad, conv_first, conv_middle, conv_last, gain):
    rows, width = inputs.shape
    mid = conv_first.shape[1]
    pairs = width // PAIR
    ghosts = lax.axis_size("ghost")
    groups = lax.axis_size("group")
    devices = ghosts * groups
    span = float(rows * ghosts)
    scale = (rows * devices) ** (-0.5)
    padded = padded_rows(rows)
    ghost = lax.axis_index("ghost")
    group = lax.axis_index("group")
    spot = jnp.stack([ghost, ghost & 1]).astype(jnp.int32)
    split = ghosts == pairs and power_of_two(ghosts)
    heights = (width, conv_middle.shape[0], mid)
    halves = power_of_two(ghosts) and power_of_two(groups) and ghosts > 1
    halves = halves and all(h % (8 * devices) == 0 for h in heights)
    unit = 2 * rows * width * mid

    ext = pltpu.VMEM((24 + padded + LINE + 8, mid), F32)
    flat = pltpu.VMEM((rows, mid), F32)
    cols = (3, padded + 2 * LINE, mid)
    big = (pairs, TALL, PAIR)
    one = (1, TALL, PAIR)

    stats_outs = [shape((TALL, PAIR))] * ghosts if split else [shape(big)]
    h1pad, s1, h2, s2, *stats = call(
        functools.partial(forward_kernel, split=split),
        [shape((padded, mid), BF16), shape((rows, mid)), shape((rows, mid), BF16),
         shape((rows, mid))] + stats_outs,
        (spot, inputs, conv_first, conv_middle, conv_last),
        (ext, pltpu.VMEM(cols, BF16), flat, pltpu.VMEM((rows, width), F32), pltpu.VMEM(big, F32)),
        scalars=1, flops=5 * unit,
    )
    if split:
        terms = [stats[0][None]]
        for flip in range(1, ghosts):
            terms.append(swap(stats[flip], "ghost", ghosts, flip)[None])
        own = one
    else:
        terms = [lax.psum(stats[0], "ghost")]
        own = big
    share, kept = call(
        functools.partial(whiten_kernel, span=span, pieces=len(terms)),
        [shape(own), shape((own[0], 2 * NEWTON + 1, PAIR, PAIR))],
        tuple(terms), flops=10**7,
    )
    given = [share]
    if split:
        for flip in range(1, ghosts):
            given.append(swap(share, "ghost", ghosts, flip))
    cen, dwb, dpre, wpairs, stats = call(
        functools.partial(backward_kernel, split=split, shares=len(given)),
        [shape((rows, width), BF16), shape((rows, width), BF16), shape((rows, width)),
         shape(big), shape(big)],
        (spot, inputs, out_grad, h2, conv_last, gain.reshape(1, width), *given),
        (pltpu.VMEM(big, F32),), scalars=1, flops=3 * unit,
    )
    if split:
        total = lax.all_to_all(stats, "ghost", 0, 0, tiled=True)
    else:
        total = lax.psum(stats, "ghost")
    (spairs,) = call(
        functools.partial(pull_kernel, span=span), [shape(big)], (total, kept), flops=10**7
    )
    if split:
        spairs = lax.all_to_all(spairs, "ghost", 0, 0, tiled=True)

    def parts(height, lanes):
        if halves:
            return [shape((height // 2, lanes))] * 2
        return [shape((height, lanes))]

    def piece(height):
        return height // devices if halves else 0

    def gather(part, lead):
        if halves:
            return (scatter_sum(*part, (groups, ghosts), lead) * scale).reshape(-1)
        flat_part = (part[0] * scale).reshape(-1)
        return lax.psum_scatter(
            flat_part, ("group", "ghost"), scatter_dimension=0, tiled=True
        )

    dcols, *last_part = call(
        functools.partial(last_kernel, piece=piece(mid)),
        [shape(cols, BF16)] + parts(mid, width),
        (spot, dwb, cen, h2, s2, conv_last, wpairs, spairs),
        (ext, flat, pltpu.VMEM((rows, width), BF16), pltpu.VMEM((mid, width), F32)),
        scalars=1, flops=4 * unit,
    )
    dmid1, *middle_part = call(
        functools.partial(middle_kernel, piece=piece(9 * mid)),
        [shape((rows, mid), BF16)] + parts(9 * mid, mid),
        (spot, dcols, h1pad, conv_middle, s1),
        (ext, flat, pltpu.VMEM((9 * mid, mid), F32)),
        scalars=1, flops=5 * unit,
    )
    first_part = call(
        functools.partial(first_kernel, piece=piece(width)),
        parts(width, mid), (spot, inputs, dmid1), (pltpu.VMEM((width, mid), F32),),
        scalars=1, flops=unit,
    )
    (input_grad,) = call(
        input_kernel, [shape((rows, width), BF16)], (dmid1, conv_first, dpre), flops=unit
    )
    gains = spairs[:, GROUP + 1, :].reshape(-1) * scale
    share = width // devices
    if split:
        table = gains.reshape(groups, ghosts * share)
        total = lax.dynamic_index_in_dim(table, group, 0, keepdims=False)
        for shift in range(1, groups):
            to = (group + shift) % groups
            sent = lax.dynamic_index_in_dim(table, to, 0, keepdims=False)
            total = total + lax.ppermute(
                sent, "group", [(at, (at + shift) % groups) for at in range(groups)]
            )
        gain_grad = lax.dynamic_slice_in_dim(total, ghost * share, share)
    else:
        gain_grad = lax.psum(gains, "group")
        gain_grad = lax.dynamic_slice_in_dim(gain_grad, (group * ghosts + ghost) * share, share)
    return (
        input_grad, gather(first_part, 0), gather(middle_part, 1), gather(last_part, 0), gain_grad
    )


def solution(mesh):
    in_specs = (P(("group", "ghost"), None), P(("group", "ghost"), None), P(), P(), P(), P())
    out_specs = (
        P(("group", "ghost"), None),
        P(("group", "ghost")),
        P(("group", "ghost")),
        P(("group", "ghost")),
        P(("group", "ghost")),
    )
    return jax.shard_map(shards, mesh=mesh, in_specs=in_specs, out_specs=out_specs, check_vma=False)
```

```python
import functools

import jax
import jax.numpy as jnp
from jax import lax
from jax.experimental import pallas as pl
from jax.experimental.pallas import tpu as pltpu
from jax.sharding import PartitionSpec as P

GROUP = 64
NEWTON = 5
SIDE = 14
LINE = 16
PAIR = 2 * GROUP
TALL = GROUP + 8
epsilon = 1e-05

F32 = jnp.float32
BF16 = jnp.bfloat16


def dot(left, right):
    return jnp.dot(left, right, preferred_element_type=F32)


def dot_t(left, right):
    return lax.dot_general(left, right, (((0,), (0,)), ((), ())), preferred_element_type=F32)


def dot_nt(left, right):
    return lax.dot_general(left, right, (((1,), (1,)), ((), ())), preferred_element_type=F32)


def exact(left, right):
    return jnp.dot(left, right, preferred_element_type=F32, precision=lax.Precision.HIGHEST)


def sigmoid(value):
    return 1.0 / (1.0 + jnp.exp(-value))


def chunk_of(rows, most):
    best = 16
    for size in range(16, most + 1, 16):
        if rows % size == 0:
            best = size
    return best


def left_half(shape):
    return lax.broadcasted_iota(jnp.int32, shape, 1) < GROUP


def spread(packed):
    left = left_half(packed.shape)
    zero = jnp.zeros_like(packed)
    return jnp.concatenate([jnp.where(left, packed, zero), jnp.where(left, zero, packed)], axis=0)


def pack(square):
    top, bottom = square[:GROUP], square[GROUP:]
    return jnp.where(left_half(top.shape), top, bottom)


def vectors(*rows):
    at = lax.broadcasted_iota(jnp.int32, (8, PAIR), 0)
    tile = jnp.zeros((8, PAIR), F32)
    for place, row in enumerate(rows):
        tile = jnp.where(at == place, row, tile)
    return tile


def fold(value):
    rows, lanes = value.shape
    return jnp.sum(value.reshape(rows // 8, 8, lanes), axis=0)


def pad_lines(source, ext, rows):
    for line in range(rows // SIDE):
        place = 24 + LINE * (line + line // SIDE)
        ext[place : place + SIDE, :] = source[SIDE * line : SIDE * (line + 1), :]


def unpad_lines(source, target, rows):
    for line in range(rows // SIDE):
        place = LINE * (line + line // SIDE)
        target[SIDE * line : SIDE * (line + 1), :] = source[place : place + SIDE, :]


def padded_rows(rows):
    return rows // (SIDE * SIDE) * (SIDE + 1) * LINE


def shifted(ext, cols):
    length = cols.shape[1]
    for col in range(3):
        cols[col] = ext[7 + col : 7 + col + length, :].astype(BF16)


def emit_split(source, keep, send, core, plan):
    for start, height, first, size, mine in plan:
        lanes = keep.shape[1]
        for wide in range(source.shape[1] // lanes):
            to = slice(start + wide * height, start + (wide + 1) * height)
            cols = slice(wide * lanes, (wide + 1) * lanes)
            for target, half in ((keep, core), (send, 1 - core)):
                place = pl.multiple_of((mine + half) * size + first, 8)
                target[to, :] = source[pl.ds(place, height), cols]


def plan_of(parts, piece, wide, groups, ghosts):
    plan = []
    start = 0
    for first, height, bits in parts:
        steps = [("ghost", bit) for bit in bits]
        steps += [("group", bit) for bit in range(groups.bit_length() - 1)]
        for at in range(2 ** len(steps)):
            source = 0
            for place, (axis, bit) in enumerate(steps):
                value = (at >> (len(steps) - 1 - place)) & 1
                source += value << bit if axis == "ghost" else (value << bit) * ghosts
            plan.append((start, height, first, piece, source))
            start += height * wide
    return plan


def half_of(left, right, bit, start=0, rows=None):
    rows = (left.shape[0] if rows is None else rows) // 2
    mine = pl.ds(pl.multiple_of(start + bit * rows, 8), rows)
    other = pl.ds(pl.multiple_of(start + (1 - bit) * rows, 8), rows)
    return left[mine, :] + right[mine, :], left[other, :] + right[other, :]


def put_pair(both, spot, pair, top, low):
    side = jnp.bitwise_xor(pair % 2, spot[1])
    place = jnp.bitwise_xor(pair // 2, lax.shift_right_logical(spot[0], 1))
    both[side, place, :GROUP, :] = top
    both[side, place, GROUP:, :] = low


def spread_kernel(keep, given, *outs):
    for at, out in enumerate(outs):
        out[...] = keep[at] + given[at]


def stack_kernel(*refs):
    for at, ref in enumerate(refs[:-1]):
        refs[-1][at] = ref[...]


def forward_kernel(spot, x, w1, wm, w3, h1pad, s1, h2, s2, *rest, split):
    rows = x.shape[0]
    outs, (ext, cols, flat, branch, stats) = rest[:-5], rest[-5:]
    chunk = chunk_of(rows, 128)
    ext[...] = jnp.zeros_like(ext)

    def first(at, carry):
        here = pl.ds(pl.multiple_of(at * chunk, 16), chunk)
        act = dot(x[here, :], w1[...])
        sig = sigmoid(act)
        flat[here, :] = act * sig
        s1[here, :] = sig * (1.0 + act * (1.0 - sig))
        return carry

    lax.fori_loop(0, rows // chunk, first, 0)
    pad_lines(flat, ext, rows)
    shifted(ext, cols)
    padded = padded_rows(rows)
    h1pad[...] = cols[1, LINE : LINE + padded, :]
    big = chunk_of(padded, 256)

    def middle(at, carry):
        base = pl.multiple_of(at * big, 16)
        total = jnp.zeros((big, wm.shape[1]), F32)
        for row in range(3):
            for col in range(3):
                left = cols[col, pl.ds(base + LINE * row, big), :]
                k = 3 * row + col
                depth = left.shape[1]
                total = total + dot(left, wm[k * depth : (k + 1) * depth, :])
        ext[pl.ds(base, big), :] = total
        return carry

    lax.fori_loop(0, padded // big, middle, 0)
    unpad_lines(ext, flat, rows)
    width = w3.shape[1]

    def last(at, total):
        here = pl.ds(pl.multiple_of(at * chunk, 16), chunk)
        act = flat[here, :]
        sig = sigmoid(act)
        hidden = (act * sig).astype(BF16)
        h2[here, :] = hidden
        s2[here, :] = sig * (1.0 + act * (1.0 - sig))
        out = dot(hidden, w3[...])
        branch[here, :] = out
        return total + fold(out)

    total = lax.fori_loop(0, rows // chunk, last, jnp.zeros((8, width), F32))
    total = jnp.sum(total, axis=0, keepdims=True)
    mean = total / rows
    for quad in range(width // 256):
        lanes = slice(256 * quad, 256 * (quad + 1))
        centered = (branch[:, lanes] - mean[:, lanes]).astype(BF16)
        square = dot_t(centered, centered)
        for half in range(2):
            pair = 2 * quad + half
            ch = slice(PAIR * pair, PAIR * (pair + 1))
            row = mean[:, ch]
            tile = vectors(row)
            outer = lax.dot_general(
                tile, tile, (((0,), (0,)), ((), ())), preferred_element_type=F32,
                precision=lax.Precision.HIGHEST,
            )
            inner = square[PAIR * half : PAIR * (half + 1), PAIR * half : PAIR * (half + 1)]
            top, low = pack(inner + outer * rows), vectors(total[:, ch])
            if split:
                put_pair(stats, spot, pair, top, low)
            else:
                stats[pair, :GROUP, :] = top
                stats[pair, GROUP:, :] = low
    for at, out in enumerate(outs):
        out[...] = stats[at] if split else stats[...]


def identity():
    shape = (PAIR, PAIR)
    return jnp.where(
        lax.broadcasted_iota(jnp.int32, shape, 0) == lax.broadcasted_iota(jnp.int32, shape, 1),
        1.0, 0.0,
    ).astype(F32)


def per_block(square):
    row_sums = jnp.sum(square, axis=1, keepdims=True)
    top = jnp.sum(row_sums[:GROUP], axis=0, keepdims=True)
    bottom = jnp.sum(row_sums[GROUP:], axis=0, keepdims=True)
    upper = lax.broadcasted_iota(jnp.int32, (PAIR, 1), 0) < GROUP
    return jnp.where(upper, top, bottom)


def whiten_one(total, span, keep, at):
    mean = total[GROUP : GROUP + 1, :] / span
    tile = vectors(mean)
    outer = lax.dot_general(
        tile, tile, (((0,), (0,)), ((), ())), preferred_element_type=F32,
        precision=lax.Precision.HIGHEST,
    )
    eye = identity()
    blocks = spread(jnp.ones((GROUP, PAIR), F32))
    cov = spread(total[:GROUP, :]) / span - outer * blocks + epsilon * eye
    trace = per_block(cov * eye)
    normed = cov / trace
    keep[at, 0] = normed
    keep[at, 1] = eye / trace
    power = 1.5 * eye - 0.5 * normed
    for sweep in range(NEWTON - 1):
        square = exact(power, power)
        side = exact(power, normed)
        keep[at, 2 + 2 * sweep] = power
        keep[at, 3 + 2 * sweep] = exact(square, power)
        power = 1.5 * power - 0.5 * exact(square, side)
    keep[at, 2 * NEWTON] = power
    return jnp.concatenate([pack(power / jnp.sqrt(trace)), vectors(mean)], axis=0)


def pull_one(total, span, keep, at):
    eye = identity()
    normed = keep[at, 0]
    inverse = per_block(keep[at, 1]) / GROUP
    cross = spread(total[:GROUP, :])
    cross = cross + cross.T
    root = jnp.sqrt(inverse)
    power = keep[at, 2 * NEWTON]
    grad = cross * root
    trace_grad = -0.5 * inverse * root * per_block(cross * power)
    normed_grad = jnp.zeros_like(grad)
    for sweep in reversed(range(NEWTON - 1)):
        power_k = keep[at, 2 + 2 * sweep]
        cubed = keep[at, 3 + 2 * sweep]
        product = exact(cubed, grad)
        normed_grad = normed_grad - 0.25 * (product + product.T)
        turned = exact(grad, normed)
        turned = exact(turned + turned.T, power_k)
        outer = exact(turned, power_k)
        inner = exact(power_k, turned)
        grad = 1.5 * grad - 0.25 * (outer + outer.T + inner)
    normed_grad = normed_grad - 0.5 * grad
    trace_grad = trace_grad - inverse * per_block(normed_grad * normed)
    both = normed_grad * inverse + eye * trace_grad
    whiten = power * root
    bias = -exact(vectors(total[GROUP : GROUP + 1, :] / span), whiten.T)
    return jnp.concatenate(
        [pack(both / span), vectors(bias[0:1, :], total[GROUP + 1 : GROUP + 2, :])], axis=0
    )


def total_of(terms, at):
    if len(terms) == 1:
        return terms[0][at]
    total = terms[0][...]
    for term in terms[1:]:
        total = total + term[...]
    return total


def whiten_kernel(*refs, span):
    terms, (out, keep) = refs[:-2], refs[-2:]
    for at in range(keep.shape[0]):
        result = whiten_one(total_of(terms, at), span, keep, at)
        if len(terms) == 1:
            out[at] = result
        else:
            out[...] = result


def pull_kernel(*refs, span):
    terms, (keep, out) = refs[:-2], refs[-2:]
    for at in range(keep.shape[0]):
        result = pull_one(total_of(terms, at), span, keep, at)
        if len(terms) == 1:
            out[at] = result
        else:
            out[...] = result


def place_pairs(spot, given, pairs, split):
    if split:
        for side, shares in enumerate(given):
            for at in range(shares.shape[0]):
                chip = jnp.bitwise_xor(at, lax.shift_right_logical(spot[0], 1))
                pairs[2 * chip + jnp.bitwise_xor(side, spot[1])] = shares[at]
    else:
        pairs[...] = given[0][...]


def quad_matrix(pairs, quad):
    zero = jnp.zeros((PAIR, PAIR), F32)
    first = spread(pairs[2 * quad, :GROUP, :])
    second = spread(pairs[2 * quad + 1, :GROUP, :])
    top = jnp.concatenate([first, zero], axis=1)
    bottom = jnp.concatenate([zero, second], axis=1)
    return jnp.concatenate([top, bottom], axis=0).astype(BF16)


def row_of(pairs, quad, place):
    at = GROUP + place
    return jnp.concatenate(
        [pairs[2 * quad, at : at + 1, :], pairs[2 * quad + 1, at : at + 1, :]], axis=1
    )


def backward_kernel(spot, x, og, h2, w3, gain, *rest, split, shares):
    given, rest = rest[:shares], rest[shares:]
    (cen, dwb, dpre_out, w_out), outs, (pairs, stats) = rest[:4], rest[4:-2], rest[-2:]
    rows, width = x.shape
    place_pairs(spot, given, pairs, split)
    w_out[...] = pairs[...]
    chunk = chunk_of(rows, 128)
    for quad in range(width // 256):
        lanes = slice(256 * quad, 256 * (quad + 1))
        whiten = quad_matrix(pairs, quad)
        mean = row_of(pairs, quad, 0)
        scale = gain[:, lanes]

        def step(at, carry, lanes=lanes, whiten=whiten, mean=mean, scale=scale):
            col_sum, gain_sum = carry
            here = pl.ds(pl.multiple_of(at * chunk, 16), chunk)
            centered = (dot(h2[here, :], w3[:, lanes]) - mean).astype(BF16)
            cen[here, lanes] = centered
            white = dot(centered, whiten)
            pre = x[here, lanes].astype(F32) + scale * white
            sig = sigmoid(pre)
            dpre = og[here, lanes].astype(F32) * (sig * (1.0 + pre * (1.0 - sig)))
            dpre_out[here, lanes] = dpre
            dwhite = scale * dpre
            dwb[here, lanes] = dwhite.astype(BF16)
            return col_sum + fold(dwhite), gain_sum + fold(dpre * white)

        zero = jnp.zeros((8, 256), F32)
        col_sum, gain_sum = lax.fori_loop(0, rows // chunk, step, (zero, zero))
        col_sum = jnp.sum(col_sum, axis=0, keepdims=True)
        gain_sum = jnp.sum(gain_sum, axis=0, keepdims=True)
        square = dot_t(cen[:, lanes], dwb[:, lanes])
        for half in range(2):
            ch = slice(PAIR * half, PAIR * (half + 1))
            pair = 2 * quad + half
            top, low = pack(square[ch, ch]), vectors(col_sum[:, ch], gain_sum[:, ch])
            if split:
                put_pair(stats, spot, pair, top, low)
            else:
                stats[pair, :GROUP, :] = top
                stats[pair, GROUP:, :] = low
    for at, out in enumerate(outs):
        out[...] = stats[at] if split else stats[...]


def last_kernel(spot, dwb, cen, h2, s2, w3, wpairs, *rest, plan, split, shares):
    given, rest = rest[:shares], rest[shares:]
    (cols, gains), outs, (ext, flat, dbranch, part, spairs) = rest[:2], rest[2:-5], rest[-5:]
    place_pairs(spot, given, spairs, split)
    gains[...] = spairs[:, GROUP + 1, :]
    rows, width = dwb.shape
    chunk = chunk_of(rows, 128)
    ext[...] = jnp.zeros_like(ext)
    for quad in range(width // 256):
        lanes = slice(256 * quad, 256 * (quad + 1))
        whiten = quad_matrix(wpairs, quad)
        sym = quad_matrix(spairs, quad)
        bias = row_of(spairs, quad, 0)

        def step(at, carry, lanes=lanes, whiten=whiten, sym=sym, bias=bias):
            here = pl.ds(pl.multiple_of(at * chunk, 16), chunk)
            value = dot_nt(dwb[here, lanes], whiten) + dot(cen[here, lanes], sym) + bias
            dbranch[here, lanes] = value.astype(BF16)
            return carry

        lax.fori_loop(0, rows // chunk, step, 0)

    def middle(at, carry):
        here = pl.ds(pl.multiple_of(at * chunk, 16), chunk)
        flat[here, :] = dot_nt(dbranch[here, :], w3[...]) * s2[here, :]
        return carry

    lax.fori_loop(0, rows // chunk, middle, 0)
    pad_lines(flat, ext, rows)
    shifted(ext, cols)
    for quad in range(width // 256):
        lanes = slice(256 * quad, 256 * (quad + 1))
        part[:, lanes] = dot_t(h2[...], dbranch[:, lanes])
    finish(part, outs, spot, plan)


def finish(part, outs, spot, plan):
    if plan:
        emit_split(part, outs[0], outs[1], spot[1], plan)
    else:
        outs[0][...] = part[...]


def slope_kernel(spot, cols, wm, s1, x, dmid1, *rest, plan):
    outs, (ext, flat, part) = rest[:-3], rest[-3:]
    rows, depth = s1.shape
    padded = padded_rows(rows)
    big = chunk_of(padded, 256)

    def step(at, carry):
        base = pl.multiple_of(at * big, 16)
        total = jnp.zeros((big, depth), F32)
        for row in range(3):
            for col in range(3):
                near = cols[2 - col, pl.ds(base + LINE * (2 - row), big), :]
                k = 3 * row + col
                total = total + dot_nt(near, wm[k * depth : (k + 1) * depth, :])
        ext[pl.ds(base, big), :] = total
        return carry

    lax.fori_loop(0, padded // big, step, 0)
    unpad_lines(ext, flat, rows)
    dmid1[...] = (flat[...] * s1[...]).astype(BF16)
    for quad in range(x.shape[1] // 256):
        lanes = slice(256 * quad, 256 * (quad + 1))
        part[lanes, :] = dot_t(x[:, lanes], dmid1[...])
    finish(part, outs, spot, plan)


def middle_kernel(spot, cols, h1pad, *rest, plan):
    outs, part = rest[:-1], rest[-1]
    padded, depth = h1pad.shape
    for row in range(3):
        for col in range(3):
            k = 3 * row + col
            near = cols[2 - col, LINE * (2 - row) : LINE * (2 - row) + padded, :]
            part[k * depth : (k + 1) * depth, :] = dot_t(h1pad[...], near)
    finish(part, outs, spot, plan)


def pair_step(spot, left_keep, left_given, right_keep, right_given, *outs, bits):
    given = ((left_keep, left_given, bits[0]), (right_keep, right_given, bits[1]))
    for at, (keep, got, bit) in enumerate(given):
        outs[2 * at][...], outs[2 * at + 1][...] = half_of(keep, got, spot[bit])


def open_step(spot, keep, given, *outs, cut, bits):
    rows = keep.shape[0]
    spans = ((0, cut), (cut, rows - cut))
    for at, ((start, size), bit) in enumerate(zip(spans, bits)):
        outs[2 * at][...], outs[2 * at + 1][...] = half_of(keep, given, spot[bit], start, size)


def join_step(spot, left_keep, left_given, right_keep, right_given, *outs, bit):
    at = 0
    for keep, got in ((left_keep, left_given), (right_keep, right_given)):
        mine, other = half_of(keep, got, spot[bit])
        outs[0][at : at + mine.shape[0], :] = mine
        outs[1][at : at + mine.shape[0], :] = other
        at += mine.shape[0]


def last_step(spot, keep, given, *outs, spans, bit):
    to = 0
    for start, size in spans:
        mine, other = half_of(keep, given, spot[bit], start, size)
        outs[0][to : to + size // 2, :] = mine
        outs[1][to : to + size // 2, :] = other
        to += size // 2


def input_kernel(dmid1, w1, dpre, out):
    rows = dpre.shape[0]
    chunk = chunk_of(rows, 128)

    def step(at, carry):
        here = pl.ds(pl.multiple_of(at * chunk, 16), chunk)
        out[here, :] = (dot_nt(dmid1[here, :], w1[...]) + dpre[here, :]).astype(BF16)
        return carry

    lax.fori_loop(0, rows // chunk, step, 0)


def call(kernel, outs, args, scratch=(), scalars=0, flops=0, ties=()):
    args = tuple(args) + tuple(ties)
    specs = [pl.BlockSpec(memory_space=pltpu.SMEM)] * scalars
    specs += [pl.BlockSpec(memory_space=pltpu.VMEM)] * (len(args) - scalars - len(ties))
    specs += [pl.BlockSpec(memory_space=pl.ANY)] * len(ties)
    count = len(args) - len(ties)

    def body(*refs):
        kernel(*refs[:count], *refs[len(args) :])

    size = sum(a.size * a.dtype.itemsize for a in args)
    size += sum(o.size * o.dtype.itemsize for o in outs)
    return pl.pallas_call(
        body,
        out_shape=tuple(outs),
        in_specs=specs,
        out_specs=tuple(pl.BlockSpec(memory_space=pltpu.VMEM) for _ in outs),
        scratch_shapes=list(scratch),
        cost_estimate=pl.CostEstimate(flops=flops, bytes_accessed=size, transcendentals=0),
        compiler_params=pltpu.CompilerParams(vmem_limit_bytes=40 * 2**20),
    )(*args)


def shape(dims, dtype=F32):
    return jax.ShapeDtypeStruct(dims, dtype)


def swap(value, axis, size, flip):
    return lax.ppermute(value, axis, [(at, at ^ flip) for at in range(size)])


def shards(inputs, out_grad, conv_first, conv_middle, conv_last, gain):
    rows, width = inputs.shape
    mid = conv_first.shape[1]
    pairs = width // PAIR
    ghosts = lax.axis_size("ghost")
    groups = lax.axis_size("group")
    devices = ghosts * groups
    span = float(rows * ghosts)
    scale = (rows * devices) ** (-0.5)
    padded = padded_rows(rows)
    ghost = lax.axis_index("ghost")
    group = lax.axis_index("group")
    bits = [ghost] + [(ghost >> bit) & 1 for bit in range(3)]
    bits += [(group >> bit) & 1 for bit in range(2)]
    spot = jnp.stack(bits).astype(jnp.int32)
    core, across, along, near, far = 1, 2, 3, 4, 5
    split = ghosts == 8 and pairs == 8 and groups == 4
    unit = 2 * rows * width * mid

    ext = pltpu.VMEM((24 + padded + LINE + 8, mid), F32)
    flat = pltpu.VMEM((rows, mid), F32)
    cols = (3, padded + 2 * LINE, mid)
    big = (pairs, TALL, PAIR)
    one = (TALL, PAIR)
    half = (pairs // 2,) + one
    stats_outs = [shape(half)] * 2 if split else [shape(big)]
    stats_held = pltpu.VMEM((2,) + half if split else big, F32)

    def collect(stats):
        if not split:
            return [lax.psum(stats[0], "ghost")]
        keep, send = stats
        own, *others = call(
            spread_kernel, [shape(one)] * 4, (keep, swap(send, "ghost", ghosts, 1))
        )
        return [own] + [
            swap(other, "ghost", ghosts, 2 * (at + 1)) for at, other in enumerate(others)
        ]

    def share_out(own):
        if not split:
            return [own]
        terms = [own] + [swap(own, "ghost", ghosts, 2 * flip) for flip in (1, 2, 3)]
        (mine,) = call(stack_kernel, [shape(half)], terms)
        return [mine, swap(mine, "ghost", ghosts, 1)]

    own = one if split else big
    held = 1 if split else pairs
    h1pad, s1, h2, s2, *stats = call(
        functools.partial(forward_kernel, split=split),
        [shape((padded, mid), BF16), shape((rows, mid)), shape((rows, mid), BF16),
         shape((rows, mid))] + stats_outs,
        (spot, inputs, conv_first, conv_middle, conv_last),
        (ext, pltpu.VMEM(cols, BF16), flat, pltpu.VMEM((rows, width), F32), stats_held),
        scalars=1, flops=5 * unit,
    )
    share, kept = call(
        functools.partial(whiten_kernel, span=span),
        [shape(own), shape((held, 2 * NEWTON + 1, PAIR, PAIR))], collect(stats), flops=10**7,
    )
    given = share_out(share)
    cen, dwb, dpre, wpairs, *stats = call(
        functools.partial(backward_kernel, split=split, shares=len(given)),
        [shape((rows, width), BF16), shape((rows, width), BF16), shape((rows, width)),
         shape(big)] + stats_outs,
        (spot, inputs, out_grad, h2, conv_last, gain.reshape(1, width), *given),
        (pltpu.VMEM(big, F32), stats_held), scalars=1, flops=3 * unit,
    )
    (pulled,) = call(
        functools.partial(pull_kernel, span=span), [shape(own)], (*collect(stats), kept),
        flops=10**7,
    )
    given = share_out(pulled)

    def parts(height, lanes):
        if split:
            return [shape((height * lanes // 512, 256))] * 2
        return [shape((height, lanes))]

    def plan(height, wide, order):
        if not split:
            return None
        piece = height // devices
        if len(order) == 1:
            return plan_of([(0, piece, order[0])], piece, wide, groups, ghosts)
        cut = piece // 16 * 8 + 8 * (piece // 8 % 2)
        return plan_of(
            [(0, cut, order[0]), (cut, piece - cut, order[1])], piece, wide, groups, ghosts
        )

    dcols, gains, *last_part = call(
        functools.partial(
            last_kernel, plan=plan(mid, width // 256, ((1, 2),)), split=split, shares=len(given)
        ),
        [shape(cols, BF16), shape((pairs, PAIR))] + parts(mid, width),
        (spot, dwb, cen, h2, s2, conv_last, wpairs, *given),
        (ext, flat, pltpu.VMEM((rows, width), BF16), pltpu.VMEM((mid, width), F32),
         pltpu.VMEM(big, F32)),
        scalars=1, flops=4 * unit,
    )
    dmid1, *first_part = call(
        functools.partial(slope_kernel, plan=plan(width, 1, ((2, 1),))),
        [shape((rows, mid), BF16)] + parts(width, mid),
        (spot, dcols, conv_middle, s1, inputs),
        (ext, flat, pltpu.VMEM((width, mid), F32)), scalars=1, flops=4 * unit,
    )
    middle_part = call(
        functools.partial(middle_kernel, plan=plan(9 * mid, 1, ((1, 2), (2, 1)))),
        parts(9 * mid, mid), (spot, dcols, h1pad), (pltpu.VMEM((9 * mid, mid), F32),),
        scalars=1, flops=3 * unit,
    )
    gains = gains.reshape(-1) * scale
    portion = width // devices
    if not split:
        (input_grad,) = call(
            input_kernel, [shape((rows, width), BF16)], (dmid1, conv_first, dpre), flops=unit
        )
        grads = [
            lax.psum_scatter(
                (part[0] * scale).reshape(-1), ("group", "ghost"), scatter_dimension=0, tiled=True
            )
            for part in (first_part, middle_part, last_part)
        ]
        gain_grad = lax.dynamic_slice_in_dim(
            lax.psum(gains, "group"), (group * ghosts + ghost) * portion, portion
        )
        return (input_grad, *grads, gain_grad)

    def rows_of(height):
        return shape((height, 256))

    def step(kernel, heights, *args, ties=()):
        return call(
            kernel, [rows_of(h) for h in heights for _ in range(2)], (spot,) + args, scalars=1,
            ties=ties,
        )

    last_keep, last_send = last_part
    first_keep, first_send = first_part
    middle_keep, middle_send = middle_part
    last_rows, first_rows = last_keep.shape[0], first_keep.shape[0]
    middle_rows = middle_keep.shape[0]
    cut = 16 * plan(9 * mid, 1, ((1, 2), (2, 1)))[0][1]
    last_got = swap(last_send, "ghost", ghosts, 1)
    first_got = swap(first_send, "ghost", ghosts, 1)
    middle_got = swap(middle_send, "ghost", ghosts, 1)
    last_keep, last_send, first_keep, first_send = step(
        functools.partial(pair_step, bits=(across, along)), (last_rows // 2, first_rows // 2),
        last_keep, last_got, first_keep, first_got,
    )
    (input_grad,) = call(
        input_kernel, [shape((rows, width), BF16)], (dmid1, conv_first, dpre), flops=unit,
        ties=(last_keep,),
    )
    last_got = swap(last_send, "ghost", ghosts, 2)
    first_got = swap(first_send, "ghost", ghosts, 4)
    one_keep, one_send, two_keep, two_send = step(
        functools.partial(open_step, cut=cut, bits=(across, along)),
        (cut // 2, (middle_rows - cut) // 2), middle_keep, middle_got, ties=(input_grad,),
    )
    one_got = swap(one_send, "ghost", ghosts, 2)
    two_got = swap(two_send, "ghost", ghosts, 4)
    last_keep, last_send, first_keep, first_send = step(
        functools.partial(pair_step, bits=(along, across)), (last_rows // 4, first_rows // 4),
        last_keep, last_got, first_keep, first_got, ties=(one_keep,),
    )
    last_got = swap(last_send, "ghost", ghosts, 4)
    first_got = swap(first_send, "ghost", ghosts, 2)
    low_keep, low_send = step(
        functools.partial(join_step, bit=near), ((last_rows + first_rows) // 8,),
        last_keep, last_got, first_keep, first_got,
    )
    low_got = swap(low_send, "group", groups, 1)
    one_keep, one_send, two_keep, two_send = step(
        functools.partial(pair_step, bits=(along, across)), (cut // 4, (middle_rows - cut) // 4),
        one_keep, one_got, two_keep, two_got, ties=(low_keep,),
    )
    one_got = swap(one_send, "ghost", ghosts, 4)
    two_got = swap(two_send, "ghost", ghosts, 2)
    spans = ((0, last_rows // 8), (last_rows // 8, first_rows // 8))
    low_keep, low_send = step(
        functools.partial(last_step, spans=spans, bit=far), ((last_rows + first_rows) // 16,),
        low_keep, low_got, ties=(one_keep,),
    )
    low_got = swap(low_send, "group", groups, 2)
    high_keep, high_send = step(
        functools.partial(join_step, bit=near), (middle_rows // 8,),
        one_keep, one_got, two_keep, two_got, ties=(low_keep,),
    )
    high_got = swap(high_send, "group", groups, 1)
    spans = ((0, cut // 8), (cut // 8, (middle_rows - cut) // 8))
    high_keep, high_send = step(
        functools.partial(last_step, spans=spans, bit=far), (middle_rows // 16,),
        high_keep, high_got,
    )
    high_got = swap(high_send, "group", groups, 2)
    low = (low_keep + low_got) * scale
    tall = last_rows // 16
    wide = width // 256
    last_grad = low[:tall].reshape(wide, tall // wide, 256).swapaxes(0, 1).reshape(-1)
    first_grad = low[tall:].reshape(-1)
    middle_grad = ((high_keep + high_got) * scale).reshape(-1)

    table = gains.reshape(groups, ghosts * portion)
    total = lax.dynamic_index_in_dim(table, group, 0, keepdims=False)
    for shift in range(1, groups):
        to = (group + shift) % groups
        sent = lax.dynamic_index_in_dim(table, to, 0, keepdims=False)
        total = total + lax.ppermute(
            sent, "group", [(at, (at + shift) % groups) for at in range(groups)]
        )
    gain_grad = lax.dynamic_slice_in_dim(total, ghost * portion, portion)
    return (input_grad, first_grad, middle_grad, last_grad, gain_grad)


def solution(mesh):
    in_specs = (P(("group", "ghost"), None), P(("group", "ghost"), None), P(), P(), P(), P())
    out_specs = (
        P(("group", "ghost"), None),
        P(("group", "ghost")),
        P(("group", "ghost")),
        P(("group", "ghost")),
        P(("group", "ghost")),
    )
    return jax.shard_map(shards, mesh=mesh, in_specs=in_specs, out_specs=out_specs, check_vma=False)
```

```python
import functools

import jax
import jax.numpy as jnp
from jax import lax
from jax.experimental import pallas as pl
from jax.experimental.pallas import tpu as pltpu
from jax.sharding import PartitionSpec as P

GROUP = 64
NEWTON = 5
SIDE = 14
LINE = 16
PAIR = 2 * GROUP
TALL = GROUP + 8
epsilon = 1e-05

F32 = jnp.float32
BF16 = jnp.bfloat16


def dot(left, right):
    return jnp.dot(left, right, preferred_element_type=F32)


def dot_t(left, right):
    return lax.dot_general(left, right, (((0,), (0,)), ((), ())), preferred_element_type=F32)


def dot_nt(left, right):
    return lax.dot_general(left, right, (((1,), (1,)), ((), ())), preferred_element_type=F32)


def halves_of(value):
    high = value.astype(BF16)
    return high, (value - high.astype(F32)).astype(BF16)


def exact(left, right):
    a, b = halves_of(left)
    c, d = halves_of(right)
    low = dot(jnp.concatenate([a, b], axis=1), jnp.concatenate([d, c], axis=0))
    return low + dot(a, c)


def outer_of(row):
    tile = vectors(row)
    return lax.dot_general(
        tile, tile, (((0,), (0,)), ((), ())), preferred_element_type=F32,
        precision=lax.Precision.HIGHEST,
    )


def sigmoid(value):
    return 1.0 / (1.0 + jnp.exp(-value))


def chunk_of(rows, most):
    best = 16
    for size in range(16, most + 1, 16):
        if rows % size == 0:
            best = size
    return best


def left_half(shape):
    return lax.broadcasted_iota(jnp.int32, shape, 1) < GROUP


def spread(packed):
    left = left_half(packed.shape)
    zero = jnp.zeros_like(packed)
    return jnp.concatenate([jnp.where(left, packed, zero), jnp.where(left, zero, packed)], axis=0)


def pack(square):
    top, bottom = square[:GROUP], square[GROUP:]
    return jnp.where(left_half(top.shape), top, bottom)


def vectors(*rows):
    at = lax.broadcasted_iota(jnp.int32, (8, PAIR), 0)
    tile = jnp.zeros((8, PAIR), F32)
    for place, row in enumerate(rows):
        tile = jnp.where(at == place, row, tile)
    return tile


def fold(value):
    rows, lanes = value.shape
    return jnp.sum(value.reshape(rows // 8, 8, lanes), axis=0)


def pad_lines(source, ext, rows):
    for line in range(rows // SIDE):
        place = 24 + LINE * (line + line // SIDE)
        ext[place : place + SIDE, :] = source[SIDE * line : SIDE * (line + 1), :]


def unpad_lines(source, target, rows):
    for line in range(rows // SIDE):
        place = LINE * (line + line // SIDE)
        target[SIDE * line : SIDE * (line + 1), :] = source[place : place + SIDE, :]


def padded_rows(rows):
    return rows // (SIDE * SIDE) * (SIDE + 1) * LINE


def shifted(ext, cols):
    length = cols.shape[1]
    for col in range(3):
        cols[col] = ext[7 + col : 7 + col + length, :].astype(BF16)


def emit_split(source, keep, send, core, plan):
    for start, height, first, size, mine in plan:
        lanes = keep.shape[1]
        for wide in range(source.shape[1] // lanes):
            to = slice(start + wide * height, start + (wide + 1) * height)
            cols = slice(wide * lanes, (wide + 1) * lanes)
            for target, half in ((keep, core), (send, 1 - core)):
                place = pl.multiple_of((mine + half) * size + first, 8)
                target[to, :] = source[pl.ds(place, height), cols]


def plan_of(parts, piece, wide, groups, ghosts):
    plan = []
    start = 0
    for first, height, bits in parts:
        steps = [("ghost", bit) for bit in bits]
        steps += [("group", bit) for bit in range(groups.bit_length() - 1)]
        for at in range(2 ** len(steps)):
            source = 0
            for place, (axis, bit) in enumerate(steps):
                value = (at >> (len(steps) - 1 - place)) & 1
                source += value << bit if axis == "ghost" else (value << bit) * ghosts
            plan.append((start, height, first, piece, source))
            start += height * wide
    return plan


def half_of(left, right, bit, start=0, rows=None):
    rows = (left.shape[0] if rows is None else rows) // 2
    mine = pl.ds(pl.multiple_of(start + bit * rows, 8), rows)
    other = pl.ds(pl.multiple_of(start + (1 - bit) * rows, 8), rows)
    return left[mine, :] + right[mine, :], left[other, :] + right[other, :]


def emit_pairs(stats, outs, spot):
    shape = (GROUP, PAIR)
    row = lax.broadcasted_iota(jnp.int32, shape, 0)
    lane = lax.broadcasted_iota(jnp.int32, shape, 1)
    left = lane < GROUP
    col = jnp.where(left, lane, lane - GROUP)
    for parity in range(2):
        for slot in range(stats.shape[0] // 4):
            pair = 4 * slot + parity, 4 * slot + 2 + parity
            first, second = (stats[p, :GROUP, :] for p in pair)
            upper = jnp.where(left, first, pltpu.roll(second, GROUP, 1))
            lower = jnp.where(left, pltpu.roll(first, GROUP, 1), second)
            rows = [
                jnp.sum(jnp.where(row == col, m, 0.0), axis=0, keepdims=True)
                for m in (first, second)
            ]
            for place in range(2):
                rows += [stats[p, GROUP + place : GROUP + place + 1, :] for p in pair]
            both = jnp.concatenate([jnp.where(row <= col, upper, lower), vectors(*rows)], axis=0)

            @pl.when(spot[1] == parity)
            def _(both=both, slot=slot):
                outs[0][slot] = both

            @pl.when(spot[1] != parity)
            def _(both=both, slot=slot):
                outs[1][slot] = both


def take_pairs(total, packed):
    result = []
    if not packed:
        for at in range(total.shape[0]):
            vecs = [total[at, GROUP + p : GROUP + p + 1, :] for p in range(2)]
            result.append((spread(total[at, :GROUP, :]), *vecs))
        return result
    shape = (PAIR, PAIR)
    row = lax.broadcasted_iota(jnp.int32, shape, 0)
    col = lax.broadcasted_iota(jnp.int32, shape, 1)
    mask = jnp.where(row < GROUP, row - col, col - row) < 0
    eye = identity()
    for slot in range(total.shape[0]):
        both = total[slot, :GROUP, :]
        turned = pltpu.roll(both, GROUP, 1)
        left = left_half(both.shape)
        for at in range(2):
            twice = jnp.where(left, *((both, turned) if at == 0 else (turned, both)))
            part = jnp.where(mask, spread(twice), 0.0)
            line = [total[slot, GROUP + 2 * p + at : GROUP + 2 * p + at + 1, :] for p in range(3)]
            result.append((part + part.T + eye * line[0], line[1], line[2]))
    return result


def add_kernel(left, right, out):
    out[...] = left[...] + right[...]


def forward_kernel(spot, x, w1, wm, w3, h1pad, s1, h2, s2, *rest, split):
    rows = x.shape[0]
    outs, (ext, cols, flat, branch, stats) = rest[:-5], rest[-5:]
    chunk = chunk_of(rows, 128)
    ext[...] = jnp.zeros_like(ext)

    def first(at, carry):
        here = pl.ds(pl.multiple_of(at * chunk, 16), chunk)
        act = dot(x[here, :], w1[...])
        sig = sigmoid(act)
        flat[here, :] = act * sig
        s1[here, :] = sig * (1.0 + act * (1.0 - sig))
        return carry

    lax.fori_loop(0, rows // chunk, first, 0)
    pad_lines(flat, ext, rows)
    shifted(ext, cols)
    padded = padded_rows(rows)
    h1pad[...] = cols[1, LINE : LINE + padded, :]
    big = chunk_of(padded, 256)

    def middle(at, carry):
        base = pl.multiple_of(at * big, 16)
        total = jnp.zeros((big, wm.shape[1]), F32)
        for row in range(3):
            for col in range(3):
                left = cols[col, pl.ds(base + LINE * row, big), :]
                k = 3 * row + col
                depth = left.shape[1]
                total = total + dot(left, wm[k * depth : (k + 1) * depth, :])
        ext[pl.ds(base, big), :] = total
        return carry

    lax.fori_loop(0, padded // big, middle, 0)
    unpad_lines(ext, flat, rows)
    width = w3.shape[1]

    def last(at, total):
        here = pl.ds(pl.multiple_of(at * chunk, 16), chunk)
        act = flat[here, :]
        sig = sigmoid(act)
        hidden = (act * sig).astype(BF16)
        h2[here, :] = hidden
        s2[here, :] = sig * (1.0 + act * (1.0 - sig))
        out = dot(hidden, w3[...])
        branch[here, :] = out
        return total + fold(out)

    total = lax.fori_loop(0, rows // chunk, last, jnp.zeros((8, width), F32))
    total = jnp.sum(total, axis=0, keepdims=True)
    mean = total / rows
    for quad in range(width // 256):
        lanes = slice(256 * quad, 256 * (quad + 1))
        centered = (branch[:, lanes] - mean[:, lanes]).astype(BF16)
        square = dot_t(centered, centered)
        for half in range(2):
            pair = 2 * quad + half
            ch = slice(PAIR * pair, PAIR * (pair + 1))
            row = mean[:, ch]
            outer = outer_of(row)
            inner = square[PAIR * half : PAIR * (half + 1), PAIR * half : PAIR * (half + 1)]
            top, low = pack(inner + outer * rows), vectors(total[:, ch])
            stats[pair, :GROUP, :] = top
            stats[pair, GROUP:, :] = low
    if split:
        emit_pairs(stats, outs, spot)
    else:
        outs[0][...] = stats[...]


def identity():
    shape = (PAIR, PAIR)
    return jnp.where(
        lax.broadcasted_iota(jnp.int32, shape, 0) == lax.broadcasted_iota(jnp.int32, shape, 1),
        1.0, 0.0,
    ).astype(F32)


def per_block(square):
    row_sums = jnp.sum(square, axis=1, keepdims=True)
    top = jnp.sum(row_sums[:GROUP], axis=0, keepdims=True)
    bottom = jnp.sum(row_sums[GROUP:], axis=0, keepdims=True)
    upper = lax.broadcasted_iota(jnp.int32, (PAIR, 1), 0) < GROUP
    return jnp.where(upper, top, bottom)


def total_of(terms):
    total = terms[0][...]
    for term in terms[1:]:
        total = total + term[...]
    return total


def whiten_kernel(*refs, span, packed):
    terms, (out, keep) = refs[:-2], refs[-2:]
    given = take_pairs(total_of(terms), packed)
    eye = identity()
    blocks = spread(jnp.ones((GROUP, PAIR), F32))
    means = [sums / span for _, sums, _ in given]
    covs = [
        moments / span - outer_of(mean) * blocks + epsilon * eye
        for (moments, _, _), mean in zip(given, means)
    ]
    traces = [per_block(cov * eye) for cov in covs]
    normed = [cov / trace for cov, trace in zip(covs, traces)]
    powers = [1.5 * eye - 0.5 * norm for norm in normed]
    for at, trace in enumerate(traces):
        keep[at, 0] = normed[at]
        keep[at, 1] = eye / trace
    for sweep in range(NEWTON - 1):
        squares = [exact(power, power) for power in powers]
        sides = [exact(power, norm) for power, norm in zip(powers, normed)]
        for at, power in enumerate(powers):
            keep[at, 2 + 2 * sweep] = power
            keep[at, 3 + 2 * sweep] = squares[at]
        powers = [
            1.5 * power - 0.5 * exact(square, side)
            for power, square, side in zip(powers, squares, sides)
        ]
    for at, power in enumerate(powers):
        keep[at, 2 * NEWTON] = power
        out[at, :GROUP, :] = pack(power / jnp.sqrt(traces[at]))
        out[at, GROUP:, :] = vectors(means[at])


def pull_kernel(*refs, span, packed):
    terms, (keep, out) = refs[:-2], refs[-2:]
    given = take_pairs(total_of(terms), packed)
    eye = identity()
    every = range(len(given))
    normed = [keep[at, 0] for at in every]
    inverse = [per_block(keep[at, 1]) / GROUP for at in every]
    roots = [jnp.sqrt(value) for value in inverse]
    powers = [keep[at, 2 * NEWTON] for at in every]
    grads = [given[at][0] * roots[at] for at in every]
    trace_grads = [
        -0.5 * inverse[at] * roots[at] * per_block(given[at][0] * powers[at]) for at in every
    ]
    normed_grads = [jnp.zeros_like(grads[0])] * len(given)
    for sweep in reversed(range(NEWTON - 1)):
        power = [keep[at, 2 + 2 * sweep] for at in every]
        turned = [exact(grads[at], normed[at]) for at in every]
        inner = [exact(power[at], grads[at]) for at in every]
        turned = [exact(turned[at] + turned[at].T, power[at]) for at in every]
        inner = [exact(keep[at, 3 + 2 * sweep], inner[at]) for at in every]
        normed_grads = [normed_grads[at] - 0.25 * (inner[at] + inner[at].T) for at in every]
        outer = [exact(turned[at], power[at]) for at in every]
        inner = [exact(power[at], turned[at]) for at in every]
        grads = [
            1.5 * grads[at] - 0.25 * (outer[at] + outer[at].T + inner[at]) for at in every
        ]
    for at in every:
        normed_grad = normed_grads[at] - 0.5 * grads[at]
        trace_grad = trace_grads[at] - inverse[at] * per_block(normed_grad * normed[at])
        both = normed_grad * inverse[at] + eye * trace_grad
        bias = -exact(vectors(given[at][1] / span), (powers[at] * roots[at]).T)
        out[at, :GROUP, :] = pack(both / span)
        out[at, GROUP:, :] = vectors(bias[0:1, :], given[at][2])


def place_pairs(spot, given, pairs, split):
    if split:
        for side, shares in enumerate(given):
            for at in range(shares.shape[0]):
                pairs[2 * at + jnp.bitwise_xor(side, spot[1])] = shares[at]
    else:
        pairs[...] = given[0][...]


def quad_matrix(pairs, quad):
    zero = jnp.zeros((PAIR, PAIR), F32)
    first = spread(pairs[2 * quad, :GROUP, :])
    second = spread(pairs[2 * quad + 1, :GROUP, :])
    top = jnp.concatenate([first, zero], axis=1)
    bottom = jnp.concatenate([zero, second], axis=1)
    return jnp.concatenate([top, bottom], axis=0).astype(BF16)


def row_of(pairs, quad, place):
    at = GROUP + place
    return jnp.concatenate(
        [pairs[2 * quad, at : at + 1, :], pairs[2 * quad + 1, at : at + 1, :]], axis=1
    )


def backward_kernel(spot, x, og, h2, w3, gain, *rest, split, shares):
    given, rest = rest[:shares], rest[shares:]
    (cen, dwb, dpre_out, w_out), outs, (pairs, stats) = rest[:4], rest[4:-2], rest[-2:]
    rows, width = x.shape
    place_pairs(spot, given, pairs, split)
    w_out[...] = pairs[...]
    chunk = chunk_of(rows, 128)
    for quad in range(width // 256):
        lanes = slice(256 * quad, 256 * (quad + 1))
        whiten = quad_matrix(pairs, quad)
        mean = row_of(pairs, quad, 0)
        scale = gain[:, lanes]

        def step(at, carry, lanes=lanes, whiten=whiten, mean=mean, scale=scale):
            col_sum, gain_sum = carry
            here = pl.ds(pl.multiple_of(at * chunk, 16), chunk)
            centered = (dot(h2[here, :], w3[:, lanes]) - mean).astype(BF16)
            cen[here, lanes] = centered
            white = dot(centered, whiten)
            pre = x[here, lanes].astype(F32) + scale * white
            sig = sigmoid(pre)
            dpre = og[here, lanes].astype(F32) * (sig * (1.0 + pre * (1.0 - sig)))
            dpre_out[here, lanes] = dpre
            dwhite = scale * dpre
            dwb[here, lanes] = dwhite.astype(BF16)
            return col_sum + fold(dwhite), gain_sum + fold(dpre * white)

        zero = jnp.zeros((8, 256), F32)
        col_sum, gain_sum = lax.fori_loop(0, rows // chunk, step, (zero, zero))
        col_sum = jnp.sum(col_sum, axis=0, keepdims=True)
        gain_sum = jnp.sum(gain_sum, axis=0, keepdims=True)
        square = dot_t(cen[:, lanes], dwb[:, lanes])
        for half in range(2):
            ch = slice(PAIR * half, PAIR * (half + 1))
            pair = 2 * quad + half
            inner = square[ch, ch]
            stats[pair, :GROUP, :] = pack(inner + inner.T)
            stats[pair, GROUP:, :] = vectors(col_sum[:, ch], gain_sum[:, ch])
    if split:
        emit_pairs(stats, outs, spot)
    else:
        outs[0][...] = stats[...]


def last_kernel(spot, dwb, cen, h2, s2, w3, wpairs, *rest, plan, split, shares):
    given, rest = rest[:shares], rest[shares:]
    (cols, gains), outs, (ext, flat, dbranch, part, spairs) = rest[:2], rest[2:-5], rest[-5:]
    place_pairs(spot, given, spairs, split)
    gains[...] = spairs[:, GROUP + 1, :]
    rows, width = dwb.shape
    chunk = chunk_of(rows, 128)
    ext[...] = jnp.zeros_like(ext)
    for quad in range(width // 256):
        lanes = slice(256 * quad, 256 * (quad + 1))
        whiten = quad_matrix(wpairs, quad)
        sym = quad_matrix(spairs, quad)
        bias = row_of(spairs, quad, 0)

        def step(at, carry, lanes=lanes, whiten=whiten, sym=sym, bias=bias):
            here = pl.ds(pl.multiple_of(at * chunk, 16), chunk)
            value = dot_nt(dwb[here, lanes], whiten) + dot(cen[here, lanes], sym) + bias
            dbranch[here, lanes] = value.astype(BF16)
            return carry

        lax.fori_loop(0, rows // chunk, step, 0)

    def middle(at, carry):
        here = pl.ds(pl.multiple_of(at * chunk, 16), chunk)
        flat[here, :] = dot_nt(dbranch[here, :], w3[...]) * s2[here, :]
        return carry

    lax.fori_loop(0, rows // chunk, middle, 0)
    pad_lines(flat, ext, rows)
    shifted(ext, cols)
    for quad in range(width // 256):
        lanes = slice(256 * quad, 256 * (quad + 1))
        part[:, lanes] = dot_t(h2[...], dbranch[:, lanes])
    finish(part, outs, spot, plan)


def finish(part, outs, spot, plan):
    if plan:
        emit_split(part, outs[0], outs[1], spot[1], plan)
    else:
        outs[0][...] = part[...]


def slope_kernel(spot, cols, wm, s1, x, dmid1, *rest, plan):
    outs, (ext, flat, part) = rest[:-3], rest[-3:]
    rows, depth = s1.shape
    padded = padded_rows(rows)
    big = chunk_of(padded, 256)

    def step(at, carry):
        base = pl.multiple_of(at * big, 16)
        total = jnp.zeros((big, depth), F32)
        for row in range(3):
            for col in range(3):
                near = cols[2 - col, pl.ds(base + LINE * (2 - row), big), :]
                k = 3 * row + col
                total = total + dot_nt(near, wm[k * depth : (k + 1) * depth, :])
        ext[pl.ds(base, big), :] = total
        return carry

    lax.fori_loop(0, padded // big, step, 0)
    unpad_lines(ext, flat, rows)
    dmid1[...] = (flat[...] * s1[...]).astype(BF16)
    for quad in range(x.shape[1] // 256):
        lanes = slice(256 * quad, 256 * (quad + 1))
        part[lanes, :] = dot_t(x[:, lanes], dmid1[...])
    finish(part, outs, spot, plan)


def middle_kernel(spot, cols, h1pad, *rest, plan):
    outs, part = rest[:-1], rest[-1]
    padded, depth = h1pad.shape
    for row in range(3):
        for col in range(3):
            k = 3 * row + col
            near = cols[2 - col, LINE * (2 - row) : LINE * (2 - row) + padded, :]
            part[k * depth : (k + 1) * depth, :] = dot_t(h1pad[...], near)
    finish(part, outs, spot, plan)


def pair_step(spot, left_keep, left_given, right_keep, right_given, *outs, bits):
    given = ((left_keep, left_given, bits[0]), (right_keep, right_given, bits[1]))
    for at, (keep, got, bit) in enumerate(given):
        outs[2 * at][...], outs[2 * at + 1][...] = half_of(keep, got, spot[bit])


def open_step(spot, keep, given, *outs, cut, bits):
    rows = keep.shape[0]
    spans = ((0, cut), (cut, rows - cut))
    for at, ((start, size), bit) in enumerate(zip(spans, bits)):
        outs[2 * at][...], outs[2 * at + 1][...] = half_of(keep, given, spot[bit], start, size)


def join_step(spot, left_keep, left_given, right_keep, right_given, *rest, bit):
    extra, outs = rest[:-2], rest[-2:]
    at = 0
    for keep, got in ((left_keep, left_given), (right_keep, right_given)):
        mine, other = half_of(keep, got, spot[bit])
        outs[0][at : at + mine.shape[0], :] = mine
        outs[1][at : at + mine.shape[0], :] = other
        at += mine.shape[0]
    for ref in extra:
        for out in outs:
            out[at:, :PAIR] = ref[...]
            out[at:, PAIR:] = jnp.zeros_like(ref)


def last_step(spot, keep, given, *outs, spans, bit):
    to = 0
    for start, size in spans:
        mine, other = half_of(keep, given, spot[bit], start, size)
        outs[0][to : to + size // 2, :] = mine
        outs[1][to : to + size // 2, :] = other
        to += size // 2
    rest = keep.shape[0] - start - size
    if rest:
        total = keep[start + size :, :] + given[start + size :, :]
        outs[0][to:, :] = total
        outs[1][to:, :] = total


def both_step(spot, middle_keep, middle_given, *rest, cut, bits):
    open_step(spot, middle_keep, middle_given, *rest[4:8], cut=cut, bits=bits)
    pair_step(spot, *rest[:4], *rest[8:], bits=bits[::-1])


def input_kernel(dmid1, w1, dpre, out):
    rows = dpre.shape[0]
    chunk = chunk_of(rows, 128)

    def step(at, carry):
        here = pl.ds(pl.multiple_of(at * chunk, 16), chunk)
        out[here, :] = (dot_nt(dmid1[here, :], w1[...]) + dpre[here, :]).astype(BF16)
        return carry

    lax.fori_loop(0, rows // chunk, step, 0)


def call(kernel, outs, args, scratch=(), scalars=0, flops=0, ties=()):
    args = tuple(args) + tuple(ties)
    specs = [pl.BlockSpec(memory_space=pltpu.SMEM)] * scalars
    specs += [pl.BlockSpec(memory_space=pltpu.VMEM)] * (len(args) - scalars - len(ties))
    specs += [pl.BlockSpec(memory_space=pl.ANY)] * len(ties)
    count = len(args) - len(ties)

    def body(*refs):
        kernel(*refs[:count], *refs[len(args) :])

    size = sum(a.size * a.dtype.itemsize for a in args)
    size += sum(o.size * o.dtype.itemsize for o in outs)
    return pl.pallas_call(
        body,
        out_shape=tuple(outs),
        in_specs=specs,
        out_specs=tuple(pl.BlockSpec(memory_space=pltpu.VMEM) for _ in outs),
        scratch_shapes=list(scratch),
        cost_estimate=pl.CostEstimate(flops=flops, bytes_accessed=size, transcendentals=0),
        compiler_params=pltpu.CompilerParams(vmem_limit_bytes=40 * 2**20),
    )(*args)


def shape(dims, dtype=F32):
    return jax.ShapeDtypeStruct(dims, dtype)


def swap(value, axis, size, flip):
    return lax.ppermute(value, axis, [(at, at ^ flip) for at in range(size)])


def shards(inputs, out_grad, conv_first, conv_middle, conv_last, gain):
    rows, width = inputs.shape
    mid = conv_first.shape[1]
    pairs = width // PAIR
    ghosts = lax.axis_size("ghost")
    groups = lax.axis_size("group")
    devices = ghosts * groups
    span = float(rows * ghosts)
    scale = (rows * devices) ** (-0.5)
    padded = padded_rows(rows)
    ghost = lax.axis_index("ghost")
    group = lax.axis_index("group")
    bits = [ghost] + [(ghost >> bit) & 1 for bit in range(3)]
    bits += [(group >> bit) & 1 for bit in range(2)]
    spot = jnp.stack(bits).astype(jnp.int32)
    core, across, along, near, far = 1, 2, 3, 4, 5
    split = ghosts == 8 and pairs == 8 and groups == 4
    unit = 2 * rows * width * mid

    ext = pltpu.VMEM((24 + padded + LINE + 8, mid), F32)
    flat = pltpu.VMEM((rows, mid), F32)
    cols = (3, padded + 2 * LINE, mid)
    big = (pairs, TALL, PAIR)
    half = (pairs // 2, TALL, PAIR)
    packed = (pairs // 4, TALL, PAIR)
    stats_outs = [shape(packed)] * 2 if split else [shape(big)]
    stats_held = pltpu.VMEM(big, F32)

    def collect(stats):
        if not split:
            return [lax.psum(stats[0], "ghost")]
        total, send = stats
        given = swap(send, "ghost", ghosts, 1)
        (total,) = call(add_kernel, [shape(packed)], (total, given))
        (total,) = call(add_kernel, [shape(packed)], (total, swap(total, "ghost", ghosts, 2)))
        return [total, swap(total, "ghost", ghosts, 4)]

    def share_out(own):
        return [own, swap(own, "ghost", ghosts, 1)] if split else [own]

    own = half if split else big
    held = own[0]
    h1pad, s1, h2, s2, *stats = call(
        functools.partial(forward_kernel, split=split),
        [shape((padded, mid), BF16), shape((rows, mid)), shape((rows, mid), BF16),
         shape((rows, mid))] + stats_outs,
        (spot, inputs, conv_first, conv_middle, conv_last),
        (ext, pltpu.VMEM(cols, BF16), flat, pltpu.VMEM((rows, width), F32), stats_held),
        scalars=1, flops=5 * unit,
    )
    share, kept = call(
        functools.partial(whiten_kernel, span=span, packed=split),
        [shape(own), shape((held, 2 * NEWTON + 1, PAIR, PAIR))], collect(stats), flops=10**7,
    )
    given = share_out(share)
    cen, dwb, dpre, wpairs, *stats = call(
        functools.partial(backward_kernel, split=split, shares=len(given)),
        [shape((rows, width), BF16), shape((rows, width), BF16), shape((rows, width)),
         shape(big)] + stats_outs,
        (spot, inputs, out_grad, h2, conv_last, gain.reshape(1, width), *given),
        (pltpu.VMEM(big, F32), stats_held), scalars=1, flops=3 * unit,
    )
    (pulled,) = call(
        functools.partial(pull_kernel, span=span, packed=split), [shape(own)], (*collect(stats), kept),
        flops=10**7,
    )
    given = share_out(pulled)

    def parts(height, lanes):
        if split:
            return [shape((height * lanes // 512, 256))] * 2
        return [shape((height, lanes))]

    def plan(height, wide, order):
        if not split:
            return None
        piece = height // devices
        if len(order) == 1:
            return plan_of([(0, piece, order[0])], piece, wide, groups, ghosts)
        cut = piece // 16 * 8 + 8 * (piece // 8 % 2)
        return plan_of(
            [(0, cut, order[0]), (cut, piece - cut, order[1])], piece, wide, groups, ghosts
        )

    dcols, gains, *last_part = call(
        functools.partial(
            last_kernel, plan=plan(mid, width // 256, ((1, 2),)), split=split, shares=len(given)
        ),
        [shape(cols, BF16), shape((pairs, PAIR))] + parts(mid, width),
        (spot, dwb, cen, h2, s2, conv_last, wpairs, *given),
        (ext, flat, pltpu.VMEM((rows, width), BF16), pltpu.VMEM((mid, width), F32),
         pltpu.VMEM(big, F32)),
        scalars=1, flops=4 * unit,
    )
    dmid1, *first_part = call(
        functools.partial(slope_kernel, plan=plan(width, 1, ((2, 1),))),
        [shape((rows, mid), BF16)] + parts(width, mid),
        (spot, dcols, conv_middle, s1, inputs),
        (ext, flat, pltpu.VMEM((width, mid), F32)), scalars=1, flops=4 * unit,
    )
    middle_part = call(
        functools.partial(middle_kernel, plan=plan(9 * mid, 1, ((1, 2), (2, 1)))),
        parts(9 * mid, mid), (spot, dcols, h1pad), (pltpu.VMEM((9 * mid, mid), F32),),
        scalars=1, flops=3 * unit,
    )
    portion = width // devices
    if not split:
        (input_grad,) = call(
            input_kernel, [shape((rows, width), BF16)], (dmid1, conv_first, dpre), flops=unit
        )
        grads = [
            lax.psum_scatter(
                (part[0] * scale).reshape(-1), ("group", "ghost"), scatter_dimension=0, tiled=True
            )
            for part in (first_part, middle_part, last_part)
        ]
        gain_grad = lax.dynamic_slice_in_dim(
            lax.psum(gains.reshape(-1) * scale, "group"), (group * ghosts + ghost) * portion, portion
        )
        return (input_grad, *grads, gain_grad)

    def rows_of(height):
        return shape((height, 256))

    def step(kernel, heights, *args, ties=()):
        return call(
            kernel, [rows_of(h) for h in heights for _ in range(2)], (spot,) + args, scalars=1,
            ties=ties,
        )

    last_keep, last_send = last_part
    first_keep, first_send = first_part
    middle_keep, middle_send = middle_part
    last_rows, first_rows = last_keep.shape[0], first_keep.shape[0]
    middle_rows = middle_keep.shape[0]
    cut = 16 * plan(9 * mid, 1, ((1, 2), (2, 1)))[0][1]
    last_got = swap(last_send, "ghost", ghosts, 1)
    first_got = swap(first_send, "ghost", ghosts, 1)
    middle_got = swap(middle_send, "ghost", ghosts, 1)
    last_keep, last_send, first_keep, first_send = step(
        functools.partial(pair_step, bits=(across, along)), (last_rows // 2, first_rows // 2),
        last_keep, last_got, first_keep, first_got,
    )
    (input_grad,) = call(
        input_kernel, [shape((rows, width), BF16)], (dmid1, conv_first, dpre), flops=unit,
        ties=(last_keep,),
    )
    last_got = swap(last_send, "ghost", ghosts, 2)
    first_got = swap(first_send, "ghost", ghosts, 4)
    (one_keep, one_send, two_keep, two_send, last_keep, last_send, first_keep, first_send) = step(
        functools.partial(both_step, cut=cut, bits=(across, along)),
        (cut // 2, (middle_rows - cut) // 2, last_rows // 4, first_rows // 4),
        middle_keep, middle_got, last_keep, last_got, first_keep, first_got, ties=(input_grad,),
    )
    one_got = swap(one_send, "ghost", ghosts, 2)
    two_got = swap(two_send, "ghost", ghosts, 4)
    last_got = swap(last_send, "ghost", ghosts, 4)
    first_got = swap(first_send, "ghost", ghosts, 2)
    low_keep, low_send = step(
        functools.partial(join_step, bit=near), ((last_rows + first_rows) // 8 + 8,),
        last_keep, last_got, first_keep, first_got, gains,
    )
    low_got = swap(low_send, "group", groups, 1)
    one_keep, one_send, two_keep, two_send = step(
        functools.partial(pair_step, bits=(along, across)), (cut // 4, (middle_rows - cut) // 4),
        one_keep, one_got, two_keep, two_got, ties=(low_keep,),
    )
    one_got = swap(one_send, "ghost", ghosts, 4)
    two_got = swap(two_send, "ghost", ghosts, 2)
    spans = ((0, last_rows // 8), (last_rows // 8, first_rows // 8))
    low_keep, low_send = step(
        functools.partial(last_step, spans=spans, bit=far), ((last_rows + first_rows) // 16 + 8,),
        low_keep, low_got, ties=(one_keep,),
    )
    low_got = swap(low_send, "group", groups, 2)
    high_keep, high_send = step(
        functools.partial(join_step, bit=near), (middle_rows // 8,),
        one_keep, one_got, two_keep, two_got, ties=(low_keep,),
    )
    high_got = swap(high_send, "group", groups, 1)
    spans = ((0, cut // 8), (cut // 8, (middle_rows - cut) // 8))
    high_keep, high_send = step(
        functools.partial(last_step, spans=spans, bit=far), (middle_rows // 16,),
        high_keep, high_got,
    )
    high_got = swap(high_send, "group", groups, 2)
    low = (low_keep + low_got) * scale
    tall = last_rows // 16
    wide = width // 256
    last_grad = low[:tall].reshape(wide, tall // wide, 256).swapaxes(0, 1).reshape(-1)
    first_grad = low[tall : 2 * tall].reshape(-1)
    middle_grad = ((high_keep + high_got) * scale).reshape(-1)
    gains = low[2 * tall :, :PAIR].reshape(-1)
    gain_grad = lax.dynamic_slice_in_dim(gains, (group * ghosts + ghost) * portion, portion)
    return (input_grad, first_grad, middle_grad, last_grad, gain_grad)


def solution(mesh):
    in_specs = (P(("group", "ghost"), None), P(("group", "ghost"), None), P(), P(), P(), P())
    out_specs = (
        P(("group", "ghost"), None),
        P(("group", "ghost")),
        P(("group", "ghost")),
        P(("group", "ghost")),
        P(("group", "ghost")),
    )
    return jax.shard_map(shards, mesh=mesh, in_specs=in_specs, out_specs=out_specs, check_vma=False)
```

```python
import functools

import jax
import jax.numpy as jnp
from jax import lax
from jax.experimental import pallas as pl
from jax.experimental.pallas import tpu as pltpu
from jax.sharding import PartitionSpec as P

GROUP = 64
NEWTON = 5
SIDE = 14
LINE = 16
PAIR = 2 * GROUP
TALL = GROUP + 8
epsilon = 1e-05

F32 = jnp.float32
BF16 = jnp.bfloat16


def dot(left, right):
    return jnp.dot(left, right, preferred_element_type=F32)


def dot_t(left, right):
    return lax.dot_general(left, right, (((0,), (0,)), ((), ())), preferred_element_type=F32)


def dot_nt(left, right):
    return lax.dot_general(left, right, (((1,), (1,)), ((), ())), preferred_element_type=F32)


def halves_of(value):
    high = value.astype(BF16)
    return high, (value - high.astype(F32)).astype(BF16)


def exact(left, right):
    a, b = halves_of(left)
    c, d = halves_of(right)
    low = dot(jnp.concatenate([a, b], axis=1), jnp.concatenate([d, c], axis=0))
    return low + dot(a, c)


def outer_of(row):
    tile = vectors(row)
    return lax.dot_general(
        tile, tile, (((0,), (0,)), ((), ())), preferred_element_type=F32,
        precision=lax.Precision.HIGHEST,
    )


def sigmoid(value):
    return 0.5 * jnp.tanh(0.5 * value) + 0.5


def two_rows(row):
    high, low = halves_of(jnp.broadcast_to(row, (16, row.shape[1])))
    at = lax.broadcasted_iota(jnp.int32, high.shape, 0)
    return jnp.where(at == 0, high.astype(F32), jnp.where(at == 1, low.astype(F32), 0.0)).astype(
        BF16
    )


def row_times(row, matrix, product=dot):
    return jnp.sum(product(two_rows(row), matrix), axis=0, keepdims=True)


def rank_one(left, right):
    tiles = []
    for row, order in ((left, (0, 1, 0)), (right, (0, 0, 1))):
        pair = halves_of(jnp.broadcast_to(row, (16, row.shape[1])))
        at = lax.broadcasted_iota(jnp.int32, pair[0].shape, 0)
        tile = jnp.zeros(pair[0].shape, F32)
        for place, which in enumerate(order):
            tile = jnp.where(at == place, pair[which].astype(F32), tile)
        tiles.append(tile.astype(BF16))
    return dot_t(*tiles)


def chunk_of(rows, most):
    best = 16
    for size in range(16, most + 1, 16):
        if rows % size == 0:
            best = size
    return best


def left_half(shape):
    return lax.broadcasted_iota(jnp.int32, shape, 1) < GROUP


def spread(packed):
    left = left_half(packed.shape)
    zero = jnp.zeros_like(packed)
    return jnp.concatenate([jnp.where(left, packed, zero), jnp.where(left, zero, packed)], axis=0)


def pack(square):
    top, bottom = square[:GROUP], square[GROUP:]
    return jnp.where(left_half(top.shape), top, bottom)


def vectors(*rows):
    at = lax.broadcasted_iota(jnp.int32, (8, PAIR), 0)
    tile = jnp.zeros((8, PAIR), F32)
    for place, row in enumerate(rows):
        tile = jnp.where(at == place, row, tile)
    return tile


def fold(value):
    rows, lanes = value.shape
    return jnp.sum(value.reshape(rows // 8, 8, lanes), axis=0)


def pad_lines(source, ext, rows):
    for line in range(rows // SIDE):
        place = 24 + LINE * (line + line // SIDE)
        ext[place : place + SIDE, :] = source[SIDE * line : SIDE * (line + 1), :]


def unpad_lines(source, target, rows):
    for line in range(rows // SIDE):
        place = LINE * (line + line // SIDE)
        target[SIDE * line : SIDE * (line + 1), :] = source[place : place + SIDE, :]


def padded_rows(rows):
    return rows // (SIDE * SIDE) * (SIDE + 1) * LINE


def shifted(ext, cols):
    length = cols.shape[1]
    for col in range(3):
        cols[col] = ext[7 + col : 7 + col + length, :].astype(BF16)


def emit_split(source, keep, send, core, plan):
    for start, height, first, size, mine in plan:
        lanes = keep.shape[1]
        for wide in range(source.shape[1] // lanes):
            to = slice(start + wide * height, start + (wide + 1) * height)
            cols = slice(wide * lanes, (wide + 1) * lanes)
            for target, half in ((keep, core), (send, 1 - core)):
                place = pl.multiple_of((mine + half) * size + first, 8)
                target[to, :] = source[pl.ds(place, height), cols]


def plan_of(parts, piece, wide, groups, ghosts, start=0):
    plan = []
    for first, height, bits in parts:
        steps = [("ghost", bit) for bit in bits]
        steps += [("group", bit) for bit in range(groups.bit_length() - 1)]
        for at in range(2 ** len(steps)):
            source = 0
            for place, (axis, bit) in enumerate(steps):
                value = (at >> (len(steps) - 1 - place)) & 1
                source += value << bit if axis == "ghost" else (value << bit) * ghosts
            plan.append((start, height, first, piece, source))
            start += height * wide
    return plan


def half_of(left, right, bit, start=0, rows=None):
    rows = (left.shape[0] if rows is None else rows) // 2
    mine = pl.ds(pl.multiple_of(start + bit * rows, 8), rows)
    other = pl.ds(pl.multiple_of(start + (1 - bit) * rows, 8), rows)
    return left[mine, :] + right[mine, :], left[other, :] + right[other, :]


def emit_pairs(stats, outs, spot):
    shape = (GROUP, PAIR)
    row = lax.broadcasted_iota(jnp.int32, shape, 0)
    lane = lax.broadcasted_iota(jnp.int32, shape, 1)
    left = lane < GROUP
    col = jnp.where(left, lane, lane - GROUP)
    for parity in range(2):
        for slot in range(stats.shape[0] // 4):
            pair = 4 * slot + parity, 4 * slot + 2 + parity
            first, second = (stats[p, :GROUP, :] for p in pair)
            upper = jnp.where(left, first, pltpu.roll(second, GROUP, 1))
            lower = jnp.where(left, pltpu.roll(first, GROUP, 1), second)
            rows = [
                jnp.sum(jnp.where(row == col, m, 0.0), axis=0, keepdims=True)
                for m in (first, second)
            ]
            for place in range(2):
                rows += [stats[p, GROUP + place : GROUP + place + 1, :] for p in pair]
            both = jnp.concatenate([jnp.where(row <= col, upper, lower), vectors(*rows)], axis=0)

            @pl.when(spot[1] == parity)
            def _(both=both, slot=slot):
                outs[0][slot] = both

            @pl.when(spot[1] != parity)
            def _(both=both, slot=slot):
                outs[1][slot] = both


def take_pairs(total, packed):
    result = []
    if not packed:
        for at in range(total.shape[0]):
            vecs = [total[at, GROUP + p : GROUP + p + 1, :] for p in range(2)]
            result.append((spread(total[at, :GROUP, :]), *vecs))
        return result
    shape = (PAIR, PAIR)
    row = lax.broadcasted_iota(jnp.int32, shape, 0)
    col = lax.broadcasted_iota(jnp.int32, shape, 1)
    mask = jnp.where(row < GROUP, row - col, col - row) < 0
    eye = identity()
    for slot in range(total.shape[0]):
        both = total[slot, :GROUP, :]
        turned = pltpu.roll(both, GROUP, 1)
        left = left_half(both.shape)
        for at in range(2):
            twice = jnp.where(left, *((both, turned) if at == 0 else (turned, both)))
            part = jnp.where(mask, spread(twice), 0.0)
            line = [total[slot, GROUP + 2 * p + at : GROUP + 2 * p + at + 1, :] for p in range(3)]
            result.append((part + part.T + eye * line[0], line[1], line[2]))
    return result


def add_kernel(left, right, out):
    out[...] = left[...] + right[...]


def forward_kernel(
    spot, x_far, w1_far, wm_far, w3_far, h1pad, s1, h2, s2, cen, means, sums, *rest, split
):
    outs, (x, w1, wm, w3, sems, ext, cols, flat, branch, stats) = rest[:-10], rest[-10:]
    rows = x.shape[0]
    part = chunk_of(rows, 128)

    def slab(at):
        here = pl.ds(pl.multiple_of(at * part, 16), part)
        return pltpu.make_async_copy(x_far.at[here, :], x.at[here, :], sems.at[3 + at])

    weights = [
        pltpu.make_async_copy(far, ref, sems.at[at])
        for at, (far, ref) in enumerate(((w1_far, w1), (wm_far, wm), (w3_far, w3)))
    ]
    weights[0].start()
    for at in range(rows // part):
        slab(at).start()
    weights[1].start()
    weights[2].start()
    chunk = chunk_of(rows, 128)
    ext[...] = jnp.zeros_like(ext)

    weights[0].wait()

    def first(at, carry):
        here = pl.ds(pl.multiple_of(at * chunk, 16), chunk)
        slab(at).wait()
        act = dot(x[here, :], w1[...])
        sig = sigmoid(act)
        flat[here, :] = act * sig
        s1[here, :] = sig * (1.0 + act * (1.0 - sig))
        return carry

    lax.fori_loop(0, rows // chunk, first, 0)
    pad_lines(flat, ext, rows)
    shifted(ext, cols)
    padded = padded_rows(rows)
    h1pad[...] = cols[1, LINE : LINE + padded, :]
    big = chunk_of(padded, 256)
    weights[1].wait()

    def middle(at, carry):
        base = pl.multiple_of(at * big, 16)
        total = jnp.zeros((big, wm.shape[1]), F32)
        for row in range(3):
            for col in range(3):
                left = cols[col, pl.ds(base + LINE * row, big), :]
                k = 3 * row + col
                depth = left.shape[1]
                total = total + dot(left, wm[k * depth : (k + 1) * depth, :])
        ext[pl.ds(base, big), :] = total
        return carry

    lax.fori_loop(0, padded // big, middle, 0)
    unpad_lines(ext, flat, rows)
    width = w3.shape[1]
    weights[2].wait()

    def last(at, carry):
        total, hidden_sum = carry
        here = pl.ds(pl.multiple_of(at * chunk, 16), chunk)
        act = flat[here, :]
        sig = sigmoid(act)
        hidden = (act * sig).astype(BF16)
        h2[here, :] = hidden
        s2[here, :] = sig * (1.0 + act * (1.0 - sig))
        out = dot(hidden, w3[...])
        branch[here, :] = out
        return total + fold(out), hidden_sum + fold(hidden.astype(F32))

    zeros = jnp.zeros((8, width), F32), jnp.zeros((8, w3.shape[0]), F32)
    total, hidden_sum = lax.fori_loop(0, rows // chunk, last, zeros)
    sums[...] = jnp.broadcast_to(jnp.sum(hidden_sum, axis=0, keepdims=True), sums.shape)
    total = jnp.sum(total, axis=0, keepdims=True)
    mean = total / rows
    means[...] = jnp.broadcast_to(mean, means.shape)
    for quad in range(width // 256):
        lanes = slice(256 * quad, 256 * (quad + 1))
        centered = (branch[:, lanes] - mean[:, lanes]).astype(BF16)
        cen[:, lanes] = centered
        square = dot_t(centered, centered)
        for half in range(2):
            pair = 2 * quad + half
            ch = slice(PAIR * pair, PAIR * (pair + 1))
            row = mean[:, ch]
            outer = outer_of(row)
            inner = square[PAIR * half : PAIR * (half + 1), PAIR * half : PAIR * (half + 1)]
            top, low = pack(inner + outer * rows), vectors(total[:, ch])
            stats[pair, :GROUP, :] = top
            stats[pair, GROUP:, :] = low
    if split:
        emit_pairs(stats, outs, spot)
    else:
        outs[0][...] = stats[...]


def identity():
    shape = (PAIR, PAIR)
    return jnp.where(
        lax.broadcasted_iota(jnp.int32, shape, 0) == lax.broadcasted_iota(jnp.int32, shape, 1),
        1.0, 0.0,
    ).astype(F32)


def per_block(square):
    row_sums = jnp.sum(square, axis=1, keepdims=True)
    top = jnp.sum(row_sums[:GROUP], axis=0, keepdims=True)
    bottom = jnp.sum(row_sums[GROUP:], axis=0, keepdims=True)
    upper = lax.broadcasted_iota(jnp.int32, (PAIR, 1), 0) < GROUP
    return jnp.where(upper, top, bottom)


def total_of(terms):
    total = terms[0][...]
    for term in terms[1:]:
        total = total + term[...]
    return total


def whiten_kernel(*refs, span, packed):
    terms, (out, keep) = refs[:-2], refs[-2:]
    given = take_pairs(total_of(terms), packed)
    eye = identity()
    blocks = spread(jnp.ones((GROUP, PAIR), F32))
    means = [sums / span for _, sums, _ in given]
    covs = [
        moments / span - outer_of(mean) * blocks + epsilon * eye
        for (moments, _, _), mean in zip(given, means)
    ]
    traces = [per_block(cov * eye) for cov in covs]
    normed = [cov / trace for cov, trace in zip(covs, traces)]
    powers = [1.5 * eye - 0.5 * norm for norm in normed]
    for at, trace in enumerate(traces):
        keep[at, 0] = normed[at]
        keep[at, 1] = eye / trace
    for sweep in range(NEWTON - 1):
        squares = [exact(power, power) for power in powers]
        sides = [exact(power, norm) for power, norm in zip(powers, normed)]
        for at, power in enumerate(powers):
            keep[at, 2 + 2 * sweep] = power
            keep[at, 3 + 2 * sweep] = squares[at]
        powers = [
            1.5 * power - 0.5 * exact(square, side)
            for power, square, side in zip(powers, squares, sides)
        ]
    for at, power in enumerate(powers):
        keep[at, 2 * NEWTON] = power
        out[at, :GROUP, :] = pack(power / jnp.sqrt(traces[at]))
        out[at, GROUP:, :] = vectors(means[at])


def pull_kernel(*refs, span, packed):
    terms, (keep, out) = refs[:-2], refs[-2:]
    given = take_pairs(total_of(terms), packed)
    eye = identity()
    every = range(len(given))
    normed = [keep[at, 0] for at in every]
    inverse = [per_block(keep[at, 1]) / GROUP for at in every]
    roots = [jnp.sqrt(value) for value in inverse]
    powers = [keep[at, 2 * NEWTON] for at in every]
    grads = [given[at][0] * roots[at] for at in every]
    trace_grads = [
        -0.5 * inverse[at] * roots[at] * per_block(given[at][0] * powers[at]) for at in every
    ]
    normed_grads = [jnp.zeros_like(grads[0])] * len(given)
    for sweep in reversed(range(NEWTON - 1)):
        power = [keep[at, 2 + 2 * sweep] for at in every]
        turned = [exact(grads[at], normed[at]) for at in every]
        inner = [exact(power[at], grads[at]) for at in every]
        turned = [exact(turned[at] + turned[at].T, power[at]) for at in every]
        inner = [exact(keep[at, 3 + 2 * sweep], inner[at]) for at in every]
        normed_grads = [normed_grads[at] - 0.25 * (inner[at] + inner[at].T) for at in every]
        outer = [exact(turned[at], power[at]) for at in every]
        inner = [exact(power[at], turned[at]) for at in every]
        grads = [
            1.5 * grads[at] - 0.25 * (outer[at] + outer[at].T + inner[at]) for at in every
        ]
    for at in every:
        normed_grad = normed_grads[at] - 0.5 * grads[at]
        trace_grad = trace_grads[at] - inverse[at] * per_block(normed_grad * normed[at])
        both = normed_grad * inverse[at] + eye * trace_grad
        bias = -exact(vectors(given[at][1] / span), (powers[at] * roots[at]).T)
        out[at, :GROUP, :] = pack(both / span)
        out[at, GROUP:, :] = vectors(bias[0:1, :], given[at][2])


def place_pairs(spot, given, pairs, split):
    if split:
        for side, shares in enumerate(given):
            for at in range(shares.shape[0]):
                pairs[2 * at + jnp.bitwise_xor(side, spot[1])] = shares[at]
    else:
        pairs[...] = given[0][...]


def quad_matrix(pairs, quad):
    zero = jnp.zeros((PAIR, PAIR), F32)
    first = spread(pairs[2 * quad, :GROUP, :])
    second = spread(pairs[2 * quad + 1, :GROUP, :])
    top = jnp.concatenate([first, zero], axis=1)
    bottom = jnp.concatenate([zero, second], axis=1)
    return jnp.concatenate([top, bottom], axis=0).astype(BF16)


def row_of(pairs, quad, place):
    at = GROUP + place
    return jnp.concatenate(
        [pairs[2 * quad, at : at + 1, :], pairs[2 * quad + 1, at : at + 1, :]], axis=1
    )


def backward_kernel(spot, x, og, cen, means, gain, *rest, split, shares):
    given, rest = rest[:shares], rest[shares:]
    (dwb, dpre_out, w_out), outs, (pairs, stats) = rest[:3], rest[3:-2], rest[-2:]
    rows, width = x.shape
    place_pairs(spot, given, pairs, split)
    w_out[...] = pairs[...]
    chunk = chunk_of(rows, 128)
    for quad in range(width // 256):
        lanes = slice(256 * quad, 256 * (quad + 1))
        whiten = quad_matrix(pairs, quad)
        away = means[0:1, lanes] - row_of(pairs, quad, 0)
        shift = row_times(away, whiten)
        scale = gain[:, lanes]

        def step(at, carry, lanes=lanes, whiten=whiten, shift=shift, scale=scale):
            col_sum, gain_sum = carry
            here = pl.ds(pl.multiple_of(at * chunk, 16), chunk)
            white = dot(cen[here, lanes], whiten) + shift
            pre = x[here, lanes].astype(F32) + scale * white
            sig = sigmoid(pre)
            dpre = og[here, lanes].astype(F32) * (sig * (1.0 + pre * (1.0 - sig)))
            dpre_out[here, lanes] = dpre
            dwhite = scale * dpre
            dwb[here, lanes] = dwhite.astype(BF16)
            return col_sum + fold(dwhite), gain_sum + fold(dpre * white)

        zero = jnp.zeros((8, 256), F32)
        col_sum, gain_sum = lax.fori_loop(0, rows // chunk, step, (zero, zero))
        col_sum = jnp.sum(col_sum, axis=0, keepdims=True)
        gain_sum = jnp.sum(gain_sum, axis=0, keepdims=True)
        square = dot_t(cen[:, lanes], dwb[:, lanes]) + rank_one(away, col_sum)
        for half in range(2):
            ch = slice(PAIR * half, PAIR * (half + 1))
            pair = 2 * quad + half
            inner = square[ch, ch]
            stats[pair, :GROUP, :] = pack(inner + inner.T)
            stats[pair, GROUP:, :] = vectors(col_sum[:, ch], gain_sum[:, ch])
    if split:
        emit_pairs(stats, outs, spot)
    else:
        outs[0][...] = stats[...]


def own_kernel(h2, cen, out):
    for quad in range(cen.shape[1] // 256):
        lanes = slice(256 * quad, 256 * (quad + 1))
        out[:, lanes] = dot_t(h2[...], cen[:, lanes]).astype(BF16)


def turn_kernel(dwb, wpairs, w3, turned, flow):
    rows, width = dwb.shape
    chunk = chunk_of(rows, 128)
    for quad in range(width // 256):
        lanes = slice(256 * quad, 256 * (quad + 1))
        whiten = quad_matrix(wpairs, quad).T

        def step(at, carry, lanes=lanes, whiten=whiten):
            here = pl.ds(pl.multiple_of(at * chunk, 16), chunk)
            turned[here, lanes] = dot(dwb[here, lanes], whiten).astype(BF16)
            return carry

        lax.fori_loop(0, rows // chunk, step, 0)
    flow[...] = dot_nt(turned[...], w3[...])


def turned_kernel(h2, turned, out):
    for quad in range(turned.shape[1] // 256):
        lanes = slice(256 * quad, 256 * (quad + 1))
        out[:, lanes] = dot_t(h2[...], turned[:, lanes])


def last_kernel(spot, flow, cen, means, s2, w3, wpairs, *rest, split, shares):
    given, (cols, gains, spairs, bias_out, ext, flat, joint) = rest[:shares], rest[shares:]
    rows, width = cen.shape
    place_pairs(spot, given, spairs, split)
    gains[...] = spairs[:, GROUP + 1, :]
    chunk = chunk_of(rows, 128)
    ext[...] = jnp.zeros_like(ext)
    low = jnp.zeros((1, w3.shape[0]), F32)
    for quad in range(width // 256):
        lanes = slice(256 * quad, 256 * (quad + 1))
        sym = quad_matrix(spairs, quad)
        away = means[0:1, lanes] - row_of(wpairs, quad, 0)
        bias = row_of(spairs, quad, 0) + row_times(away, sym)
        bias_out[:, lanes] = jnp.broadcast_to(bias, (8, 256))
        low = low + row_times(bias, w3[:, lanes], dot_nt)
        joint[lanes, :] = dot_nt(sym, w3[:, lanes]).astype(BF16)

    def middle(at, carry):
        here = pl.ds(pl.multiple_of(at * chunk, 16), chunk)
        flat[here, :] = (flow[here, :] + dot(cen[here, :], joint[...]) + low) * s2[here, :]
        return carry

    lax.fori_loop(0, rows // chunk, middle, 0)
    pad_lines(flat, ext, rows)
    shifted(ext, cols)


def finish(part, outs, spot, plan):
    if plan:
        emit_split(part, outs[0], outs[1], spot[1], plan)
    else:
        outs[0][...] = part[...]


def slope_kernel(
    spot, cols, wm, s1, x, turned, own, sums, spairs, bias, dmid1, *rest, plans
):
    outs, (ext, flat, part, part_last) = rest[:-4], rest[-4:]
    rows, depth = s1.shape
    padded = padded_rows(rows)
    big = chunk_of(padded, 256)

    def step(at, carry):
        base = pl.multiple_of(at * big, 16)
        total = jnp.zeros((big, depth), F32)
        for row in range(3):
            for col in range(3):
                near = cols[2 - col, pl.ds(base + LINE * (2 - row), big), :]
                k = 3 * row + col
                total = total + dot_nt(near, wm[k * depth : (k + 1) * depth, :])
        ext[pl.ds(base, big), :] = total
        return carry

    lax.fori_loop(0, padded // big, step, 0)
    unpad_lines(ext, flat, rows)
    dmid1[...] = (flat[...] * s1[...]).astype(BF16)
    for quad in range(x.shape[1] // 256):
        lanes = slice(256 * quad, 256 * (quad + 1))
        part[lanes, :] = dot_t(x[:, lanes], dmid1[...])
        sym = quad_matrix(spairs, quad)
        part_last[:, lanes] = (
            turned[:, lanes]
            + dot(own[:, lanes], sym)
            + rank_one(sums[0:1, :], bias[0:1, lanes])
        )
    if plans:
        emit_split(part_last, outs[0], outs[1], spot[1], plans[0])
        emit_split(part, outs[0], outs[1], spot[1], plans[1])
    else:
        outs[0][...] = part_last[...]
        outs[1][...] = part[...]


def middle_kernel(spot, cols, h1pad, *rest, plan):
    outs, part = rest[:-1], rest[-1]
    padded, depth = h1pad.shape
    for row in range(3):
        for col in range(3):
            k = 3 * row + col
            near = cols[2 - col, LINE * (2 - row) : LINE * (2 - row) + padded, :]
            part[k * depth : (k + 1) * depth, :] = dot_t(h1pad[...], near)
    finish(part, outs, spot, plan)


def pair_step(spot, left_keep, left_given, right_keep, right_given, *outs, bits):
    given = ((left_keep, left_given, bits[0]), (right_keep, right_given, bits[1]))
    for at, (keep, got, bit) in enumerate(given):
        outs[2 * at][...], outs[2 * at + 1][...] = half_of(keep, got, spot[bit])


def open_step(spot, keep, given, *outs, cut, bits):
    rows = keep.shape[0]
    spans = ((0, cut), (cut, rows - cut))
    for at, ((start, size), bit) in enumerate(zip(spans, bits)):
        outs[2 * at][...], outs[2 * at + 1][...] = half_of(keep, given, spot[bit], start, size)


def join_step(spot, left_keep, left_given, right_keep, right_given, *rest, bit):
    extra, outs = rest[:-2], rest[-2:]
    at = 0
    for keep, got in ((left_keep, left_given), (right_keep, right_given)):
        mine, other = half_of(keep, got, spot[bit])
        outs[0][at : at + mine.shape[0], :] = mine
        outs[1][at : at + mine.shape[0], :] = other
        at += mine.shape[0]
    for ref in extra:
        for out in outs:
            out[at:, :PAIR] = ref[...]
            out[at:, PAIR:] = jnp.zeros_like(ref)


def last_step(spot, keep, given, *outs, spans, bit):
    to = 0
    for start, size in spans:
        mine, other = half_of(keep, given, spot[bit], start, size)
        outs[0][to : to + size // 2, :] = mine
        outs[1][to : to + size // 2, :] = other
        to += size // 2
    rest = keep.shape[0] - start - size
    if rest:
        total = keep[start + size :, :] + given[start + size :, :]
        outs[0][to:, :] = total
        outs[1][to:, :] = total


def start_step(spot, low_keep, low_given, middle_keep, middle_given, *outs, cut, bits):
    open_step(spot, low_keep, low_given, *outs[:4], cut=low_keep.shape[0] // 2, bits=bits)
    open_step(spot, middle_keep, middle_given, *outs[4:], cut=cut, bits=bits)


def tail_step(
    spot, one_keep, one_given, two_keep, two_given, low_keep, low_given, *outs, spans, bits
):
    join_step(spot, one_keep, one_given, two_keep, two_given, *outs[:2], bit=bits[0])
    last_step(spot, low_keep, low_given, *outs[2:], spans=spans, bit=bits[1])


def input_kernel(dmid1, w1, dpre, out):
    rows = dpre.shape[0]
    chunk = chunk_of(rows, 128)

    def step(at, carry):
        here = pl.ds(pl.multiple_of(at * chunk, 16), chunk)
        out[here, :] = (dot_nt(dmid1[here, :], w1[...]) + dpre[here, :]).astype(BF16)
        return carry

    lax.fori_loop(0, rows // chunk, step, 0)


def call(kernel, outs, args, scratch=(), scalars=0, flops=0, ties=(), far=0):
    args = tuple(args) + tuple(ties)
    specs = [pl.BlockSpec(memory_space=pltpu.SMEM)] * scalars
    specs += [pl.BlockSpec(memory_space=pl.ANY)] * far
    specs += [pl.BlockSpec(memory_space=pltpu.VMEM)] * (len(args) - scalars - len(ties) - far)
    specs += [pl.BlockSpec(memory_space=pl.ANY)] * len(ties)
    count = len(args) - len(ties)

    def body(*refs):
        kernel(*refs[:count], *refs[len(args) :])

    size = sum(a.size * a.dtype.itemsize for a in args)
    size += sum(o.size * o.dtype.itemsize for o in outs)
    return pl.pallas_call(
        body,
        out_shape=tuple(outs),
        in_specs=specs,
        out_specs=tuple(pl.BlockSpec(memory_space=pltpu.VMEM) for _ in outs),
        scratch_shapes=list(scratch),
        cost_estimate=pl.CostEstimate(flops=flops, bytes_accessed=size, transcendentals=0),
        compiler_params=pltpu.CompilerParams(vmem_limit_bytes=40 * 2**20),
    )(*args)


def shape(dims, dtype=F32):
    return jax.ShapeDtypeStruct(dims, dtype)


def swap(value, axis, size, flip):
    return lax.ppermute(value, axis, [(at, at ^ flip) for at in range(size)])


def shards(inputs, out_grad, conv_first, conv_middle, conv_last, gain):
    rows, width = inputs.shape
    mid = conv_first.shape[1]
    pairs = width // PAIR
    ghosts = lax.axis_size("ghost")
    groups = lax.axis_size("group")
    devices = ghosts * groups
    span = float(rows * ghosts)
    scale = (rows * devices) ** (-0.5)
    padded = padded_rows(rows)
    ghost = lax.axis_index("ghost")
    group = lax.axis_index("group")
    bits = [ghost] + [(ghost >> bit) & 1 for bit in range(3)]
    bits += [(group >> bit) & 1 for bit in range(2)]
    spot = jnp.stack(bits).astype(jnp.int32)
    core, across, along, near, far = 1, 2, 3, 4, 5
    split = ghosts == 8 and pairs == 8 and groups == 4
    unit = 2 * rows * width * mid

    ext = pltpu.VMEM((24 + padded + LINE + 8, mid), F32)
    flat = pltpu.VMEM((rows, mid), F32)
    cols = (3, padded + 2 * LINE, mid)
    big = (pairs, TALL, PAIR)
    half = (pairs // 2, TALL, PAIR)
    packed = (pairs // 4, TALL, PAIR)
    stats_outs = [shape(packed)] * 2 if split else [shape(big)]
    stats_held = pltpu.VMEM(big, F32)

    def collect(stats):
        if not split:
            return [lax.psum(stats[0], "ghost")]
        total, send = stats
        given = swap(send, "ghost", ghosts, 1)
        (total,) = call(add_kernel, [shape(packed)], (total, given))
        (total,) = call(add_kernel, [shape(packed)], (total, swap(total, "ghost", ghosts, 2)))
        return [total, swap(total, "ghost", ghosts, 4)]

    def share_out(own):
        return [own, swap(own, "ghost", ghosts, 1)] if split else [own]

    own = half if split else big
    held = own[0]
    chunks = rows // chunk_of(rows, 128)
    h1pad, s1, h2, s2, cen, means, sums, *stats = call(
        functools.partial(forward_kernel, split=split),
        [shape((padded, mid), BF16), shape((rows, mid)), shape((rows, mid), BF16),
         shape((rows, mid)), shape((rows, width), BF16), shape((8, width)), shape((8, mid))]
        + stats_outs,
        (spot, inputs, conv_first, conv_middle, conv_last),
        (pltpu.VMEM((rows, width), BF16), pltpu.VMEM(conv_first.shape, BF16),
         pltpu.VMEM(conv_middle.shape, BF16), pltpu.VMEM(conv_last.shape, BF16),
         pltpu.SemaphoreType.DMA((3 + chunks,)),
         ext, pltpu.VMEM(cols, BF16), flat, pltpu.VMEM((rows, width), F32), stats_held),
        scalars=1, flops=5 * unit, far=4,
    )
    (own_part,) = call(own_kernel, [shape((mid, width), BF16)], (h2, cen), flops=unit)
    share, kept = call(
        functools.partial(whiten_kernel, span=span, packed=split),
        [shape(own), shape((held, 2 * NEWTON + 1, PAIR, PAIR))], collect(stats), flops=10**7,
    )
    given = share_out(share)
    dwb, dpre, wpairs, *stats = call(
        functools.partial(backward_kernel, split=split, shares=len(given)),
        [shape((rows, width), BF16), shape((rows, width)), shape(big)] + stats_outs,
        (spot, inputs, out_grad, cen, means, gain.reshape(1, width), *given),
        (pltpu.VMEM(big, F32), stats_held), scalars=1, flops=2 * unit,
    )
    turned, flow = call(
        turn_kernel, [shape((rows, width), BF16), shape((rows, mid))], (dwb, wpairs, conv_last),
        flops=2 * unit,
    )
    (turned_part,) = call(turned_kernel, [shape((mid, width))], (h2, turned), flops=unit)
    (pulled,) = call(
        functools.partial(pull_kernel, span=span, packed=split), [shape(own)], (*collect(stats), kept),
        flops=10**7,
    )
    given = share_out(pulled)

    def plan(height, wide, order, start=0):
        if not split:
            return None
        piece = height // devices
        if len(order) == 1:
            return plan_of([(0, piece, order[0])], piece, wide, groups, ghosts, start)
        cut = piece // 16 * 8 + 8 * (piece // 8 % 2)
        return plan_of(
            [(0, cut, order[0]), (cut, piece - cut, order[1])], piece, wide, groups, ghosts, start
        )

    dcols, gains, spairs, bias = call(
        functools.partial(last_kernel, split=split, shares=len(given)),
        [shape(cols, BF16), shape((pairs, PAIR)), shape(big), shape((8, width))],
        (spot, flow, cen, means, s2, conv_last, wpairs, *given),
        (ext, flat, pltpu.VMEM((width, mid), BF16)), scalars=1, flops=2 * unit,
    )
    low_rows = mid * width // 512
    middle_rows = 9 * mid // 2
    middle_plan = plan(9 * mid, 1, ((1, 2), (2, 1)))
    middle_part = call(
        functools.partial(middle_kernel, plan=middle_plan),
        [shape((middle_rows, mid))] * 2 if split else [shape((9 * mid, mid))],
        (spot, dcols, h1pad), (pltpu.VMEM((9 * mid, mid), F32),), scalars=1, flops=3 * unit,
    )
    plans = (
        plan(mid, width // 256, ((1, 2),)), plan(width, 1, ((2, 1),), low_rows)
    ) if split else None
    dmid1, *low_part = call(
        functools.partial(slope_kernel, plans=plans),
        [shape((rows, mid), BF16)]
        + ([shape((2 * low_rows, 256))] * 2 if split else [shape((mid, width)), shape((width, mid))]),
        (spot, dcols, conv_middle, s1, inputs, turned_part, own_part, sums, spairs, bias),
        (ext, flat, pltpu.VMEM((width, mid), F32), pltpu.VMEM((mid, width), F32)),
        scalars=1, flops=4 * unit,
    )
    portion = width // devices
    if not split:
        (input_grad,) = call(
            input_kernel, [shape((rows, width), BF16)], (dmid1, conv_first, dpre), flops=unit
        )
        grads = [
            lax.psum_scatter(
                (part[0] * scale).reshape(-1), ("group", "ghost"), scatter_dimension=0, tiled=True
            )
            for part in (low_part[1:], middle_part, low_part)
        ]
        gain_grad = lax.dynamic_slice_in_dim(
            lax.psum(gains.reshape(-1) * scale, "group"), (group * ghosts + ghost) * portion, portion
        )
        return (input_grad, *grads, gain_grad)

    def rows_of(height):
        return shape((height, 256))

    def step(kernel, heights, *args, ties=()):
        return call(
            kernel, [rows_of(h) for h in heights for _ in range(2)], (spot,) + args, scalars=1,
            ties=ties,
        )

    low_keep, low_send = low_part
    middle_keep, middle_send = middle_part
    cut = 16 * middle_plan[0][1]
    rest = middle_rows - cut
    middle_got = swap(middle_send, "ghost", ghosts, 1)
    low_got = swap(low_send, "ghost", ghosts, 1)
    (last_keep, last_send, first_keep, first_send, one_keep, one_send, two_keep, two_send) = step(
        functools.partial(start_step, cut=cut, bits=(across, along)),
        (low_rows // 2, low_rows // 2, cut // 2, rest // 2),
        low_keep, low_got, middle_keep, middle_got,
    )
    last_got = swap(last_send, "ghost", ghosts, 2)
    first_got = swap(first_send, "ghost", ghosts, 4)
    one_got = swap(one_send, "ghost", ghosts, 2)
    two_got = swap(two_send, "ghost", ghosts, 4)
    (input_grad,) = call(
        input_kernel, [shape((rows, width), BF16)], (dmid1, conv_first, dpre), flops=unit,
        ties=(one_keep,),
    )
    last_keep, last_send, first_keep, first_send = step(
        functools.partial(pair_step, bits=(along, across)), (low_rows // 4, low_rows // 4),
        last_keep, last_got, first_keep, first_got,
    )
    last_got = swap(last_send, "ghost", ghosts, 4)
    first_got = swap(first_send, "ghost", ghosts, 2)
    one_keep, one_send, two_keep, two_send = step(
        functools.partial(pair_step, bits=(along, across)), (cut // 4, rest // 4),
        one_keep, one_got, two_keep, two_got, ties=(last_keep,),
    )
    one_got = swap(one_send, "ghost", ghosts, 4)
    two_got = swap(two_send, "ghost", ghosts, 2)
    low_keep, low_send = step(
        functools.partial(join_step, bit=near), (low_rows // 4 + 8,),
        last_keep, last_got, first_keep, first_got, gains, ties=(one_keep,),
    )
    low_got = swap(low_send, "group", groups, 1)
    spans = ((0, low_rows // 8), (low_rows // 8, low_rows // 8))
    high_keep, high_send, low_keep, low_send = step(
        functools.partial(tail_step, spans=spans, bits=(near, far)),
        (middle_rows // 8, low_rows // 8 + 8),
        one_keep, one_got, two_keep, two_got, low_keep, low_got,
    )
    high_got = swap(high_send, "group", groups, 1)
    low_got = swap(low_send, "group", groups, 2)
    spans = ((0, cut // 8), (cut // 8, rest // 8))
    high_keep, high_send = step(
        functools.partial(last_step, spans=spans, bit=far), (middle_rows // 16,),
        high_keep, high_got,
    )
    high_got = swap(high_send, "group", groups, 2)
    low = (low_keep + low_got) * scale
    tall = low_rows // 16
    wide = width // 256
    last_grad = low[:tall].reshape(wide, tall // wide, 256).swapaxes(0, 1).reshape(-1)
    first_grad = low[tall : 2 * tall].reshape(-1)
    middle_grad = ((high_keep + high_got) * scale).reshape(-1)
    gains = low[2 * tall :, :PAIR].reshape(-1)
    gain_grad = lax.dynamic_slice_in_dim(gains, (group * ghosts + ghost) * portion, portion)
    return (input_grad, first_grad, middle_grad, last_grad, gain_grad)


def solution(mesh):
    in_specs = (P(("group", "ghost"), None), P(("group", "ghost"), None), P(), P(), P(), P())
    out_specs = (
        P(("group", "ghost"), None),
        P(("group", "ghost")),
        P(("group", "ghost")),
        P(("group", "ghost")),
        P(("group", "ghost")),
    )
    return jax.shard_map(shards, mesh=mesh, in_specs=in_specs, out_specs=out_specs, check_vma=False)
```

```python
import functools

import jax
import jax.numpy as jnp
from jax import lax
from jax.experimental import pallas as pl
from jax.experimental.pallas import tpu as pltpu
from jax.sharding import PartitionSpec as P

GROUP = 64
NEWTON = 5
SIDE = 14
LINE = 16
PAIR = 2 * GROUP
TALL = GROUP + 8
epsilon = 1e-05

F32 = jnp.float32
BF16 = jnp.bfloat16


def dot(left, right):
    return jnp.dot(left, right, preferred_element_type=F32)


def dot_t(left, right):
    return lax.dot_general(left, right, (((0,), (0,)), ((), ())), preferred_element_type=F32)


def dot_nt(left, right):
    return lax.dot_general(left, right, (((1,), (1,)), ((), ())), preferred_element_type=F32)


def halves_of(value):
    high = value.astype(BF16)
    return high, (value - high.astype(F32)).astype(BF16)


def exact(left, right):
    a, b = halves_of(left)
    c, d = halves_of(right)
    low = dot(jnp.concatenate([a, b], axis=1), jnp.concatenate([d, c], axis=0))
    return low + dot(a, c)


def outer_of(row):
    tile = vectors(row)
    return lax.dot_general(
        tile, tile, (((0,), (0,)), ((), ())), preferred_element_type=F32,
        precision=lax.Precision.HIGHEST,
    )


def sigmoid(value):
    return 0.5 * jnp.tanh(0.5 * value) + 0.5


def two_rows(row):
    high, low = halves_of(jnp.broadcast_to(row, (16, row.shape[1])))
    at = lax.broadcasted_iota(jnp.int32, high.shape, 0)
    return jnp.where(at == 0, high.astype(F32), jnp.where(at == 1, low.astype(F32), 0.0)).astype(
        BF16
    )


def row_times(row, matrix, product=dot):
    return jnp.sum(product(two_rows(row), matrix), axis=0, keepdims=True)


def rank_one(left, right):
    tiles = []
    for row, order in ((left, (0, 1, 0)), (right, (0, 0, 1))):
        pair = halves_of(jnp.broadcast_to(row, (16, row.shape[1])))
        at = lax.broadcasted_iota(jnp.int32, pair[0].shape, 0)
        tile = jnp.zeros(pair[0].shape, F32)
        for place, which in enumerate(order):
            tile = jnp.where(at == place, pair[which].astype(F32), tile)
        tiles.append(tile.astype(BF16))
    return dot_t(*tiles)


def chunk_of(rows, most):
    best = 16
    for size in range(16, most + 1, 16):
        if rows % size == 0:
            best = size
    return best


def loop(count, body, carry):
    for at in range(count):
        carry = body(at, carry)
    return carry


def left_half(shape):
    return lax.broadcasted_iota(jnp.int32, shape, 1) < GROUP


def spread(packed):
    left = left_half(packed.shape)
    zero = jnp.zeros_like(packed)
    return jnp.concatenate([jnp.where(left, packed, zero), jnp.where(left, zero, packed)], axis=0)


def pack(square):
    top, bottom = square[:GROUP], square[GROUP:]
    return jnp.where(left_half(top.shape), top, bottom)


def vectors(*rows):
    at = lax.broadcasted_iota(jnp.int32, (8, PAIR), 0)
    tile = jnp.zeros((8, PAIR), F32)
    for place, row in enumerate(rows):
        tile = jnp.where(at == place, row, tile)
    return tile


def fold(value):
    rows, lanes = value.shape
    return jnp.sum(value.reshape(rows // 8, 8, lanes), axis=0)


def pad_lines(source, ext, rows):
    for line in range(rows // SIDE):
        place = 24 + LINE * (line + line // SIDE)
        ext[place : place + SIDE, :] = source[SIDE * line : SIDE * (line + 1), :]


def unpad_lines(source, target, rows):
    for line in range(rows // SIDE):
        place = LINE * (line + line // SIDE)
        target[SIDE * line : SIDE * (line + 1), :] = source[place : place + SIDE, :]


def padded_rows(rows):
    return rows // (SIDE * SIDE) * (SIDE + 1) * LINE


def shifted(ext, cols):
    length = cols.shape[1]
    for col in range(3):
        cols[col] = ext[7 + col : 7 + col + length, :].astype(BF16)


def emit_split(source, keep, send, core, plan):
    for start, height, first, size, mine in plan:
        lanes = keep.shape[1]
        for wide in range(source.shape[1] // lanes):
            to = slice(start + wide * height, start + (wide + 1) * height)
            cols = slice(wide * lanes, (wide + 1) * lanes)
            for target, half in ((keep, core), (send, 1 - core)):
                place = pl.multiple_of((mine + half) * size + first, 8)
                target[to, :] = source[pl.ds(place, height), cols]


def plan_of(parts, piece, wide, ghosts, start=0):
    plan = []
    for first, height, steps in parts:
        for at in range(2 ** len(steps)):
            source = 0
            for place, (axis, bit) in enumerate(steps):
                value = (at >> (len(steps) - 1 - place)) & 1
                source += value << bit if axis == "ghost" else (value << bit) * ghosts
            plan.append((start, height, first, piece, source))
            start += height * wide
    return plan


def half_of(left, right, bit, start=0, rows=None):
    rows = (left.shape[0] if rows is None else rows) // 2
    mine = pl.ds(pl.multiple_of(start + bit * rows, 8), rows)
    other = pl.ds(pl.multiple_of(start + (1 - bit) * rows, 8), rows)
    return left[mine, :] + right[mine, :], left[other, :] + right[other, :]


def emit_pairs(stats, outs, spot):
    shape = (GROUP, PAIR)
    row = lax.broadcasted_iota(jnp.int32, shape, 0)
    lane = lax.broadcasted_iota(jnp.int32, shape, 1)
    left = lane < GROUP
    col = jnp.where(left, lane, lane - GROUP)
    for parity in range(2):
        for slot in range(stats.shape[0] // 4):
            pair = 4 * slot + parity, 4 * slot + 2 + parity
            first, second = (stats[p, :GROUP, :] for p in pair)
            upper = jnp.where(left, first, pltpu.roll(second, GROUP, 1))
            lower = jnp.where(left, pltpu.roll(first, GROUP, 1), second)
            rows = [
                jnp.sum(jnp.where(row == col, m, 0.0), axis=0, keepdims=True)
                for m in (first, second)
            ]
            for place in range(2):
                rows += [stats[p, GROUP + place : GROUP + place + 1, :] for p in pair]
            both = jnp.concatenate([jnp.where(row <= col, upper, lower), vectors(*rows)], axis=0)

            @pl.when(spot[1] == parity)
            def _(both=both, slot=slot):
                outs[0][slot] = both

            @pl.when(spot[1] != parity)
            def _(both=both, slot=slot):
                outs[1][slot] = both


def take_pairs(total, packed):
    result = []
    if not packed:
        for at in range(total.shape[0]):
            vecs = [total[at, GROUP + p : GROUP + p + 1, :] for p in range(2)]
            result.append((spread(total[at, :GROUP, :]), *vecs))
        return result
    shape = (PAIR, PAIR)
    row = lax.broadcasted_iota(jnp.int32, shape, 0)
    col = lax.broadcasted_iota(jnp.int32, shape, 1)
    mask = jnp.where(row < GROUP, row - col, col - row) < 0
    eye = identity()
    for slot in range(total.shape[0]):
        both = total[slot, :GROUP, :]
        turned = pltpu.roll(both, GROUP, 1)
        left = left_half(both.shape)
        for at in range(2):
            twice = jnp.where(left, *((both, turned) if at == 0 else (turned, both)))
            part = jnp.where(mask, spread(twice), 0.0)
            line = [total[slot, GROUP + 2 * p + at : GROUP + 2 * p + at + 1, :] for p in range(3)]
            result.append((part + part.T + eye * line[0], line[1], line[2]))
    return result


def add_kernel(left, right, out):
    out[...] = left[...] + right[...]


def forward_kernel(
    spot, x_far, w1_far, wm_far, w3_far, h1pad, s1, h2, s2, cen, means, sums, *rest, split
):
    outs, (x, w1, wm, w3, sems, ext, cols, flat, branch, stats) = rest[:-10], rest[-10:]
    rows = x.shape[0]
    part = chunk_of(rows, 128)

    def slab(at):
        here = slice(at * part, (at + 1) * part)
        return pltpu.make_async_copy(x_far.at[here, :], x.at[here, :], sems.at[3 + at])

    weights = [
        pltpu.make_async_copy(far, ref, sems.at[at])
        for at, (far, ref) in enumerate(((w1_far, w1), (wm_far, wm), (w3_far, w3)))
    ]
    weights[0].start()
    for at in range(rows // part):
        slab(at).start()
    weights[1].start()
    weights[2].start()
    chunk = chunk_of(rows, 128)
    ext[...] = jnp.zeros_like(ext)

    weights[0].wait()

    def first(at, carry):
        here = slice(at * chunk, (at + 1) * chunk)
        slab(at).wait()
        act = dot(x[here, :], w1[...])
        sig = sigmoid(act)
        flat[here, :] = act * sig
        s1[here, :] = sig * (1.0 + act * (1.0 - sig))
        return carry

    loop(rows // chunk, first, 0)
    pad_lines(flat, ext, rows)
    shifted(ext, cols)
    padded = padded_rows(rows)
    h1pad[...] = cols[1, LINE : LINE + padded, :]
    big = chunk_of(padded, 256)
    weights[1].wait()

    def middle(at, carry):
        base = at * big
        total = jnp.zeros((big, wm.shape[1]), F32)
        for row in range(3):
            for col in range(3):
                left = cols[col, pl.ds(base + LINE * row, big), :]
                k = 3 * row + col
                depth = left.shape[1]
                total = total + dot(left, wm[k * depth : (k + 1) * depth, :])
        ext[pl.ds(base, big), :] = total
        return carry

    loop(padded // big, middle, 0)
    unpad_lines(ext, flat, rows)
    width = w3.shape[1]
    weights[2].wait()

    def last(at, carry):
        total, hidden_sum = carry
        here = slice(at * chunk, (at + 1) * chunk)
        act = flat[here, :]
        sig = sigmoid(act)
        hidden = (act * sig).astype(BF16)
        h2[here, :] = hidden
        s2[here, :] = sig * (1.0 + act * (1.0 - sig))
        out = dot(hidden, w3[...])
        branch[here, :] = out
        return total + fold(out), hidden_sum + fold(hidden.astype(F32))

    zeros = jnp.zeros((8, width), F32), jnp.zeros((8, w3.shape[0]), F32)
    total, hidden_sum = loop(rows // chunk, last, zeros)
    sums[...] = jnp.broadcast_to(jnp.sum(hidden_sum, axis=0, keepdims=True), sums.shape)
    total = jnp.sum(total, axis=0, keepdims=True)
    mean = total / rows
    means[...] = jnp.broadcast_to(mean, means.shape)
    for quad in range(width // 256):
        lanes = slice(256 * quad, 256 * (quad + 1))
        centered = (branch[:, lanes] - mean[:, lanes]).astype(BF16)
        cen[:, lanes] = centered
        square = dot_t(centered, centered)
        for half in range(2):
            pair = 2 * quad + half
            ch = slice(PAIR * pair, PAIR * (pair + 1))
            row = mean[:, ch]
            outer = outer_of(row)
            inner = square[PAIR * half : PAIR * (half + 1), PAIR * half : PAIR * (half + 1)]
            top, low = pack(inner + outer * rows), vectors(total[:, ch])
            stats[pair, :GROUP, :] = top
            stats[pair, GROUP:, :] = low
    if split:
        emit_pairs(stats, outs, spot)
    else:
        outs[0][...] = stats[...]


def identity():
    shape = (PAIR, PAIR)
    return jnp.where(
        lax.broadcasted_iota(jnp.int32, shape, 0) == lax.broadcasted_iota(jnp.int32, shape, 1),
        1.0, 0.0,
    ).astype(F32)


def per_block(square):
    row_sums = jnp.sum(square, axis=1, keepdims=True)
    top = jnp.sum(row_sums[:GROUP], axis=0, keepdims=True)
    bottom = jnp.sum(row_sums[GROUP:], axis=0, keepdims=True)
    upper = lax.broadcasted_iota(jnp.int32, (PAIR, 1), 0) < GROUP
    return jnp.where(upper, top, bottom)


def total_of(terms):
    total = terms[0][...]
    for term in terms[1:]:
        total = total + term[...]
    return total


def whiten_kernel(*refs, span, packed):
    terms, (out, keep) = refs[:-2], refs[-2:]
    given = take_pairs(total_of(terms), packed)
    eye = identity()
    blocks = spread(jnp.ones((GROUP, PAIR), F32))
    means = [sums / span for _, sums, _ in given]
    covs = [
        moments / span - outer_of(mean) * blocks + epsilon * eye
        for (moments, _, _), mean in zip(given, means)
    ]
    traces = [per_block(cov * eye) for cov in covs]
    normed = [cov / trace for cov, trace in zip(covs, traces)]
    powers = [1.5 * eye - 0.5 * norm for norm in normed]
    for at, trace in enumerate(traces):
        keep[at, 0] = normed[at]
        keep[at, 1] = eye / trace
    for sweep in range(NEWTON - 1):
        squares = [exact(power, power) for power in powers]
        sides = [exact(power, norm) for power, norm in zip(powers, normed)]
        for at, power in enumerate(powers):
            keep[at, 2 + 2 * sweep] = power
            keep[at, 3 + 2 * sweep] = squares[at]
        powers = [
            1.5 * power - 0.5 * exact(square, side)
            for power, square, side in zip(powers, squares, sides)
        ]
    for at, power in enumerate(powers):
        keep[at, 2 * NEWTON] = power
        out[at, :GROUP, :] = pack(power / jnp.sqrt(traces[at]))
        out[at, GROUP:, :] = vectors(means[at])


def pull_kernel(*refs, span, packed):
    terms, (keep, out) = refs[:-2], refs[-2:]
    given = take_pairs(total_of(terms), packed)
    eye = identity()
    every = range(len(given))
    normed = [keep[at, 0] for at in every]
    inverse = [per_block(keep[at, 1]) / GROUP for at in every]
    roots = [jnp.sqrt(value) for value in inverse]
    powers = [keep[at, 2 * NEWTON] for at in every]
    grads = [given[at][0] * roots[at] for at in every]
    trace_grads = [
        -0.5 * inverse[at] * roots[at] * per_block(given[at][0] * powers[at]) for at in every
    ]
    normed_grads = [jnp.zeros_like(grads[0])] * len(given)
    for sweep in reversed(range(NEWTON - 1)):
        power = [keep[at, 2 + 2 * sweep] for at in every]
        turned = [exact(grads[at], normed[at]) for at in every]
        inner = [exact(power[at], grads[at]) for at in every]
        turned = [exact(turned[at] + turned[at].T, power[at]) for at in every]
        inner = [exact(keep[at, 3 + 2 * sweep], inner[at]) for at in every]
        normed_grads = [normed_grads[at] - 0.25 * (inner[at] + inner[at].T) for at in every]
        outer = [exact(turned[at], power[at]) for at in every]
        inner = [exact(power[at], turned[at]) for at in every]
        grads = [
            1.5 * grads[at] - 0.25 * (outer[at] + outer[at].T + inner[at]) for at in every
        ]
    for at in every:
        normed_grad = normed_grads[at] - 0.5 * grads[at]
        trace_grad = trace_grads[at] - inverse[at] * per_block(normed_grad * normed[at])
        both = normed_grad * inverse[at] + eye * trace_grad
        bias = -exact(vectors(given[at][1] / span), (powers[at] * roots[at]).T)
        out[at, :GROUP, :] = pack(both / span)
        out[at, GROUP:, :] = vectors(bias[0:1, :], given[at][2])


def place_pairs(spot, given, pairs, split):
    if split:
        for side, shares in enumerate(given):
            for at in range(shares.shape[0]):
                pairs[2 * at + jnp.bitwise_xor(side, spot[1])] = shares[at]
    else:
        pairs[...] = given[0][...]


def quad_matrix(pairs, quad):
    zero = jnp.zeros((PAIR, PAIR), F32)
    first = spread(pairs[2 * quad, :GROUP, :])
    second = spread(pairs[2 * quad + 1, :GROUP, :])
    top = jnp.concatenate([first, zero], axis=1)
    bottom = jnp.concatenate([zero, second], axis=1)
    return jnp.concatenate([top, bottom], axis=0).astype(BF16)


def row_of(pairs, quad, place):
    at = GROUP + place
    return jnp.concatenate(
        [pairs[2 * quad, at : at + 1, :], pairs[2 * quad + 1, at : at + 1, :]], axis=1
    )


def backward_kernel(spot, x, og, cen, means, gain, *rest, split, shares):
    given, rest = rest[:shares], rest[shares:]
    (dwb, dpre_out, w_out), outs, (pairs, stats) = rest[:3], rest[3:-2], rest[-2:]
    rows, width = x.shape
    place_pairs(spot, given, pairs, split)
    w_out[...] = pairs[...]
    chunk = chunk_of(rows, 128)
    for quad in range(width // 256):
        lanes = slice(256 * quad, 256 * (quad + 1))
        whiten = quad_matrix(pairs, quad)
        away = means[0:1, lanes] - row_of(pairs, quad, 0)
        shift = row_times(away, whiten)
        scale = gain[:, lanes]

        def step(at, carry, lanes=lanes, whiten=whiten, shift=shift, scale=scale):
            col_sum, gain_sum = carry
            here = slice(at * chunk, (at + 1) * chunk)
            white = dot(cen[here, lanes], whiten) + shift
            pre = x[here, lanes].astype(F32) + scale * white
            sig = sigmoid(pre)
            dpre = og[here, lanes].astype(F32) * (sig * (1.0 + pre * (1.0 - sig)))
            dpre_out[here, lanes] = dpre
            dwhite = scale * dpre
            dwb[here, lanes] = dwhite.astype(BF16)
            return col_sum + fold(dwhite), gain_sum + fold(dpre * white)

        zero = jnp.zeros((8, 256), F32)
        col_sum, gain_sum = loop(rows // chunk, step, (zero, zero))
        col_sum = jnp.sum(col_sum, axis=0, keepdims=True)
        gain_sum = jnp.sum(gain_sum, axis=0, keepdims=True)
        square = dot_t(cen[:, lanes], dwb[:, lanes]) + rank_one(away, col_sum)
        for half in range(2):
            ch = slice(PAIR * half, PAIR * (half + 1))
            pair = 2 * quad + half
            inner = square[ch, ch]
            stats[pair, :GROUP, :] = pack(inner + inner.T)
            stats[pair, GROUP:, :] = vectors(col_sum[:, ch], gain_sum[:, ch])
    if split:
        emit_pairs(stats, outs, spot)
    else:
        outs[0][...] = stats[...]


def own_kernel(h2, cen, out):
    for quad in range(cen.shape[1] // 256):
        lanes = slice(256 * quad, 256 * (quad + 1))
        out[:, lanes] = dot_t(h2[...], cen[:, lanes]).astype(BF16)


def turn_kernel(dwb, wpairs, w3, turned, flow):
    rows, width = dwb.shape
    chunk = chunk_of(rows, 128)
    for quad in range(width // 256):
        lanes = slice(256 * quad, 256 * (quad + 1))
        whiten = quad_matrix(wpairs, quad).T

        def step(at, carry, lanes=lanes, whiten=whiten):
            here = slice(at * chunk, (at + 1) * chunk)
            turned[here, lanes] = dot(dwb[here, lanes], whiten).astype(BF16)
            return carry

        loop(rows // chunk, step, 0)
    flow[...] = dot_nt(turned[...], w3[...])


def turned_kernel(h2, turned, out):
    for quad in range(turned.shape[1] // 256):
        lanes = slice(256 * quad, 256 * (quad + 1))
        out[:, lanes] = dot_t(h2[...], turned[:, lanes])


def last_kernel(spot, flow, cen, means, s2, w3, wpairs, *rest, split, shares):
    given, (cols, gains, spairs, bias_out, ext, flat, joint) = rest[:shares], rest[shares:]
    rows, width = cen.shape
    place_pairs(spot, given, spairs, split)
    gains[...] = spairs[:, GROUP + 1, :]
    chunk = chunk_of(rows, 128)
    ext[...] = jnp.zeros_like(ext)
    low = jnp.zeros((1, w3.shape[0]), F32)
    for quad in range(width // 256):
        lanes = slice(256 * quad, 256 * (quad + 1))
        sym = quad_matrix(spairs, quad)
        away = means[0:1, lanes] - row_of(wpairs, quad, 0)
        bias = row_of(spairs, quad, 0) + row_times(away, sym)
        bias_out[:, lanes] = jnp.broadcast_to(bias, (8, 256))
        low = low + row_times(bias, w3[:, lanes], dot_nt)
        joint[lanes, :] = dot_nt(sym, w3[:, lanes]).astype(BF16)

    def middle(at, carry):
        here = slice(at * chunk, (at + 1) * chunk)
        flat[here, :] = (flow[here, :] + dot(cen[here, :], joint[...]) + low) * s2[here, :]
        return carry

    loop(rows // chunk, middle, 0)
    pad_lines(flat, ext, rows)
    shifted(ext, cols)


def finish(part, outs, spot, plan):
    if plan:
        emit_split(part, outs[0], outs[1], spot[1], plan)
    else:
        outs[0][...] = part[...]


def slope_kernel(spot, cols, wm, s1, x, dmid1, *rest, plan):
    outs, (ext, flat, part) = rest[:-3], rest[-3:]
    rows, depth = s1.shape
    padded = padded_rows(rows)
    big = chunk_of(padded, 256)

    def step(at, carry):
        base = at * big
        total = jnp.zeros((big, depth), F32)
        for row in range(3):
            for col in range(3):
                near = cols[2 - col, pl.ds(base + LINE * (2 - row), big), :]
                k = 3 * row + col
                total = total + dot_nt(near, wm[k * depth : (k + 1) * depth, :])
        ext[pl.ds(base, big), :] = total
        return carry

    loop(padded // big, step, 0)
    unpad_lines(ext, flat, rows)
    dmid1[...] = (flat[...] * s1[...]).astype(BF16)
    for quad in range(x.shape[1] // 256):
        lanes = slice(256 * quad, 256 * (quad + 1))
        part[lanes, :] = dot_t(x[:, lanes], dmid1[...])
    finish(part, outs, spot, plan)


def middle_kernel(spot, cols, h1pad, turned, own, sums, spairs, bias, *rest, plans):
    outs, (part, part_last) = rest[:-2], rest[-2:]
    padded, depth = h1pad.shape
    for row in range(3):
        for col in range(3):
            k = 3 * row + col
            near = cols[2 - col, LINE * (2 - row) : LINE * (2 - row) + padded, :]
            part[k * depth : (k + 1) * depth, :] = dot_t(h1pad[...], near)
    for quad in range(turned.shape[1] // 256):
        lanes = slice(256 * quad, 256 * (quad + 1))
        sym = quad_matrix(spairs, quad)
        part_last[:, lanes] = (
            turned[:, lanes]
            + dot(own[:, lanes], sym)
            + rank_one(sums[0:1, :], bias[0:1, lanes])
        )
    if plans:
        emit_split(part, outs[0], outs[1], spot[1], plans[0])
        emit_split(part_last, outs[0], outs[1], spot[1], plans[1])
    else:
        outs[0][...] = part[...]
        outs[1][...] = part_last[...]


def spans_step(spot, *refs, steps, extra=0):
    count = 2 * (1 + max(span[0] for spans in steps for span in spans))
    given, outs = refs[: count + extra], refs[count + extra :]
    for at, spans in enumerate(steps):
        to = 0
        for source, start, size, bit in spans:
            mine, other = half_of(given[2 * source], given[2 * source + 1], spot[bit], start, size)
            outs[2 * at][to : to + size // 2, :] = mine
            outs[2 * at + 1][to : to + size // 2, :] = other
            to += size // 2
        left = outs[2 * at].shape[0] - to
        if not left:
            continue
        if extra:
            rows = jnp.concatenate([given[-1][...]] * (outs[0].shape[1] // PAIR), axis=1)
        else:
            tail = given[0].shape[0] - left
            rows = given[0][tail:, :] + given[1][tail:, :]
        for out in outs[2 * at : 2 * at + 2]:
            out[to:, :] = rows


def close_kernel(spot, keep, given, first, middle, last, gain, *, tall, high, scale):
    total = (keep[...] + given[...]) * scale
    for half in range(2):
        lanes = slice(PAIR * half, PAIR * (half + 1))
        step = tall // 4
        for wide in range(4):
            last[pl.ds(2 * wide + half, step, 8), :] = total[step * wide : step * (wide + 1), lanes]
        middle[pl.ds(half, high, 2), :] = total[tall : tall + high, lanes]
        first[pl.ds(half, tall, 2), :] = total[tall + high : 2 * tall + high, lanes]
    gain[...] = total[2 * tall + high :, :PAIR]


def input_kernel(dmid1, w1, dpre, out, token):
    token[...] = jnp.zeros_like(token)
    rows = dpre.shape[0]
    chunk = chunk_of(rows, 128)

    def step(at, carry):
        here = slice(at * chunk, (at + 1) * chunk)
        out[here, :] = (dot_nt(dmid1[here, :], w1[...]) + dpre[here, :]).astype(BF16)
        return carry

    loop(rows // chunk, step, 0)


def call(kernel, outs, args, scratch=(), scalars=0, flops=0, ties=(), far=0, room=40):
    args = tuple(args) + tuple(ties)
    specs = [pl.BlockSpec(memory_space=pltpu.SMEM)] * scalars
    specs += [pl.BlockSpec(memory_space=pl.ANY)] * far
    specs += [pl.BlockSpec(memory_space=pltpu.VMEM)] * (len(args) - scalars - len(ties) - far)
    specs += [pl.BlockSpec(memory_space=pl.ANY)] * len(ties)
    count = len(args) - len(ties)

    def body(*refs):
        kernel(*refs[:count], *refs[len(args) :])

    size = sum(a.size * a.dtype.itemsize for a in args)
    size += sum(o.size * o.dtype.itemsize for o in outs)
    return pl.pallas_call(
        body,
        out_shape=tuple(outs),
        in_specs=specs,
        out_specs=tuple(pl.BlockSpec(memory_space=pltpu.VMEM) for _ in outs),
        scratch_shapes=list(scratch),
        cost_estimate=pl.CostEstimate(flops=flops, bytes_accessed=size, transcendentals=0),
        compiler_params=pltpu.CompilerParams(vmem_limit_bytes=room * 2**20),
    )(*args)


def shape(dims, dtype=F32):
    return jax.ShapeDtypeStruct(dims, dtype)


def swap(value, axis, size, flip):
    return lax.ppermute(value, axis, [(at, at ^ flip) for at in range(size)])


def shards(inputs, out_grad, conv_first, conv_middle, conv_last, gain):
    rows, width = inputs.shape
    mid = conv_first.shape[1]
    pairs = width // PAIR
    ghosts = lax.axis_size("ghost")
    groups = lax.axis_size("group")
    devices = ghosts * groups
    span = float(rows * ghosts)
    scale = (rows * devices) ** (-0.5)
    padded = padded_rows(rows)
    ghost = lax.axis_index("ghost")
    group = lax.axis_index("group")
    bits = [ghost] + [(ghost >> bit) & 1 for bit in range(3)]
    bits += [(group >> bit) & 1 for bit in range(2)]
    spot = jnp.stack(bits).astype(jnp.int32)
    core, across, along, near, far = 1, 2, 3, 4, 5
    split = ghosts == 8 and pairs == 8 and groups == 4
    unit = 2 * rows * width * mid

    ext = pltpu.VMEM((24 + padded + LINE + 8, mid), F32)
    flat = pltpu.VMEM((rows, mid), F32)
    cols = (3, padded + 2 * LINE, mid)
    big = (pairs, TALL, PAIR)
    half = (pairs // 2, TALL, PAIR)
    packed = (pairs // 4, TALL, PAIR)
    stats_outs = [shape(packed)] * 2 if split else [shape(big)]
    stats_held = pltpu.VMEM(big, F32)

    def collect(stats, ties):
        if not split:
            return [lax.psum(stats[0], "ghost")]
        total, send = stats
        given = swap(send, "ghost", ghosts, 1)
        (total,) = call(add_kernel, [shape(packed)], (total, given))
        given = swap(total, "ghost", ghosts, 2)
        (total,) = call(add_kernel, [shape(packed)], (total, given), ties=ties)
        return [total, swap(total, "ghost", ghosts, 4)]

    def share_out(own):
        return [own, swap(own, "ghost", ghosts, 1)] if split else [own]

    own = half if split else big
    held = own[0]
    chunks = rows // chunk_of(rows, 128)
    h1pad, s1, h2, s2, cen, means, sums, *stats = call(
        functools.partial(forward_kernel, split=split),
        [shape((padded, mid), BF16), shape((rows, mid)), shape((rows, mid), BF16),
         shape((rows, mid)), shape((rows, width), BF16), shape((8, width)), shape((8, mid))]
        + stats_outs,
        (spot, inputs, conv_first, conv_middle, conv_last),
        (pltpu.VMEM((rows, width), BF16), pltpu.VMEM(conv_first.shape, BF16),
         pltpu.VMEM(conv_middle.shape, BF16), pltpu.VMEM(conv_last.shape, BF16),
         pltpu.SemaphoreType.DMA((3 + chunks,)),
         ext, pltpu.VMEM(cols, BF16), flat, pltpu.VMEM((rows, width), F32), stats_held),
        scalars=1, flops=5 * unit, far=4, room=40,
    )
    (own_part,) = call(own_kernel, [shape((mid, width), BF16)], (h2, cen), flops=unit)
    share, kept = call(
        functools.partial(whiten_kernel, span=span, packed=split),
        [shape(own), shape((held, 2 * NEWTON + 1, PAIR, PAIR))], collect(stats, (own_part,)), flops=10**7,
    )
    given = share_out(share)
    dwb, dpre, wpairs, *stats = call(
        functools.partial(backward_kernel, split=split, shares=len(given)),
        [shape((rows, width), BF16), shape((rows, width)), shape(big)] + stats_outs,
        (spot, inputs, out_grad, cen, means, gain.reshape(1, width), *given),
        (pltpu.VMEM(big, F32), stats_held), scalars=1, flops=2 * unit,
    )
    turned, flow = call(
        turn_kernel, [shape((rows, width), BF16), shape((rows, mid))], (dwb, wpairs, conv_last),
        flops=2 * unit,
    )
    (turned_part,) = call(turned_kernel, [shape((mid, width))], (h2, turned), flops=unit)
    (pulled,) = call(
        functools.partial(pull_kernel, span=span, packed=split), [shape(own)], (*collect(stats, (flow,)), kept),
        flops=10**7, ties=(turned_part,),
    )
    given = share_out(pulled)

    dcols, gains, spairs, bias = call(
        functools.partial(last_kernel, split=split, shares=len(given)),
        [shape(cols, BF16), shape((pairs, PAIR)), shape(big), shape((8, width))],
        (spot, flow, cen, means, s2, conv_last, wpairs, *given),
        (ext, flat, pltpu.VMEM((width, mid), BF16)), scalars=1, flops=2 * unit,
    )
    half_rows = mid * width // 512
    orders = (
        (("ghost", 1), ("ghost", 2), ("group", 0), ("group", 1)),
        (("ghost", 2), ("group", 0), ("ghost", 1), ("group", 1)),
        (("group", 0), ("ghost", 1), ("ghost", 2), ("group", 1)),
    )
    high, tall = 9 * mid // devices, width // devices
    cut = high // 24 * 8
    middle_plan = last_plan = first_plan = None
    if split:
        middle_plan = plan_of(
            [(0, cut, orders[0]), (cut, high - cut, orders[1])], high, 1, ghosts
        )
        last_plan = plan_of(
            [(0, mid // devices, orders[0])], mid // devices, width // 256, ghosts, 9 * mid // 2
        )
        first_plan = plan_of([(0, tall, orders[2])], tall, 1, ghosts)
    middle_part = call(
        functools.partial(middle_kernel, plans=(middle_plan, last_plan) if split else None),
        [shape((9 * mid // 2 + half_rows, mid))] * 2 if split
        else [shape((9 * mid, mid)), shape((mid, width))],
        (spot, dcols, h1pad, turned_part, own_part, sums, spairs, bias),
        (pltpu.VMEM((9 * mid, mid), F32), pltpu.VMEM((mid, width), F32)),
        scalars=1, flops=3 * unit,
    )
    dmid1, *first_part = call(
        functools.partial(slope_kernel, plan=first_plan),
        [shape((rows, mid), BF16)]
        + ([shape((half_rows, mid))] * 2 if split else [shape((width, mid))]),
        (spot, dcols, conv_middle, s1, inputs),
        (ext, flat, pltpu.VMEM((width, mid), F32)), scalars=1, flops=4 * unit,
    )
    portion = width // devices
    if not split:
        input_grad, _ = call(
            input_kernel, [shape((rows, width), BF16), shape((8, PAIR))],
            (dmid1, conv_first, dpre), flops=unit,
        )
        grads = [
            lax.psum_scatter(
                (part[0] * scale).reshape(-1), ("group", "ghost"), scatter_dimension=0, tiled=True
            )
            for part in (first_part, middle_part, middle_part[1:])
        ]
        gain_grad = lax.dynamic_slice_in_dim(
            lax.psum(gains.reshape(-1) * scale, "group"), (group * ghosts + ghost) * portion, portion
        )
        return (input_grad, *grads, gain_grad)

    def move(parts, ways):
        result = []
        for at, (axis, flip) in enumerate(ways):
            result.append(parts[2 * at])
            result.append(swap(parts[2 * at + 1], axis, groups if axis == "group" else ghosts, flip))
        return result

    def run(steps, given, extra=(), more=0, ties=()):
        outs = []
        for at, spans in enumerate(steps):
            height = sum(span[2] for span in spans) // 2 + (more if at == 0 else 0)
            outs += [shape((height, mid))] * 2
        return call(
            functools.partial(spans_step, steps=steps, extra=len(extra)), outs,
            (spot, *given, *extra), scalars=1, ties=ties,
        )

    core_way, x_way, y_way = (("ghost", 1 << bit) for bit in range(3))
    near_way, far_way = ("group", 1), ("group", 2)
    given = move([*middle_part, *first_part], (core_way, core_way))
    pieces = devices // 2
    a_low, a_high, b_all = half_rows, pieces * cut, pieces * (high - cut)
    parts = run(
        (((0, a_high + b_all, a_low, across), (0, 0, a_high, across)),
         ((0, a_high, b_all, along),), ((1, 0, half_rows, near),)), given,
    )
    given = move(parts, (x_way, y_way, near_way))
    input_grad, token = call(
        input_kernel, [shape((rows, width), BF16), shape((8, PAIR))], (dmid1, conv_first, dpre),
        flops=unit, ties=(parts[0],),
    )
    a_low, a_high, b_all, c_all = a_low // 2, a_high // 2, b_all // 2, half_rows // 2
    parts = run(
        (((0, 0, a_low, along), (0, a_low, a_high, along)), ((1, 0, b_all, near),),
         ((2, 0, c_all, across),)), given, ties=(token,),
    )
    given = move(parts, (y_way, near_way, x_way))
    a_low, a_high, b_all, c_all = a_low // 2, a_high // 2, b_all // 2, c_all // 2
    parts = run(
        (((0, 0, a_low, near), (0, a_low, a_high, near)), ((1, 0, b_all, across),),
         ((2, 0, c_all, along),)), given, extra=(gains,), more=8,
    )
    given = move(parts, (near_way, x_way, y_way))
    a_low, a_high, b_all, c_all = a_low // 2, a_high // 2, b_all // 2, c_all // 2
    parts = run(
        (((0, 0, a_low, far), (0, a_low, a_high, far), (1, 0, b_all, far), (2, 0, c_all, far)),),
        given, more=8,
    )
    given = move(parts, (far_way,))
    first_grad, middle_grad, last_grad, gain_grad = call(
        functools.partial(close_kernel, tall=tall, high=high, scale=scale),
        [shape((2 * tall, PAIR)), shape((2 * high, PAIR)), shape((2 * tall, PAIR)),
         shape((8, PAIR))],
        (spot, *given), scalars=1,
    )
    gain_grad = lax.dynamic_slice_in_dim(
        gain_grad.reshape(-1), (group * ghosts + ghost) * portion, portion
    )
    return (
        input_grad, first_grad.reshape(-1), middle_grad.reshape(-1), last_grad.reshape(-1),
        gain_grad,
    )


def solution(mesh):
    in_specs = (P(("group", "ghost"), None), P(("group", "ghost"), None), P(), P(), P(), P())
    out_specs = (
        P(("group", "ghost"), None),
        P(("group", "ghost")),
        P(("group", "ghost")),
        P(("group", "ghost")),
        P(("group", "ghost")),
    )
    return jax.shard_map(shards, mesh=mesh, in_specs=in_specs, out_specs=out_specs, check_vma=False)
```

```python
import functools

import jax
import jax.numpy as jnp
from jax import lax
from jax.experimental import pallas as pl
from jax.experimental.pallas import tpu as pltpu
from jax.sharding import PartitionSpec as P

GROUP = 64
NEWTON = 5
SIDE = 14
LINE = 16
PAIR = 2 * GROUP
TALL = GROUP + 8
epsilon = 1e-05

F32 = jnp.float32
BF16 = jnp.bfloat16


def dot(left, right):
    return jnp.dot(left, right, preferred_element_type=F32)


def dot_t(left, right):
    return lax.dot_general(left, right, (((0,), (0,)), ((), ())), preferred_element_type=F32)


def dot_nt(left, right):
    return lax.dot_general(left, right, (((1,), (1,)), ((), ())), preferred_element_type=F32)


def halves_of(value):
    high = value.astype(BF16)
    return high, (value - high.astype(F32)).astype(BF16)


def exact(left, right):
    a, b = halves_of(left)
    c, d = halves_of(right)
    low = dot(jnp.concatenate([a, b], axis=1), jnp.concatenate([d, c], axis=0))
    return low + dot(a, c)


def outer_of(row):
    tile = vectors(row)
    return lax.dot_general(
        tile, tile, (((0,), (0,)), ((), ())), preferred_element_type=F32,
        precision=lax.Precision.HIGHEST,
    )


def sigmoid(value):
    return 0.5 * jnp.tanh(0.5 * value) + 0.5


def two_rows(row):
    high, low = halves_of(jnp.broadcast_to(row, (16, row.shape[1])))
    at = lax.broadcasted_iota(jnp.int32, high.shape, 0)
    return jnp.where(at == 0, high.astype(F32), jnp.where(at == 1, low.astype(F32), 0.0)).astype(
        BF16
    )


def row_times(row, matrix, product=dot):
    return jnp.sum(product(two_rows(row), matrix), axis=0, keepdims=True)


def rank_one(left, right):
    tiles = []
    for row, order in ((left, (0, 1, 0)), (right, (0, 0, 1))):
        pair = halves_of(jnp.broadcast_to(row, (16, row.shape[1])))
        at = lax.broadcasted_iota(jnp.int32, pair[0].shape, 0)
        tile = jnp.zeros(pair[0].shape, F32)
        for place, which in enumerate(order):
            tile = jnp.where(at == place, pair[which].astype(F32), tile)
        tiles.append(tile.astype(BF16))
    return dot_t(*tiles)


def chunk_of(rows, most):
    best = 16
    for size in range(16, most + 1, 16):
        if rows % size == 0:
            best = size
    return best


def loop(count, body, carry):
    for at in range(count):
        carry = body(at, carry)
    return carry


def left_half(shape):
    return lax.broadcasted_iota(jnp.int32, shape, 1) < GROUP


def spread(packed):
    left = left_half(packed.shape)
    zero = jnp.zeros_like(packed)
    return jnp.concatenate([jnp.where(left, packed, zero), jnp.where(left, zero, packed)], axis=0)


def pack(square):
    top, bottom = square[:GROUP], square[GROUP:]
    return jnp.where(left_half(top.shape), top, bottom)


def vectors(*rows):
    at = lax.broadcasted_iota(jnp.int32, (8, PAIR), 0)
    tile = jnp.zeros((8, PAIR), F32)
    for place, row in enumerate(rows):
        tile = jnp.where(at == place, row, tile)
    return tile


def fold(value):
    rows, lanes = value.shape
    return jnp.sum(value.reshape(rows // 8, 8, lanes), axis=0)


def pad_lines(source, ext, rows):
    for line in range(rows // SIDE):
        place = 24 + LINE * (line + line // SIDE)
        ext[place : place + SIDE, :] = source[SIDE * line : SIDE * (line + 1), :]


def unpad_lines(source, target, rows):
    for line in range(rows // SIDE):
        place = LINE * (line + line // SIDE)
        target[SIDE * line : SIDE * (line + 1), :] = source[place : place + SIDE, :]


def padded_rows(rows):
    return rows // (SIDE * SIDE) * (SIDE + 1) * LINE


def shifted(ext, cols):
    length = cols.shape[1]
    for col in range(3):
        cols[col] = ext[7 + col : 7 + col + length, :].astype(BF16)


def emit_split(source, keep, send, core, plan):
    for start, height, first, size, mine in plan:
        lanes = keep.shape[1]
        for wide in range(source.shape[1] // lanes):
            to = slice(start + wide * height, start + (wide + 1) * height)
            cols = slice(wide * lanes, (wide + 1) * lanes)
            for target, half in ((keep, core), (send, 1 - core)):
                place = pl.multiple_of((mine + half) * size + first, 8)
                target[to, :] = source[pl.ds(place, height), cols]


def plan_of(parts, piece, wide, ghosts, start=0):
    plan = []
    for first, height, steps in parts:
        for at in range(2 ** len(steps)):
            source = 0
            for place, (axis, bit) in enumerate(steps):
                value = (at >> (len(steps) - 1 - place)) & 1
                source += value << bit if axis == "ghost" else (value << bit) * ghosts
            plan.append((start, height, first, piece, source))
            start += height * wide
    return plan


def half_of(left, right, bit, start=0, rows=None):
    rows = (left.shape[0] if rows is None else rows) // 2
    mine = pl.ds(pl.multiple_of(start + bit * rows, 8), rows)
    other = pl.ds(pl.multiple_of(start + (1 - bit) * rows, 8), rows)
    return left[mine, :] + right[mine, :], left[other, :] + right[other, :]


def emit_pairs(stats, outs, spot):
    shape = (GROUP, PAIR)
    row = lax.broadcasted_iota(jnp.int32, shape, 0)
    lane = lax.broadcasted_iota(jnp.int32, shape, 1)
    left = lane < GROUP
    col = jnp.where(left, lane, lane - GROUP)
    for parity in range(2):
        for slot in range(stats.shape[0] // 4):
            pair = 4 * slot + parity, 4 * slot + 2 + parity
            first, second = (stats[p, :GROUP, :] for p in pair)
            upper = jnp.where(left, first, pltpu.roll(second, GROUP, 1))
            lower = jnp.where(left, pltpu.roll(first, GROUP, 1), second)
            rows = [
                jnp.sum(jnp.where(row == col, m, 0.0), axis=0, keepdims=True)
                for m in (first, second)
            ]
            for place in range(2):
                rows += [stats[p, GROUP + place : GROUP + place + 1, :] for p in pair]
            both = jnp.concatenate([jnp.where(row <= col, upper, lower), vectors(*rows)], axis=0)

            @pl.when(spot[1] == parity)
            def _(both=both, slot=slot):
                outs[0][slot] = both

            @pl.when(spot[1] != parity)
            def _(both=both, slot=slot):
                outs[1][slot] = both


def take_pairs(total, packed):
    result = []
    if not packed:
        for at in range(total.shape[0]):
            vecs = [total[at, GROUP + p : GROUP + p + 1, :] for p in range(2)]
            result.append((spread(total[at, :GROUP, :]), *vecs))
        return result
    shape = (PAIR, PAIR)
    row = lax.broadcasted_iota(jnp.int32, shape, 0)
    col = lax.broadcasted_iota(jnp.int32, shape, 1)
    mask = jnp.where(row < GROUP, row - col, col - row) < 0
    eye = identity()
    for slot in range(total.shape[0]):
        both = total[slot, :GROUP, :]
        turned = pltpu.roll(both, GROUP, 1)
        left = left_half(both.shape)
        for at in range(2):
            twice = jnp.where(left, *((both, turned) if at == 0 else (turned, both)))
            part = jnp.where(mask, spread(twice), 0.0)
            line = [total[slot, GROUP + 2 * p + at : GROUP + 2 * p + at + 1, :] for p in range(3)]
            result.append((part + part.T + eye * line[0], line[1], line[2]))
    return result


def add_kernel(left, right, out):
    out[...] = left[...] + right[...]


def forward_kernel(
    spot, x_far, w1_far, wm_far, w3_far, h1pad, s1, h2, s2, cen, means, sums, *rest, split
):
    outs, (x, w1, wm, w3, sems, ext, cols, flat, branch, stats) = rest[:-10], rest[-10:]
    rows = x.shape[0]
    part = chunk_of(rows, 128)

    def slab(at):
        here = slice(at * part, (at + 1) * part)
        return pltpu.make_async_copy(x_far.at[here, :], x.at[here, :], sems.at[3 + at])

    weights = [
        pltpu.make_async_copy(far, ref, sems.at[at])
        for at, (far, ref) in enumerate(((w1_far, w1), (wm_far, wm), (w3_far, w3)))
    ]
    weights[0].start()
    for at in range(rows // part):
        slab(at).start()
    weights[1].start()
    weights[2].start()
    chunk = chunk_of(rows, 128)
    ext[...] = jnp.zeros_like(ext)

    weights[0].wait()

    def first(at, carry):
        here = slice(at * chunk, (at + 1) * chunk)
        slab(at).wait()
        act = dot(x[here, :], w1[...])
        sig = sigmoid(act)
        flat[here, :] = act * sig
        s1[here, :] = sig * (1.0 + act * (1.0 - sig))
        return carry

    loop(rows // chunk, first, 0)
    pad_lines(flat, ext, rows)
    shifted(ext, cols)
    padded = padded_rows(rows)
    h1pad[...] = cols[1, LINE : LINE + padded, :]
    big = chunk_of(padded, 256)
    weights[1].wait()

    def middle(at, carry):
        base = at * big
        total = jnp.zeros((big, wm.shape[1]), F32)
        for row in range(3):
            for col in range(3):
                left = cols[col, pl.ds(base + LINE * row, big), :]
                k = 3 * row + col
                depth = left.shape[1]
                total = total + dot(left, wm[k * depth : (k + 1) * depth, :])
        ext[pl.ds(base, big), :] = total
        return carry

    loop(padded // big, middle, 0)
    unpad_lines(ext, flat, rows)
    width = w3.shape[1]
    weights[2].wait()

    def last(at, carry):
        total, hidden_sum = carry
        here = slice(at * chunk, (at + 1) * chunk)
        act = flat[here, :]
        sig = sigmoid(act)
        hidden = (act * sig).astype(BF16)
        h2[here, :] = hidden
        s2[here, :] = sig * (1.0 + act * (1.0 - sig))
        out = dot(hidden, w3[...])
        branch[here, :] = out
        return total + fold(out), hidden_sum + fold(hidden.astype(F32))

    zeros = jnp.zeros((8, width), F32), jnp.zeros((8, w3.shape[0]), F32)
    total, hidden_sum = loop(rows // chunk, last, zeros)
    sums[...] = jnp.broadcast_to(jnp.sum(hidden_sum, axis=0, keepdims=True), sums.shape)
    total = jnp.sum(total, axis=0, keepdims=True)
    mean = total / rows
    means[...] = jnp.broadcast_to(mean, means.shape)
    for quad in range(width // 256):
        lanes = slice(256 * quad, 256 * (quad + 1))
        centered = (branch[:, lanes] - mean[:, lanes]).astype(BF16)
        cen[:, lanes] = centered
        square = dot_t(centered, centered)
        for half in range(2):
            pair = 2 * quad + half
            ch = slice(PAIR * pair, PAIR * (pair + 1))
            row = mean[:, ch]
            outer = outer_of(row)
            inner = square[PAIR * half : PAIR * (half + 1), PAIR * half : PAIR * (half + 1)]
            top, low = pack(inner + outer * rows), vectors(total[:, ch])
            stats[pair, :GROUP, :] = top
            stats[pair, GROUP:, :] = low
    if split:
        emit_pairs(stats, outs, spot)
    else:
        outs[0][...] = stats[...]


def identity():
    shape = (PAIR, PAIR)
    return jnp.where(
        lax.broadcasted_iota(jnp.int32, shape, 0) == lax.broadcasted_iota(jnp.int32, shape, 1),
        1.0, 0.0,
    ).astype(F32)


def per_block(square):
    row_sums = jnp.sum(square, axis=1, keepdims=True)
    top = jnp.sum(row_sums[:GROUP], axis=0, keepdims=True)
    bottom = jnp.sum(row_sums[GROUP:], axis=0, keepdims=True)
    upper = lax.broadcasted_iota(jnp.int32, (PAIR, 1), 0) < GROUP
    return jnp.where(upper, top, bottom)


def total_of(terms):
    total = terms[0][...]
    for term in terms[1:]:
        total = total + term[...]
    return total


def whiten_kernel(*refs, span, packed):
    terms, (out, keep) = refs[:-2], refs[-2:]
    given = take_pairs(total_of(terms), packed)
    eye = identity()
    blocks = spread(jnp.ones((GROUP, PAIR), F32))
    means = [sums / span for _, sums, _ in given]
    covs = [
        moments / span - outer_of(mean) * blocks + epsilon * eye
        for (moments, _, _), mean in zip(given, means)
    ]
    traces = [per_block(cov * eye) for cov in covs]
    normed = [cov / trace for cov, trace in zip(covs, traces)]
    powers = [1.5 * eye - 0.5 * norm for norm in normed]
    for at, trace in enumerate(traces):
        keep[at, 0] = normed[at]
        keep[at, 1] = eye / trace
    for sweep in range(NEWTON - 1):
        squares = [exact(power, power) for power in powers]
        sides = [exact(power, norm) for power, norm in zip(powers, normed)]
        for at, power in enumerate(powers):
            keep[at, 2 + 2 * sweep] = power
            keep[at, 3 + 2 * sweep] = squares[at]
        powers = [
            1.5 * power - 0.5 * exact(square, side)
            for power, square, side in zip(powers, squares, sides)
        ]
    for at, power in enumerate(powers):
        keep[at, 2 * NEWTON] = power
        out[at, :GROUP, :] = pack(power / jnp.sqrt(traces[at]))
        out[at, GROUP:, :] = vectors(means[at])


def pull_kernel(*refs, span, packed):
    terms, (keep, out) = refs[:-2], refs[-2:]
    given = take_pairs(total_of(terms), packed)
    eye = identity()
    every = range(len(given))
    normed = [keep[at, 0] for at in every]
    inverse = [per_block(keep[at, 1]) / GROUP for at in every]
    roots = [jnp.sqrt(value) for value in inverse]
    powers = [keep[at, 2 * NEWTON] for at in every]
    grads = [given[at][0] * roots[at] for at in every]
    trace_grads = [
        -0.5 * inverse[at] * roots[at] * per_block(given[at][0] * powers[at]) for at in every
    ]
    normed_grads = [jnp.zeros_like(grads[0])] * len(given)
    for sweep in reversed(range(NEWTON - 1)):
        power = [keep[at, 2 + 2 * sweep] for at in every]
        turned = [exact(grads[at], normed[at]) for at in every]
        inner = [exact(power[at], grads[at]) for at in every]
        turned = [exact(turned[at] + turned[at].T, power[at]) for at in every]
        inner = [exact(keep[at, 3 + 2 * sweep], inner[at]) for at in every]
        normed_grads = [normed_grads[at] - 0.25 * (inner[at] + inner[at].T) for at in every]
        outer = [exact(turned[at], power[at]) for at in every]
        inner = [exact(power[at], turned[at]) for at in every]
        grads = [
            1.5 * grads[at] - 0.25 * (outer[at] + outer[at].T + inner[at]) for at in every
        ]
    for at in every:
        normed_grad = normed_grads[at] - 0.5 * grads[at]
        trace_grad = trace_grads[at] - inverse[at] * per_block(normed_grad * normed[at])
        both = normed_grad * inverse[at] + eye * trace_grad
        bias = -exact(vectors(given[at][1] / span), (powers[at] * roots[at]).T)
        out[at, :GROUP, :] = pack(both / span)
        out[at, GROUP:, :] = vectors(bias[0:1, :], given[at][2])


def place_pairs(spot, given, pairs, split):
    if split:
        for side, shares in enumerate(given):
            for at in range(shares.shape[0]):
                pairs[2 * at + jnp.bitwise_xor(side, spot[1])] = shares[at]
    else:
        pairs[...] = given[0][...]


def quad_matrix(pairs, quad):
    zero = jnp.zeros((PAIR, PAIR), F32)
    first = spread(pairs[2 * quad, :GROUP, :])
    second = spread(pairs[2 * quad + 1, :GROUP, :])
    top = jnp.concatenate([first, zero], axis=1)
    bottom = jnp.concatenate([zero, second], axis=1)
    return jnp.concatenate([top, bottom], axis=0).astype(BF16)


def row_of(pairs, quad, place):
    at = GROUP + place
    return jnp.concatenate(
        [pairs[2 * quad, at : at + 1, :], pairs[2 * quad + 1, at : at + 1, :]], axis=1
    )


def backward_kernel(spot, x, og, cen, means, gain, *rest, split, shares):
    given, rest = rest[:shares], rest[shares:]
    (dwb, dpre_out, w_out), outs, (pairs, stats) = rest[:3], rest[3:-2], rest[-2:]
    rows, width = x.shape
    place_pairs(spot, given, pairs, split)
    w_out[...] = pairs[...]
    chunk = chunk_of(rows, 128)
    for quad in range(width // 256):
        lanes = slice(256 * quad, 256 * (quad + 1))
        whiten = quad_matrix(pairs, quad)
        away = means[0:1, lanes] - row_of(pairs, quad, 0)
        shift = row_times(away, whiten)
        scale = gain[:, lanes]

        def step(at, carry, lanes=lanes, whiten=whiten, shift=shift, scale=scale):
            col_sum, gain_sum = carry
            here = slice(at * chunk, (at + 1) * chunk)
            white = dot(cen[here, lanes], whiten) + shift
            pre = x[here, lanes].astype(F32) + scale * white
            sig = sigmoid(pre)
            dpre = og[here, lanes].astype(F32) * (sig * (1.0 + pre * (1.0 - sig)))
            dpre_out[here, lanes] = dpre
            dwhite = scale * dpre
            dwb[here, lanes] = dwhite.astype(BF16)
            return col_sum + fold(dwhite), gain_sum + fold(dpre * white)

        zero = jnp.zeros((8, 256), F32)
        col_sum, gain_sum = loop(rows // chunk, step, (zero, zero))
        col_sum = jnp.sum(col_sum, axis=0, keepdims=True)
        gain_sum = jnp.sum(gain_sum, axis=0, keepdims=True)
        square = dot_t(cen[:, lanes], dwb[:, lanes]) + rank_one(away, col_sum)
        for half in range(2):
            ch = slice(PAIR * half, PAIR * (half + 1))
            pair = 2 * quad + half
            inner = square[ch, ch]
            stats[pair, :GROUP, :] = pack(inner + inner.T)
            stats[pair, GROUP:, :] = vectors(col_sum[:, ch], gain_sum[:, ch])
    if split:
        emit_pairs(stats, outs, spot)
    else:
        outs[0][...] = stats[...]


def own_kernel(h2, cen, out):
    for quad in range(cen.shape[1] // 256):
        lanes = slice(256 * quad, 256 * (quad + 1))
        out[:, lanes] = dot_t(h2[...], cen[:, lanes]).astype(BF16)


def turn_kernel(dwb, wpairs, w3, turned, flow):
    rows, width = dwb.shape
    chunk = chunk_of(rows, 128)
    for quad in range(width // 256):
        lanes = slice(256 * quad, 256 * (quad + 1))
        whiten = quad_matrix(wpairs, quad).T

        def step(at, carry, lanes=lanes, whiten=whiten):
            here = slice(at * chunk, (at + 1) * chunk)
            turned[here, lanes] = dot(dwb[here, lanes], whiten).astype(BF16)
            return carry

        loop(rows // chunk, step, 0)
    flow[...] = dot_nt(turned[...], w3[...])


def turned_kernel(h2, turned, out):
    for quad in range(turned.shape[1] // 256):
        lanes = slice(256 * quad, 256 * (quad + 1))
        out[:, lanes] = dot_t(h2[...], turned[:, lanes])


def last_kernel(spot, flow, cen, means, s2, w3, wpairs, *rest, split, shares):
    given, (cols, gains, spairs, bias_out, ext, flat, joint) = rest[:shares], rest[shares:]
    rows, width = cen.shape
    place_pairs(spot, given, spairs, split)
    gains[...] = spairs[:, GROUP + 1, :]
    chunk = chunk_of(rows, 128)
    ext[...] = jnp.zeros_like(ext)
    low = jnp.zeros((1, w3.shape[0]), F32)
    for quad in range(width // 256):
        lanes = slice(256 * quad, 256 * (quad + 1))
        sym = quad_matrix(spairs, quad)
        away = means[0:1, lanes] - row_of(wpairs, quad, 0)
        bias = row_of(spairs, quad, 0) + row_times(away, sym)
        bias_out[:, lanes] = jnp.broadcast_to(bias, (8, 256))
        low = low + row_times(bias, w3[:, lanes], dot_nt)
        joint[lanes, :] = dot_nt(sym, w3[:, lanes]).astype(BF16)

    def middle(at, carry):
        here = slice(at * chunk, (at + 1) * chunk)
        flat[here, :] = (flow[here, :] + dot(cen[here, :], joint[...]) + low) * s2[here, :]
        return carry

    loop(rows // chunk, middle, 0)
    pad_lines(flat, ext, rows)
    shifted(ext, cols)


def finish(part, outs, spot, plan):
    if plan:
        emit_split(part, outs[0], outs[1], spot[1], plan)
    else:
        outs[0][...] = part[...]


def slope_kernel(spot, cols, wm, s1, x, dmid1, *rest, plan):
    outs, (ext, flat, part) = rest[:-3], rest[-3:]
    rows, depth = s1.shape
    padded = padded_rows(rows)
    big = chunk_of(padded, 256)

    def step(at, carry):
        base = at * big
        total = jnp.zeros((big, depth), F32)
        for row in range(3):
            for col in range(3):
                near = cols[2 - col, pl.ds(base + LINE * (2 - row), big), :]
                k = 3 * row + col
                total = total + dot_nt(near, wm[k * depth : (k + 1) * depth, :])
        ext[pl.ds(base, big), :] = total
        return carry

    loop(padded // big, step, 0)
    unpad_lines(ext, flat, rows)
    dmid1[...] = (flat[...] * s1[...]).astype(BF16)
    for quad in range(x.shape[1] // 256):
        lanes = slice(256 * quad, 256 * (quad + 1))
        part[lanes, :] = dot_t(x[:, lanes], dmid1[...])
    finish(part, outs, spot, plan)


def middle_kernel(spot, cols, h1pad, turned, own, sums, spairs, bias, *rest, plans):
    outs, (part, part_last) = rest[:-2], rest[-2:]
    padded, depth = h1pad.shape
    for row in range(3):
        for col in range(3):
            k = 3 * row + col
            near = cols[2 - col, LINE * (2 - row) : LINE * (2 - row) + padded, :]
            part[k * depth : (k + 1) * depth, :] = dot_t(h1pad[...], near)
    for quad in range(turned.shape[1] // 256):
        lanes = slice(256 * quad, 256 * (quad + 1))
        sym = quad_matrix(spairs, quad)
        part_last[:, lanes] = (
            turned[:, lanes]
            + dot(own[:, lanes], sym)
            + rank_one(sums[0:1, :], bias[0:1, lanes])
        )
    if plans:
        emit_split(part, outs[0], outs[1], spot[1], plans[0])
        emit_split(part_last, outs[0], outs[1], spot[1], plans[1])
    else:
        outs[0][...] = part[...]
        outs[1][...] = part_last[...]


def spans_step(spot, *refs, steps, extra=0):
    count = 2 * (1 + max(span[0] for spans in steps for span in spans))
    given, outs = refs[: count + extra], refs[count + extra :]
    for at, spans in enumerate(steps):
        to = 0
        for source, start, size, bit in spans:
            mine, other = half_of(given[2 * source], given[2 * source + 1], spot[bit], start, size)
            outs[2 * at][to : to + size // 2, :] = mine
            outs[2 * at + 1][to : to + size // 2, :] = other
            to += size // 2
        left = outs[2 * at].shape[0] - to
        if not left:
            continue
        if extra:
            rows = jnp.concatenate([given[-1][...]] * (outs[0].shape[1] // PAIR), axis=1)
        else:
            tail = given[0].shape[0] - left
            rows = given[0][tail:, :] + given[1][tail:, :]
        for out in outs[2 * at : 2 * at + 2]:
            out[to:, :] = rows


def close_kernel(spot, keep, given, first, middle, last, gain, *, tall, high, scale):
    total = (keep[...] + given[...]) * scale
    for half in range(2):
        lanes = slice(PAIR * half, PAIR * (half + 1))
        step = tall // 4
        for wide in range(4):
            last[pl.ds(2 * wide + half, step, 8), :] = total[step * wide : step * (wide + 1), lanes]
        middle[pl.ds(half, high, 2), :] = total[tall : tall + high, lanes]
        first[pl.ds(half, tall, 2), :] = total[tall + high : 2 * tall + high, lanes]
    size = gain.shape[1]
    each = PAIR // size
    rows = total[2 * tall + high :, :PAIR]
    device = spot[6]
    at = lax.broadcasted_iota(jnp.int32, rows.shape, 0)
    row = jnp.sum(jnp.where(at == device // each, rows, 0.0), axis=0, keepdims=True)
    mine = jnp.zeros((1, size), F32)
    for place in range(each):
        mine = jnp.where(device % each == place, row[:, place * size : (place + 1) * size], mine)
    gain[...] = mine


def input_kernel(dmid1, w1, dpre, out, token):
    token[...] = jnp.zeros_like(token)
    rows = dpre.shape[0]
    chunk = chunk_of(rows, 128)

    def step(at, carry):
        here = slice(at * chunk, (at + 1) * chunk)
        out[here, :] = (dot_nt(dmid1[here, :], w1[...]) + dpre[here, :]).astype(BF16)
        return carry

    loop(rows // chunk, step, 0)


def call(kernel, outs, args, scratch=(), scalars=0, flops=0, ties=(), far=0, room=40):
    args = tuple(args) + tuple(ties)
    specs = [pl.BlockSpec(memory_space=pltpu.SMEM)] * scalars
    specs += [pl.BlockSpec(memory_space=pl.ANY)] * far
    specs += [pl.BlockSpec(memory_space=pltpu.VMEM)] * (len(args) - scalars - len(ties) - far)
    specs += [pl.BlockSpec(memory_space=pl.ANY)] * len(ties)
    count = len(args) - len(ties)

    def body(*refs):
        kernel(*refs[:count], *refs[len(args) :])

    size = sum(a.size * a.dtype.itemsize for a in args)
    size += sum(o.size * o.dtype.itemsize for o in outs)
    return pl.pallas_call(
        body,
        out_shape=tuple(outs),
        in_specs=specs,
        out_specs=tuple(pl.BlockSpec(memory_space=pltpu.VMEM) for _ in outs),
        scratch_shapes=list(scratch),
        cost_estimate=pl.CostEstimate(flops=flops, bytes_accessed=size, transcendentals=0),
        compiler_params=pltpu.CompilerParams(vmem_limit_bytes=room * 2**20),
    )(*args)


def shape(dims, dtype=F32):
    return jax.ShapeDtypeStruct(dims, dtype)


def swap(value, axis, size, flip):
    return lax.ppermute(value, axis, [(at, at ^ flip) for at in range(size)])


def shards(inputs, out_grad, conv_first, conv_middle, conv_last, gain):
    rows, width = inputs.shape
    mid = conv_first.shape[1]
    pairs = width // PAIR
    ghosts = lax.axis_size("ghost")
    groups = lax.axis_size("group")
    devices = ghosts * groups
    span = float(rows * ghosts)
    scale = (rows * devices) ** (-0.5)
    padded = padded_rows(rows)
    ghost = lax.axis_index("ghost")
    group = lax.axis_index("group")
    bits = [ghost] + [(ghost >> bit) & 1 for bit in range(3)]
    bits += [(group >> bit) & 1 for bit in range(2)] + [group * ghosts + ghost]
    spot = jnp.stack(bits).astype(jnp.int32)
    core, across, along, near, far = 1, 2, 3, 4, 5
    split = ghosts == 8 and pairs == 8 and groups == 4
    unit = 2 * rows * width * mid

    ext = pltpu.VMEM((24 + padded + LINE + 8, mid), F32)
    flat = pltpu.VMEM((rows, mid), F32)
    cols = (3, padded + 2 * LINE, mid)
    big = (pairs, TALL, PAIR)
    half = (pairs // 2, TALL, PAIR)
    packed = (pairs // 4, TALL, PAIR)
    stats_outs = [shape(packed)] * 2 if split else [shape(big)]
    stats_held = pltpu.VMEM(big, F32)

    def collect(stats, ties):
        if not split:
            return [lax.psum(stats[0], "ghost")]
        total, send = stats
        given = swap(send, "ghost", ghosts, 1)
        (total,) = call(add_kernel, [shape(packed)], (total, given))
        given = swap(total, "ghost", ghosts, 2)
        (total,) = call(add_kernel, [shape(packed)], (total, given), ties=ties)
        return [total, swap(total, "ghost", ghosts, 4)]

    def share_out(own):
        return [own, swap(own, "ghost", ghosts, 1)] if split else [own]

    own = half if split else big
    held = own[0]
    chunks = rows // chunk_of(rows, 128)
    h1pad, s1, h2, s2, cen, means, sums, *stats = call(
        functools.partial(forward_kernel, split=split),
        [shape((padded, mid), BF16), shape((rows, mid)), shape((rows, mid), BF16),
         shape((rows, mid)), shape((rows, width), BF16), shape((8, width)), shape((8, mid))]
        + stats_outs,
        (spot, *(
            pltpu.with_memory_space_constraint(value, pltpu.HBM)
            for value in (inputs, conv_first, conv_middle, conv_last)
        )),
        (pltpu.VMEM((rows, width), BF16), pltpu.VMEM(conv_first.shape, BF16),
         pltpu.VMEM(conv_middle.shape, BF16), pltpu.VMEM(conv_last.shape, BF16),
         pltpu.SemaphoreType.DMA((3 + chunks,)),
         ext, pltpu.VMEM(cols, BF16), flat, pltpu.VMEM((rows, width), F32), stats_held),
        scalars=1, flops=5 * unit, far=4, room=40,
    )
    (own_part,) = call(own_kernel, [shape((mid, width), BF16)], (h2, cen), flops=unit)
    share, kept = call(
        functools.partial(whiten_kernel, span=span, packed=split),
        [shape(own), shape((held, 2 * NEWTON + 1, PAIR, PAIR))], collect(stats, (own_part,)), flops=10**7,
    )
    given = share_out(share)
    dwb, dpre, wpairs, *stats = call(
        functools.partial(backward_kernel, split=split, shares=len(given)),
        [shape((rows, width), BF16), shape((rows, width)), shape(big)] + stats_outs,
        (spot, inputs, out_grad, cen, means, gain.reshape(1, width), *given),
        (pltpu.VMEM(big, F32), stats_held), scalars=1, flops=2 * unit,
    )
    turned, flow = call(
        turn_kernel, [shape((rows, width), BF16), shape((rows, mid))], (dwb, wpairs, conv_last),
        flops=2 * unit,
    )
    (turned_part,) = call(turned_kernel, [shape((mid, width))], (h2, turned), flops=unit)
    (pulled,) = call(
        functools.partial(pull_kernel, span=span, packed=split), [shape(own)], (*collect(stats, (flow,)), kept),
        flops=10**7, ties=(turned_part,),
    )
    given = share_out(pulled)

    dcols, gains, spairs, bias = call(
        functools.partial(last_kernel, split=split, shares=len(given)),
        [shape(cols, BF16), shape((pairs, PAIR)), shape(big), shape((8, width))],
        (spot, flow, cen, means, s2, conv_last, wpairs, *given),
        (ext, flat, pltpu.VMEM((width, mid), BF16)), scalars=1, flops=2 * unit,
    )
    half_rows = mid * width // 512
    orders = (
        (("ghost", 1), ("ghost", 2), ("group", 0), ("group", 1)),
        (("ghost", 2), ("group", 0), ("ghost", 1), ("group", 1)),
        (("group", 0), ("ghost", 1), ("ghost", 2), ("group", 1)),
    )
    high, tall = 9 * mid // devices, width // devices
    cut = high // 24 * 8
    middle_plan = last_plan = first_plan = None
    if split:
        middle_plan = plan_of(
            [(0, cut, orders[0]), (cut, high - cut, orders[1])], high, 1, ghosts
        )
        last_plan = plan_of(
            [(0, mid // devices, orders[0])], mid // devices, width // 256, ghosts, 9 * mid // 2
        )
        first_plan = plan_of([(0, tall, orders[2])], tall, 1, ghosts)
    middle_part = call(
        functools.partial(middle_kernel, plans=(middle_plan, last_plan) if split else None),
        [shape((9 * mid // 2 + half_rows, mid))] * 2 if split
        else [shape((9 * mid, mid)), shape((mid, width))],
        (spot, dcols, h1pad, turned_part, own_part, sums, spairs, bias),
        (pltpu.VMEM((9 * mid, mid), F32), pltpu.VMEM((mid, width), F32)),
        scalars=1, flops=3 * unit,
    )
    dmid1, *first_part = call(
        functools.partial(slope_kernel, plan=first_plan),
        [shape((rows, mid), BF16)]
        + ([shape((half_rows, mid))] * 2 if split else [shape((width, mid))]),
        (spot, dcols, conv_middle, s1, inputs),
        (ext, flat, pltpu.VMEM((width, mid), F32)), scalars=1, flops=4 * unit,
    )
    portion = width // devices
    if not split:
        input_grad, _ = call(
            input_kernel, [shape((rows, width), BF16), shape((8, PAIR))],
            (dmid1, conv_first, dpre), flops=unit,
        )
        grads = [
            lax.psum_scatter(
                (part[0] * scale).reshape(-1), ("group", "ghost"), scatter_dimension=0, tiled=True
            )
            for part in (first_part, middle_part, middle_part[1:])
        ]
        gain_grad = lax.dynamic_slice_in_dim(
            lax.psum(gains.reshape(-1) * scale, "group"), (group * ghosts + ghost) * portion, portion
        )
        return (input_grad, *grads, gain_grad)

    def move(parts, ways):
        result = []
        for at, (axis, flip) in enumerate(ways):
            result.append(parts[2 * at])
            result.append(swap(parts[2 * at + 1], axis, groups if axis == "group" else ghosts, flip))
        return result

    def run(steps, given, extra=(), more=0, ties=()):
        outs = []
        for at, spans in enumerate(steps):
            height = sum(span[2] for span in spans) // 2 + (more if at == 0 else 0)
            outs += [shape((height, mid))] * 2
        return call(
            functools.partial(spans_step, steps=steps, extra=len(extra)), outs,
            (spot, *given, *extra), scalars=1, ties=ties,
        )

    core_way, x_way, y_way = (("ghost", 1 << bit) for bit in range(3))
    near_way, far_way = ("group", 1), ("group", 2)
    given = move(middle_part, (core_way,))
    first_given = move(first_part, (core_way,))
    pieces = devices // 2
    a_low, a_high, b_all = half_rows, pieces * cut, pieces * (high - cut)
    parts = run(
        (((0, a_high + b_all, a_low, across), (0, 0, a_high, across)),
         ((0, a_high, b_all, along),)), given,
    )
    given = move(parts, (x_way, y_way))
    parts = run((((0, 0, half_rows, near),),), first_given, ties=(parts[0],))
    given += move(parts, (near_way,))
    input_grad, token = call(
        input_kernel, [shape((rows, width), BF16), shape((8, PAIR))], (dmid1, conv_first, dpre),
        flops=unit, ties=(parts[0],),
    )
    a_low, a_high, b_all, c_all = a_low // 2, a_high // 2, b_all // 2, half_rows // 2
    parts = run(
        (((0, 0, a_low, along), (0, a_low, a_high, along)), ((1, 0, b_all, near),),
         ((2, 0, c_all, across),)), given, ties=(token,),
    )
    given = move(parts, (y_way, near_way, x_way))
    a_low, a_high, b_all, c_all = a_low // 2, a_high // 2, b_all // 2, c_all // 2
    parts = run(
        (((0, 0, a_low, near), (0, a_low, a_high, near)), ((1, 0, b_all, across),),
         ((2, 0, c_all, along),)), given, extra=(gains,), more=8,
    )
    given = move(parts, (near_way, x_way, y_way))
    a_low, a_high, b_all, c_all = a_low // 2, a_high // 2, b_all // 2, c_all // 2
    parts = run(
        (((0, 0, a_low, far), (0, a_low, a_high, far), (1, 0, b_all, far), (2, 0, c_all, far)),),
        given, more=8,
    )
    given = move(parts, (far_way,))
    first_grad, middle_grad, last_grad, gain_grad = call(
        functools.partial(close_kernel, tall=tall, high=high, scale=scale),
        [shape((2 * tall, PAIR)), shape((2 * high, PAIR)), shape((2 * tall, PAIR)),
         shape((1, portion))],
        (spot, *given), scalars=1,
    )
    return (
        input_grad, first_grad.reshape(-1), middle_grad.reshape(-1), last_grad.reshape(-1),
        gain_grad.reshape(-1),
    )


def solution(mesh):
    in_specs = (P(("group", "ghost"), None), P(("group", "ghost"), None), P(), P(), P(), P())
    out_specs = (
        P(("group", "ghost"), None),
        P(("group", "ghost")),
        P(("group", "ghost")),
        P(("group", "ghost")),
        P(("group", "ghost")),
    )
    return jax.shard_map(shards, mesh=mesh, in_specs=in_specs, out_specs=out_specs, check_vma=False)
```

```python
import functools

import jax
import jax.numpy as jnp
from jax import lax
from jax.experimental import pallas as pl
from jax.experimental.pallas import tpu as pltpu
from jax.sharding import PartitionSpec as P

GROUP = 64
NEWTON = 5
SIDE = 14
LINE = 16
PAIR = 2 * GROUP
TALL = GROUP + 8
epsilon = 1e-05

F32 = jnp.float32
BF16 = jnp.bfloat16


def dot(left, right):
    return jnp.dot(left, right, preferred_element_type=F32)


def dot_t(left, right):
    return lax.dot_general(left, right, (((0,), (0,)), ((), ())), preferred_element_type=F32)


def dot_nt(left, right):
    return lax.dot_general(left, right, (((1,), (1,)), ((), ())), preferred_element_type=F32)


def halves_of(value):
    high = value.astype(BF16)
    return high, (value - high.astype(F32)).astype(BF16)


def exact(left, right):
    a, b = halves_of(left)
    c, d = halves_of(right)
    low = dot(jnp.concatenate([a, b], axis=1), jnp.concatenate([d, c], axis=0))
    return low + dot(a, c)


def exact_two(left, first, second):
    both = exact(left, jnp.concatenate([first, second], axis=1))
    return both[:, : first.shape[1]], both[:, first.shape[1] :]


def outer_of(row):
    tile = vectors(row)
    return lax.dot_general(
        tile, tile, (((0,), (0,)), ((), ())), preferred_element_type=F32,
        precision=lax.Precision.HIGHEST,
    )


def sigmoid(value):
    return 0.5 * jnp.tanh(0.5 * value) + 0.5


def two_rows(row):
    high, low = halves_of(jnp.broadcast_to(row, (16, row.shape[1])))
    at = lax.broadcasted_iota(jnp.int32, high.shape, 0)
    return jnp.where(at == 0, high.astype(F32), jnp.where(at == 1, low.astype(F32), 0.0)).astype(
        BF16
    )


def row_times(row, matrix, product=dot):
    return jnp.sum(product(two_rows(row), matrix), axis=0, keepdims=True)


def rank_one(left, right):
    tiles = []
    for row, order in ((left, (0, 1, 0)), (right, (0, 0, 1))):
        pair = halves_of(jnp.broadcast_to(row, (16, row.shape[1])))
        at = lax.broadcasted_iota(jnp.int32, pair[0].shape, 0)
        tile = jnp.zeros(pair[0].shape, F32)
        for place, which in enumerate(order):
            tile = jnp.where(at == place, pair[which].astype(F32), tile)
        tiles.append(tile.astype(BF16))
    return dot_t(*tiles)


def chunk_of(rows, most):
    best = 16
    for size in range(16, most + 1, 16):
        if rows % size == 0:
            best = size
    return best


def loop(count, body, carry):
    for at in range(count):
        carry = body(at, carry)
    return carry


def left_half(shape):
    return lax.broadcasted_iota(jnp.int32, shape, 1) < GROUP


def spread(packed):
    left = left_half(packed.shape)
    zero = jnp.zeros_like(packed)
    return jnp.concatenate([jnp.where(left, packed, zero), jnp.where(left, zero, packed)], axis=0)


def pack(square):
    top, bottom = square[:GROUP], square[GROUP:]
    return jnp.where(left_half(top.shape), top, bottom)


def vectors(*rows):
    at = lax.broadcasted_iota(jnp.int32, (8, PAIR), 0)
    tile = jnp.zeros((8, PAIR), F32)
    for place, row in enumerate(rows):
        tile = jnp.where(at == place, row, tile)
    return tile


def fold(value):
    rows, lanes = value.shape
    return jnp.sum(value.reshape(rows // 8, 8, lanes), axis=0)


def pad_lines(source, ext, rows):
    for line in range(rows // SIDE):
        place = 24 + LINE * (line + line // SIDE)
        ext[place : place + SIDE, :] = source[SIDE * line : SIDE * (line + 1), :]


def unpad_lines(source, target, rows):
    for line in range(rows // SIDE):
        place = LINE * (line + line // SIDE)
        target[SIDE * line : SIDE * (line + 1), :] = source[place : place + SIDE, :]


def padded_rows(rows):
    return rows // (SIDE * SIDE) * (SIDE + 1) * LINE


def shifted(ext, cols):
    length = cols.shape[1]
    for col in range(3):
        cols[col] = ext[7 + col : 7 + col + length, :].astype(BF16)


def emit_split(source, keep, send, core, plan):
    for start, height, first, size, mine in plan:
        lanes = keep.shape[1]
        for wide in range(source.shape[1] // lanes):
            to = slice(start + wide * height, start + (wide + 1) * height)
            cols = slice(wide * lanes, (wide + 1) * lanes)
            for target, half in ((keep, core), (send, 1 - core)):
                place = pl.multiple_of((mine + half) * size + first, 8)
                target[to, :] = source[pl.ds(place, height), cols]


def plan_of(parts, piece, wide, ghosts, start=0):
    plan = []
    for first, height, steps in parts:
        for at in range(2 ** len(steps)):
            source = 0
            for place, (axis, bit) in enumerate(steps):
                value = (at >> (len(steps) - 1 - place)) & 1
                source += value << bit if axis == "ghost" else (value << bit) * ghosts
            plan.append((start, height, first, piece, source))
            start += height * wide
    return plan


def half_of(left, right, bit, start=0, rows=None):
    rows = (left.shape[0] if rows is None else rows) // 2
    mine = pl.ds(pl.multiple_of(start + bit * rows, 8), rows)
    other = pl.ds(pl.multiple_of(start + (1 - bit) * rows, 8), rows)
    return left[mine, :] + right[mine, :], left[other, :] + right[other, :]


def emit_pairs(stats, outs, spot):
    shape = (GROUP, PAIR)
    row = lax.broadcasted_iota(jnp.int32, shape, 0)
    lane = lax.broadcasted_iota(jnp.int32, shape, 1)
    left = lane < GROUP
    col = jnp.where(left, lane, lane - GROUP)
    for parity in range(2):
        for slot in range(stats.shape[0] // 4):
            pair = 4 * slot + parity, 4 * slot + 2 + parity
            first, second = (stats[p, :GROUP, :] for p in pair)
            upper = jnp.where(left, first, pltpu.roll(second, GROUP, 1))
            lower = jnp.where(left, pltpu.roll(first, GROUP, 1), second)
            rows = [
                jnp.sum(jnp.where(row == col, m, 0.0), axis=0, keepdims=True)
                for m in (first, second)
            ]
            for place in range(2):
                rows += [stats[p, GROUP + place : GROUP + place + 1, :] for p in pair]
            both = jnp.concatenate([jnp.where(row <= col, upper, lower), vectors(*rows)], axis=0)

            @pl.when(spot[1] == parity)
            def _(both=both, slot=slot):
                outs[0][slot] = both

            @pl.when(spot[1] != parity)
            def _(both=both, slot=slot):
                outs[1][slot] = both


def take_pairs(total, packed):
    result = []
    if not packed:
        for at in range(total.shape[0]):
            vecs = [total[at, GROUP + p : GROUP + p + 1, :] for p in range(2)]
            result.append((spread(total[at, :GROUP, :]), *vecs))
        return result
    shape = (PAIR, PAIR)
    row = lax.broadcasted_iota(jnp.int32, shape, 0)
    col = lax.broadcasted_iota(jnp.int32, shape, 1)
    mask = jnp.where(row < GROUP, row - col, col - row) < 0
    eye = identity()
    for slot in range(total.shape[0]):
        both = total[slot, :GROUP, :]
        turned = pltpu.roll(both, GROUP, 1)
        left = left_half(both.shape)
        for at in range(2):
            twice = jnp.where(left, *((both, turned) if at == 0 else (turned, both)))
            part = jnp.where(mask, spread(twice), 0.0)
            line = [total[slot, GROUP + 2 * p + at : GROUP + 2 * p + at + 1, :] for p in range(3)]
            result.append((part + part.T + eye * line[0], line[1], line[2]))
    return result


def add_kernel(left, right, out):
    out[...] = left[...] + right[...]


def forward_kernel(
    spot, x_far, w1_far, wm_far, w3_far, h1pad, s1, h2, s2, cen, means, sums, *rest, split
):
    outs, (x, w1, wm, w3, sems, ext, cols, flat, stats) = rest[:-9], rest[-9:]
    rows = x.shape[0]
    part = chunk_of(rows, 128)

    def slab(at):
        here = slice(at * part, (at + 1) * part)
        return pltpu.make_async_copy(x_far.at[here, :], x.at[here, :], sems.at[3 + at])

    weights = [
        pltpu.make_async_copy(far, ref, sems.at[at])
        for at, (far, ref) in enumerate(((w1_far, w1), (wm_far, wm), (w3_far, w3)))
    ]
    weights[0].start()
    for at in range(rows // part):
        slab(at).start()
    weights[1].start()
    weights[2].start()
    chunk = chunk_of(rows, 128)
    ext[...] = jnp.zeros_like(ext)

    weights[0].wait()

    def first(at, carry):
        here = slice(at * chunk, (at + 1) * chunk)
        slab(at).wait()
        act = dot(x[here, :], w1[...])
        sig = sigmoid(act)
        flat[here, :] = act * sig
        s1[here, :] = sig * (1.0 + act * (1.0 - sig))
        return carry

    loop(rows // chunk, first, 0)
    pad_lines(flat, ext, rows)
    shifted(ext, cols)
    padded = padded_rows(rows)
    h1pad[...] = cols[1, LINE : LINE + padded, :]
    big = chunk_of(padded, 256)
    weights[1].wait()

    def middle(at, carry):
        base = at * big
        total = jnp.zeros((big, wm.shape[1]), F32)
        for row in range(3):
            for col in range(3):
                left = cols[col, pl.ds(base + LINE * row, big), :]
                k = 3 * row + col
                depth = left.shape[1]
                total = total + dot(left, wm[k * depth : (k + 1) * depth, :])
        ext[pl.ds(base, big), :] = total
        return carry

    loop(padded // big, middle, 0)
    unpad_lines(ext, flat, rows)
    width = w3.shape[1]
    weights[2].wait()

    def second(at, hidden_sum):
        here = slice(at * chunk, (at + 1) * chunk)
        act = flat[here, :]
        sig = sigmoid(act)
        hidden = (act * sig).astype(BF16)
        h2[here, :] = hidden
        s2[here, :] = sig * (1.0 + act * (1.0 - sig))
        return hidden_sum + fold(hidden.astype(F32))

    zeros = jnp.zeros((8, w3.shape[0]), F32)
    hidden_sum = loop(rows // chunk, second, zeros)
    hidden_sum = jnp.sum(hidden_sum, axis=0, keepdims=True)
    sums[...] = jnp.broadcast_to(hidden_sum, sums.shape)
    total = row_times(hidden_sum, w3[...])
    mean = total / rows
    means[...] = jnp.broadcast_to(mean, means.shape)
    for quad in range(width // 256):
        lanes = slice(256 * quad, 256 * (quad + 1))
        centered = (dot(h2[...], w3[:, lanes]) - mean[:, lanes]).astype(BF16)
        cen[:, lanes] = centered
        square = dot_t(centered, centered)
        for half in range(2):
            pair = 2 * quad + half
            ch = slice(PAIR * pair, PAIR * (pair + 1))
            row = mean[:, ch]
            outer = outer_of(row)
            inner = square[PAIR * half : PAIR * (half + 1), PAIR * half : PAIR * (half + 1)]
            top, low = pack(inner + outer * rows), vectors(total[:, ch])
            stats[pair, :GROUP, :] = top
            stats[pair, GROUP:, :] = low
    if split:
        emit_pairs(stats, outs, spot)
    else:
        outs[0][...] = stats[...]


def identity():
    shape = (PAIR, PAIR)
    return jnp.where(
        lax.broadcasted_iota(jnp.int32, shape, 0) == lax.broadcasted_iota(jnp.int32, shape, 1),
        1.0, 0.0,
    ).astype(F32)


def per_block(square):
    row_sums = jnp.sum(square, axis=1, keepdims=True)
    top = jnp.sum(row_sums[:GROUP], axis=0, keepdims=True)
    bottom = jnp.sum(row_sums[GROUP:], axis=0, keepdims=True)
    upper = lax.broadcasted_iota(jnp.int32, (PAIR, 1), 0) < GROUP
    return jnp.where(upper, top, bottom)


def total_of(terms):
    total = terms[0][...]
    for term in terms[1:]:
        total = total + term[...]
    return total


def whiten_kernel(*refs, span, packed):
    terms, (out, keep) = refs[:-2], refs[-2:]
    given = take_pairs(total_of(terms), packed)
    eye = identity()
    blocks = spread(jnp.ones((GROUP, PAIR), F32))
    means = [sums / span for _, sums, _ in given]
    covs = [
        moments / span - outer_of(mean) * blocks + epsilon * eye
        for (moments, _, _), mean in zip(given, means)
    ]
    traces = [per_block(cov * eye) for cov in covs]
    normed = [cov / trace for cov, trace in zip(covs, traces)]
    powers = [1.5 * eye - 0.5 * norm for norm in normed]
    for at, trace in enumerate(traces):
        keep[at, 0] = normed[at]
        keep[at, 1] = eye / trace
    for sweep in range(NEWTON - 1):
        both = [exact_two(power, power, norm) for power, norm in zip(powers, normed)]
        squares, sides = zip(*both)
        for at, power in enumerate(powers):
            keep[at, 2 + 2 * sweep] = power
            keep[at, 3 + 2 * sweep] = squares[at]
        powers = [
            1.5 * power - 0.5 * exact(square, side)
            for power, square, side in zip(powers, squares, sides)
        ]
    for at, power in enumerate(powers):
        keep[at, 2 * NEWTON] = power
        out[at, :GROUP, :] = pack(power / jnp.sqrt(traces[at]))
        out[at, GROUP:, :] = vectors(means[at])


def pull_kernel(*refs, span, packed):
    terms, (keep, out) = refs[:-2], refs[-2:]
    given = take_pairs(total_of(terms), packed)
    eye = identity()
    every = range(len(given))
    normed = [keep[at, 0] for at in every]
    inverse = [per_block(keep[at, 1]) / GROUP for at in every]
    roots = [jnp.sqrt(value) for value in inverse]
    powers = [keep[at, 2 * NEWTON] for at in every]
    grads = [given[at][0] * roots[at] for at in every]
    trace_grads = [
        -0.5 * inverse[at] * roots[at] * per_block(given[at][0] * powers[at]) for at in every
    ]
    normed_grads = [jnp.zeros_like(grads[0])] * len(given)
    for sweep in reversed(range(NEWTON - 1)):
        power = [keep[at, 2 + 2 * sweep] for at in every]
        square = [keep[at, 3 + 2 * sweep] for at in every]
        turned, side = zip(*(exact_two(grads[at], normed[at], power[at]) for at in every))
        turned = [turned[at] + turned[at].T for at in every]
        turned, outer = zip(*(exact_two(turned[at], power[at], square[at]) for at in every))
        side = [exact(side[at], square[at]) for at in every]
        normed_grads = [normed_grads[at] - 0.25 * (side[at] + side[at].T) for at in every]
        inner = [exact(power[at], turned[at]) for at in every]
        grads = [
            1.5 * grads[at] - 0.25 * (outer[at] + outer[at].T + inner[at]) for at in every
        ]
    for at in every:
        normed_grad = normed_grads[at] - 0.5 * grads[at]
        trace_grad = trace_grads[at] - inverse[at] * per_block(normed_grad * normed[at])
        both = normed_grad * inverse[at] + eye * trace_grad
        bias = -exact(vectors(given[at][1] / span), (powers[at] * roots[at]).T)
        out[at, :GROUP, :] = pack(both / span)
        out[at, GROUP:, :] = vectors(bias[0:1, :], given[at][2])


def place_pairs(spot, given, pairs, split):
    if split:
        for side, shares in enumerate(given):
            for at in range(shares.shape[0]):
                pairs[2 * at + jnp.bitwise_xor(side, spot[1])] = shares[at]
    else:
        pairs[...] = given[0][...]


def quad_matrix(pairs, quad):
    zero = jnp.zeros((PAIR, PAIR), F32)
    first = spread(pairs[2 * quad, :GROUP, :])
    second = spread(pairs[2 * quad + 1, :GROUP, :])
    top = jnp.concatenate([first, zero], axis=1)
    bottom = jnp.concatenate([zero, second], axis=1)
    return jnp.concatenate([top, bottom], axis=0).astype(BF16)


def row_of(pairs, quad, place):
    at = GROUP + place
    return jnp.concatenate(
        [pairs[2 * quad, at : at + 1, :], pairs[2 * quad + 1, at : at + 1, :]], axis=1
    )


def backward_kernel(spot, x, og, cen, means, gain, *rest, split, shares):
    given, rest = rest[:shares], rest[shares:]
    (dwb, dpre_out, w_out), outs, (pairs, stats) = rest[:3], rest[3:-2], rest[-2:]
    rows, width = x.shape
    place_pairs(spot, given, pairs, split)
    w_out[...] = pairs[...]
    chunk = chunk_of(rows, 128)
    for quad in range(width // 256):
        lanes = slice(256 * quad, 256 * (quad + 1))
        whiten = quad_matrix(pairs, quad)
        away = means[0:1, lanes] - row_of(pairs, quad, 0)
        shift = row_times(away, whiten)
        scale = gain[:, lanes]

        def step(at, carry, lanes=lanes, whiten=whiten, shift=shift, scale=scale):
            col_sum, gain_sum = carry
            here = slice(at * chunk, (at + 1) * chunk)
            white = dot(cen[here, lanes], whiten) + shift
            pre = x[here, lanes].astype(F32) + scale * white
            sig = sigmoid(pre)
            dpre = og[here, lanes].astype(F32) * (sig * (1.0 + pre * (1.0 - sig)))
            dpre_out[here, lanes] = dpre
            dwhite = scale * dpre
            dwb[here, lanes] = dwhite.astype(BF16)
            return col_sum + fold(dwhite), gain_sum + fold(dpre * white)

        zero = jnp.zeros((8, 256), F32)
        col_sum, gain_sum = loop(rows // chunk, step, (zero, zero))
        col_sum = jnp.sum(col_sum, axis=0, keepdims=True)
        gain_sum = jnp.sum(gain_sum, axis=0, keepdims=True)
        square = dot_t(cen[:, lanes], dwb[:, lanes]) + rank_one(away, col_sum)
        for half in range(2):
            ch = slice(PAIR * half, PAIR * (half + 1))
            pair = 2 * quad + half
            inner = square[ch, ch]
            stats[pair, :GROUP, :] = pack(inner + inner.T)
            stats[pair, GROUP:, :] = vectors(col_sum[:, ch], gain_sum[:, ch])
    if split:
        emit_pairs(stats, outs, spot)
    else:
        outs[0][...] = stats[...]


def own_kernel(h2, cen, out):
    for quad in range(cen.shape[1] // 256):
        lanes = slice(256 * quad, 256 * (quad + 1))
        out[:, lanes] = dot_t(h2[...], cen[:, lanes]).astype(BF16)


def turn_kernel(dwb, wpairs, w3, turned, flow):
    rows, width = dwb.shape
    chunk = chunk_of(rows, 128)
    for quad in range(width // 256):
        lanes = slice(256 * quad, 256 * (quad + 1))
        whiten = quad_matrix(wpairs, quad).T

        def step(at, carry, lanes=lanes, whiten=whiten):
            here = slice(at * chunk, (at + 1) * chunk)
            turned[here, lanes] = dot(dwb[here, lanes], whiten).astype(BF16)
            return carry

        loop(rows // chunk, step, 0)
    flow[...] = dot_nt(turned[...], w3[...])


def turned_kernel(h2, turned, out):
    for quad in range(turned.shape[1] // 256):
        lanes = slice(256 * quad, 256 * (quad + 1))
        out[:, lanes] = dot_t(h2[...], turned[:, lanes])


def last_kernel(spot, flow, cen, means, s2, w3, wpairs, *rest, split, shares):
    given, (cols, gains, spairs, bias_out, ext, flat, joint) = rest[:shares], rest[shares:]
    rows, width = cen.shape
    place_pairs(spot, given, spairs, split)
    gains[...] = spairs[:, GROUP + 1, :]
    chunk = chunk_of(rows, 128)
    ext[...] = jnp.zeros_like(ext)
    low = jnp.zeros((1, w3.shape[0]), F32)
    for quad in range(width // 256):
        lanes = slice(256 * quad, 256 * (quad + 1))
        sym = quad_matrix(spairs, quad)
        away = means[0:1, lanes] - row_of(wpairs, quad, 0)
        bias = row_of(spairs, quad, 0) + row_times(away, sym)
        bias_out[:, lanes] = jnp.broadcast_to(bias, (8, 256))
        low = low + row_times(bias, w3[:, lanes], dot_nt)
        joint[lanes, :] = dot_nt(sym, w3[:, lanes]).astype(BF16)

    def middle(at, carry):
        here = slice(at * chunk, (at + 1) * chunk)
        flat[here, :] = (flow[here, :] + dot(cen[here, :], joint[...]) + low) * s2[here, :]
        return carry

    loop(rows // chunk, middle, 0)
    pad_lines(flat, ext, rows)
    shifted(ext, cols)


def finish(part, outs, spot, plan):
    if plan:
        emit_split(part, outs[0], outs[1], spot[1], plan)
    else:
        outs[0][...] = part[...]


def slope_kernel(spot, cols, wm, s1, x, dmid1, *rest, plan):
    outs, (ext, flat, part) = rest[:-3], rest[-3:]
    rows, depth = s1.shape
    padded = padded_rows(rows)
    big = chunk_of(padded, 256)

    def step(at, carry):
        base = at * big
        total = jnp.zeros((big, depth), F32)
        for row in range(3):
            for col in range(3):
                near = cols[2 - col, pl.ds(base + LINE * (2 - row), big), :]
                k = 3 * row + col
                total = total + dot_nt(near, wm[k * depth : (k + 1) * depth, :])
        ext[pl.ds(base, big), :] = total
        return carry

    loop(padded // big, step, 0)
    unpad_lines(ext, flat, rows)
    dmid1[...] = (flat[...] * s1[...]).astype(BF16)
    for quad in range(x.shape[1] // 256):
        lanes = slice(256 * quad, 256 * (quad + 1))
        part[lanes, :] = dot_t(x[:, lanes], dmid1[...])
    finish(part, outs, spot, plan)


def middle_kernel(spot, cols, h1pad, turned, own, sums, spairs, bias, *rest, plans):
    outs, (part, part_last) = rest[:-2], rest[-2:]
    padded, depth = h1pad.shape
    for row in range(3):
        for col in range(3):
            k = 3 * row + col
            near = cols[2 - col, LINE * (2 - row) : LINE * (2 - row) + padded, :]
            part[k * depth : (k + 1) * depth, :] = dot_t(h1pad[...], near)
    for quad in range(turned.shape[1] // 256):
        lanes = slice(256 * quad, 256 * (quad + 1))
        sym = quad_matrix(spairs, quad)
        part_last[:, lanes] = (
            turned[:, lanes]
            + dot(own[:, lanes], sym)
            + rank_one(sums[0:1, :], bias[0:1, lanes])
        )
    if plans:
        emit_split(part, outs[0], outs[1], spot[1], plans[0])
        emit_split(part_last, outs[0], outs[1], spot[1], plans[1])
    else:
        outs[0][...] = part[...]
        outs[1][...] = part_last[...]


def spans_step(spot, *refs, steps, extra=0):
    count = 2 * (1 + max(span[0] for spans in steps for span in spans))
    given, outs = refs[: count + extra], refs[count + extra :]
    for at, spans in enumerate(steps):
        to = 0
        for source, start, size, bit in spans:
            mine, other = half_of(given[2 * source], given[2 * source + 1], spot[bit], start, size)
            outs[2 * at][to : to + size // 2, :] = mine
            outs[2 * at + 1][to : to + size // 2, :] = other
            to += size // 2
        left = outs[2 * at].shape[0] - to
        if not left:
            continue
        if extra:
            rows = jnp.concatenate([given[-1][...]] * (outs[0].shape[1] // PAIR), axis=1)
        else:
            tail = given[0].shape[0] - left
            rows = given[0][tail:, :] + given[1][tail:, :]
        for out in outs[2 * at : 2 * at + 2]:
            out[to:, :] = rows


def close_kernel(spot, keep, given, first, middle, last, gain, *, tall, high, scale):
    total = (keep[...] + given[...]) * scale
    for half in range(2):
        lanes = slice(PAIR * half, PAIR * (half + 1))
        step = tall // 4
        for wide in range(4):
            last[pl.ds(2 * wide + half, step, 8), :] = total[step * wide : step * (wide + 1), lanes]
        middle[pl.ds(half, high, 2), :] = total[tall : tall + high, lanes]
        first[pl.ds(half, tall, 2), :] = total[tall + high : 2 * tall + high, lanes]
    size = gain.shape[1]
    each = PAIR // size
    rows = total[2 * tall + high :, :PAIR]
    device = spot[6]
    at = lax.broadcasted_iota(jnp.int32, rows.shape, 0)
    row = jnp.sum(jnp.where(at == device // each, rows, 0.0), axis=0, keepdims=True)
    mine = jnp.zeros((1, size), F32)
    for place in range(each):
        mine = jnp.where(device % each == place, row[:, place * size : (place + 1) * size], mine)
    gain[...] = mine


def input_kernel(dmid1, w1, dpre, out, token):
    token[...] = jnp.zeros_like(token)
    rows = dpre.shape[0]
    chunk = chunk_of(rows, 128)

    def step(at, carry):
        here = slice(at * chunk, (at + 1) * chunk)
        out[here, :] = (dot_nt(dmid1[here, :], w1[...]) + dpre[here, :]).astype(BF16)
        return carry

    loop(rows // chunk, step, 0)


def call(kernel, outs, args, scratch=(), scalars=0, flops=0, ties=(), far=0, room=40):
    args = tuple(args) + tuple(ties)
    specs = [pl.BlockSpec(memory_space=pltpu.SMEM)] * scalars
    specs += [pl.BlockSpec(memory_space=pl.ANY)] * far
    specs += [pl.BlockSpec(memory_space=pltpu.VMEM)] * (len(args) - scalars - len(ties) - far)
    specs += [pl.BlockSpec(memory_space=pl.ANY)] * len(ties)
    count = len(args) - len(ties)

    def body(*refs):
        kernel(*refs[:count], *refs[len(args) :])

    size = sum(a.size * a.dtype.itemsize for a in args)
    size += sum(o.size * o.dtype.itemsize for o in outs)
    return pl.pallas_call(
        body,
        out_shape=tuple(outs),
        in_specs=specs,
        out_specs=tuple(pl.BlockSpec(memory_space=pltpu.VMEM) for _ in outs),
        scratch_shapes=list(scratch),
        cost_estimate=pl.CostEstimate(flops=flops, bytes_accessed=size, transcendentals=0),
        compiler_params=pltpu.CompilerParams(vmem_limit_bytes=room * 2**20),
    )(*args)


def shape(dims, dtype=F32):
    return jax.ShapeDtypeStruct(dims, dtype)


def swap(value, axis, size, flip):
    return lax.ppermute(value, axis, [(at, at ^ flip) for at in range(size)])


def shards(inputs, out_grad, conv_first, conv_middle, conv_last, gain):
    rows, width = inputs.shape
    mid = conv_first.shape[1]
    pairs = width // PAIR
    ghosts = lax.axis_size("ghost")
    groups = lax.axis_size("group")
    devices = ghosts * groups
    span = float(rows * ghosts)
    scale = (rows * devices) ** (-0.5)
    padded = padded_rows(rows)
    ghost = lax.axis_index("ghost")
    group = lax.axis_index("group")
    bits = [ghost] + [(ghost >> bit) & 1 for bit in range(3)]
    bits += [(group >> bit) & 1 for bit in range(2)] + [group * ghosts + ghost]
    spot = jnp.stack(bits).astype(jnp.int32)
    core, across, along, near, far = 1, 2, 3, 4, 5
    split = ghosts == 8 and pairs == 8 and groups == 4
    unit = 2 * rows * width * mid

    ext = pltpu.VMEM((24 + padded + LINE + 8, mid), F32)
    flat = pltpu.VMEM((rows, mid), F32)
    cols = (3, padded + 2 * LINE, mid)
    big = (pairs, TALL, PAIR)
    half = (pairs // 2, TALL, PAIR)
    packed = (pairs // 4, TALL, PAIR)
    stats_outs = [shape(packed)] * 2 if split else [shape(big)]
    stats_held = pltpu.VMEM(big, F32)

    def collect(stats, ties):
        if not split:
            return [lax.psum(stats[0], "ghost")]
        total, send = stats
        given = swap(send, "ghost", ghosts, 1)
        (total,) = call(add_kernel, [shape(packed)], (total, given))
        given = swap(total, "ghost", ghosts, 2)
        (total,) = call(add_kernel, [shape(packed)], (total, given), ties=ties)
        return [total, swap(total, "ghost", ghosts, 4)]

    def share_out(own):
        return [own, swap(own, "ghost", ghosts, 1)] if split else [own]

    own = half if split else big
    held = own[0]
    chunks = rows // chunk_of(rows, 128)
    h1pad, s1, h2, s2, cen, means, sums, *stats = call(
        functools.partial(forward_kernel, split=split),
        [shape((padded, mid), BF16), shape((rows, mid)), shape((rows, mid), BF16),
         shape((rows, mid)), shape((rows, width), BF16), shape((8, width)), shape((8, mid))]
        + stats_outs,
        (spot, *(
            pltpu.with_memory_space_constraint(value, pltpu.HBM)
            for value in (inputs, conv_first, conv_middle, conv_last)
        )),
        (pltpu.VMEM((rows, width), BF16), pltpu.VMEM(conv_first.shape, BF16),
         pltpu.VMEM(conv_middle.shape, BF16), pltpu.VMEM(conv_last.shape, BF16),
         pltpu.SemaphoreType.DMA((3 + chunks,)),
         ext, pltpu.VMEM(cols, BF16), flat, stats_held),
        scalars=1, flops=5 * unit, far=4, room=40,
    )
    (own_part,) = call(own_kernel, [shape((mid, width), BF16)], (h2, cen), flops=unit)
    share, kept = call(
        functools.partial(whiten_kernel, span=span, packed=split),
        [shape(own), shape((held, 2 * NEWTON + 1, PAIR, PAIR))], collect(stats, (own_part,)), flops=10**7,
    )
    given = share_out(share)
    dwb, dpre, wpairs, *stats = call(
        functools.partial(backward_kernel, split=split, shares=len(given)),
        [shape((rows, width), BF16), shape((rows, width)), shape(big)] + stats_outs,
        (spot, inputs, out_grad, cen, means, gain.reshape(1, width), *given),
        (pltpu.VMEM(big, F32), stats_held), scalars=1, flops=2 * unit,
    )
    turned, flow = call(
        turn_kernel, [shape((rows, width), BF16), shape((rows, mid))], (dwb, wpairs, conv_last),
        flops=2 * unit,
    )
    (turned_part,) = call(turned_kernel, [shape((mid, width))], (h2, turned), flops=unit)
    (pulled,) = call(
        functools.partial(pull_kernel, span=span, packed=split), [shape(own)], (*collect(stats, (flow,)), kept),
        flops=10**7, ties=(turned_part,),
    )
    given = share_out(pulled)

    dcols, gains, spairs, bias = call(
        functools.partial(last_kernel, split=split, shares=len(given)),
        [shape(cols, BF16), shape((pairs, PAIR)), shape(big), shape((8, width))],
        (spot, flow, cen, means, s2, conv_last, wpairs, *given),
        (ext, flat, pltpu.VMEM((width, mid), BF16)), scalars=1, flops=2 * unit,
    )
    half_rows = mid * width // 512
    orders = (
        (("ghost", 1), ("ghost", 2), ("group", 0), ("group", 1)),
        (("ghost", 2), ("group", 0), ("ghost", 1), ("group", 1)),
        (("group", 0), ("ghost", 1), ("ghost", 2), ("group", 1)),
    )
    high, tall = 9 * mid // devices, width // devices
    cut = high // 24 * 8
    middle_plan = last_plan = first_plan = None
    if split:
        middle_plan = plan_of(
            [(0, cut, orders[0]), (cut, high - cut, orders[1])], high, 1, ghosts
        )
        last_plan = plan_of(
            [(0, mid // devices, orders[0])], mid // devices, width // 256, ghosts, 9 * mid // 2
        )
        first_plan = plan_of([(0, tall, orders[2])], tall, 1, ghosts)
    middle_part = call(
        functools.partial(middle_kernel, plans=(middle_plan, last_plan) if split else None),
        [shape((9 * mid // 2 + half_rows, mid))] * 2 if split
        else [shape((9 * mid, mid)), shape((mid, width))],
        (spot, dcols, h1pad, turned_part, own_part, sums, spairs, bias),
        (pltpu.VMEM((9 * mid, mid), F32), pltpu.VMEM((mid, width), F32)),
        scalars=1, flops=3 * unit,
    )
    dmid1, *first_part = call(
        functools.partial(slope_kernel, plan=first_plan),
        [shape((rows, mid), BF16)]
        + ([shape((half_rows, mid))] * 2 if split else [shape((width, mid))]),
        (spot, dcols, conv_middle, s1, inputs),
        (ext, flat, pltpu.VMEM((width, mid), F32)), scalars=1, flops=4 * unit,
    )
    portion = width // devices
    if not split:
        input_grad, _ = call(
            input_kernel, [shape((rows, width), BF16), shape((8, PAIR))],
            (dmid1, conv_first, dpre), flops=unit,
        )
        grads = [
            lax.psum_scatter(
                (part[0] * scale).reshape(-1), ("group", "ghost"), scatter_dimension=0, tiled=True
            )
            for part in (first_part, middle_part, middle_part[1:])
        ]
        gain_grad = lax.dynamic_slice_in_dim(
            lax.psum(gains.reshape(-1) * scale, "group"), (group * ghosts + ghost) * portion, portion
        )
        return (input_grad, *grads, gain_grad)

    def move(parts, ways):
        result = []
        for at, (axis, flip) in enumerate(ways):
            result.append(parts[2 * at])
            result.append(swap(parts[2 * at + 1], axis, groups if axis == "group" else ghosts, flip))
        return result

    def run(steps, given, extra=(), more=0, ties=()):
        outs = []
        for at, spans in enumerate(steps):
            height = sum(span[2] for span in spans) // 2 + (more if at == 0 else 0)
            outs += [shape((height, mid))] * 2
        return call(
            functools.partial(spans_step, steps=steps, extra=len(extra)), outs,
            (spot, *given, *extra), scalars=1, ties=ties,
        )

    core_way, x_way, y_way = (("ghost", 1 << bit) for bit in range(3))
    near_way, far_way = ("group", 1), ("group", 2)
    given = move(middle_part, (core_way,))
    first_given = move(first_part, (core_way,))
    pieces = devices // 2
    a_low, a_high, b_all = half_rows, pieces * cut, pieces * (high - cut)
    parts = run(
        (((0, a_high + b_all, a_low, across), (0, 0, a_high, across)),
         ((0, a_high, b_all, along),)), given,
    )
    given = move(parts, (x_way, y_way))
    parts = run((((0, 0, half_rows, near),),), first_given, ties=(parts[0],))
    given += move(parts, (near_way,))
    input_grad, token = call(
        input_kernel, [shape((rows, width), BF16), shape((8, PAIR))], (dmid1, conv_first, dpre),
        flops=unit, ties=(parts[0],),
    )
    a_low, a_high, b_all, c_all = a_low // 2, a_high // 2, b_all // 2, half_rows // 2
    parts = run(
        (((0, 0, a_low, along), (0, a_low, a_high, along)), ((1, 0, b_all, near),),
         ((2, 0, c_all, across),)), given, ties=(token,),
    )
    given = move(parts, (y_way, near_way, x_way))
    a_low, a_high, b_all, c_all = a_low // 2, a_high // 2, b_all // 2, c_all // 2
    parts = run(
        (((0, 0, a_low, near), (0, a_low, a_high, near)), ((1, 0, b_all, across),),
         ((2, 0, c_all, along),)), given, extra=(gains,), more=8,
    )
    given = move(parts, (near_way, x_way, y_way))
    a_low, a_high, b_all, c_all = a_low // 2, a_high // 2, b_all // 2, c_all // 2
    parts = run(
        (((0, 0, a_low, far), (0, a_low, a_high, far), (1, 0, b_all, far), (2, 0, c_all, far)),),
        given, more=8,
    )
    given = move(parts, (far_way,))
    first_grad, middle_grad, last_grad, gain_grad = call(
        functools.partial(close_kernel, tall=tall, high=high, scale=scale),
        [shape((2 * tall, PAIR)), shape((2 * high, PAIR)), shape((2 * tall, PAIR)),
         shape((1, portion))],
        (spot, *given), scalars=1,
    )
    return (
        input_grad, first_grad.reshape(-1), middle_grad.reshape(-1), last_grad.reshape(-1),
        gain_grad.reshape(-1),
    )


def solution(mesh):
    in_specs = (P(("group", "ghost"), None), P(("group", "ghost"), None), P(), P(), P(), P())
    out_specs = (
        P(("group", "ghost"), None),
        P(("group", "ghost")),
        P(("group", "ghost")),
        P(("group", "ghost")),
        P(("group", "ghost")),
    )
    return jax.shard_map(shards, mesh=mesh, in_specs=in_specs, out_specs=out_specs, check_vma=False)
```

```python
import functools

import jax
import jax.numpy as jnp
from jax import lax
from jax.experimental import pallas as pl
from jax.experimental.pallas import tpu as pltpu
from jax.sharding import PartitionSpec as P

GROUP = 64
NEWTON = 5
SIDE = 14
LINE = 16
PAIR = 2 * GROUP
TALL = GROUP + 8
epsilon = 1e-05

F32 = jnp.float32
BF16 = jnp.bfloat16


def dot(left, right):
    return jnp.dot(left, right, preferred_element_type=F32)


def dot_t(left, right):
    return lax.dot_general(left, right, (((0,), (0,)), ((), ())), preferred_element_type=F32)


def dot_nt(left, right):
    return lax.dot_general(left, right, (((1,), (1,)), ((), ())), preferred_element_type=F32)


def halves_of(value):
    high = value.astype(BF16)
    return high, (value - high.astype(F32)).astype(BF16)


def exact(left, right):
    a, b = halves_of(left)
    c, d = halves_of(right)
    low = dot(jnp.concatenate([a, b], axis=1), jnp.concatenate([d, c], axis=0))
    return low + dot(a, c)


def exact_two(left, first, second):
    both = exact(left, jnp.concatenate([first, second], axis=1))
    return both[:, : first.shape[1]], both[:, first.shape[1] :]


def outer_of(row):
    tile = vectors(row)
    return lax.dot_general(
        tile, tile, (((0,), (0,)), ((), ())), preferred_element_type=F32,
        precision=lax.Precision.HIGHEST,
    )


def sigmoid(value):
    return 0.5 * jnp.tanh(0.5 * value) + 0.5


def two_rows(row):
    high, low = halves_of(jnp.broadcast_to(row, (16, row.shape[1])))
    at = lax.broadcasted_iota(jnp.int32, high.shape, 0)
    return jnp.where(at == 0, high.astype(F32), jnp.where(at == 1, low.astype(F32), 0.0)).astype(
        BF16
    )


def row_times(row, matrix, product=dot):
    return jnp.sum(product(two_rows(row), matrix), axis=0, keepdims=True)


def rank_one(left, right):
    tiles = []
    for row, order in ((left, (0, 1, 0)), (right, (0, 0, 1))):
        pair = halves_of(jnp.broadcast_to(row, (16, row.shape[1])))
        at = lax.broadcasted_iota(jnp.int32, pair[0].shape, 0)
        tile = jnp.zeros(pair[0].shape, F32)
        for place, which in enumerate(order):
            tile = jnp.where(at == place, pair[which].astype(F32), tile)
        tiles.append(tile.astype(BF16))
    return dot_t(*tiles)


def chunk_of(rows, most):
    best = 16
    for size in range(16, most + 1, 16):
        if rows % size == 0:
            best = size
    return best


def loop(count, body, carry):
    for at in range(count):
        carry = body(at, carry)
    return carry


def left_half(shape):
    return lax.broadcasted_iota(jnp.int32, shape, 1) < GROUP


def spread(packed):
    left = left_half(packed.shape)
    zero = jnp.zeros_like(packed)
    return jnp.concatenate([jnp.where(left, packed, zero), jnp.where(left, zero, packed)], axis=0)


def pack(square):
    top, bottom = square[:GROUP], square[GROUP:]
    return jnp.where(left_half(top.shape), top, bottom)


def vectors(*rows):
    at = lax.broadcasted_iota(jnp.int32, (8, PAIR), 0)
    tile = jnp.zeros((8, PAIR), F32)
    for place, row in enumerate(rows):
        tile = jnp.where(at == place, row, tile)
    return tile


def fold(value):
    rows, lanes = value.shape
    return jnp.sum(value.reshape(rows // 8, 8, lanes), axis=0)


def pad_lines(source, ext, rows):
    for line in range(rows // SIDE):
        place = 24 + LINE * (line + line // SIDE)
        ext[place : place + SIDE, :] = source[SIDE * line : SIDE * (line + 1), :]


def unpad_lines(source, target, rows):
    for line in range(rows // SIDE):
        place = LINE * (line + line // SIDE)
        target[SIDE * line : SIDE * (line + 1), :] = source[place : place + SIDE, :]


def padded_rows(rows):
    return rows // (SIDE * SIDE) * (SIDE + 1) * LINE


def shifted(ext, cols):
    length = cols.shape[1]
    for col in range(3):
        cols[col] = ext[7 + col : 7 + col + length, :].astype(BF16)


def emit_split(source, keep, send, core, plan):
    for start, height, first, size, mine in plan:
        lanes = keep.shape[1]
        for wide in range(source.shape[1] // lanes):
            to = slice(start + wide * height, start + (wide + 1) * height)
            cols = slice(wide * lanes, (wide + 1) * lanes)
            for target, half in ((keep, core), (send, 1 - core)):
                place = pl.multiple_of((mine + half) * size + first, 8)
                target[to, :] = source[pl.ds(place, height), cols]


def plan_of(parts, piece, wide, ghosts, start=0):
    plan = []
    for first, height, steps in parts:
        for at in range(2 ** len(steps)):
            source = 0
            for place, (axis, bit) in enumerate(steps):
                value = (at >> (len(steps) - 1 - place)) & 1
                source += value << bit if axis == "ghost" else (value << bit) * ghosts
            plan.append((start, height, first, piece, source))
            start += height * wide
    return plan


def half_of(left, right, bit, start=0, rows=None):
    rows = (left.shape[0] if rows is None else rows) // 2
    mine = pl.ds(pl.multiple_of(start + bit * rows, 8), rows)
    other = pl.ds(pl.multiple_of(start + (1 - bit) * rows, 8), rows)
    return left[mine, :] + right[mine, :], left[other, :] + right[other, :]


def emit_pairs(stats, outs, spot):
    shape = (GROUP, PAIR)
    row = lax.broadcasted_iota(jnp.int32, shape, 0)
    lane = lax.broadcasted_iota(jnp.int32, shape, 1)
    left = lane < GROUP
    col = jnp.where(left, lane, lane - GROUP)
    for parity in range(2):
        for slot in range(stats.shape[0] // 4):
            pair = 4 * slot + parity, 4 * slot + 2 + parity
            first, second = (stats[p, :GROUP, :] for p in pair)
            upper = jnp.where(left, first, pltpu.roll(second, GROUP, 1))
            lower = jnp.where(left, pltpu.roll(first, GROUP, 1), second)
            rows = [
                jnp.sum(jnp.where(row == col, m, 0.0), axis=0, keepdims=True)
                for m in (first, second)
            ]
            for place in range(2):
                rows += [stats[p, GROUP + place : GROUP + place + 1, :] for p in pair]
            both = jnp.concatenate([jnp.where(row <= col, upper, lower), vectors(*rows)], axis=0)

            @pl.when(spot[1] == parity)
            def _(both=both, slot=slot):
                outs[0][slot] = both

            @pl.when(spot[1] != parity)
            def _(both=both, slot=slot):
                outs[1][slot] = both


def take_pairs(total, packed):
    result = []
    if not packed:
        for at in range(total.shape[0]):
            vecs = [total[at, GROUP + p : GROUP + p + 1, :] for p in range(2)]
            result.append((spread(total[at, :GROUP, :]), *vecs))
        return result
    shape = (PAIR, PAIR)
    row = lax.broadcasted_iota(jnp.int32, shape, 0)
    col = lax.broadcasted_iota(jnp.int32, shape, 1)
    mask = jnp.where(row < GROUP, row - col, col - row) < 0
    eye = identity()
    for slot in range(total.shape[0]):
        both = total[slot, :GROUP, :]
        turned = pltpu.roll(both, GROUP, 1)
        left = left_half(both.shape)
        for at in range(2):
            twice = jnp.where(left, *((both, turned) if at == 0 else (turned, both)))
            part = jnp.where(mask, spread(twice), 0.0)
            line = [total[slot, GROUP + 2 * p + at : GROUP + 2 * p + at + 1, :] for p in range(3)]
            result.append((part + part.T + eye * line[0], line[1], line[2]))
    return result


def add_kernel(left, right, out):
    out[...] = left[...] + right[...]


def forward_kernel(
    spot, x_far, w1_far, wm_far, w3_far, h1pad, s1, h2, s2, cen, means, sums, *rest, split
):
    outs, (x, w1, wm, w3, sems, ext, cols, flat, stats) = rest[:-9], rest[-9:]
    rows = x.shape[0]
    part = chunk_of(rows, 128)

    def slab(at):
        here = slice(at * part, (at + 1) * part)
        return pltpu.make_async_copy(x_far.at[here, :], x.at[here, :], sems.at[3 + at])

    weights = [
        pltpu.make_async_copy(far, ref, sems.at[at])
        for at, (far, ref) in enumerate(((w1_far, w1), (wm_far, wm), (w3_far, w3)))
    ]
    weights[0].start()
    for at in range(rows // part):
        slab(at).start()
    weights[1].start()
    weights[2].start()
    chunk = chunk_of(rows, 128)
    ext[...] = jnp.zeros_like(ext)

    weights[0].wait()

    slabs = rows // part
    for start, stop in ((0, (slabs + 1) // 2), ((slabs + 1) // 2, slabs)):
        for at in range(start, stop):
            slab(at).wait()
        here = slice(start * part, stop * part)
        flat[here, :] = dot(x[here, :], w1[...])

        def first(at, carry, start=start):
            here = slice((start + at) * part, (start + at + 1) * part)
            act = flat[here, :]
            sig = sigmoid(act)
            flat[here, :] = act * sig
            s1[here, :] = sig * (1.0 + act * (1.0 - sig))
            return carry

        loop(stop - start, first, 0)
    pad_lines(flat, ext, rows)
    shifted(ext, cols)
    padded = padded_rows(rows)
    h1pad[...] = cols[1, LINE : LINE + padded, :]
    big = chunk_of(padded, 512)
    weights[1].wait()

    def middle(at, carry):
        base = at * big
        total = jnp.zeros((big, wm.shape[1]), F32)
        for row in range(3):
            for col in range(3):
                left = cols[col, pl.ds(base + LINE * row, big), :]
                k = 3 * row + col
                depth = left.shape[1]
                total = total + dot(left, wm[k * depth : (k + 1) * depth, :])
        ext[pl.ds(base, big), :] = total
        return carry

    loop(padded // big, middle, 0)
    unpad_lines(ext, flat, rows)
    width = w3.shape[1]
    weights[2].wait()

    def second(at, hidden_sum):
        here = slice(at * chunk, (at + 1) * chunk)
        act = flat[here, :]
        sig = sigmoid(act)
        hidden = (act * sig).astype(BF16)
        h2[here, :] = hidden
        s2[here, :] = sig * (1.0 + act * (1.0 - sig))
        return hidden_sum + fold(hidden.astype(F32))

    zeros = jnp.zeros((8, w3.shape[0]), F32)
    hidden_sum = loop(rows // chunk, second, zeros)
    hidden_sum = jnp.sum(hidden_sum, axis=0, keepdims=True)
    sums[...] = jnp.broadcast_to(hidden_sum, sums.shape)
    total = row_times(hidden_sum, w3[...])
    mean = total / rows
    means[...] = jnp.broadcast_to(mean, means.shape)
    for quad in range(width // 256):
        lanes = slice(256 * quad, 256 * (quad + 1))
        centered = (dot(h2[...], w3[:, lanes]) - mean[:, lanes]).astype(BF16)
        cen[:, lanes] = centered
        square = dot_t(centered, centered)
        for half in range(2):
            pair = 2 * quad + half
            ch = slice(PAIR * pair, PAIR * (pair + 1))
            row = mean[:, ch]
            outer = outer_of(row)
            inner = square[PAIR * half : PAIR * (half + 1), PAIR * half : PAIR * (half + 1)]
            top, low = pack(inner + outer * rows), vectors(total[:, ch])
            stats[pair, :GROUP, :] = top
            stats[pair, GROUP:, :] = low
    if split:
        emit_pairs(stats, outs, spot)
    else:
        outs[0][...] = stats[...]


def identity():
    shape = (PAIR, PAIR)
    return jnp.where(
        lax.broadcasted_iota(jnp.int32, shape, 0) == lax.broadcasted_iota(jnp.int32, shape, 1),
        1.0, 0.0,
    ).astype(F32)


def per_block(square):
    row_sums = jnp.sum(square, axis=1, keepdims=True)
    top = jnp.sum(row_sums[:GROUP], axis=0, keepdims=True)
    bottom = jnp.sum(row_sums[GROUP:], axis=0, keepdims=True)
    upper = lax.broadcasted_iota(jnp.int32, (PAIR, 1), 0) < GROUP
    return jnp.where(upper, top, bottom)


def total_of(terms):
    total = terms[0][...]
    for term in terms[1:]:
        total = total + term[...]
    return total


def whiten_kernel(*refs, span, packed):
    terms, (out, keep) = refs[:-2], refs[-2:]
    given = take_pairs(total_of(terms), packed)
    eye = identity()
    blocks = spread(jnp.ones((GROUP, PAIR), F32))
    means = [sums / span for _, sums, _ in given]
    covs = [
        moments / span - outer_of(mean) * blocks + epsilon * eye
        for (moments, _, _), mean in zip(given, means)
    ]
    traces = [per_block(cov * eye) for cov in covs]
    normed = [cov / trace for cov, trace in zip(covs, traces)]
    powers = [1.5 * eye - 0.5 * norm for norm in normed]
    for at, trace in enumerate(traces):
        keep[at, 0] = normed[at]
        keep[at, 1] = eye / trace
    for sweep in range(NEWTON - 1):
        both = [exact_two(power, power, norm) for power, norm in zip(powers, normed)]
        squares, sides = zip(*both)
        for at, power in enumerate(powers):
            keep[at, 2 + 2 * sweep] = power
            keep[at, 3 + 2 * sweep] = squares[at]
        powers = [
            1.5 * power - 0.5 * exact(square, side)
            for power, square, side in zip(powers, squares, sides)
        ]
    for at, power in enumerate(powers):
        keep[at, 2 * NEWTON] = power
        out[at, :GROUP, :] = pack(power / jnp.sqrt(traces[at]))
        out[at, GROUP:, :] = vectors(means[at])


def pull_kernel(*refs, span, packed):
    terms, (keep, out) = refs[:-2], refs[-2:]
    given = take_pairs(total_of(terms), packed)
    eye = identity()
    every = range(len(given))
    normed = [keep[at, 0] for at in every]
    inverse = [per_block(keep[at, 1]) / GROUP for at in every]
    roots = [jnp.sqrt(value) for value in inverse]
    powers = [keep[at, 2 * NEWTON] for at in every]
    grads = [given[at][0] * roots[at] for at in every]
    trace_grads = [
        -0.5 * inverse[at] * roots[at] * per_block(given[at][0] * powers[at]) for at in every
    ]
    normed_grads = [jnp.zeros_like(grads[0])] * len(given)
    for sweep in reversed(range(NEWTON - 1)):
        power = [keep[at, 2 + 2 * sweep] for at in every]
        square = [keep[at, 3 + 2 * sweep] for at in every]
        turned, side = zip(*(exact_two(grads[at], normed[at], power[at]) for at in every))
        turned = [turned[at] + turned[at].T for at in every]
        turned, outer = zip(*(exact_two(turned[at], power[at], square[at]) for at in every))
        side = [exact(side[at], square[at]) for at in every]
        normed_grads = [normed_grads[at] - 0.25 * (side[at] + side[at].T) for at in every]
        inner = [exact(power[at], turned[at]) for at in every]
        grads = [
            1.5 * grads[at] - 0.25 * (outer[at] + outer[at].T + inner[at]) for at in every
        ]
    for at in every:
        normed_grad = normed_grads[at] - 0.5 * grads[at]
        trace_grad = trace_grads[at] - inverse[at] * per_block(normed_grad * normed[at])
        both = normed_grad * inverse[at] + eye * trace_grad
        bias = -exact(vectors(given[at][1] / span), (powers[at] * roots[at]).T)
        out[at, :GROUP, :] = pack(both / span)
        out[at, GROUP:, :] = vectors(bias[0:1, :], given[at][2])


def place_pairs(spot, given, pairs, split):
    if split:
        for side, shares in enumerate(given):
            for at in range(shares.shape[0]):
                pairs[2 * at + jnp.bitwise_xor(side, spot[1])] = shares[at]
    else:
        pairs[...] = given[0][...]


def quad_matrix(pairs, quad):
    zero = jnp.zeros((PAIR, PAIR), F32)
    first = spread(pairs[2 * quad, :GROUP, :])
    second = spread(pairs[2 * quad + 1, :GROUP, :])
    top = jnp.concatenate([first, zero], axis=1)
    bottom = jnp.concatenate([zero, second], axis=1)
    return jnp.concatenate([top, bottom], axis=0).astype(BF16)


def row_of(pairs, quad, place):
    at = GROUP + place
    return jnp.concatenate(
        [pairs[2 * quad, at : at + 1, :], pairs[2 * quad + 1, at : at + 1, :]], axis=1
    )


def backward_kernel(spot, x, og, cen, means, gain, *rest, split, shares):
    given, rest = rest[:shares], rest[shares:]
    (dwb, dpre_out, w_out), outs, (pairs, stats, whites) = rest[:3], rest[3:-3], rest[-3:]
    rows, width = x.shape
    place_pairs(spot, given, pairs, split)
    w_out[...] = pairs[...]
    chunk = chunk_of(rows, 128)
    quads = width // 256
    aways, shifts = [], []

    def multiply(quad):
        lanes = slice(256 * quad, 256 * (quad + 1))
        whiten = quad_matrix(pairs, quad)
        aways.append(means[0:1, lanes] - row_of(pairs, quad, 0))
        shifts.append(row_times(aways[-1], whiten))
        whites[quad % 2] = dot(cen[:, lanes], whiten)

    multiply(0)
    for quad in range(quads):
        if quad + 1 < quads:
            multiply(quad + 1)
        lanes = slice(256 * quad, 256 * (quad + 1))
        away, shift = aways[quad], shifts[quad]
        scale = gain[:, lanes]

        def step(at, carry, quad=quad, lanes=lanes, shift=shift, scale=scale):
            col_sum, gain_sum = carry
            here = slice(at * chunk, (at + 1) * chunk)
            white = whites[quad % 2, here, :] + shift
            pre = x[here, lanes].astype(F32) + scale * white
            sig = sigmoid(pre)
            dpre = og[here, lanes].astype(F32) * (sig * (1.0 + pre * (1.0 - sig)))
            dpre_out[here, lanes] = dpre
            dwhite = scale * dpre
            dwb[here, lanes] = dwhite.astype(BF16)
            return col_sum + fold(dwhite), gain_sum + fold(dpre * white)

        zero = jnp.zeros((8, 256), F32)
        col_sum, gain_sum = loop(rows // chunk, step, (zero, zero))
        col_sum = jnp.sum(col_sum, axis=0, keepdims=True)
        gain_sum = jnp.sum(gain_sum, axis=0, keepdims=True)
        square = dot_t(cen[:, lanes], dwb[:, lanes]) + rank_one(away, col_sum)
        for half in range(2):
            ch = slice(PAIR * half, PAIR * (half + 1))
            pair = 2 * quad + half
            inner = square[ch, ch]
            stats[pair, :GROUP, :] = pack(inner + inner.T)
            stats[pair, GROUP:, :] = vectors(col_sum[:, ch], gain_sum[:, ch])
    if split:
        emit_pairs(stats, outs, spot)
    else:
        outs[0][...] = stats[...]


def own_kernel(h2, cen, out):
    for quad in range(cen.shape[1] // 256):
        lanes = slice(256 * quad, 256 * (quad + 1))
        out[:, lanes] = dot_t(h2[...], cen[:, lanes]).astype(BF16)


def turn_kernel(dwb, wpairs, w3, turned, flow):
    for quad in range(dwb.shape[1] // 256):
        lanes = slice(256 * quad, 256 * (quad + 1))
        whiten = quad_matrix(wpairs, quad).T

        turned[:, lanes] = dot(dwb[:, lanes], whiten).astype(BF16)
    flow[...] = dot_nt(turned[...], w3[...])


def turned_kernel(h2, turned, out):
    for quad in range(turned.shape[1] // 256):
        lanes = slice(256 * quad, 256 * (quad + 1))
        out[:, lanes] = dot_t(h2[...], turned[:, lanes])


def last_kernel(spot, flow, cen, means, s2, w3, wpairs, *rest, split, shares):
    given, (cols, gains, spairs, bias_out, ext, flat, joint) = rest[:shares], rest[shares:]
    rows, width = cen.shape
    place_pairs(spot, given, spairs, split)
    gains[...] = spairs[:, GROUP + 1, :]
    chunk = chunk_of(rows, 128)
    ext[...] = jnp.zeros_like(ext)
    low = jnp.zeros((1, w3.shape[0]), F32)
    for quad in range(width // 256):
        lanes = slice(256 * quad, 256 * (quad + 1))
        sym = quad_matrix(spairs, quad)
        away = means[0:1, lanes] - row_of(wpairs, quad, 0)
        bias = row_of(spairs, quad, 0) + row_times(away, sym)
        bias_out[:, lanes] = jnp.broadcast_to(bias, (8, 256))
        low = low + row_times(bias, w3[:, lanes], dot_nt)
        joint[lanes, :] = dot_nt(sym, w3[:, lanes]).astype(BF16)

    flat[...] = dot(cen[...], joint[...])

    def middle(at, carry):
        here = slice(at * chunk, (at + 1) * chunk)
        flat[here, :] = (flow[here, :] + flat[here, :] + low) * s2[here, :]
        return carry

    loop(rows // chunk, middle, 0)
    pad_lines(flat, ext, rows)
    shifted(ext, cols)


def finish(part, outs, spot, plan):
    if plan:
        emit_split(part, outs[0], outs[1], spot[1], plan)
    else:
        outs[0][...] = part[...]


def slope_kernel(spot, cols, wm, s1, x, dmid1, *rest, plan):
    outs, (ext, flat, part) = rest[:-3], rest[-3:]
    rows, depth = s1.shape
    padded = padded_rows(rows)
    big = chunk_of(padded, 512)

    def step(at, carry):
        base = at * big
        total = jnp.zeros((big, depth), F32)
        for row in range(3):
            for col in range(3):
                near = cols[2 - col, pl.ds(base + LINE * (2 - row), big), :]
                k = 3 * row + col
                total = total + dot_nt(near, wm[k * depth : (k + 1) * depth, :])
        ext[pl.ds(base, big), :] = total
        return carry

    loop(padded // big, step, 0)
    unpad_lines(ext, flat, rows)
    dmid1[...] = (flat[...] * s1[...]).astype(BF16)
    for quad in range(x.shape[1] // 256):
        lanes = slice(256 * quad, 256 * (quad + 1))
        part[lanes, :] = dot_t(x[:, lanes], dmid1[...])
    finish(part, outs, spot, plan)


def middle_kernel(spot, cols, h1pad, turned, own, sums, spairs, bias, *rest, plans):
    outs, (part, part_last) = rest[:-2], rest[-2:]
    padded, depth = h1pad.shape
    for row in range(3):
        for col in range(3):
            k = 3 * row + col
            near = cols[2 - col, LINE * (2 - row) : LINE * (2 - row) + padded, :]
            part[k * depth : (k + 1) * depth, :] = dot_t(h1pad[...], near)
    for quad in range(turned.shape[1] // 256):
        lanes = slice(256 * quad, 256 * (quad + 1))
        sym = quad_matrix(spairs, quad)
        part_last[:, lanes] = (
            turned[:, lanes]
            + dot(own[:, lanes], sym)
            + rank_one(sums[0:1, :], bias[0:1, lanes])
        )
    if plans:
        emit_split(part, outs[0], outs[1], spot[1], plans[0])
        emit_split(part_last, outs[0], outs[1], spot[1], plans[1])
    else:
        outs[0][...] = part[...]
        outs[1][...] = part_last[...]


def spans_step(spot, *refs, steps, extra=0):
    count = 2 * (1 + max(span[0] for spans in steps for span in spans))
    given, outs = refs[: count + extra], refs[count + extra :]
    for at, spans in enumerate(steps):
        to = 0
        for source, start, size, bit in spans:
            mine, other = half_of(given[2 * source], given[2 * source + 1], spot[bit], start, size)
            outs[2 * at][to : to + size // 2, :] = mine
            outs[2 * at + 1][to : to + size // 2, :] = other
            to += size // 2
        left = outs[2 * at].shape[0] - to
        if not left:
            continue
        if extra:
            rows = jnp.concatenate([given[-1][...]] * (outs[0].shape[1] // PAIR), axis=1)
        else:
            tail = given[0].shape[0] - left
            rows = given[0][tail:, :] + given[1][tail:, :]
        for out in outs[2 * at : 2 * at + 2]:
            out[to:, :] = rows


def close_kernel(spot, keep, given, first, middle, last, gain, *, tall, high, scale):
    total = (keep[...] + given[...]) * scale
    for half in range(2):
        lanes = slice(PAIR * half, PAIR * (half + 1))
        step = tall // 4
        for wide in range(4):
            last[pl.ds(2 * wide + half, step, 8), :] = total[step * wide : step * (wide + 1), lanes]
        middle[pl.ds(half, high, 2), :] = total[tall : tall + high, lanes]
        first[pl.ds(half, tall, 2), :] = total[tall + high : 2 * tall + high, lanes]
    size = gain.shape[1]
    each = PAIR // size
    rows = total[2 * tall + high :, :PAIR]
    device = spot[6]
    at = lax.broadcasted_iota(jnp.int32, rows.shape, 0)
    row = jnp.sum(jnp.where(at == device // each, rows, 0.0), axis=0, keepdims=True)
    mine = jnp.zeros((1, size), F32)
    for place in range(each):
        mine = jnp.where(device % each == place, row[:, place * size : (place + 1) * size], mine)
    gain[...] = mine


def input_kernel(dmid1, w1, dpre, out, token):
    token[...] = jnp.zeros_like(token)
    rows = dpre.shape[0]
    chunk = chunk_of(rows, 128)

    def step(at, carry):
        here = slice(at * chunk, (at + 1) * chunk)
        out[here, :] = (dot_nt(dmid1[here, :], w1[...]) + dpre[here, :]).astype(BF16)
        return carry

    loop(rows // chunk, step, 0)


def call(kernel, outs, args, scratch=(), scalars=0, flops=0, ties=(), far=0, room=40):
    args = tuple(args) + tuple(ties)
    specs = [pl.BlockSpec(memory_space=pltpu.SMEM)] * scalars
    specs += [pl.BlockSpec(memory_space=pl.ANY)] * far
    specs += [pl.BlockSpec(memory_space=pltpu.VMEM)] * (len(args) - scalars - len(ties) - far)
    specs += [pl.BlockSpec(memory_space=pl.ANY)] * len(ties)
    count = len(args) - len(ties)

    def body(*refs):
        kernel(*refs[:count], *refs[len(args) :])

    size = sum(a.size * a.dtype.itemsize for a in args)
    size += sum(o.size * o.dtype.itemsize for o in outs)
    return pl.pallas_call(
        body,
        out_shape=tuple(outs),
        in_specs=specs,
        out_specs=tuple(pl.BlockSpec(memory_space=pltpu.VMEM) for _ in outs),
        scratch_shapes=list(scratch),
        cost_estimate=pl.CostEstimate(flops=flops, bytes_accessed=size, transcendentals=0),
        compiler_params=pltpu.CompilerParams(vmem_limit_bytes=room * 2**20),
    )(*args)


def shape(dims, dtype=F32):
    return jax.ShapeDtypeStruct(dims, dtype)


def swap(value, axis, size, flip):
    return lax.ppermute(value, axis, [(at, at ^ flip) for at in range(size)])


def shards(inputs, out_grad, conv_first, conv_middle, conv_last, gain):
    rows, width = inputs.shape
    mid = conv_first.shape[1]
    pairs = width // PAIR
    ghosts = lax.axis_size("ghost")
    groups = lax.axis_size("group")
    devices = ghosts * groups
    span = float(rows * ghosts)
    scale = (rows * devices) ** (-0.5)
    padded = padded_rows(rows)
    ghost = lax.axis_index("ghost")
    group = lax.axis_index("group")
    bits = [ghost] + [(ghost >> bit) & 1 for bit in range(3)]
    bits += [(group >> bit) & 1 for bit in range(2)] + [group * ghosts + ghost]
    spot = jnp.stack(bits).astype(jnp.int32)
    core, across, along, near, far = 1, 2, 3, 4, 5
    split = ghosts == 8 and pairs == 8 and groups == 4
    unit = 2 * rows * width * mid

    ext = pltpu.VMEM((24 + padded + LINE + 8, mid), F32)
    flat = pltpu.VMEM((rows, mid), F32)
    cols = (3, padded + 2 * LINE, mid)
    big = (pairs, TALL, PAIR)
    half = (pairs // 2, TALL, PAIR)
    packed = (pairs // 4, TALL, PAIR)
    stats_outs = [shape(packed)] * 2 if split else [shape(big)]
    stats_held = pltpu.VMEM(big, F32)

    def collect(stats, ties):
        if not split:
            return [lax.psum(stats[0], "ghost")]
        total, send = stats
        given = swap(send, "ghost", ghosts, 1)
        (total,) = call(add_kernel, [shape(packed)], (total, given))
        given = swap(total, "ghost", ghosts, 2)
        (total,) = call(add_kernel, [shape(packed)], (total, given), ties=ties)
        return [total, swap(total, "ghost", ghosts, 4)]

    def share_out(own):
        return [own, swap(own, "ghost", ghosts, 1)] if split else [own]

    own = half if split else big
    held = own[0]
    chunks = rows // chunk_of(rows, 128)
    h1pad, s1, h2, s2, cen, means, sums, *stats = call(
        functools.partial(forward_kernel, split=split),
        [shape((padded, mid), BF16), shape((rows, mid)), shape((rows, mid), BF16),
         shape((rows, mid)), shape((rows, width), BF16), shape((8, width)), shape((8, mid))]
        + stats_outs,
        (spot, *(
            pltpu.with_memory_space_constraint(value, pltpu.HBM)
            for value in (inputs, conv_first, conv_middle, conv_last)
        )),
        (pltpu.VMEM((rows, width), BF16), pltpu.VMEM(conv_first.shape, BF16),
         pltpu.VMEM(conv_middle.shape, BF16), pltpu.VMEM(conv_last.shape, BF16),
         pltpu.SemaphoreType.DMA((3 + chunks,)),
         ext, pltpu.VMEM(cols, BF16), flat, stats_held),
        scalars=1, flops=5 * unit, far=4, room=40,
    )
    (own_part,) = call(own_kernel, [shape((mid, width), BF16)], (h2, cen), flops=unit)
    share, kept = call(
        functools.partial(whiten_kernel, span=span, packed=split),
        [shape(own), shape((held, 2 * NEWTON + 1, PAIR, PAIR))], collect(stats, (own_part,)), flops=10**7,
    )
    given = share_out(share)
    dwb, dpre, wpairs, *stats = call(
        functools.partial(backward_kernel, split=split, shares=len(given)),
        [shape((rows, width), BF16), shape((rows, width)), shape(big)] + stats_outs,
        (spot, inputs, out_grad, cen, means, gain.reshape(1, width), *given),
        (pltpu.VMEM(big, F32), stats_held, pltpu.VMEM((2, rows, 256), F32)), scalars=1,
        flops=2 * unit,
    )
    turned, flow = call(
        turn_kernel, [shape((rows, width), BF16), shape((rows, mid))], (dwb, wpairs, conv_last),
        flops=2 * unit,
    )
    (turned_part,) = call(turned_kernel, [shape((mid, width))], (h2, turned), flops=unit)
    (pulled,) = call(
        functools.partial(pull_kernel, span=span, packed=split), [shape(own)], (*collect(stats, (flow,)), kept),
        flops=10**7, ties=(turned_part,),
    )
    given = share_out(pulled)

    dcols, gains, spairs, bias = call(
        functools.partial(last_kernel, split=split, shares=len(given)),
        [shape(cols, BF16), shape((pairs, PAIR)), shape(big), shape((8, width))],
        (spot, flow, cen, means, s2, conv_last, wpairs, *given),
        (ext, flat, pltpu.VMEM((width, mid), BF16)), scalars=1, flops=2 * unit,
    )
    half_rows = mid * width // 512
    orders = (
        (("ghost", 1), ("ghost", 2), ("group", 0), ("group", 1)),
        (("ghost", 2), ("group", 0), ("ghost", 1), ("group", 1)),
        (("group", 0), ("ghost", 1), ("ghost", 2), ("group", 1)),
    )
    high, tall = 9 * mid // devices, width // devices
    cut = high // 24 * 8
    middle_plan = last_plan = first_plan = None
    if split:
        middle_plan = plan_of(
            [(0, cut, orders[0]), (cut, high - cut, orders[1])], high, 1, ghosts
        )
        last_plan = plan_of(
            [(0, mid // devices, orders[0])], mid // devices, width // 256, ghosts, 9 * mid // 2
        )
        first_plan = plan_of([(0, tall, orders[2])], tall, 1, ghosts)
    middle_part = call(
        functools.partial(middle_kernel, plans=(middle_plan, last_plan) if split else None),
        [shape((9 * mid // 2 + half_rows, mid))] * 2 if split
        else [shape((9 * mid, mid)), shape((mid, width))],
        (spot, dcols, h1pad, turned_part, own_part, sums, spairs, bias),
        (pltpu.VMEM((9 * mid, mid), F32), pltpu.VMEM((mid, width), F32)),
        scalars=1, flops=3 * unit,
    )
    dmid1, *first_part = call(
        functools.partial(slope_kernel, plan=first_plan),
        [shape((rows, mid), BF16)]
        + ([shape((half_rows, mid))] * 2 if split else [shape((width, mid))]),
        (spot, dcols, conv_middle, s1, inputs),
        (ext, flat, pltpu.VMEM((width, mid), F32)), scalars=1, flops=4 * unit,
    )
    portion = width // devices
    if not split:
        input_grad, _ = call(
            input_kernel, [shape((rows, width), BF16), shape((8, PAIR))],
            (dmid1, conv_first, dpre), flops=unit,
        )
        grads = [
            lax.psum_scatter(
                (part[0] * scale).reshape(-1), ("group", "ghost"), scatter_dimension=0, tiled=True
            )
            for part in (first_part, middle_part, middle_part[1:])
        ]
        gain_grad = lax.dynamic_slice_in_dim(
            lax.psum(gains.reshape(-1) * scale, "group"), (group * ghosts + ghost) * portion, portion
        )
        return (input_grad, *grads, gain_grad)

    def move(parts, ways):
        result = []
        for at, (axis, flip) in enumerate(ways):
            result.append(parts[2 * at])
            result.append(swap(parts[2 * at + 1], axis, groups if axis == "group" else ghosts, flip))
        return result

    def run(steps, given, extra=(), more=0, ties=()):
        outs = []
        for at, spans in enumerate(steps):
            height = sum(span[2] for span in spans) // 2 + (more if at == 0 else 0)
            outs += [shape((height, mid))] * 2
        return call(
            functools.partial(spans_step, steps=steps, extra=len(extra)), outs,
            (spot, *given, *extra), scalars=1, ties=ties,
        )

    core_way, x_way, y_way = (("ghost", 1 << bit) for bit in range(3))
    near_way, far_way = ("group", 1), ("group", 2)
    given = move(middle_part, (core_way,))
    first_given = move(first_part, (core_way,))
    pieces = devices // 2
    a_low, a_high, b_all = half_rows, pieces * cut, pieces * (high - cut)
    parts = run(
        (((0, a_high + b_all, a_low, across), (0, 0, a_high, across)),
         ((0, a_high, b_all, along),)), given,
    )
    given = move(parts, (x_way, y_way))
    parts = run((((0, 0, half_rows, near),),), first_given, ties=(parts[0],))
    given += move(parts, (near_way,))
    input_grad, token = call(
        input_kernel, [shape((rows, width), BF16), shape((8, PAIR))], (dmid1, conv_first, dpre),
        flops=unit, ties=(parts[0],),
    )
    a_low, a_high, b_all, c_all = a_low // 2, a_high // 2, b_all // 2, half_rows // 2
    parts = run(
        (((0, 0, a_low, along), (0, a_low, a_high, along)), ((1, 0, b_all, near),),
         ((2, 0, c_all, across),)), given, ties=(token,),
    )
    given = move(parts, (y_way, near_way, x_way))
    a_low, a_high, b_all, c_all = a_low // 2, a_high // 2, b_all // 2, c_all // 2
    parts = run(
        (((0, 0, a_low, near), (0, a_low, a_high, near)), ((1, 0, b_all, across),),
         ((2, 0, c_all, along),)), given, extra=(gains,), more=8,
    )
    given = move(parts, (near_way, x_way, y_way))
    a_low, a_high, b_all, c_all = a_low // 2, a_high // 2, b_all // 2, c_all // 2
    parts = run(
        (((0, 0, a_low, far), (0, a_low, a_high, far), (1, 0, b_all, far), (2, 0, c_all, far)),),
        given, more=8,
    )
    given = move(parts, (far_way,))
    first_grad, middle_grad, last_grad, gain_grad = call(
        functools.partial(close_kernel, tall=tall, high=high, scale=scale),
        [shape((2 * tall, PAIR)), shape((2 * high, PAIR)), shape((2 * tall, PAIR)),
         shape((1, portion))],
        (spot, *given), scalars=1,
    )
    return (
        input_grad, first_grad.reshape(-1), middle_grad.reshape(-1), last_grad.reshape(-1),
        gain_grad.reshape(-1),
    )


def solution(mesh):
    in_specs = (P(("group", "ghost"), None), P(("group", "ghost"), None), P(), P(), P(), P())
    out_specs = (
        P(("group", "ghost"), None),
        P(("group", "ghost")),
        P(("group", "ghost")),
        P(("group", "ghost")),
        P(("group", "ghost")),
    )
    return jax.shard_map(shards, mesh=mesh, in_specs=in_specs, out_specs=out_specs, check_vma=False)
```

```python
import functools

import jax
import jax.numpy as jnp
from jax import lax
from jax.experimental import pallas as pl
from jax.experimental.pallas import tpu as pltpu
from jax.sharding import PartitionSpec as P

GROUP = 64
NEWTON = 5
SIDE = 14
LINE = 16
PAIR = 2 * GROUP
TALL = GROUP + 8
epsilon = 1e-05

F32 = jnp.float32
BF16 = jnp.bfloat16


def dot(left, right):
    return jnp.dot(left, right, preferred_element_type=F32)


def dot_t(left, right):
    return lax.dot_general(left, right, (((0,), (0,)), ((), ())), preferred_element_type=F32)


def dot_nt(left, right):
    return lax.dot_general(left, right, (((1,), (1,)), ((), ())), preferred_element_type=F32)


def halves_of(value):
    high = value.astype(BF16)
    return high, (value - high.astype(F32)).astype(BF16)


def exact(left, right):
    a, b = halves_of(left)
    c, d = halves_of(right)
    low = dot(jnp.concatenate([a, b], axis=1), jnp.concatenate([d, c], axis=0))
    return low + dot(a, c)


def exact_two(left, first, second):
    both = exact(left, jnp.concatenate([first, second], axis=1))
    return both[:, : first.shape[1]], both[:, first.shape[1] :]


def outer_of(row):
    tile = vectors(row)
    return lax.dot_general(
        tile, tile, (((0,), (0,)), ((), ())), preferred_element_type=F32,
        precision=lax.Precision.HIGHEST,
    )


def sigmoid(value):
    return 0.5 * jnp.tanh(0.5 * value) + 0.5


def two_rows(row):
    high, low = halves_of(jnp.broadcast_to(row, (16, row.shape[1])))
    at = lax.broadcasted_iota(jnp.int32, high.shape, 0)
    return jnp.where(at == 0, high.astype(F32), jnp.where(at == 1, low.astype(F32), 0.0)).astype(
        BF16
    )


def row_times(row, matrix, product=dot):
    return jnp.sum(product(two_rows(row), matrix), axis=0, keepdims=True)


def rank_one(left, right):
    tiles = []
    for row, order in ((left, (0, 1, 0)), (right, (0, 0, 1))):
        pair = halves_of(jnp.broadcast_to(row, (16, row.shape[1])))
        at = lax.broadcasted_iota(jnp.int32, pair[0].shape, 0)
        tile = jnp.zeros(pair[0].shape, F32)
        for place, which in enumerate(order):
            tile = jnp.where(at == place, pair[which].astype(F32), tile)
        tiles.append(tile.astype(BF16))
    return dot_t(*tiles)


def chunk_of(rows, most):
    best = 16
    for size in range(16, most + 1, 16):
        if rows % size == 0:
            best = size
    return best


def loop(count, body, carry):
    for at in range(count):
        carry = body(at, carry)
    return carry


def left_half(shape):
    return lax.broadcasted_iota(jnp.int32, shape, 1) < GROUP


def spread(packed):
    left = left_half(packed.shape)
    zero = jnp.zeros_like(packed)
    return jnp.concatenate([jnp.where(left, packed, zero), jnp.where(left, zero, packed)], axis=0)


def pack(square):
    top, bottom = square[:GROUP], square[GROUP:]
    return jnp.where(left_half(top.shape), top, bottom)


def vectors(*rows):
    at = lax.broadcasted_iota(jnp.int32, (8, PAIR), 0)
    tile = jnp.zeros((8, PAIR), F32)
    for place, row in enumerate(rows):
        tile = jnp.where(at == place, row, tile)
    return tile


def fold(value):
    rows, lanes = value.shape
    return jnp.sum(value.reshape(rows // 8, 8, lanes), axis=0)


def pad_lines(source, ext, rows):
    for line in range(rows // SIDE):
        place = 24 + LINE * (line + line // SIDE)
        ext[place : place + SIDE, :] = source[SIDE * line : SIDE * (line + 1), :]


def unpad_lines(source, target, rows):
    for line in range(rows // SIDE):
        place = LINE * (line + line // SIDE)
        target[SIDE * line : SIDE * (line + 1), :] = source[place : place + SIDE, :]


def padded_rows(rows):
    return rows // (SIDE * SIDE) * (SIDE + 1) * LINE


def shifted(ext, cols):
    length = cols.shape[1]
    for col in range(3):
        cols[col] = ext[7 + col : 7 + col + length, :].astype(BF16)


def emit_split(source, keep, send, core, plan):
    for start, height, first, size, mine in plan:
        lanes = keep.shape[1]
        for wide in range(source.shape[1] // lanes):
            to = slice(start + wide * height, start + (wide + 1) * height)
            cols = slice(wide * lanes, (wide + 1) * lanes)
            for target, half in ((keep, core), (send, 1 - core)):
                place = pl.multiple_of((mine + half) * size + first, 8)
                target[to, :] = source[pl.ds(place, height), cols]


def plan_of(parts, piece, wide, ghosts, start=0):
    plan = []
    for first, height, steps in parts:
        for at in range(2 ** len(steps)):
            source = 0
            for place, (axis, bit) in enumerate(steps):
                value = (at >> (len(steps) - 1 - place)) & 1
                source += value << bit if axis == "ghost" else (value << bit) * ghosts
            plan.append((start, height, first, piece, source))
            start += height * wide
    return plan


def half_of(left, right, bit, start=0, rows=None):
    rows = (left.shape[0] if rows is None else rows) // 2
    mine = pl.ds(pl.multiple_of(start + bit * rows, 8), rows)
    other = pl.ds(pl.multiple_of(start + (1 - bit) * rows, 8), rows)
    return left[mine, :] + right[mine, :], left[other, :] + right[other, :]


def pack_slot(mats, vecs):
    first, second = mats
    row = lax.broadcasted_iota(jnp.int32, first.shape, 0)
    lane = lax.broadcasted_iota(jnp.int32, first.shape, 1)
    left = lane < GROUP
    col = jnp.where(left, lane, lane - GROUP)
    upper = jnp.where(left, first, pltpu.roll(second, GROUP, 1))
    lower = jnp.where(left, pltpu.roll(first, GROUP, 1), second)
    rows = [jnp.sum(jnp.where(row == col, m, 0.0), axis=0, keepdims=True) for m in mats]
    for pair in zip(*vecs):
        rows += pair
    return jnp.concatenate([jnp.where(row <= col, upper, lower), vectors(*rows)], axis=0)


def put_stats(stats, quad, mats, vecs, packed):
    if packed:
        stats[quad] = pack_slot(mats, vecs)
        return
    for half in range(2):
        stats[2 * quad + half, :GROUP, :] = mats[half]
        stats[2 * quad + half, GROUP:, :] = vectors(*vecs[half])


def lanes_of(quad, spot, side, quads):
    if side is None:
        return slice(256 * quad, 256 * (quad + 1))
    half = jnp.bitwise_xor(spot[1], side)
    return pl.ds(pl.multiple_of(256 * (half * (quads // 2) + quad), 256), 256)


def branch_quad(h2, w3, means, lanes):
    rows = h2.shape[0]
    mean = means[0:1, lanes]
    centered = (dot(h2[...], w3[:, lanes]) - mean).astype(BF16)
    square = dot_t(centered, centered)
    mats, vecs = [], []
    for half in range(2):
        ch = slice(PAIR * half, PAIR * (half + 1))
        row = mean[:, ch]
        mats.append(pack(square[ch, ch] + outer_of(row) * rows))
        vecs.append((row * rows,))
    return centered, mats, vecs


def take_pairs(total, packed):
    result = []
    if not packed:
        for at in range(total.shape[0]):
            vecs = [total[at, GROUP + p : GROUP + p + 1, :] for p in range(2)]
            result.append((spread(total[at, :GROUP, :]), *vecs))
        return result
    shape = (PAIR, PAIR)
    row = lax.broadcasted_iota(jnp.int32, shape, 0)
    col = lax.broadcasted_iota(jnp.int32, shape, 1)
    mask = jnp.where(row < GROUP, row - col, col - row) < 0
    eye = identity()
    for slot in range(total.shape[0]):
        both = total[slot, :GROUP, :]
        turned = pltpu.roll(both, GROUP, 1)
        left = left_half(both.shape)
        for at in range(2):
            twice = jnp.where(left, *((both, turned) if at == 0 else (turned, both)))
            part = jnp.where(mask, spread(twice), 0.0)
            line = [total[slot, GROUP + 2 * p + at : GROUP + 2 * p + at + 1, :] for p in range(3)]
            result.append((part + part.T + eye * line[0], line[1], line[2]))
    return result


def add_kernel(left, right, out):
    out[...] = left[...] + right[...]


def forward_kernel(
    spot, x_far, w1_far, wm_far, w3_far, h1pad, s1, h2, s2, means, sums, cen, stats, *rest, split
):
    x, w1, wm, w3, sems, ext, cols, flat = rest
    rows = x.shape[0]
    part = chunk_of(rows, 128)

    def slab(at):
        here = slice(at * part, (at + 1) * part)
        return pltpu.make_async_copy(x_far.at[here, :], x.at[here, :], sems.at[3 + at])

    weights = [
        pltpu.make_async_copy(far, ref, sems.at[at])
        for at, (far, ref) in enumerate(((w1_far, w1), (wm_far, wm), (w3_far, w3)))
    ]
    weights[0].start()
    for at in range(rows // part):
        slab(at).start()
    weights[1].start()
    weights[2].start()
    chunk = chunk_of(rows, 128)
    ext[...] = jnp.zeros_like(ext)

    weights[0].wait()

    slabs = rows // part
    for start, stop in ((0, (slabs + 1) // 2), ((slabs + 1) // 2, slabs)):
        for at in range(start, stop):
            slab(at).wait()
        here = slice(start * part, stop * part)
        flat[here, :] = dot(x[here, :], w1[...])

        def first(at, carry, start=start):
            here = slice((start + at) * part, (start + at + 1) * part)
            act = flat[here, :]
            sig = sigmoid(act)
            flat[here, :] = act * sig
            s1[here, :] = sig * (1.0 + act * (1.0 - sig))
            return carry

        loop(stop - start, first, 0)
    pad_lines(flat, ext, rows)
    shifted(ext, cols)
    padded = padded_rows(rows)
    h1pad[...] = cols[1, LINE : LINE + padded, :]
    big = chunk_of(padded, 512)
    weights[1].wait()

    def middle(at, carry):
        base = at * big
        total = jnp.zeros((big, wm.shape[1]), F32)
        for row in range(3):
            for col in range(3):
                left = cols[col, pl.ds(base + LINE * row, big), :]
                k = 3 * row + col
                depth = left.shape[1]
                total = total + dot(left, wm[k * depth : (k + 1) * depth, :])
        ext[pl.ds(base, big), :] = total
        return carry

    loop(padded // big, middle, 0)
    unpad_lines(ext, flat, rows)
    width = w3.shape[1]
    weights[2].wait()

    def second(at, hidden_sum):
        here = slice(at * chunk, (at + 1) * chunk)
        act = flat[here, :]
        sig = sigmoid(act)
        hidden = (act * sig).astype(BF16)
        h2[here, :] = hidden
        s2[here, :] = sig * (1.0 + act * (1.0 - sig))
        return hidden_sum + fold(hidden.astype(F32))

    zeros = jnp.zeros((8, w3.shape[0]), F32)
    hidden_sum = loop(rows // chunk, second, zeros)
    hidden_sum = jnp.sum(hidden_sum, axis=0, keepdims=True)
    sums[...] = jnp.broadcast_to(hidden_sum, sums.shape)
    total = row_times(hidden_sum, w3[...])
    mean = total / rows
    means[...] = jnp.broadcast_to(mean, means.shape)
    quads = width // 256
    for quad in range(quads // 2 if split else quads):
        lanes = lanes_of(quad, spot, 1 if split else None, quads)
        centered, mats, vecs = branch_quad(h2, w3, means, lanes)
        cen[:, 256 * quad : 256 * (quad + 1)] = centered
        put_stats(stats, quad, mats, vecs, split)


def own_branch_kernel(spot, h2, w3, means, cen_other, cen, stats):
    quads = w3.shape[1] // 256
    for quad in range(quads // 2):
        lanes = lanes_of(quad, spot, 0, quads)
        centered, mats, vecs = branch_quad(h2, w3, means, lanes)
        cen[:, lanes] = centered
        put_stats(stats, quad, mats, vecs, True)
        lanes = lanes_of(quad, spot, 1, quads)
        cen[:, lanes] = cen_other[:, 256 * quad : 256 * (quad + 1)]


def identity():
    shape = (PAIR, PAIR)
    return jnp.where(
        lax.broadcasted_iota(jnp.int32, shape, 0) == lax.broadcasted_iota(jnp.int32, shape, 1),
        1.0, 0.0,
    ).astype(F32)


def per_block(square):
    row_sums = jnp.sum(square, axis=1, keepdims=True)
    top = jnp.sum(row_sums[:GROUP], axis=0, keepdims=True)
    bottom = jnp.sum(row_sums[GROUP:], axis=0, keepdims=True)
    upper = lax.broadcasted_iota(jnp.int32, (PAIR, 1), 0) < GROUP
    return jnp.where(upper, top, bottom)


def total_of(terms):
    total = terms[0][...]
    for term in terms[1:]:
        total = total + term[...]
    return total


def whiten_kernel(*refs, span, packed):
    terms, (out, keep) = refs[:-2], refs[-2:]
    given = take_pairs(total_of(terms), packed)
    eye = identity()
    blocks = spread(jnp.ones((GROUP, PAIR), F32))
    means = [sums / span for _, sums, _ in given]
    covs = [
        moments / span - outer_of(mean) * blocks + epsilon * eye
        for (moments, _, _), mean in zip(given, means)
    ]
    traces = [per_block(cov * eye) for cov in covs]
    normed = [cov / trace for cov, trace in zip(covs, traces)]
    powers = [1.5 * eye - 0.5 * norm for norm in normed]
    for at, trace in enumerate(traces):
        keep[at, 0] = normed[at]
        keep[at, 1] = eye / trace
    for sweep in range(NEWTON - 1):
        both = [exact_two(power, power, norm) for power, norm in zip(powers, normed)]
        squares, sides = zip(*both)
        for at, power in enumerate(powers):
            keep[at, 2 + 2 * sweep] = power
            keep[at, 3 + 2 * sweep] = squares[at]
        powers = [
            1.5 * power - 0.5 * exact(square, side)
            for power, square, side in zip(powers, squares, sides)
        ]
    for at, power in enumerate(powers):
        keep[at, 2 * NEWTON] = power
        out[at, :GROUP, :] = pack(power / jnp.sqrt(traces[at]))
        out[at, GROUP:, :] = vectors(means[at])


def pull_kernel(*refs, span, packed):
    terms, (keep, out) = refs[:-2], refs[-2:]
    given = take_pairs(total_of(terms), packed)
    eye = identity()
    every = range(len(given))
    normed = [keep[at, 0] for at in every]
    inverse = [per_block(keep[at, 1]) / GROUP for at in every]
    roots = [jnp.sqrt(value) for value in inverse]
    powers = [keep[at, 2 * NEWTON] for at in every]
    grads = [given[at][0] * roots[at] for at in every]
    trace_grads = [
        -0.5 * inverse[at] * roots[at] * per_block(given[at][0] * powers[at]) for at in every
    ]
    normed_grads = [jnp.zeros_like(grads[0])] * len(given)
    for sweep in reversed(range(NEWTON - 1)):
        power = [keep[at, 2 + 2 * sweep] for at in every]
        square = [keep[at, 3 + 2 * sweep] for at in every]
        turned, side = zip(*(exact_two(grads[at], normed[at], power[at]) for at in every))
        turned = [turned[at] + turned[at].T for at in every]
        turned, outer = zip(*(exact_two(turned[at], power[at], square[at]) for at in every))
        side = [exact(side[at], square[at]) for at in every]
        normed_grads = [normed_grads[at] - 0.25 * (side[at] + side[at].T) for at in every]
        inner = [exact(power[at], turned[at]) for at in every]
        grads = [
            1.5 * grads[at] - 0.25 * (outer[at] + outer[at].T + inner[at]) for at in every
        ]
    for at in every:
        normed_grad = normed_grads[at] - 0.5 * grads[at]
        trace_grad = trace_grads[at] - inverse[at] * per_block(normed_grad * normed[at])
        both = normed_grad * inverse[at] + eye * trace_grad
        bias = -exact(vectors(given[at][1] / span), (powers[at] * roots[at]).T)
        out[at, :GROUP, :] = pack(both / span)
        out[at, GROUP:, :] = vectors(bias[0:1, :], given[at][2])


def place_pairs(spot, given, pairs, split):
    if split:
        for side, shares in enumerate(given):
            for at in range(shares.shape[0]):
                half = jnp.bitwise_xor(side, spot[1])
                pairs[half * shares.shape[0] + at] = shares[at]
    else:
        pairs[...] = given[0][...]


def quad_matrix(pairs, quad):
    zero = jnp.zeros((PAIR, PAIR), F32)
    first = spread(pairs[2 * quad, :GROUP, :])
    second = spread(pairs[2 * quad + 1, :GROUP, :])
    top = jnp.concatenate([first, zero], axis=1)
    bottom = jnp.concatenate([zero, second], axis=1)
    return jnp.concatenate([top, bottom], axis=0).astype(BF16)


def row_of(pairs, quad, place):
    at = GROUP + place
    return jnp.concatenate(
        [pairs[2 * quad, at : at + 1, :], pairs[2 * quad + 1, at : at + 1, :]], axis=1
    )


def backward_kernel(spot, x, og, cen, means, gain, shares, *rest, side):
    rows, width = x.shape
    quads = width // 256
    if side == 1:
        own_shares, dwb_own, dpre_own, dwb, dpre_out, w_out, stats, whites = rest
        place_pairs(spot, (own_shares, shares), w_out, True)
    else:
        dwb, dpre_out, stats, whites = rest
    count = quads if side is None else quads // 2
    chunk = chunk_of(rows, 128)
    aways, shifts = [], []

    def multiply(quad):
        lanes = lanes_of(quad, spot, side, quads)
        whiten = quad_matrix(shares, quad)
        aways.append(means[0:1, lanes] - row_of(shares, quad, 0))
        shifts.append(row_times(aways[-1], whiten))
        whites[quad % 2] = dot(cen[:, lanes], whiten)

    multiply(0)
    for quad in range(count):
        if quad + 1 < count:
            multiply(quad + 1)
        lanes = lanes_of(quad, spot, side, quads)
        to = lanes if side == 1 else slice(256 * quad, 256 * (quad + 1))
        away, shift = aways[quad], shifts[quad]
        scale = gain[:, lanes]

        def step(at, carry, quad=quad, lanes=lanes, to=to, shift=shift, scale=scale):
            col_sum, gain_sum = carry
            here = slice(at * chunk, (at + 1) * chunk)
            white = whites[quad % 2, here, :] + shift
            pre = x[here, lanes].astype(F32) + scale * white
            sig = sigmoid(pre)
            dpre = og[here, lanes].astype(F32) * (sig * (1.0 + pre * (1.0 - sig)))
            dpre_out[here, to] = dpre
            dwhite = scale * dpre
            dwb[here, to] = dwhite.astype(BF16)
            return col_sum + fold(dwhite), gain_sum + fold(dpre * white)

        zero = jnp.zeros((8, 256), F32)
        col_sum, gain_sum = loop(rows // chunk, step, (zero, zero))
        col_sum = jnp.sum(col_sum, axis=0, keepdims=True)
        gain_sum = jnp.sum(gain_sum, axis=0, keepdims=True)
        square = dot_t(cen[:, lanes], dwb[:, to]) + rank_one(away, col_sum)
        mats, vecs = [], []
        for half in range(2):
            ch = slice(PAIR * half, PAIR * (half + 1))
            inner = square[ch, ch]
            mats.append(pack(inner + inner.T))
            vecs.append((col_sum[:, ch], gain_sum[:, ch]))
        put_stats(stats, quad, mats, vecs, side is not None)
        if side == 1:
            own = lanes_of(quad, spot, 0, quads)
            at = slice(256 * quad, 256 * (quad + 1))
            dwb[:, own] = dwb_own[:, at]
            dpre_out[:, own] = dpre_own[:, at]


def own_kernel(h2, cen, out):
    for quad in range(cen.shape[1] // 256):
        lanes = slice(256 * quad, 256 * (quad + 1))
        out[:, lanes] = dot_t(h2[...], cen[:, lanes]).astype(BF16)


def turn_kernel(dwb, wpairs, w3, turned, flow):
    for quad in range(dwb.shape[1] // 256):
        lanes = slice(256 * quad, 256 * (quad + 1))
        whiten = quad_matrix(wpairs, quad).T

        turned[:, lanes] = dot(dwb[:, lanes], whiten).astype(BF16)
    flow[...] = dot_nt(turned[...], w3[...])


def turned_kernel(h2, turned, out):
    for quad in range(turned.shape[1] // 256):
        lanes = slice(256 * quad, 256 * (quad + 1))
        out[:, lanes] = dot_t(h2[...], turned[:, lanes])


def last_kernel(spot, flow, cen, means, s2, w3, wpairs, *rest, split, shares):
    given, (cols, gains, spairs, bias_out, ext, flat, joint) = rest[:shares], rest[shares:]
    rows, width = cen.shape
    place_pairs(spot, given, spairs, split)
    gains[...] = spairs[:, GROUP + 1, :]
    chunk = chunk_of(rows, 128)
    ext[...] = jnp.zeros_like(ext)
    low = jnp.zeros((1, w3.shape[0]), F32)
    for quad in range(width // 256):
        lanes = slice(256 * quad, 256 * (quad + 1))
        sym = quad_matrix(spairs, quad)
        away = means[0:1, lanes] - row_of(wpairs, quad, 0)
        bias = row_of(spairs, quad, 0) + row_times(away, sym)
        bias_out[:, lanes] = jnp.broadcast_to(bias, (8, 256))
        low = low + row_times(bias, w3[:, lanes], dot_nt)
        joint[lanes, :] = dot_nt(sym, w3[:, lanes]).astype(BF16)

    flat[...] = dot(cen[...], joint[...])

    def middle(at, carry):
        here = slice(at * chunk, (at + 1) * chunk)
        flat[here, :] = (flow[here, :] + flat[here, :] + low) * s2[here, :]
        return carry

    loop(rows // chunk, middle, 0)
    pad_lines(flat, ext, rows)
    shifted(ext, cols)


def finish(part, outs, spot, plan):
    if plan:
        emit_split(part, outs[0], outs[1], spot[1], plan)
    else:
        outs[0][...] = part[...]


def slope_kernel(spot, cols, wm, s1, x, dmid1, *rest, plan):
    outs, (ext, flat, part) = rest[:-3], rest[-3:]
    rows, depth = s1.shape
    padded = padded_rows(rows)
    big = chunk_of(padded, 512)

    def step(at, carry):
        base = at * big
        total = jnp.zeros((big, depth), F32)
        for row in range(3):
            for col in range(3):
                near = cols[2 - col, pl.ds(base + LINE * (2 - row), big), :]
                k = 3 * row + col
                total = total + dot_nt(near, wm[k * depth : (k + 1) * depth, :])
        ext[pl.ds(base, big), :] = total
        return carry

    loop(padded // big, step, 0)
    unpad_lines(ext, flat, rows)
    dmid1[...] = (flat[...] * s1[...]).astype(BF16)
    for quad in range(x.shape[1] // 256):
        lanes = slice(256 * quad, 256 * (quad + 1))
        part[lanes, :] = dot_t(x[:, lanes], dmid1[...])
    finish(part, outs, spot, plan)


def middle_kernel(spot, cols, h1pad, turned, own, sums, spairs, bias, *rest, plans):
    outs, (part, part_last) = rest[:-2], rest[-2:]
    padded, depth = h1pad.shape
    for row in range(3):
        for col in range(3):
            k = 3 * row + col
            near = cols[2 - col, LINE * (2 - row) : LINE * (2 - row) + padded, :]
            part[k * depth : (k + 1) * depth, :] = dot_t(h1pad[...], near)
    for quad in range(turned.shape[1] // 256):
        lanes = slice(256 * quad, 256 * (quad + 1))
        sym = quad_matrix(spairs, quad)
        part_last[:, lanes] = (
            turned[:, lanes]
            + dot(own[:, lanes], sym)
            + rank_one(sums[0:1, :], bias[0:1, lanes])
        )
    if plans:
        emit_split(part, outs[0], outs[1], spot[1], plans[0])
        emit_split(part_last, outs[0], outs[1], spot[1], plans[1])
    else:
        outs[0][...] = part[...]
        outs[1][...] = part_last[...]


def spans_step(spot, *refs, steps, extra=0):
    count = 2 * (1 + max(span[0] for spans in steps for span in spans))
    given, outs = refs[: count + extra], refs[count + extra :]
    for at, spans in enumerate(steps):
        to = 0
        for source, start, size, bit in spans:
            mine, other = half_of(given[2 * source], given[2 * source + 1], spot[bit], start, size)
            outs[2 * at][to : to + size // 2, :] = mine
            outs[2 * at + 1][to : to + size // 2, :] = other
            to += size // 2
        left = outs[2 * at].shape[0] - to
        if not left:
            continue
        if extra:
            rows = jnp.concatenate([given[-1][...]] * (outs[0].shape[1] // PAIR), axis=1)
        else:
            tail = given[0].shape[0] - left
            rows = given[0][tail:, :] + given[1][tail:, :]
        for out in outs[2 * at : 2 * at + 2]:
            out[to:, :] = rows


def close_kernel(spot, keep, given, first, middle, last, gain, *, tall, high, scale):
    total = (keep[...] + given[...]) * scale
    for half in range(2):
        lanes = slice(PAIR * half, PAIR * (half + 1))
        step = tall // 4
        for wide in range(4):
            last[pl.ds(2 * wide + half, step, 8), :] = total[step * wide : step * (wide + 1), lanes]
        middle[pl.ds(half, high, 2), :] = total[tall : tall + high, lanes]
        first[pl.ds(half, tall, 2), :] = total[tall + high : 2 * tall + high, lanes]
    size = gain.shape[1]
    each = PAIR // size
    rows = total[2 * tall + high :, :PAIR]
    device = spot[6]
    at = lax.broadcasted_iota(jnp.int32, rows.shape, 0)
    row = jnp.sum(jnp.where(at == device // each, rows, 0.0), axis=0, keepdims=True)
    mine = jnp.zeros((1, size), F32)
    for place in range(each):
        mine = jnp.where(device % each == place, row[:, place * size : (place + 1) * size], mine)
    gain[...] = mine


def input_kernel(dmid1, w1, dpre, out, token):
    token[...] = jnp.zeros_like(token)
    rows = dpre.shape[0]
    chunk = chunk_of(rows, 128)

    def step(at, carry):
        here = slice(at * chunk, (at + 1) * chunk)
        out[here, :] = (dot_nt(dmid1[here, :], w1[...]) + dpre[here, :]).astype(BF16)
        return carry

    loop(rows // chunk, step, 0)


def call(kernel, outs, args, scratch=(), scalars=0, flops=0, ties=(), far=0, room=40):
    args = tuple(args) + tuple(ties)
    specs = [pl.BlockSpec(memory_space=pltpu.SMEM)] * scalars
    specs += [pl.BlockSpec(memory_space=pl.ANY)] * far
    specs += [pl.BlockSpec(memory_space=pltpu.VMEM)] * (len(args) - scalars - len(ties) - far)
    specs += [pl.BlockSpec(memory_space=pl.ANY)] * len(ties)
    count = len(args) - len(ties)

    def body(*refs):
        kernel(*refs[:count], *refs[len(args) :])

    size = sum(a.size * a.dtype.itemsize for a in args)
    size += sum(o.size * o.dtype.itemsize for o in outs)
    return pl.pallas_call(
        body,
        out_shape=tuple(outs),
        in_specs=specs,
        out_specs=tuple(pl.BlockSpec(memory_space=pltpu.VMEM) for _ in outs),
        scratch_shapes=list(scratch),
        cost_estimate=pl.CostEstimate(flops=flops, bytes_accessed=size, transcendentals=0),
        compiler_params=pltpu.CompilerParams(vmem_limit_bytes=room * 2**20),
    )(*args)


def shape(dims, dtype=F32):
    return jax.ShapeDtypeStruct(dims, dtype)


def swap(value, axis, size, flip):
    return lax.ppermute(value, axis, [(at, at ^ flip) for at in range(size)])


def shards(inputs, out_grad, conv_first, conv_middle, conv_last, gain):
    rows, width = inputs.shape
    mid = conv_first.shape[1]
    pairs = width // PAIR
    ghosts = lax.axis_size("ghost")
    groups = lax.axis_size("group")
    devices = ghosts * groups
    span = float(rows * ghosts)
    scale = (rows * devices) ** (-0.5)
    padded = padded_rows(rows)
    ghost = lax.axis_index("ghost")
    group = lax.axis_index("group")
    bits = [ghost] + [(ghost >> bit) & 1 for bit in range(3)]
    bits += [(group >> bit) & 1 for bit in range(2)] + [group * ghosts + ghost]
    spot = jnp.stack(bits).astype(jnp.int32)
    core, across, along, near, far = 1, 2, 3, 4, 5
    split = ghosts == 8 and pairs == 8 and groups == 4
    unit = 2 * rows * width * mid

    ext = pltpu.VMEM((24 + padded + LINE + 8, mid), F32)
    flat = pltpu.VMEM((rows, mid), F32)
    cols = (3, padded + 2 * LINE, mid)
    big = (pairs, TALL, PAIR)
    half = (pairs // 2, TALL, PAIR)
    packed = (pairs // 4, TALL, PAIR)
    side_stats = shape(packed if split else big)
    side_width = width // 2 if split else width

    def collect(stats, ties):
        if not split:
            return [lax.psum(stats[0], "ghost")]
        send, total = stats
        given = swap(send, "ghost", ghosts, 1)
        (total,) = call(add_kernel, [shape(packed)], (total, given))
        given = swap(total, "ghost", ghosts, 2)
        (total,) = call(add_kernel, [shape(packed)], (total, given), ties=ties)
        return [total, swap(total, "ghost", ghosts, 4)]

    own = half if split else big
    held = own[0]
    chunks = rows // chunk_of(rows, 128)
    h1pad, s1, h2, s2, means, sums, cen, stats = call(
        functools.partial(forward_kernel, split=split),
        [shape((padded, mid), BF16), shape((rows, mid)), shape((rows, mid), BF16),
         shape((rows, mid)), shape((8, width)), shape((8, mid)), shape((rows, side_width), BF16),
         side_stats],
        (spot, *(
            pltpu.with_memory_space_constraint(value, pltpu.HBM)
            for value in (inputs, conv_first, conv_middle, conv_last)
        )),
        (pltpu.VMEM((rows, width), BF16), pltpu.VMEM(conv_first.shape, BF16),
         pltpu.VMEM(conv_middle.shape, BF16), pltpu.VMEM(conv_last.shape, BF16),
         pltpu.SemaphoreType.DMA((3 + chunks,)),
         ext, pltpu.VMEM(cols, BF16), flat),
        scalars=1, flops=5 * unit, far=4,
    )
    stats = [stats]
    if split:
        cen, keep = call(
            own_branch_kernel, [shape((rows, width), BF16), side_stats],
            (spot, h2, conv_last, means, cen), scalars=1, flops=unit,
        )
        stats.append(keep)
    (own_part,) = call(own_kernel, [shape((mid, width), BF16)], (h2, cen), flops=unit)
    share, kept = call(
        functools.partial(whiten_kernel, span=span, packed=split),
        [shape(own), shape((held, 2 * NEWTON + 1, PAIR, PAIR))], collect(stats, (own_part,)), flops=10**7,
    )
    places = (spot, inputs, out_grad, cen, means, gain.reshape(1, width))
    whites = (pltpu.VMEM((2, rows, 256), F32),)
    dwb, dpre, keep = call(
        functools.partial(backward_kernel, side=0 if split else None),
        [shape((rows, side_width), BF16), shape((rows, side_width)), side_stats],
        (*places, share), whites, scalars=1, flops=2 * unit,
    )
    stats, wpairs = [keep], share
    if split:
        other = swap(share, "ghost", ghosts, 1)
        dwb, dpre, wpairs, send = call(
            functools.partial(backward_kernel, side=1),
            [shape((rows, width), BF16), shape((rows, width)), shape(big), side_stats],
            (*places, other, share, dwb, dpre), whites, scalars=1, flops=2 * unit,
        )
        stats.insert(0, send)
    turned, flow = call(
        turn_kernel, [shape((rows, width), BF16), shape((rows, mid))], (dwb, wpairs, conv_last),
        flops=2 * unit,
    )
    (turned_part,) = call(turned_kernel, [shape((mid, width))], (h2, turned), flops=unit)
    (pulled,) = call(
        functools.partial(pull_kernel, span=span, packed=split), [shape(own)], (*collect(stats, (flow,)), kept),
        flops=10**7, ties=(turned_part,),
    )
    given = [pulled, swap(pulled, "ghost", ghosts, 1)] if split else [pulled]

    dcols, gains, spairs, bias = call(
        functools.partial(last_kernel, split=split, shares=len(given)),
        [shape(cols, BF16), shape((pairs, PAIR)), shape(big), shape((8, width))],
        (spot, flow, cen, means, s2, conv_last, wpairs, *given),
        (ext, flat, pltpu.VMEM((width, mid), BF16)), scalars=1, flops=2 * unit,
    )
    half_rows = mid * width // 512
    orders = (
        (("ghost", 1), ("ghost", 2), ("group", 0), ("group", 1)),
        (("ghost", 2), ("group", 0), ("ghost", 1), ("group", 1)),
        (("group", 0), ("ghost", 1), ("ghost", 2), ("group", 1)),
    )
    high, tall = 9 * mid // devices, width // devices
    cut = high // 24 * 8
    middle_plan = last_plan = first_plan = None
    if split:
        middle_plan = plan_of(
            [(0, cut, orders[0]), (cut, high - cut, orders[1])], high, 1, ghosts
        )
        last_plan = plan_of(
            [(0, mid // devices, orders[0])], mid // devices, width // 256, ghosts, 9 * mid // 2
        )
        first_plan = plan_of([(0, tall, orders[2])], tall, 1, ghosts)
    middle_part = call(
        functools.partial(middle_kernel, plans=(middle_plan, last_plan) if split else None),
        [shape((9 * mid // 2 + half_rows, mid))] * 2 if split
        else [shape((9 * mid, mid)), shape((mid, width))],
        (spot, dcols, h1pad, turned_part, own_part, sums, spairs, bias),
        (pltpu.VMEM((9 * mid, mid), F32), pltpu.VMEM((mid, width), F32)),
        scalars=1, flops=3 * unit,
    )
    dmid1, *first_part = call(
        functools.partial(slope_kernel, plan=first_plan),
        [shape((rows, mid), BF16)]
        + ([shape((half_rows, mid))] * 2 if split else [shape((width, mid))]),
        (spot, dcols, conv_middle, s1, inputs),
        (ext, flat, pltpu.VMEM((width, mid), F32)), scalars=1, flops=4 * unit,
    )
    portion = width // devices
    if not split:
        input_grad, _ = call(
            input_kernel, [shape((rows, width), BF16), shape((8, PAIR))],
            (dmid1, conv_first, dpre), flops=unit,
        )
        grads = [
            lax.psum_scatter(
                (part[0] * scale).reshape(-1), ("group", "ghost"), scatter_dimension=0, tiled=True
            )
            for part in (first_part, middle_part, middle_part[1:])
        ]
        gain_grad = lax.dynamic_slice_in_dim(
            lax.psum(gains.reshape(-1) * scale, "group"), (group * ghosts + ghost) * portion, portion
        )
        return (input_grad, *grads, gain_grad)

    def move(parts, ways):
        result = []
        for at, (axis, flip) in enumerate(ways):
            result.append(parts[2 * at])
            result.append(swap(parts[2 * at + 1], axis, groups if axis == "group" else ghosts, flip))
        return result

    def run(steps, given, extra=(), more=0, ties=()):
        outs = []
        for at, spans in enumerate(steps):
            height = sum(span[2] for span in spans) // 2 + (more if at == 0 else 0)
            outs += [shape((height, mid))] * 2
        return call(
            functools.partial(spans_step, steps=steps, extra=len(extra)), outs,
            (spot, *given, *extra), scalars=1, ties=ties,
        )

    core_way, x_way, y_way = (("ghost", 1 << bit) for bit in range(3))
    near_way, far_way = ("group", 1), ("group", 2)
    given = move(middle_part, (core_way,))
    first_given = move(first_part, (core_way,))
    pieces = devices // 2
    a_low, a_high, b_all = half_rows, pieces * cut, pieces * (high - cut)
    parts = run(
        (((0, a_high + b_all, a_low, across), (0, 0, a_high, across)),
         ((0, a_high, b_all, along),)), given,
    )
    given = move(parts, (x_way, y_way))
    parts = run((((0, 0, half_rows, near),),), first_given, ties=(parts[0],))
    given += move(parts, (near_way,))
    input_grad, token = call(
        input_kernel, [shape((rows, width), BF16), shape((8, PAIR))], (dmid1, conv_first, dpre),
        flops=unit, ties=(parts[0],),
    )
    a_low, a_high, b_all, c_all = a_low // 2, a_high // 2, b_all // 2, half_rows // 2
    parts = run(
        (((0, 0, a_low, along), (0, a_low, a_high, along)), ((1, 0, b_all, near),),
         ((2, 0, c_all, across),)), given, ties=(token,),
    )
    given = move(parts, (y_way, near_way, x_way))
    a_low, a_high, b_all, c_all = a_low // 2, a_high // 2, b_all // 2, c_all // 2
    parts = run(
        (((0, 0, a_low, near), (0, a_low, a_high, near)), ((1, 0, b_all, across),),
         ((2, 0, c_all, along),)), given, extra=(gains,), more=8,
    )
    given = move(parts, (near_way, x_way, y_way))
    a_low, a_high, b_all, c_all = a_low // 2, a_high // 2, b_all // 2, c_all // 2
    parts = run(
        (((0, 0, a_low, far), (0, a_low, a_high, far), (1, 0, b_all, far), (2, 0, c_all, far)),),
        given, more=8,
    )
    given = move(parts, (far_way,))
    first_grad, middle_grad, last_grad, gain_grad = call(
        functools.partial(close_kernel, tall=tall, high=high, scale=scale),
        [shape((2 * tall, PAIR)), shape((2 * high, PAIR)), shape((2 * tall, PAIR)),
         shape((1, portion))],
        (spot, *given), scalars=1,
    )
    return (
        input_grad, first_grad.reshape(-1), middle_grad.reshape(-1), last_grad.reshape(-1),
        gain_grad.reshape(-1),
    )


def solution(mesh):
    in_specs = (P(("group", "ghost"), None), P(("group", "ghost"), None), P(), P(), P(), P())
    out_specs = (
        P(("group", "ghost"), None),
        P(("group", "ghost")),
        P(("group", "ghost")),
        P(("group", "ghost")),
        P(("group", "ghost")),
    )
    return jax.shard_map(shards, mesh=mesh, in_specs=in_specs, out_specs=out_specs, check_vma=False)
```

```python
import functools

import jax
import jax.numpy as jnp
from jax import lax
from jax.experimental import pallas as pl
from jax.experimental.pallas import tpu as pltpu
from jax.sharding import PartitionSpec as P

GROUP = 64
NEWTON = 5
SIDE = 14
LINE = 16
PAIR = 2 * GROUP
TALL = GROUP + 8
epsilon = 1e-05

F32 = jnp.float32
BF16 = jnp.bfloat16


def dot(left, right):
    return jnp.dot(left, right, preferred_element_type=F32)


def dot_t(left, right):
    return lax.dot_general(left, right, (((0,), (0,)), ((), ())), preferred_element_type=F32)


def dot_nt(left, right):
    return lax.dot_general(left, right, (((1,), (1,)), ((), ())), preferred_element_type=F32)


def halves_of(value):
    high = value.astype(BF16)
    return high, (value - high.astype(F32)).astype(BF16)


def exact(left, right):
    a, b = halves_of(left)
    c, d = halves_of(right)
    low = dot(jnp.concatenate([a, b], axis=1), jnp.concatenate([d, c], axis=0))
    return low + dot(a, c)


def exact_two(left, first, second):
    both = exact(left, jnp.concatenate([first, second], axis=1))
    return both[:, : first.shape[1]], both[:, first.shape[1] :]


def outer_of(row):
    tile = vectors(row)
    return lax.dot_general(
        tile, tile, (((0,), (0,)), ((), ())), preferred_element_type=F32,
        precision=lax.Precision.HIGHEST,
    )


def sigmoid(value):
    return 0.5 * jnp.tanh(0.5 * value) + 0.5


def two_rows(row):
    high, low = halves_of(jnp.broadcast_to(row, (16, row.shape[1])))
    at = lax.broadcasted_iota(jnp.int32, high.shape, 0)
    return jnp.where(at == 0, high.astype(F32), jnp.where(at == 1, low.astype(F32), 0.0)).astype(
        BF16
    )


def row_times(row, matrix, product=dot):
    return jnp.sum(product(two_rows(row), matrix), axis=0, keepdims=True)


def rank_one(left, right):
    tiles = []
    for row, order in ((left, (0, 1, 0)), (right, (0, 0, 1))):
        pair = halves_of(jnp.broadcast_to(row, (16, row.shape[1])))
        at = lax.broadcasted_iota(jnp.int32, pair[0].shape, 0)
        tile = jnp.zeros(pair[0].shape, F32)
        for place, which in enumerate(order):
            tile = jnp.where(at == place, pair[which].astype(F32), tile)
        tiles.append(tile.astype(BF16))
    return dot_t(*tiles)


def chunk_of(rows, most):
    best = 16
    for size in range(16, most + 1, 16):
        if rows % size == 0:
            best = size
    return best


def loop(count, body, carry):
    for at in range(count):
        carry = body(at, carry)
    return carry


def left_half(shape):
    return lax.broadcasted_iota(jnp.int32, shape, 1) < GROUP


def spread(packed):
    left = left_half(packed.shape)
    zero = jnp.zeros_like(packed)
    return jnp.concatenate([jnp.where(left, packed, zero), jnp.where(left, zero, packed)], axis=0)


def pack(square):
    top, bottom = square[:GROUP], square[GROUP:]
    return jnp.where(left_half(top.shape), top, bottom)


def vectors(*rows):
    at = lax.broadcasted_iota(jnp.int32, (8, PAIR), 0)
    tile = jnp.zeros((8, PAIR), F32)
    for place, row in enumerate(rows):
        tile = jnp.where(at == place, row, tile)
    return tile


def fold(value):
    rows, lanes = value.shape
    return jnp.sum(value.reshape(rows // 8, 8, lanes), axis=0)


def pad_lines(source, ext, rows):
    for line in range(rows // SIDE):
        place = 24 + LINE * (line + line // SIDE)
        ext[place : place + SIDE, :] = source[SIDE * line : SIDE * (line + 1), :]


def unpad_lines(source, target, rows):
    for line in range(rows // SIDE):
        place = LINE * (line + line // SIDE)
        target[SIDE * line : SIDE * (line + 1), :] = source[place : place + SIDE, :]


def padded_rows(rows):
    return rows // (SIDE * SIDE) * (SIDE + 1) * LINE


def shifted(ext, cols):
    length = cols.shape[1]
    for col in range(3):
        cols[col] = ext[7 + col : 7 + col + length, :].astype(BF16)


def emit_split(source, keep, send, core, plan):
    for start, height, first, size, mine in plan:
        lanes = keep.shape[1]
        for wide in range(source.shape[1] // lanes):
            to = slice(start + wide * height, start + (wide + 1) * height)
            cols = slice(wide * lanes, (wide + 1) * lanes)
            for target, half in ((keep, core), (send, 1 - core)):
                place = pl.multiple_of((mine + half) * size + first, 8)
                target[to, :] = source[pl.ds(place, height), cols]


def plan_of(parts, piece, wide, ghosts, start=0):
    plan = []
    for first, height, steps in parts:
        for at in range(2 ** len(steps)):
            source = 0
            for place, (axis, bit) in enumerate(steps):
                value = (at >> (len(steps) - 1 - place)) & 1
                source += value << bit if axis == "ghost" else (value << bit) * ghosts
            plan.append((start, height, first, piece, source))
            start += height * wide
    return plan


def half_of(left, right, bit, start=0, rows=None):
    rows = (left.shape[0] if rows is None else rows) // 2
    mine = pl.ds(pl.multiple_of(start + bit * rows, 8), rows)
    other = pl.ds(pl.multiple_of(start + (1 - bit) * rows, 8), rows)
    return left[mine, :] + right[mine, :], left[other, :] + right[other, :]


def pack_slot(mats, vecs):
    first, second = mats
    row = lax.broadcasted_iota(jnp.int32, first.shape, 0)
    lane = lax.broadcasted_iota(jnp.int32, first.shape, 1)
    left = lane < GROUP
    col = jnp.where(left, lane, lane - GROUP)
    upper = jnp.where(left, first, pltpu.roll(second, GROUP, 1))
    lower = jnp.where(left, pltpu.roll(first, GROUP, 1), second)
    rows = [jnp.sum(jnp.where(row == col, m, 0.0), axis=0, keepdims=True) for m in mats]
    for pair in zip(*vecs):
        rows += pair
    return jnp.concatenate([jnp.where(row <= col, upper, lower), vectors(*rows)], axis=0)


def put_stats(stats, quad, mats, vecs, packed):
    if packed:
        stats[quad] = pack_slot(mats, vecs)
        return
    for half in range(2):
        stats[2 * quad + half, :GROUP, :] = mats[half]
        stats[2 * quad + half, GROUP:, :] = vectors(*vecs[half])


def lanes_of(quad, spot, side, quads):
    if side is None:
        return slice(256 * quad, 256 * (quad + 1))
    half = jnp.bitwise_xor(spot[1], side)
    return pl.ds(pl.multiple_of(256 * (half * (quads // 2) + quad), 256), 256)


def branch_quad(h2, w3, means, lanes):
    rows = h2.shape[0]
    mean = means[0:1, lanes]
    centered = (dot(h2[...], w3[:, lanes]) - mean).astype(BF16)
    square = dot_t(centered, centered)
    mats, vecs = [], []
    for half in range(2):
        ch = slice(PAIR * half, PAIR * (half + 1))
        row = mean[:, ch]
        mats.append(pack(square[ch, ch] + outer_of(row) * rows))
        vecs.append((row * rows,))
    return centered, mats, vecs


def take_pairs(total, packed):
    result = []
    if not packed:
        for at in range(total.shape[0]):
            vecs = [total[at, GROUP + p : GROUP + p + 1, :] for p in range(2)]
            result.append((spread(total[at, :GROUP, :]), *vecs))
        return result
    shape = (PAIR, PAIR)
    row = lax.broadcasted_iota(jnp.int32, shape, 0)
    col = lax.broadcasted_iota(jnp.int32, shape, 1)
    mask = jnp.where(row < GROUP, row - col, col - row) < 0
    eye = identity()
    for slot in range(total.shape[0]):
        both = total[slot, :GROUP, :]
        turned = pltpu.roll(both, GROUP, 1)
        left = left_half(both.shape)
        for at in range(2):
            twice = jnp.where(left, *((both, turned) if at == 0 else (turned, both)))
            part = jnp.where(mask, spread(twice), 0.0)
            line = [total[slot, GROUP + 2 * p + at : GROUP + 2 * p + at + 1, :] for p in range(3)]
            result.append((part + part.T + eye * line[0], line[1], line[2]))
    return result


def add_kernel(left, right, out):
    out[...] = left[...] + right[...]


def forward_kernel(
    spot, x_far, w1_far, wm_far, w3_far, h1pad, s1, h2, s2, means, sums, cen, stats, *rest, split
):
    x, w1, wm, w3, sems, ext, cols, flat = rest
    rows = x.shape[0]
    part = chunk_of(rows, 128)

    def slab(at):
        here = slice(at * part, (at + 1) * part)
        return pltpu.make_async_copy(x_far.at[here, :], x.at[here, :], sems.at[3 + at])

    weights = [
        pltpu.make_async_copy(far, ref, sems.at[at])
        for at, (far, ref) in enumerate(((w1_far, w1), (wm_far, wm), (w3_far, w3)))
    ]
    weights[0].start()
    for at in range(rows // part):
        slab(at).start()
    weights[1].start()
    weights[2].start()
    chunk = chunk_of(rows, 128)
    ext[...] = jnp.zeros_like(ext)

    weights[0].wait()

    slabs = rows // part
    for start, stop in ((0, (slabs + 1) // 2), ((slabs + 1) // 2, slabs)):
        for at in range(start, stop):
            slab(at).wait()
        here = slice(start * part, stop * part)
        flat[here, :] = dot(x[here, :], w1[...])

        def first(at, carry, start=start):
            here = slice((start + at) * part, (start + at + 1) * part)
            act = flat[here, :]
            sig = sigmoid(act)
            flat[here, :] = act * sig
            s1[here, :] = sig * (1.0 + act * (1.0 - sig))
            return carry

        loop(stop - start, first, 0)
    pad_lines(flat, ext, rows)
    shifted(ext, cols)
    padded = padded_rows(rows)
    h1pad[...] = cols[1, LINE : LINE + padded, :]
    big = chunk_of(padded, 512)
    weights[1].wait()

    def middle(at, carry):
        base = at * big
        total = jnp.zeros((big, wm.shape[1]), F32)
        for row in range(3):
            for col in range(3):
                left = cols[col, pl.ds(base + LINE * row, big), :]
                k = 3 * row + col
                depth = left.shape[1]
                total = total + dot(left, wm[k * depth : (k + 1) * depth, :])
        ext[pl.ds(base, big), :] = total
        return carry

    loop(padded // big, middle, 0)
    unpad_lines(ext, flat, rows)
    width = w3.shape[1]
    weights[2].wait()

    def second(at, hidden_sum):
        here = slice(at * chunk, (at + 1) * chunk)
        act = flat[here, :]
        sig = sigmoid(act)
        hidden = (act * sig).astype(BF16)
        h2[here, :] = hidden
        s2[here, :] = sig * (1.0 + act * (1.0 - sig))
        return hidden_sum + fold(hidden.astype(F32))

    zeros = jnp.zeros((8, w3.shape[0]), F32)
    hidden_sum = loop(rows // chunk, second, zeros)
    hidden_sum = jnp.sum(hidden_sum, axis=0, keepdims=True)
    sums[...] = jnp.broadcast_to(hidden_sum, sums.shape)
    total = row_times(hidden_sum, w3[...])
    mean = total / rows
    means[...] = jnp.broadcast_to(mean, means.shape)
    quads = width // 256
    for quad in range(quads // 2 if split else quads):
        lanes = lanes_of(quad, spot, 1 if split else None, quads)
        centered, mats, vecs = branch_quad(h2, w3, means, lanes)
        cen[:, 256 * quad : 256 * (quad + 1)] = centered
        put_stats(stats, quad, mats, vecs, split)


def own_branch_kernel(spot, h2, w3, means, cen, stats):
    quads = w3.shape[1] // 256
    for quad in range(quads // 2):
        lanes = lanes_of(quad, spot, 0, quads)
        centered, mats, vecs = branch_quad(h2, w3, means, lanes)
        cen[:, 256 * quad : 256 * (quad + 1)] = centered
        put_stats(stats, quad, mats, vecs, True)


def identity():
    shape = (PAIR, PAIR)
    return jnp.where(
        lax.broadcasted_iota(jnp.int32, shape, 0) == lax.broadcasted_iota(jnp.int32, shape, 1),
        1.0, 0.0,
    ).astype(F32)


def per_block(square):
    row_sums = jnp.sum(square, axis=1, keepdims=True)
    top = jnp.sum(row_sums[:GROUP], axis=0, keepdims=True)
    bottom = jnp.sum(row_sums[GROUP:], axis=0, keepdims=True)
    upper = lax.broadcasted_iota(jnp.int32, (PAIR, 1), 0) < GROUP
    return jnp.where(upper, top, bottom)


def total_of(terms):
    total = terms[0][...]
    for term in terms[1:]:
        total = total + term[...]
    return total


def whiten_kernel(*refs, span, packed):
    terms, (out, keep) = refs[:-2], refs[-2:]
    given = take_pairs(total_of(terms), packed)
    eye = identity()
    blocks = spread(jnp.ones((GROUP, PAIR), F32))
    means = [sums / span for _, sums, _ in given]
    covs = [
        moments / span - outer_of(mean) * blocks + epsilon * eye
        for (moments, _, _), mean in zip(given, means)
    ]
    traces = [per_block(cov * eye) for cov in covs]
    normed = [cov / trace for cov, trace in zip(covs, traces)]
    powers = [1.5 * eye - 0.5 * norm for norm in normed]
    for at, trace in enumerate(traces):
        keep[at, 0] = normed[at]
        keep[at, 1] = eye / trace
    for sweep in range(NEWTON - 1):
        both = [exact_two(power, power, norm) for power, norm in zip(powers, normed)]
        squares, sides = zip(*both)
        for at, power in enumerate(powers):
            keep[at, 2 + 2 * sweep] = power
            keep[at, 3 + 2 * sweep] = squares[at]
        powers = [
            1.5 * power - 0.5 * exact(square, side)
            for power, square, side in zip(powers, squares, sides)
        ]
    for at, power in enumerate(powers):
        keep[at, 2 * NEWTON] = power
        out[at, :GROUP, :] = pack(power / jnp.sqrt(traces[at]))
        out[at, GROUP:, :] = vectors(means[at])


def pull_kernel(*refs, span, packed):
    terms, (keep, out) = refs[:-2], refs[-2:]
    given = take_pairs(total_of(terms), packed)
    eye = identity()
    every = range(len(given))
    normed = [keep[at, 0] for at in every]
    inverse = [per_block(keep[at, 1]) / GROUP for at in every]
    roots = [jnp.sqrt(value) for value in inverse]
    powers = [keep[at, 2 * NEWTON] for at in every]
    grads = [given[at][0] * roots[at] for at in every]
    trace_grads = [
        -0.5 * inverse[at] * roots[at] * per_block(given[at][0] * powers[at]) for at in every
    ]
    normed_grads = [jnp.zeros_like(grads[0])] * len(given)
    for sweep in reversed(range(NEWTON - 1)):
        power = [keep[at, 2 + 2 * sweep] for at in every]
        square = [keep[at, 3 + 2 * sweep] for at in every]
        turned, side = zip(*(exact_two(grads[at], normed[at], power[at]) for at in every))
        turned = [turned[at] + turned[at].T for at in every]
        turned, outer = zip(*(exact_two(turned[at], power[at], square[at]) for at in every))
        side = [exact(side[at], square[at]) for at in every]
        normed_grads = [normed_grads[at] - 0.25 * (side[at] + side[at].T) for at in every]
        inner = [exact(power[at], turned[at]) for at in every]
        grads = [
            1.5 * grads[at] - 0.25 * (outer[at] + outer[at].T + inner[at]) for at in every
        ]
    for at in every:
        normed_grad = normed_grads[at] - 0.5 * grads[at]
        trace_grad = trace_grads[at] - inverse[at] * per_block(normed_grad * normed[at])
        both = normed_grad * inverse[at] + eye * trace_grad
        bias = -exact(vectors(given[at][1] / span), (powers[at] * roots[at]).T)
        out[at, :GROUP, :] = pack(both / span)
        out[at, GROUP:, :] = vectors(bias[0:1, :], given[at][2])


def place_pairs(spot, given, pairs, split):
    if split:
        for side, shares in enumerate(given):
            for at in range(shares.shape[0]):
                half = jnp.bitwise_xor(side, spot[1])
                pairs[half * shares.shape[0] + at] = shares[at]
    else:
        pairs[...] = given[0][...]


def quad_matrix(pairs, quad):
    zero = jnp.zeros((PAIR, PAIR), F32)
    first = spread(pairs[2 * quad, :GROUP, :])
    second = spread(pairs[2 * quad + 1, :GROUP, :])
    top = jnp.concatenate([first, zero], axis=1)
    bottom = jnp.concatenate([zero, second], axis=1)
    return jnp.concatenate([top, bottom], axis=0).astype(BF16)


def row_of(pairs, quad, place):
    at = GROUP + place
    return jnp.concatenate(
        [pairs[2 * quad, at : at + 1, :], pairs[2 * quad + 1, at : at + 1, :]], axis=1
    )


def backward_kernel(spot, x, og, cen, means, gain, shares, *rest, side):
    rows, width = x.shape
    quads = width // 256
    dwb, dpre_out, stats, whites = rest
    count = quads if side is None else quads // 2
    chunk = chunk_of(rows, 128)
    aways, shifts = [], []

    def multiply(quad):
        lanes = lanes_of(quad, spot, side, quads)
        whiten = quad_matrix(shares, quad)
        aways.append(means[0:1, lanes] - row_of(shares, quad, 0))
        shifts.append(row_times(aways[-1], whiten))
        whites[quad % 2] = dot(cen[:, 256 * quad : 256 * (quad + 1)], whiten)

    multiply(0)
    for quad in range(count):
        if quad + 1 < count:
            multiply(quad + 1)
        lanes = lanes_of(quad, spot, side, quads)
        to = slice(256 * quad, 256 * (quad + 1))
        away, shift = aways[quad], shifts[quad]
        scale = gain[:, lanes]

        def step(at, carry, quad=quad, lanes=lanes, to=to, shift=shift, scale=scale):
            col_sum, gain_sum = carry
            here = slice(at * chunk, (at + 1) * chunk)
            white = whites[quad % 2, here, :] + shift
            pre = x[here, lanes].astype(F32) + scale * white
            sig = sigmoid(pre)
            dpre = og[here, lanes].astype(F32) * (sig * (1.0 + pre * (1.0 - sig)))
            dpre_out[here, to] = dpre
            dwhite = scale * dpre
            dwb[here, to] = dwhite.astype(BF16)
            return col_sum + fold(dwhite), gain_sum + fold(dpre * white)

        zero = jnp.zeros((8, 256), F32)
        col_sum, gain_sum = loop(rows // chunk, step, (zero, zero))
        col_sum = jnp.sum(col_sum, axis=0, keepdims=True)
        gain_sum = jnp.sum(gain_sum, axis=0, keepdims=True)
        square = dot_t(cen[:, to], dwb[:, to]) + rank_one(away, col_sum)
        mats, vecs = [], []
        for half in range(2):
            ch = slice(PAIR * half, PAIR * (half + 1))
            inner = square[ch, ch]
            mats.append(pack(inner + inner.T))
            vecs.append((col_sum[:, ch], gain_sum[:, ch]))
        put_stats(stats, quad, mats, vecs, side is not None)


def sides_of(count):
    return (0, 1) if count == 2 else (None,)


def own_kernel(spot, h2, *refs):
    cens, out = refs[:-1], refs[-1]
    quads = out.shape[1] // 256
    for side, cen in zip(sides_of(len(cens)), cens):
        for quad in range(cen.shape[1] // 256):
            near = slice(256 * quad, 256 * (quad + 1))
            out[:, lanes_of(quad, spot, side, quads)] = dot_t(h2[...], cen[:, near]).astype(BF16)


def turn_kernel(spot, w3, *refs):
    given, (turned, flow) = refs[:-2], refs[-2:]
    half = len(given) // 2
    quads = turned.shape[1] // 256
    for side, dwb, shares in zip(sides_of(half), given[:half], given[half:]):
        for quad in range(dwb.shape[1] // 256):
            whiten = quad_matrix(shares, quad).T
            near = slice(256 * quad, 256 * (quad + 1))
            turned[:, lanes_of(quad, spot, side, quads)] = dot(dwb[:, near], whiten).astype(BF16)
    flow[...] = dot_nt(turned[...], w3[...])


def turned_kernel(h2, turned, out):
    for quad in range(turned.shape[1] // 256):
        lanes = slice(256 * quad, 256 * (quad + 1))
        out[:, lanes] = dot_t(h2[...], turned[:, lanes])


def last_kernel(spot, flow, means, s2, w3, *rest, split):
    count = 2 if split else 1
    cens, wshares, given = (rest[count * at : count * (at + 1)] for at in range(3))
    cols, gains, spairs, bias_out, ext, flat, joint = rest[3 * count :]
    rows = flow.shape[0]
    quads = w3.shape[1] // 256
    place_pairs(spot, given, spairs, split)
    gains[...] = spairs[:, GROUP + 1, :]
    chunk = chunk_of(rows, 128)
    ext[...] = jnp.zeros_like(ext)
    low = jnp.zeros((1, w3.shape[0]), F32)
    top = 0
    total = None
    for side, cen, whitens, shares in zip(sides_of(count), cens, wshares, given):
        start = top
        for quad in range(cen.shape[1] // 256):
            lanes = lanes_of(quad, spot, side, quads)
            sym = quad_matrix(shares, quad)
            away = means[0:1, lanes] - row_of(whitens, quad, 0)
            bias = row_of(shares, quad, 0) + row_times(away, sym)
            bias_out[:, lanes] = jnp.broadcast_to(bias, (8, 256))
            last = w3[:, lanes]
            low = low + row_times(bias, last, dot_nt)
            joint[top : top + 256, :] = dot_nt(sym, last).astype(BF16)
            top += 256
        part = dot(cen[...], joint[start:top, :])
        total = part if total is None else total + part
    flat[...] = total

    def middle(at, carry):
        here = slice(at * chunk, (at + 1) * chunk)
        flat[here, :] = (flow[here, :] + flat[here, :] + low) * s2[here, :]
        return carry

    loop(rows // chunk, middle, 0)
    pad_lines(flat, ext, rows)
    shifted(ext, cols)


def finish(part, outs, spot, plan):
    if plan:
        emit_split(part, outs[0], outs[1], spot[1], plan)
    else:
        outs[0][...] = part[...]


def slope_kernel(spot, cols, wm, s1, x, dmid1, *rest, plan):
    outs, (ext, flat, part) = rest[:-3], rest[-3:]
    rows, depth = s1.shape
    padded = padded_rows(rows)
    big = chunk_of(padded, 512)

    def step(at, carry):
        base = at * big
        total = jnp.zeros((big, depth), F32)
        for row in range(3):
            for col in range(3):
                near = cols[2 - col, pl.ds(base + LINE * (2 - row), big), :]
                k = 3 * row + col
                total = total + dot_nt(near, wm[k * depth : (k + 1) * depth, :])
        ext[pl.ds(base, big), :] = total
        return carry

    loop(padded // big, step, 0)
    unpad_lines(ext, flat, rows)
    dmid1[...] = (flat[...] * s1[...]).astype(BF16)
    for quad in range(x.shape[1] // 256):
        lanes = slice(256 * quad, 256 * (quad + 1))
        part[lanes, :] = dot_t(x[:, lanes], dmid1[...])
    finish(part, outs, spot, plan)


def middle_kernel(spot, cols, h1pad, turned, own, sums, spairs, bias, *rest, plans):
    outs, (part, part_last) = rest[:-2], rest[-2:]
    padded, depth = h1pad.shape
    for row in range(3):
        for col in range(3):
            k = 3 * row + col
            near = cols[2 - col, LINE * (2 - row) : LINE * (2 - row) + padded, :]
            part[k * depth : (k + 1) * depth, :] = dot_t(h1pad[...], near)
    for quad in range(turned.shape[1] // 256):
        lanes = slice(256 * quad, 256 * (quad + 1))
        sym = quad_matrix(spairs, quad)
        part_last[:, lanes] = (
            turned[:, lanes]
            + dot(own[:, lanes], sym)
            + rank_one(sums[0:1, :], bias[0:1, lanes])
        )
    if plans:
        emit_split(part, outs[0], outs[1], spot[1], plans[0])
        emit_split(part_last, outs[0], outs[1], spot[1], plans[1])
    else:
        outs[0][...] = part[...]
        outs[1][...] = part_last[...]


def spans_step(spot, *refs, steps, extra=0):
    count = 2 * (1 + max(span[0] for spans in steps for span in spans))
    given, outs = refs[: count + extra], refs[count + extra :]
    for at, spans in enumerate(steps):
        to = 0
        for source, start, size, bit in spans:
            mine, other = half_of(given[2 * source], given[2 * source + 1], spot[bit], start, size)
            outs[2 * at][to : to + size // 2, :] = mine
            outs[2 * at + 1][to : to + size // 2, :] = other
            to += size // 2
        left = outs[2 * at].shape[0] - to
        if not left:
            continue
        if extra:
            rows = jnp.concatenate([given[-1][...]] * (outs[0].shape[1] // PAIR), axis=1)
        else:
            tail = given[0].shape[0] - left
            rows = given[0][tail:, :] + given[1][tail:, :]
        for out in outs[2 * at : 2 * at + 2]:
            out[to:, :] = rows


def close_kernel(spot, keep, given, first, middle, last, gain, *, tall, high, scale):
    total = (keep[...] + given[...]) * scale
    for half in range(2):
        lanes = slice(PAIR * half, PAIR * (half + 1))
        step = tall // 4
        for wide in range(4):
            last[pl.ds(2 * wide + half, step, 8), :] = total[step * wide : step * (wide + 1), lanes]
        middle[pl.ds(half, high, 2), :] = total[tall : tall + high, lanes]
        first[pl.ds(half, tall, 2), :] = total[tall + high : 2 * tall + high, lanes]
    size = gain.shape[1]
    each = PAIR // size
    rows = total[2 * tall + high :, :PAIR]
    device = spot[6]
    at = lax.broadcasted_iota(jnp.int32, rows.shape, 0)
    row = jnp.sum(jnp.where(at == device // each, rows, 0.0), axis=0, keepdims=True)
    mine = jnp.zeros((1, size), F32)
    for place in range(each):
        mine = jnp.where(device % each == place, row[:, place * size : (place + 1) * size], mine)
    gain[...] = mine


def input_kernel(spot, dmid1, w1, *refs):
    dpres, (out, token) = refs[:-2], refs[-2:]
    token[...] = jnp.zeros_like(token)
    quads = out.shape[1] // 256
    for side, dpre in zip(sides_of(len(dpres)), dpres):
        for quad in range(dpre.shape[1] // 256):
            lanes = lanes_of(quad, spot, side, quads)
            near = slice(256 * quad, 256 * (quad + 1))
            out[:, lanes] = (dot_nt(dmid1[...], w1[lanes, :]) + dpre[:, near]).astype(BF16)


def call(kernel, outs, args, scratch=(), scalars=0, flops=0, ties=(), far=0, room=40):
    args = tuple(args) + tuple(ties)
    specs = [pl.BlockSpec(memory_space=pltpu.SMEM)] * scalars
    specs += [pl.BlockSpec(memory_space=pl.ANY)] * far
    specs += [pl.BlockSpec(memory_space=pltpu.VMEM)] * (len(args) - scalars - len(ties) - far)
    specs += [pl.BlockSpec(memory_space=pl.ANY)] * len(ties)
    count = len(args) - len(ties)

    def body(*refs):
        kernel(*refs[:count], *refs[len(args) :])

    size = sum(a.size * a.dtype.itemsize for a in args)
    size += sum(o.size * o.dtype.itemsize for o in outs)
    return pl.pallas_call(
        body,
        out_shape=tuple(outs),
        in_specs=specs,
        out_specs=tuple(pl.BlockSpec(memory_space=pltpu.VMEM) for _ in outs),
        scratch_shapes=list(scratch),
        cost_estimate=pl.CostEstimate(flops=flops, bytes_accessed=size, transcendentals=0),
        compiler_params=pltpu.CompilerParams(vmem_limit_bytes=room * 2**20),
    )(*args)


def shape(dims, dtype=F32):
    return jax.ShapeDtypeStruct(dims, dtype)


def swap(value, axis, size, flip):
    return lax.ppermute(value, axis, [(at, at ^ flip) for at in range(size)])


def shards(inputs, out_grad, conv_first, conv_middle, conv_last, gain):
    rows, width = inputs.shape
    mid = conv_first.shape[1]
    pairs = width // PAIR
    ghosts = lax.axis_size("ghost")
    groups = lax.axis_size("group")
    devices = ghosts * groups
    span = float(rows * ghosts)
    scale = (rows * devices) ** (-0.5)
    padded = padded_rows(rows)
    ghost = lax.axis_index("ghost")
    group = lax.axis_index("group")
    bits = [ghost] + [(ghost >> bit) & 1 for bit in range(3)]
    bits += [(group >> bit) & 1 for bit in range(2)] + [group * ghosts + ghost]
    spot = jnp.stack(bits).astype(jnp.int32)
    core, across, along, near, far = 1, 2, 3, 4, 5
    split = ghosts == 8 and pairs == 8 and groups == 4
    unit = 2 * rows * width * mid

    ext = pltpu.VMEM((24 + padded + LINE + 8, mid), F32)
    flat = pltpu.VMEM((rows, mid), F32)
    cols = (3, padded + 2 * LINE, mid)
    big = (pairs, TALL, PAIR)
    half = (pairs // 2, TALL, PAIR)
    packed = (pairs // 4, TALL, PAIR)
    side_stats = shape(packed if split else big)
    side_width = width // 2 if split else width

    def collect(stats, ties):
        if not split:
            return [lax.psum(stats[0], "ghost")]
        send, total = stats
        given = swap(send, "ghost", ghosts, 1)
        (total,) = call(add_kernel, [shape(packed)], (total, given))
        given = swap(total, "ghost", ghosts, 2)
        (total,) = call(add_kernel, [shape(packed)], (total, given), ties=ties)
        return [total, swap(total, "ghost", ghosts, 4)]

    own = half if split else big
    held = own[0]
    chunks = rows // chunk_of(rows, 128)
    h1pad, s1, h2, s2, means, sums, cen, stats = call(
        functools.partial(forward_kernel, split=split),
        [shape((padded, mid), BF16), shape((rows, mid)), shape((rows, mid), BF16),
         shape((rows, mid)), shape((8, width)), shape((8, mid)), shape((rows, side_width), BF16),
         side_stats],
        (spot, *(
            pltpu.with_memory_space_constraint(value, pltpu.HBM)
            for value in (inputs, conv_first, conv_middle, conv_last)
        )),
        (pltpu.VMEM((rows, width), BF16), pltpu.VMEM(conv_first.shape, BF16),
         pltpu.VMEM(conv_middle.shape, BF16), pltpu.VMEM(conv_last.shape, BF16),
         pltpu.SemaphoreType.DMA((3 + chunks,)),
         ext, pltpu.VMEM(cols, BF16), flat),
        scalars=1, flops=5 * unit, far=4,
    )
    stats, cens = [stats], (cen,)
    if split:
        cen, keep = call(
            own_branch_kernel, [shape((rows, side_width), BF16), side_stats],
            (spot, h2, conv_last, means), scalars=1, flops=unit,
        )
        stats.append(keep)
        cens = (cen, *cens)
    (own_part,) = call(
        own_kernel, [shape((mid, width), BF16)], (spot, h2, *cens), scalars=1, flops=unit
    )
    share, kept = call(
        functools.partial(whiten_kernel, span=span, packed=split),
        [shape(own), shape((held, 2 * NEWTON + 1, PAIR, PAIR))], collect(stats, (own_part,)), flops=10**7,
    )
    whites = (pltpu.VMEM((2, rows, 256), F32),)
    shares = [share, swap(share, "ghost", ghosts, 1)] if split else [share]
    dwbs, dpres, back = [], [], []
    for side, cen, whiten in zip(sides_of(len(shares)), cens, shares):
        dwb, dpre, part = call(
            functools.partial(backward_kernel, side=side),
            [shape((rows, side_width), BF16), shape((rows, side_width)), side_stats],
            (spot, inputs, out_grad, cen, means, gain.reshape(1, width), whiten), whites,
            scalars=1, flops=2 * unit, ties=dpres,
        )
        dwbs.append(dwb)
        dpres.append(dpre)
        back.insert(0, part)
    stats = back
    turned, flow = call(
        turn_kernel, [shape((rows, width), BF16), shape((rows, mid))],
        (spot, conv_last, *dwbs, *shares), scalars=1, flops=2 * unit,
    )
    (turned_part,) = call(turned_kernel, [shape((mid, width))], (h2, turned), flops=unit)
    (pulled,) = call(
        functools.partial(pull_kernel, span=span, packed=split), [shape(own)], (*collect(stats, (flow,)), kept),
        flops=10**7, ties=(turned_part,),
    )
    given = [pulled, swap(pulled, "ghost", ghosts, 1)] if split else [pulled]

    dcols, gains, spairs, bias = call(
        functools.partial(last_kernel, split=split),
        [shape(cols, BF16), shape((pairs, PAIR)), shape(big), shape((8, width))],
        (spot, flow, means, s2, conv_last, *cens, *shares, *given),
        (ext, flat, pltpu.VMEM((width, mid), BF16)), scalars=1, flops=2 * unit,
    )
    half_rows = mid * width // 512
    orders = (
        (("ghost", 1), ("ghost", 2), ("group", 0), ("group", 1)),
        (("ghost", 2), ("group", 0), ("ghost", 1), ("group", 1)),
        (("group", 0), ("ghost", 1), ("ghost", 2), ("group", 1)),
    )
    high, tall = 9 * mid // devices, width // devices
    cut = high // 24 * 8
    middle_plan = last_plan = first_plan = None
    if split:
        middle_plan = plan_of(
            [(0, cut, orders[0]), (cut, high - cut, orders[1])], high, 1, ghosts
        )
        last_plan = plan_of(
            [(0, mid // devices, orders[0])], mid // devices, width // 256, ghosts, 9 * mid // 2
        )
        first_plan = plan_of([(0, tall, orders[2])], tall, 1, ghosts)
    middle_part = call(
        functools.partial(middle_kernel, plans=(middle_plan, last_plan) if split else None),
        [shape((9 * mid // 2 + half_rows, mid))] * 2 if split
        else [shape((9 * mid, mid)), shape((mid, width))],
        (spot, dcols, h1pad, turned_part, own_part, sums, spairs, bias),
        (pltpu.VMEM((9 * mid, mid), F32), pltpu.VMEM((mid, width), F32)),
        scalars=1, flops=3 * unit,
    )
    dmid1, *first_part = call(
        functools.partial(slope_kernel, plan=first_plan),
        [shape((rows, mid), BF16)]
        + ([shape((half_rows, mid))] * 2 if split else [shape((width, mid))]),
        (spot, dcols, conv_middle, s1, inputs),
        (ext, flat, pltpu.VMEM((width, mid), F32)), scalars=1, flops=4 * unit,
    )
    portion = width // devices
    if not split:
        input_grad, _ = call(
            input_kernel, [shape((rows, width), BF16), shape((8, PAIR))],
            (spot, dmid1, conv_first, *dpres), scalars=1, flops=unit,
        )
        grads = [
            lax.psum_scatter(
                (part[0] * scale).reshape(-1), ("group", "ghost"), scatter_dimension=0, tiled=True
            )
            for part in (first_part, middle_part, middle_part[1:])
        ]
        gain_grad = lax.dynamic_slice_in_dim(
            lax.psum(gains.reshape(-1) * scale, "group"), (group * ghosts + ghost) * portion, portion
        )
        return (input_grad, *grads, gain_grad)

    def move(parts, ways):
        result = []
        for at, (axis, flip) in enumerate(ways):
            result.append(parts[2 * at])
            result.append(swap(parts[2 * at + 1], axis, groups if axis == "group" else ghosts, flip))
        return result

    def run(steps, given, extra=(), more=0, ties=()):
        outs = []
        for at, spans in enumerate(steps):
            height = sum(span[2] for span in spans) // 2 + (more if at == 0 else 0)
            outs += [shape((height, mid))] * 2
        return call(
            functools.partial(spans_step, steps=steps, extra=len(extra)), outs,
            (spot, *given, *extra), scalars=1, ties=ties,
        )

    core_way, x_way, y_way = (("ghost", 1 << bit) for bit in range(3))
    near_way, far_way = ("group", 1), ("group", 2)
    given = move(middle_part, (core_way,))
    first_given = move(first_part, (core_way,))
    pieces = devices // 2
    a_low, a_high, b_all = half_rows, pieces * cut, pieces * (high - cut)
    parts = run(
        (((0, a_high + b_all, a_low, across), (0, 0, a_high, across)),
         ((0, a_high, b_all, along),)), given,
    )
    given = move(parts, (x_way, y_way))
    parts = run((((0, 0, half_rows, near),),), first_given, ties=(parts[0],))
    given += move(parts, (near_way,))
    input_grad, token = call(
        input_kernel, [shape((rows, width), BF16), shape((8, PAIR))],
        (spot, dmid1, conv_first, *dpres), scalars=1, flops=unit, ties=(parts[0],),
    )
    a_low, a_high, b_all, c_all = a_low // 2, a_high // 2, b_all // 2, half_rows // 2
    parts = run(
        (((0, 0, a_low, along), (0, a_low, a_high, along)), ((1, 0, b_all, near),),
         ((2, 0, c_all, across),)), given, ties=(token,),
    )
    given = move(parts, (y_way, near_way, x_way))
    a_low, a_high, b_all, c_all = a_low // 2, a_high // 2, b_all // 2, c_all // 2
    parts = run(
        (((0, 0, a_low, near), (0, a_low, a_high, near)), ((1, 0, b_all, across),),
         ((2, 0, c_all, along),)), given, extra=(gains,), more=8,
    )
    given = move(parts, (near_way, x_way, y_way))
    a_low, a_high, b_all, c_all = a_low // 2, a_high // 2, b_all // 2, c_all // 2
    parts = run(
        (((0, 0, a_low, far), (0, a_low, a_high, far), (1, 0, b_all, far), (2, 0, c_all, far)),),
        given, more=8,
    )
    given = move(parts, (far_way,))
    first_grad, middle_grad, last_grad, gain_grad = call(
        functools.partial(close_kernel, tall=tall, high=high, scale=scale),
        [shape((2 * tall, PAIR)), shape((2 * high, PAIR)), shape((2 * tall, PAIR)),
         shape((1, portion))],
        (spot, *given), scalars=1,
    )
    return (
        input_grad, first_grad.reshape(-1), middle_grad.reshape(-1), last_grad.reshape(-1),
        gain_grad.reshape(-1),
    )


def solution(mesh):
    in_specs = (P(("group", "ghost"), None), P(("group", "ghost"), None), P(), P(), P(), P())
    out_specs = (
        P(("group", "ghost"), None),
        P(("group", "ghost")),
        P(("group", "ghost")),
        P(("group", "ghost")),
        P(("group", "ghost")),
    )
    return jax.shard_map(shards, mesh=mesh, in_specs=in_specs, out_specs=out_specs, check_vma=False)
```

```python
import functools

import jax
import jax.numpy as jnp
from jax import lax
from jax.experimental import pallas as pl
from jax.experimental.pallas import tpu as pltpu
from jax.sharding import PartitionSpec as P

GROUP = 64
NEWTON = 5
SIDE = 14
LINE = 16
PAIR = 2 * GROUP
TALL = GROUP + 8
epsilon = 1e-05

F32 = jnp.float32
BF16 = jnp.bfloat16


def dot(left, right):
    return jnp.dot(left, right, preferred_element_type=F32)


def dot_t(left, right):
    return lax.dot_general(left, right, (((0,), (0,)), ((), ())), preferred_element_type=F32)


def dot_nt(left, right):
    return lax.dot_general(left, right, (((1,), (1,)), ((), ())), preferred_element_type=F32)


def halves_of(value):
    high = value.astype(BF16)
    return high, (value - high.astype(F32)).astype(BF16)


def exact(left, right):
    a, b = halves_of(left)
    c, d = halves_of(right)
    low = dot(jnp.concatenate([a, b], axis=1), jnp.concatenate([d, c], axis=0))
    return low + dot(a, c)


def exact_two(left, first, second):
    both = exact(left, jnp.concatenate([first, second], axis=1))
    return both[:, : first.shape[1]], both[:, first.shape[1] :]


def outer_of(row):
    tile = vectors(row)
    return lax.dot_general(
        tile, tile, (((0,), (0,)), ((), ())), preferred_element_type=F32,
        precision=lax.Precision.HIGHEST,
    )


def sigmoid(value):
    return 0.5 * jnp.tanh(0.5 * value) + 0.5


def two_rows(row):
    high, low = halves_of(jnp.broadcast_to(row, (16, row.shape[1])))
    at = lax.broadcasted_iota(jnp.int32, high.shape, 0)
    return jnp.where(at == 0, high.astype(F32), jnp.where(at == 1, low.astype(F32), 0.0)).astype(
        BF16
    )


def row_times(row, matrix, product=dot):
    return jnp.sum(product(two_rows(row), matrix), axis=0, keepdims=True)


def rank_one(left, right):
    tiles = []
    for row, order in ((left, (0, 1, 0)), (right, (0, 0, 1))):
        pair = halves_of(jnp.broadcast_to(row, (16, row.shape[1])))
        at = lax.broadcasted_iota(jnp.int32, pair[0].shape, 0)
        tile = jnp.zeros(pair[0].shape, F32)
        for place, which in enumerate(order):
            tile = jnp.where(at == place, pair[which].astype(F32), tile)
        tiles.append(tile.astype(BF16))
    return dot_t(*tiles)


def chunk_of(rows, most):
    best = 16
    for size in range(16, most + 1, 16):
        if rows % size == 0:
            best = size
    return best


def loop(count, body, carry):
    for at in range(count):
        carry = body(at, carry)
    return carry


def left_half(shape):
    return lax.broadcasted_iota(jnp.int32, shape, 1) < GROUP


def spread(packed):
    left = left_half(packed.shape)
    zero = jnp.zeros_like(packed)
    return jnp.concatenate([jnp.where(left, packed, zero), jnp.where(left, zero, packed)], axis=0)


def pack(square):
    top, bottom = square[:GROUP], square[GROUP:]
    return jnp.where(left_half(top.shape), top, bottom)


def vectors(*rows):
    at = lax.broadcasted_iota(jnp.int32, (8, PAIR), 0)
    tile = jnp.zeros((8, PAIR), F32)
    for place, row in enumerate(rows):
        tile = jnp.where(at == place, row, tile)
    return tile


def fold(value):
    rows, lanes = value.shape
    return jnp.sum(value.reshape(rows // 8, 8, lanes), axis=0)


def pad_lines(source, ext, rows):
    for line in range(rows // SIDE):
        place = 24 + LINE * (line + line // SIDE)
        ext[place : place + SIDE, :] = source[SIDE * line : SIDE * (line + 1), :]


def unpad_lines(source, target, rows):
    for line in range(rows // SIDE):
        place = LINE * (line + line // SIDE)
        target[SIDE * line : SIDE * (line + 1), :] = source[place : place + SIDE, :]


def padded_rows(rows):
    return rows // (SIDE * SIDE) * (SIDE + 1) * LINE


def shifted(ext, cols):
    length = cols.shape[1]
    for col in range(3):
        cols[col] = ext[7 + col : 7 + col + length, :].astype(BF16)


def emit_split(source, keep, send, core, plan):
    for start, height, first, size, mine in plan:
        lanes = keep.shape[1]
        for wide in range(source.shape[1] // lanes):
            to = slice(start + wide * height, start + (wide + 1) * height)
            cols = slice(wide * lanes, (wide + 1) * lanes)
            for target, half in ((keep, core), (send, 1 - core)):
                place = pl.multiple_of((mine + half) * size + first, 8)
                target[to, :] = source[pl.ds(place, height), cols]


def plan_of(parts, piece, wide, ghosts, start=0):
    plan = []
    for first, height, steps in parts:
        for at in range(2 ** len(steps)):
            source = 0
            for place, (axis, bit) in enumerate(steps):
                value = (at >> (len(steps) - 1 - place)) & 1
                source += value << bit if axis == "ghost" else (value << bit) * ghosts
            plan.append((start, height, first, piece, source))
            start += height * wide
    return plan


def half_of(left, right, bit, start=0, rows=None):
    rows = (left.shape[0] if rows is None else rows) // 2
    mine = pl.ds(pl.multiple_of(start + bit * rows, 8), rows)
    other = pl.ds(pl.multiple_of(start + (1 - bit) * rows, 8), rows)
    return left[mine, :] + right[mine, :], left[other, :] + right[other, :]


def pack_slot(mats, vecs):
    first, second = mats
    row = lax.broadcasted_iota(jnp.int32, first.shape, 0)
    lane = lax.broadcasted_iota(jnp.int32, first.shape, 1)
    left = lane < GROUP
    col = jnp.where(left, lane, lane - GROUP)
    upper = jnp.where(left, first, pltpu.roll(second, GROUP, 1))
    lower = jnp.where(left, pltpu.roll(first, GROUP, 1), second)
    rows = [jnp.sum(jnp.where(row == col, m, 0.0), axis=0, keepdims=True) for m in mats]
    for pair in zip(*vecs):
        rows += pair
    return jnp.concatenate([jnp.where(row <= col, upper, lower), vectors(*rows)], axis=0)


def put_stats(stats, quad, mats, vecs, packed):
    if packed:
        stats[quad] = pack_slot(mats, vecs)
        return
    for half in range(2):
        stats[2 * quad + half, :GROUP, :] = mats[half]
        stats[2 * quad + half, GROUP:, :] = vectors(*vecs[half])


def lanes_of(quad, spot, side, quads):
    if side is None:
        return slice(256 * quad, 256 * (quad + 1))
    half = jnp.bitwise_xor(spot[1], side)
    return pl.ds(pl.multiple_of(256 * (half * (quads // 2) + quad), 256), 256)


def branch_quad(h2, w3, means, lanes):
    rows = h2.shape[0]
    mean = means[0:1, lanes]
    centered = (dot(h2[...], w3[:, lanes]) - mean).astype(BF16)
    square = dot_t(centered, centered)
    mats, vecs = [], []
    for half in range(2):
        ch = slice(PAIR * half, PAIR * (half + 1))
        row = mean[:, ch]
        mats.append(pack(square[ch, ch] + outer_of(row) * rows))
        vecs.append((row * rows,))
    return centered, mats, vecs


def take_pairs(total, packed):
    result = []
    if not packed:
        for at in range(total.shape[0]):
            vecs = [total[at, GROUP + p : GROUP + p + 1, :] for p in range(2)]
            result.append((spread(total[at, :GROUP, :]), *vecs))
        return result
    shape = (PAIR, PAIR)
    row = lax.broadcasted_iota(jnp.int32, shape, 0)
    col = lax.broadcasted_iota(jnp.int32, shape, 1)
    mask = jnp.where(row < GROUP, row - col, col - row) < 0
    eye = identity()
    for slot in range(total.shape[0]):
        both = total[slot, :GROUP, :]
        turned = pltpu.roll(both, GROUP, 1)
        left = left_half(both.shape)
        for at in range(2):
            twice = jnp.where(left, *((both, turned) if at == 0 else (turned, both)))
            part = jnp.where(mask, spread(twice), 0.0)
            line = [total[slot, GROUP + 2 * p + at : GROUP + 2 * p + at + 1, :] for p in range(3)]
            result.append((part + part.T + eye * line[0], line[1], line[2]))
    return result


def add_kernel(left, right, out):
    out[...] = left[...] + right[...]


def forward_kernel(
    spot, x_far, w1_far, wm_far, w3_far, h1pad, s1, h2, s2, means, sums, cen, stats, *rest, split
):
    x, w1, wm, w3, sems, ext, cols, flat = rest
    rows = x.shape[0]
    part = chunk_of(rows, 128)

    def slab(at):
        here = slice(at * part, (at + 1) * part)
        return pltpu.make_async_copy(x_far.at[here, :], x.at[here, :], sems.at[3 + at])

    weights = [
        pltpu.make_async_copy(far, ref, sems.at[at])
        for at, (far, ref) in enumerate(((w1_far, w1), (wm_far, wm), (w3_far, w3)))
    ]
    weights[0].start()
    for at in range(rows // part):
        slab(at).start()
    weights[1].start()
    weights[2].start()
    chunk = chunk_of(rows, 128)
    ext[...] = jnp.zeros_like(ext)

    weights[0].wait()

    slabs = rows // part
    for start, stop in ((0, (slabs + 1) // 2), ((slabs + 1) // 2, slabs)):
        for at in range(start, stop):
            slab(at).wait()
        here = slice(start * part, stop * part)
        flat[here, :] = dot(x[here, :], w1[...])

        def first(at, carry, start=start):
            here = slice((start + at) * part, (start + at + 1) * part)
            act = flat[here, :]
            sig = sigmoid(act)
            flat[here, :] = act * sig
            s1[here, :] = sig * (1.0 + act * (1.0 - sig))
            return carry

        loop(stop - start, first, 0)
    pad_lines(flat, ext, rows)
    shifted(ext, cols)
    padded = padded_rows(rows)
    h1pad[...] = cols[1, LINE : LINE + padded, :]
    big = chunk_of(padded, 512)
    weights[1].wait()

    def middle(at, carry):
        base = at * big
        total = jnp.zeros((big, wm.shape[1]), F32)
        for row in range(3):
            for col in range(3):
                left = cols[col, pl.ds(base + LINE * row, big), :]
                k = 3 * row + col
                depth = left.shape[1]
                total = total + dot(left, wm[k * depth : (k + 1) * depth, :])
        ext[pl.ds(base, big), :] = total
        return carry

    loop(padded // big, middle, 0)
    unpad_lines(ext, flat, rows)
    width = w3.shape[1]
    weights[2].wait()

    def second(at, hidden_sum):
        here = slice(at * chunk, (at + 1) * chunk)
        act = flat[here, :]
        sig = sigmoid(act)
        hidden = (act * sig).astype(BF16)
        h2[here, :] = hidden
        s2[here, :] = sig * (1.0 + act * (1.0 - sig))
        return hidden_sum + fold(hidden.astype(F32))

    zeros = jnp.zeros((8, w3.shape[0]), F32)
    hidden_sum = loop(rows // chunk, second, zeros)
    hidden_sum = jnp.sum(hidden_sum, axis=0, keepdims=True)
    sums[...] = jnp.broadcast_to(hidden_sum, sums.shape)
    total = row_times(hidden_sum, w3[...])
    mean = total / rows
    means[...] = jnp.broadcast_to(mean, means.shape)
    quads = width // 256
    for quad in range(quads // 2 if split else quads):
        lanes = lanes_of(quad, spot, 1 if split else None, quads)
        centered, mats, vecs = branch_quad(h2, w3, means, lanes)
        cen[:, 256 * quad : 256 * (quad + 1)] = centered
        put_stats(stats, quad, mats, vecs, split)


def own_branch_kernel(spot, h2, w3, means, cen, stats):
    quads = w3.shape[1] // 256
    for quad in range(quads // 2):
        lanes = lanes_of(quad, spot, 0, quads)
        centered, mats, vecs = branch_quad(h2, w3, means, lanes)
        cen[:, 256 * quad : 256 * (quad + 1)] = centered
        put_stats(stats, quad, mats, vecs, True)


def identity():
    shape = (PAIR, PAIR)
    return jnp.where(
        lax.broadcasted_iota(jnp.int32, shape, 0) == lax.broadcasted_iota(jnp.int32, shape, 1),
        1.0, 0.0,
    ).astype(F32)


def per_block(square):
    row_sums = jnp.sum(square, axis=1, keepdims=True)
    top = jnp.sum(row_sums[:GROUP], axis=0, keepdims=True)
    bottom = jnp.sum(row_sums[GROUP:], axis=0, keepdims=True)
    upper = lax.broadcasted_iota(jnp.int32, (PAIR, 1), 0) < GROUP
    return jnp.where(upper, top, bottom)


def total_of(terms):
    total = terms[0][...]
    for term in terms[1:]:
        total = total + term[...]
    return total


def whiten_kernel(*refs, span, packed):
    terms, (out, keep) = refs[:-2], refs[-2:]
    given = take_pairs(total_of(terms), packed)
    eye = identity()
    blocks = spread(jnp.ones((GROUP, PAIR), F32))
    means = [sums / span for _, sums, _ in given]
    covs = [
        moments / span - outer_of(mean) * blocks + epsilon * eye
        for (moments, _, _), mean in zip(given, means)
    ]
    traces = [per_block(cov * eye) for cov in covs]
    normed = [cov / trace for cov, trace in zip(covs, traces)]
    powers = [1.5 * eye - 0.5 * norm for norm in normed]
    for at, trace in enumerate(traces):
        keep[at, 0] = normed[at]
        keep[at, 1] = eye / trace
    for sweep in range(NEWTON - 1):
        both = [exact_two(power, power, norm) for power, norm in zip(powers, normed)]
        squares, sides = zip(*both)
        for at, power in enumerate(powers):
            keep[at, 2 + 2 * sweep] = power
            keep[at, 3 + 2 * sweep] = squares[at]
        powers = [
            1.5 * power - 0.5 * exact(square, side)
            for power, square, side in zip(powers, squares, sides)
        ]
    for at, power in enumerate(powers):
        keep[at, 2 * NEWTON] = power
        out[at, :GROUP, :] = pack(power / jnp.sqrt(traces[at]))
        out[at, GROUP:, :] = vectors(means[at])


def pull_kernel(*refs, span, packed):
    terms, (keep, out) = refs[:-2], refs[-2:]
    given = take_pairs(total_of(terms), packed)
    eye = identity()
    every = range(len(given))
    normed = [keep[at, 0] for at in every]
    inverse = [per_block(keep[at, 1]) / GROUP for at in every]
    roots = [jnp.sqrt(value) for value in inverse]
    powers = [keep[at, 2 * NEWTON] for at in every]
    grads = [given[at][0] * roots[at] for at in every]
    trace_grads = [
        -0.5 * inverse[at] * roots[at] * per_block(given[at][0] * powers[at]) for at in every
    ]
    normed_grads = [jnp.zeros_like(grads[0])] * len(given)
    for sweep in reversed(range(NEWTON - 1)):
        power = [keep[at, 2 + 2 * sweep] for at in every]
        square = [keep[at, 3 + 2 * sweep] for at in every]
        turned, side = zip(*(exact_two(grads[at], normed[at], power[at]) for at in every))
        turned = [turned[at] + turned[at].T for at in every]
        turned, outer = zip(*(exact_two(turned[at], power[at], square[at]) for at in every))
        side = [exact(side[at], square[at]) for at in every]
        normed_grads = [normed_grads[at] - 0.25 * (side[at] + side[at].T) for at in every]
        inner = [exact(power[at], turned[at]) for at in every]
        grads = [
            1.5 * grads[at] - 0.25 * (outer[at] + outer[at].T + inner[at]) for at in every
        ]
    for at in every:
        normed_grad = normed_grads[at] - 0.5 * grads[at]
        trace_grad = trace_grads[at] - inverse[at] * per_block(normed_grad * normed[at])
        both = normed_grad * inverse[at] + eye * trace_grad
        bias = -exact(vectors(given[at][1] / span), (powers[at] * roots[at]).T)
        out[at, :GROUP, :] = pack(both / span)
        out[at, GROUP:, :] = vectors(bias[0:1, :], given[at][2])


def place_pairs(spot, given, pairs, split):
    if split:
        for side, shares in enumerate(given):
            for at in range(shares.shape[0]):
                half = jnp.bitwise_xor(side, spot[1])
                pairs[half * shares.shape[0] + at] = shares[at]
    else:
        pairs[...] = given[0][...]


def quad_matrix(pairs, quad):
    zero = jnp.zeros((PAIR, PAIR), F32)
    first = spread(pairs[2 * quad, :GROUP, :])
    second = spread(pairs[2 * quad + 1, :GROUP, :])
    top = jnp.concatenate([first, zero], axis=1)
    bottom = jnp.concatenate([zero, second], axis=1)
    return jnp.concatenate([top, bottom], axis=0).astype(BF16)


def row_of(pairs, quad, place):
    at = GROUP + place
    return jnp.concatenate(
        [pairs[2 * quad, at : at + 1, :], pairs[2 * quad + 1, at : at + 1, :]], axis=1
    )


def backward_kernel(spot, x, og, cen, means, gain, shares, *rest, side):
    rows, width = x.shape
    quads = width // 256
    dwb, dpre_out, stats, whites = rest
    count = quads if side is None else quads // 2
    chunk = chunk_of(rows, 128)
    aways, shifts = [], []

    def multiply(quad):
        lanes = lanes_of(quad, spot, side, quads)
        whiten = quad_matrix(shares, quad)
        aways.append(means[0:1, lanes] - row_of(shares, quad, 0))
        shifts.append(row_times(aways[-1], whiten))
        whites[quad % 2] = dot(cen[:, 256 * quad : 256 * (quad + 1)], whiten)

    multiply(0)
    for quad in range(count):
        if quad + 1 < count:
            multiply(quad + 1)
        lanes = lanes_of(quad, spot, side, quads)
        to = slice(256 * quad, 256 * (quad + 1))
        away, shift = aways[quad], shifts[quad]
        scale = gain[:, lanes]

        def step(at, carry, quad=quad, lanes=lanes, to=to, shift=shift, scale=scale):
            col_sum, gain_sum = carry
            here = slice(at * chunk, (at + 1) * chunk)
            white = whites[quad % 2, here, :] + shift
            pre = x[here, lanes].astype(F32) + scale * white
            sig = sigmoid(pre)
            dpre = og[here, lanes].astype(F32) * (sig * (1.0 + pre * (1.0 - sig)))
            dpre_out[here, to] = dpre
            dwhite = scale * dpre
            dwb[here, to] = dwhite.astype(BF16)
            return col_sum + fold(dwhite), gain_sum + fold(dpre * white)

        zero = jnp.zeros((8, 256), F32)
        col_sum, gain_sum = loop(rows // chunk, step, (zero, zero))
        col_sum = jnp.sum(col_sum, axis=0, keepdims=True)
        gain_sum = jnp.sum(gain_sum, axis=0, keepdims=True)
        square = dot_t(cen[:, to], dwb[:, to]) + rank_one(away, col_sum)
        mats, vecs = [], []
        for half in range(2):
            ch = slice(PAIR * half, PAIR * (half + 1))
            inner = square[ch, ch]
            mats.append(pack(inner + inner.T))
            vecs.append((col_sum[:, ch], gain_sum[:, ch]))
        put_stats(stats, quad, mats, vecs, side is not None)


def sides_of(count):
    return (0, 1) if count == 2 else (None,)


def own_kernel(spot, h2, *refs):
    cens, out = refs[:-1], refs[-1]
    quads = out.shape[1] // 256
    for side, cen in zip(sides_of(len(cens)), cens):
        for quad in range(cen.shape[1] // 256):
            near = slice(256 * quad, 256 * (quad + 1))
            out[:, lanes_of(quad, spot, side, quads)] = dot_t(h2[...], cen[:, near]).astype(BF16)


def turn_kernel(spot, w3, *refs):
    given, (turned, flow) = refs[:-2], refs[-2:]
    half = len(given) // 2
    quads = turned.shape[1] // 256
    for side, dwb, shares in zip(sides_of(half), given[:half], given[half:]):
        for quad in range(dwb.shape[1] // 256):
            whiten = quad_matrix(shares, quad).T
            near = slice(256 * quad, 256 * (quad + 1))
            turned[:, lanes_of(quad, spot, side, quads)] = dot(dwb[:, near], whiten).astype(BF16)
    flow[...] = dot_nt(turned[...], w3[...])


def turned_kernel(h2, turned, out):
    for quad in range(turned.shape[1] // 256):
        lanes = slice(256 * quad, 256 * (quad + 1))
        out[:, lanes] = dot_t(h2[...], turned[:, lanes])


def last_kernel(spot, flow, means, s2, w3, h1pad, turned, own, sums, *rest, plans):
    count = 2 if plans else 1
    cens, wshares, given = (rest[count * at : count * (at + 1)] for at in range(3))
    cols, gains, *outs = rest[3 * count : -7]
    spairs, bias_out, ext, flat, joint, part, part_last = rest[-7:]
    rows = flow.shape[0]
    quads = w3.shape[1] // 256
    place_pairs(spot, given, spairs, count == 2)
    gains[...] = spairs[:, GROUP + 1, :]
    chunk = chunk_of(rows, 128)
    ext[...] = jnp.zeros_like(ext)
    low = jnp.zeros((1, w3.shape[0]), F32)
    top = 0
    total = None
    for side, cen, whitens, shares in zip(sides_of(count), cens, wshares, given):
        start = top
        for quad in range(cen.shape[1] // 256):
            lanes = lanes_of(quad, spot, side, quads)
            sym = quad_matrix(shares, quad)
            away = means[0:1, lanes] - row_of(whitens, quad, 0)
            bias = row_of(shares, quad, 0) + row_times(away, sym)
            bias_out[:, lanes] = jnp.broadcast_to(bias, (8, 256))
            last = w3[:, lanes]
            low = low + row_times(bias, last, dot_nt)
            joint[top : top + 256, :] = dot_nt(sym, last).astype(BF16)
            top += 256
        product = dot(cen[...], joint[start:top, :])
        total = product if total is None else total + product
    flat[...] = total

    def middle(at, carry):
        here = slice(at * chunk, (at + 1) * chunk)
        flat[here, :] = (flow[here, :] + flat[here, :] + low) * s2[here, :]
        return carry

    loop(rows // chunk, middle, 0)
    pad_lines(flat, ext, rows)
    shifted(ext, cols)
    padded, depth = h1pad.shape
    for row in range(3):
        for col in range(3):
            k = 3 * row + col
            near = cols[2 - col, LINE * (2 - row) : LINE * (2 - row) + padded, :]
            part[k * depth : (k + 1) * depth, :] = dot_t(h1pad[...], near)
    for quad in range(turned.shape[1] // 256):
        lanes = slice(256 * quad, 256 * (quad + 1))
        sym = quad_matrix(spairs, quad)
        part_last[:, lanes] = (
            turned[:, lanes]
            + dot(own[:, lanes], sym)
            + rank_one(sums[0:1, :], bias_out[0:1, lanes])
        )
    if plans:
        emit_split(part, outs[0], outs[1], spot[1], plans[0])
        emit_split(part_last, outs[0], outs[1], spot[1], plans[1])
    else:
        outs[0][...] = part[...]
        outs[1][...] = part_last[...]


def finish(part, outs, spot, plan):
    if plan:
        emit_split(part, outs[0], outs[1], spot[1], plan)
    else:
        outs[0][...] = part[...]


def slope_kernel(spot, cols, wm, s1, x, dmid1, *rest, plan):
    outs, (ext, flat, part) = rest[:-3], rest[-3:]
    rows, depth = s1.shape
    padded = padded_rows(rows)
    big = chunk_of(padded, 512)

    def step(at, carry):
        base = at * big
        total = jnp.zeros((big, depth), F32)
        for row in range(3):
            for col in range(3):
                near = cols[2 - col, pl.ds(base + LINE * (2 - row), big), :]
                k = 3 * row + col
                total = total + dot_nt(near, wm[k * depth : (k + 1) * depth, :])
        ext[pl.ds(base, big), :] = total
        return carry

    loop(padded // big, step, 0)
    unpad_lines(ext, flat, rows)
    dmid1[...] = (flat[...] * s1[...]).astype(BF16)
    for quad in range(x.shape[1] // 256):
        lanes = slice(256 * quad, 256 * (quad + 1))
        part[lanes, :] = dot_t(x[:, lanes], dmid1[...])
    finish(part, outs, spot, plan)


def spans_step(spot, *refs, steps, extra=0):
    count = 2 * (1 + max(span[0] for spans in steps for span in spans))
    given, outs = refs[: count + extra], refs[count + extra :]
    for at, spans in enumerate(steps):
        to = 0
        for source, start, size, bit in spans:
            mine, other = half_of(given[2 * source], given[2 * source + 1], spot[bit], start, size)
            outs[2 * at][to : to + size // 2, :] = mine
            outs[2 * at + 1][to : to + size // 2, :] = other
            to += size // 2
        left = outs[2 * at].shape[0] - to
        if not left:
            continue
        if extra:
            rows = jnp.concatenate([given[-1][...]] * (outs[0].shape[1] // PAIR), axis=1)
        else:
            tail = given[0].shape[0] - left
            rows = given[0][tail:, :] + given[1][tail:, :]
        for out in outs[2 * at : 2 * at + 2]:
            out[to:, :] = rows


def close_kernel(spot, keep, given, first, middle, last, gain, *, tall, high, scale):
    total = (keep[...] + given[...]) * scale
    for half in range(2):
        lanes = slice(PAIR * half, PAIR * (half + 1))
        step = tall // 4
        for wide in range(4):
            last[pl.ds(2 * wide + half, step, 8), :] = total[step * wide : step * (wide + 1), lanes]
        middle[pl.ds(half, high, 2), :] = total[tall : tall + high, lanes]
        first[pl.ds(half, tall, 2), :] = total[tall + high : 2 * tall + high, lanes]
    size = gain.shape[1]
    each = PAIR // size
    rows = total[2 * tall + high :, :PAIR]
    device = spot[6]
    at = lax.broadcasted_iota(jnp.int32, rows.shape, 0)
    row = jnp.sum(jnp.where(at == device // each, rows, 0.0), axis=0, keepdims=True)
    mine = jnp.zeros((1, size), F32)
    for place in range(each):
        mine = jnp.where(device % each == place, row[:, place * size : (place + 1) * size], mine)
    gain[...] = mine


def input_kernel(spot, dmid1, w1, *refs):
    dpres, (out, token) = refs[:-2], refs[-2:]
    token[...] = jnp.zeros_like(token)
    quads = out.shape[1] // 256
    for side, dpre in zip(sides_of(len(dpres)), dpres):
        for quad in range(dpre.shape[1] // 256):
            lanes = lanes_of(quad, spot, side, quads)
            near = slice(256 * quad, 256 * (quad + 1))
            out[:, lanes] = (dot_nt(dmid1[...], w1[lanes, :]) + dpre[:, near]).astype(BF16)


def call(kernel, outs, args, scratch=(), scalars=0, flops=0, ties=(), far=0, room=40):
    args = tuple(args) + tuple(ties)
    specs = [pl.BlockSpec(memory_space=pltpu.SMEM)] * scalars
    specs += [pl.BlockSpec(memory_space=pl.ANY)] * far
    specs += [pl.BlockSpec(memory_space=pltpu.VMEM)] * (len(args) - scalars - len(ties) - far)
    specs += [pl.BlockSpec(memory_space=pl.ANY)] * len(ties)
    count = len(args) - len(ties)

    def body(*refs):
        kernel(*refs[:count], *refs[len(args) :])

    size = sum(a.size * a.dtype.itemsize for a in args)
    size += sum(o.size * o.dtype.itemsize for o in outs)
    return pl.pallas_call(
        body,
        out_shape=tuple(outs),
        in_specs=specs,
        out_specs=tuple(pl.BlockSpec(memory_space=pltpu.VMEM) for _ in outs),
        scratch_shapes=list(scratch),
        cost_estimate=pl.CostEstimate(flops=flops, bytes_accessed=size, transcendentals=0),
        compiler_params=pltpu.CompilerParams(vmem_limit_bytes=room * 2**20),
    )(*args)


def shape(dims, dtype=F32):
    return jax.ShapeDtypeStruct(dims, dtype)


def swap(value, axis, size, flip):
    return lax.ppermute(value, axis, [(at, at ^ flip) for at in range(size)])


def shards(inputs, out_grad, conv_first, conv_middle, conv_last, gain):
    rows, width = inputs.shape
    mid = conv_first.shape[1]
    pairs = width // PAIR
    ghosts = lax.axis_size("ghost")
    groups = lax.axis_size("group")
    devices = ghosts * groups
    span = float(rows * ghosts)
    scale = (rows * devices) ** (-0.5)
    padded = padded_rows(rows)
    ghost = lax.axis_index("ghost")
    group = lax.axis_index("group")
    bits = [ghost] + [(ghost >> bit) & 1 for bit in range(3)]
    bits += [(group >> bit) & 1 for bit in range(2)] + [group * ghosts + ghost]
    spot = jnp.stack(bits).astype(jnp.int32)
    core, across, along, near, far = 1, 2, 3, 4, 5
    split = ghosts == 8 and pairs == 8 and groups == 4
    unit = 2 * rows * width * mid

    ext = pltpu.VMEM((24 + padded + LINE + 8, mid), F32)
    flat = pltpu.VMEM((rows, mid), F32)
    cols = (3, padded + 2 * LINE, mid)
    big = (pairs, TALL, PAIR)
    half = (pairs // 2, TALL, PAIR)
    packed = (pairs // 4, TALL, PAIR)
    side_stats = shape(packed if split else big)
    side_width = width // 2 if split else width

    def collect(stats, ties):
        if not split:
            return [lax.psum(stats[0], "ghost")]
        send, total = stats
        given = swap(send, "ghost", ghosts, 1)
        (total,) = call(add_kernel, [shape(packed)], (total, given))
        given = swap(total, "ghost", ghosts, 2)
        (total,) = call(add_kernel, [shape(packed)], (total, given), ties=ties)
        return [total, swap(total, "ghost", ghosts, 4)]

    own = half if split else big
    held = own[0]
    chunks = rows // chunk_of(rows, 128)
    h1pad, s1, h2, s2, means, sums, cen, stats = call(
        functools.partial(forward_kernel, split=split),
        [shape((padded, mid), BF16), shape((rows, mid)), shape((rows, mid), BF16),
         shape((rows, mid)), shape((8, width)), shape((8, mid)), shape((rows, side_width), BF16),
         side_stats],
        (spot, *(
            pltpu.with_memory_space_constraint(value, pltpu.HBM)
            for value in (inputs, conv_first, conv_middle, conv_last)
        )),
        (pltpu.VMEM((rows, width), BF16), pltpu.VMEM(conv_first.shape, BF16),
         pltpu.VMEM(conv_middle.shape, BF16), pltpu.VMEM(conv_last.shape, BF16),
         pltpu.SemaphoreType.DMA((3 + chunks,)),
         ext, pltpu.VMEM(cols, BF16), flat),
        scalars=1, flops=5 * unit, far=4,
    )
    stats, cens = [stats], (cen,)
    if split:
        cen, keep = call(
            own_branch_kernel, [shape((rows, side_width), BF16), side_stats],
            (spot, h2, conv_last, means), scalars=1, flops=unit,
        )
        stats.append(keep)
        cens = (cen, *cens)
    (own_part,) = call(
        own_kernel, [shape((mid, width), BF16)], (spot, h2, *cens), scalars=1, flops=unit
    )
    share, kept = call(
        functools.partial(whiten_kernel, span=span, packed=split),
        [shape(own), shape((held, 2 * NEWTON + 1, PAIR, PAIR))], collect(stats, (own_part,)), flops=10**7,
    )
    whites = (pltpu.VMEM((2, rows, 256), F32),)
    shares = [share, swap(share, "ghost", ghosts, 1)] if split else [share]
    dwbs, dpres, back = [], [], []
    for side, cen, whiten in zip(sides_of(len(shares)), cens, shares):
        dwb, dpre, part = call(
            functools.partial(backward_kernel, side=side),
            [shape((rows, side_width), BF16), shape((rows, side_width)), side_stats],
            (spot, inputs, out_grad, cen, means, gain.reshape(1, width), whiten), whites,
            scalars=1, flops=2 * unit, ties=dpres,
        )
        dwbs.append(dwb)
        dpres.append(dpre)
        back.insert(0, part)
    stats = back
    turned, flow = call(
        turn_kernel, [shape((rows, width), BF16), shape((rows, mid))],
        (spot, conv_last, *dwbs, *shares), scalars=1, flops=2 * unit,
    )
    (turned_part,) = call(turned_kernel, [shape((mid, width))], (h2, turned), flops=unit)
    (pulled,) = call(
        functools.partial(pull_kernel, span=span, packed=split), [shape(own)], (*collect(stats, (flow,)), kept),
        flops=10**7, ties=(turned_part,),
    )
    given = [pulled, swap(pulled, "ghost", ghosts, 1)] if split else [pulled]

    half_rows = mid * width // 512
    orders = (
        (("ghost", 1), ("ghost", 2), ("group", 0), ("group", 1)),
        (("ghost", 2), ("group", 0), ("ghost", 1), ("group", 1)),
        (("group", 0), ("ghost", 1), ("ghost", 2), ("group", 1)),
    )
    high, tall = 9 * mid // devices, width // devices
    cut = high // 24 * 8
    middle_plan = last_plan = first_plan = None
    if split:
        middle_plan = plan_of(
            [(0, cut, orders[0]), (cut, high - cut, orders[1])], high, 1, ghosts
        )
        last_plan = plan_of(
            [(0, mid // devices, orders[0])], mid // devices, width // 256, ghosts, 9 * mid // 2
        )
        first_plan = plan_of([(0, tall, orders[2])], tall, 1, ghosts)
    dcols, gains, *middle_part = call(
        functools.partial(last_kernel, plans=(middle_plan, last_plan) if split else None),
        [shape(cols, BF16), shape((pairs, PAIR))]
        + ([shape((9 * mid // 2 + half_rows, mid))] * 2 if split
           else [shape((9 * mid, mid)), shape((mid, width))]),
        (spot, flow, means, s2, conv_last, h1pad, turned_part, own_part, sums,
         *cens, *shares, *given),
        (pltpu.VMEM(big, F32), pltpu.VMEM((8, width), F32), ext, flat,
         pltpu.VMEM((width, mid), BF16), pltpu.VMEM((9 * mid, mid), F32),
         pltpu.VMEM((mid, width), F32)),
        scalars=1, flops=5 * unit,
    )
    dmid1, *first_part = call(
        functools.partial(slope_kernel, plan=first_plan),
        [shape((rows, mid), BF16)]
        + ([shape((half_rows, mid))] * 2 if split else [shape((width, mid))]),
        (spot, dcols, conv_middle, s1, inputs),
        (ext, flat, pltpu.VMEM((width, mid), F32)), scalars=1, flops=4 * unit,
    )
    portion = width // devices
    if not split:
        input_grad, _ = call(
            input_kernel, [shape((rows, width), BF16), shape((8, PAIR))],
            (spot, dmid1, conv_first, *dpres), scalars=1, flops=unit,
        )
        grads = [
            lax.psum_scatter(
                (part[0] * scale).reshape(-1), ("group", "ghost"), scatter_dimension=0, tiled=True
            )
            for part in (first_part, middle_part, middle_part[1:])
        ]
        gain_grad = lax.dynamic_slice_in_dim(
            lax.psum(gains.reshape(-1) * scale, "group"), (group * ghosts + ghost) * portion, portion
        )
        return (input_grad, *grads, gain_grad)

    def move(parts, ways):
        result = []
        for at, (axis, flip) in enumerate(ways):
            result.append(parts[2 * at])
            result.append(swap(parts[2 * at + 1], axis, groups if axis == "group" else ghosts, flip))
        return result

    def run(steps, given, extra=(), more=0, ties=()):
        outs = []
        for at, spans in enumerate(steps):
            height = sum(span[2] for span in spans) // 2 + (more if at == 0 else 0)
            outs += [shape((height, mid))] * 2
        return call(
            functools.partial(spans_step, steps=steps, extra=len(extra)), outs,
            (spot, *given, *extra), scalars=1, ties=ties,
        )

    core_way, x_way, y_way = (("ghost", 1 << bit) for bit in range(3))
    near_way, far_way = ("group", 1), ("group", 2)
    given = move(middle_part, (core_way,))
    first_given = move(first_part, (core_way,))
    pieces = devices // 2
    a_low, a_high, b_all = half_rows, pieces * cut, pieces * (high - cut)
    parts = run(
        (((0, a_high + b_all, a_low, across), (0, 0, a_high, across)),
         ((0, a_high, b_all, along),)), given,
    )
    given = move(parts, (x_way, y_way))
    parts = run((((0, 0, half_rows, near),),), first_given, ties=(parts[0],))
    given += move(parts, (near_way,))
    input_grad, token = call(
        input_kernel, [shape((rows, width), BF16), shape((8, PAIR))],
        (spot, dmid1, conv_first, *dpres), scalars=1, flops=unit, ties=(parts[0],),
    )
    a_low, a_high, b_all, c_all = a_low // 2, a_high // 2, b_all // 2, half_rows // 2
    parts = run(
        (((0, 0, a_low, along), (0, a_low, a_high, along)), ((1, 0, b_all, near),),
         ((2, 0, c_all, across),)), given, ties=(token,),
    )
    given = move(parts, (y_way, near_way, x_way))
    a_low, a_high, b_all, c_all = a_low // 2, a_high // 2, b_all // 2, c_all // 2
    parts = run(
        (((0, 0, a_low, near), (0, a_low, a_high, near)), ((1, 0, b_all, across),),
         ((2, 0, c_all, along),)), given, extra=(gains,), more=8,
    )
    given = move(parts, (near_way, x_way, y_way))
    a_low, a_high, b_all, c_all = a_low // 2, a_high // 2, b_all // 2, c_all // 2
    parts = run(
        (((0, 0, a_low, far), (0, a_low, a_high, far), (1, 0, b_all, far), (2, 0, c_all, far)),),
        given, more=8,
    )
    given = move(parts, (far_way,))
    first_grad, middle_grad, last_grad, gain_grad = call(
        functools.partial(close_kernel, tall=tall, high=high, scale=scale),
        [shape((2 * tall, PAIR)), shape((2 * high, PAIR)), shape((2 * tall, PAIR)),
         shape((1, portion))],
        (spot, *given), scalars=1,
    )
    return (
        input_grad, first_grad.reshape(-1), middle_grad.reshape(-1), last_grad.reshape(-1),
        gain_grad.reshape(-1),
    )


def solution(mesh):
    in_specs = (P(("group", "ghost"), None), P(("group", "ghost"), None), P(), P(), P(), P())
    out_specs = (
        P(("group", "ghost"), None),
        P(("group", "ghost")),
        P(("group", "ghost")),
        P(("group", "ghost")),
        P(("group", "ghost")),
    )
    return jax.shard_map(shards, mesh=mesh, in_specs=in_specs, out_specs=out_specs, check_vma=False)
```

```python
import functools

import jax
import jax.numpy as jnp
from jax import lax
from jax.experimental import pallas as pl
from jax.experimental.pallas import tpu as pltpu
from jax.sharding import PartitionSpec as P

GROUP = 64
NEWTON = 5
SIDE = 14
LINE = 16
PAIR = 2 * GROUP
TALL = GROUP + 8
epsilon = 1e-05

F32 = jnp.float32
BF16 = jnp.bfloat16


def dot(left, right):
    return jnp.dot(left, right, preferred_element_type=F32)


def dot_t(left, right):
    return lax.dot_general(left, right, (((0,), (0,)), ((), ())), preferred_element_type=F32)


def dot_nt(left, right):
    return lax.dot_general(left, right, (((1,), (1,)), ((), ())), preferred_element_type=F32)


def halves_of(value):
    high = value.astype(BF16)
    return high, (value - high.astype(F32)).astype(BF16)


def exact(left, right):
    a, b = halves_of(left)
    c, d = halves_of(right)
    low = dot(jnp.concatenate([a, b], axis=1), jnp.concatenate([d, c], axis=0))
    return low + dot(a, c)


def exact_two(left, first, second):
    both = exact(left, jnp.concatenate([first, second], axis=1))
    return both[:, : first.shape[1]], both[:, first.shape[1] :]


def outer_of(row):
    tile = vectors(row)
    return lax.dot_general(
        tile, tile, (((0,), (0,)), ((), ())), preferred_element_type=F32,
        precision=lax.Precision.HIGHEST,
    )


def sigmoid(value):
    return 0.5 * jnp.tanh(0.5 * value) + 0.5


def two_rows(row):
    high, low = halves_of(jnp.broadcast_to(row, (16, row.shape[1])))
    at = lax.broadcasted_iota(jnp.int32, high.shape, 0)
    return jnp.where(at == 0, high.astype(F32), jnp.where(at == 1, low.astype(F32), 0.0)).astype(
        BF16
    )


def row_times(row, matrix, product=dot):
    return jnp.sum(product(two_rows(row), matrix), axis=0, keepdims=True)


def rank_one(left, right):
    tiles = []
    for row, order in ((left, (0, 1, 0)), (right, (0, 0, 1))):
        pair = halves_of(jnp.broadcast_to(row, (16, row.shape[1])))
        at = lax.broadcasted_iota(jnp.int32, pair[0].shape, 0)
        tile = jnp.zeros(pair[0].shape, F32)
        for place, which in enumerate(order):
            tile = jnp.where(at == place, pair[which].astype(F32), tile)
        tiles.append(tile.astype(BF16))
    return dot_t(*tiles)


def chunk_of(rows, most):
    best = 16
    for size in range(16, most + 1, 16):
        if rows % size == 0:
            best = size
    return best


def loop(count, body, carry):
    for at in range(count):
        carry = body(at, carry)
    return carry


def left_half(shape):
    return lax.broadcasted_iota(jnp.int32, shape, 1) < GROUP


def spread(packed):
    left = left_half(packed.shape)
    zero = jnp.zeros_like(packed)
    return jnp.concatenate([jnp.where(left, packed, zero), jnp.where(left, zero, packed)], axis=0)


def pack(square):
    top, bottom = square[:GROUP], square[GROUP:]
    return jnp.where(left_half(top.shape), top, bottom)


def vectors(*rows):
    at = lax.broadcasted_iota(jnp.int32, (8, PAIR), 0)
    tile = jnp.zeros((8, PAIR), F32)
    for place, row in enumerate(rows):
        tile = jnp.where(at == place, row, tile)
    return tile


def fold(value):
    rows, lanes = value.shape
    return jnp.sum(value.reshape(rows // 8, 8, lanes), axis=0)


def pad_lines(source, ext, rows):
    for line in range(rows // SIDE):
        place = 24 + LINE * (line + line // SIDE)
        ext[place : place + SIDE, :] = source[SIDE * line : SIDE * (line + 1), :]


def unpad_lines(source, target, rows):
    for line in range(rows // SIDE):
        place = LINE * (line + line // SIDE)
        target[SIDE * line : SIDE * (line + 1), :] = source[place : place + SIDE, :]


def padded_rows(rows):
    return rows // (SIDE * SIDE) * (SIDE + 1) * LINE


def shifted(ext, cols):
    length = cols.shape[1]
    for col in range(3):
        cols[col] = ext[7 + col : 7 + col + length, :].astype(BF16)


def emit_split(source, keep, send, core, plan):
    for start, height, first, size, mine in plan:
        lanes = keep.shape[1]
        for wide in range(source.shape[1] // lanes):
            to = slice(start + wide * height, start + (wide + 1) * height)
            cols = slice(wide * lanes, (wide + 1) * lanes)
            for target, half in ((keep, core), (send, 1 - core)):
                place = pl.multiple_of((mine + half) * size + first, 8)
                target[to, :] = source[pl.ds(place, height), cols]


def plan_of(parts, piece, wide, ghosts, start=0):
    plan = []
    for first, height, steps in parts:
        for at in range(2 ** len(steps)):
            source = 0
            for place, (axis, bit) in enumerate(steps):
                value = (at >> (len(steps) - 1 - place)) & 1
                source += value << bit if axis == "ghost" else (value << bit) * ghosts
            plan.append((start, height, first, piece, source))
            start += height * wide
    return plan


def half_of(left, right, bit, start=0, rows=None):
    rows = (left.shape[0] if rows is None else rows) // 2
    mine = pl.ds(pl.multiple_of(start + bit * rows, 8), rows)
    other = pl.ds(pl.multiple_of(start + (1 - bit) * rows, 8), rows)
    return left[mine, :] + right[mine, :], left[other, :] + right[other, :]


def pack_slot(mats, vecs):
    first, second = mats
    row = lax.broadcasted_iota(jnp.int32, first.shape, 0)
    lane = lax.broadcasted_iota(jnp.int32, first.shape, 1)
    left = lane < GROUP
    col = jnp.where(left, lane, lane - GROUP)
    upper = jnp.where(left, first, pltpu.roll(second, GROUP, 1))
    lower = jnp.where(left, pltpu.roll(first, GROUP, 1), second)
    rows = [jnp.sum(jnp.where(row == col, m, 0.0), axis=0, keepdims=True) for m in mats]
    for pair in zip(*vecs):
        rows += pair
    return jnp.concatenate([jnp.where(row <= col, upper, lower), vectors(*rows)], axis=0)


def put_stats(stats, quad, mats, vecs, packed):
    if packed:
        stats[quad] = pack_slot(mats, vecs)
        return
    for half in range(2):
        stats[2 * quad + half, :GROUP, :] = mats[half]
        stats[2 * quad + half, GROUP:, :] = vectors(*vecs[half])


def lanes_of(quad, spot, side, quads):
    if side is None:
        return slice(256 * quad, 256 * (quad + 1))
    half = jnp.bitwise_xor(spot[1], side)
    return pl.ds(pl.multiple_of(256 * (half * (quads // 2) + quad), 256), 256)


def branch_quad(h2, w3, means, lanes):
    rows = h2.shape[0]
    mean = means[0:1, lanes]
    centered = (dot(h2[...], w3[:, lanes]) - mean).astype(BF16)
    square = dot_t(centered, centered)
    mats, vecs = [], []
    for half in range(2):
        ch = slice(PAIR * half, PAIR * (half + 1))
        row = mean[:, ch]
        mats.append(pack(square[ch, ch] + outer_of(row) * rows))
        vecs.append((row * rows,))
    return centered, mats, vecs


def take_pairs(total, packed):
    result = []
    if not packed:
        for at in range(total.shape[0]):
            vecs = [total[at, GROUP + p : GROUP + p + 1, :] for p in range(2)]
            result.append((spread(total[at, :GROUP, :]), *vecs))
        return result
    shape = (PAIR, PAIR)
    row = lax.broadcasted_iota(jnp.int32, shape, 0)
    col = lax.broadcasted_iota(jnp.int32, shape, 1)
    mask = jnp.where(row < GROUP, row - col, col - row) < 0
    eye = identity()
    for slot in range(total.shape[0]):
        both = total[slot, :GROUP, :]
        turned = pltpu.roll(both, GROUP, 1)
        left = left_half(both.shape)
        for at in range(2):
            twice = jnp.where(left, *((both, turned) if at == 0 else (turned, both)))
            part = jnp.where(mask, spread(twice), 0.0)
            line = [total[slot, GROUP + 2 * p + at : GROUP + 2 * p + at + 1, :] for p in range(3)]
            result.append((part + part.T + eye * line[0], line[1], line[2]))
    return result


def add_kernel(left, right, out):
    out[...] = left[...] + right[...]


def forward_kernel(
    spot, x_far, w1_far, wm_far, w3_far, h1pad, s1, h2, s2, means, sums, cen, stats, *rest, split
):
    x, w1, wm, w3, sems, ext, cols, flat = rest
    rows = x.shape[0]
    part = chunk_of(rows, 128)

    def slab(at):
        here = slice(at * part, (at + 1) * part)
        return pltpu.make_async_copy(x_far.at[here, :], x.at[here, :], sems.at[3 + at])

    weights = [
        pltpu.make_async_copy(far, ref, sems.at[at])
        for at, (far, ref) in enumerate(((w1_far, w1), (wm_far, wm), (w3_far, w3)))
    ]
    weights[0].start()
    for at in range(rows // part):
        slab(at).start()
    weights[1].start()
    weights[2].start()
    chunk = chunk_of(rows, 128)
    ext[...] = jnp.zeros_like(ext)

    weights[0].wait()

    slabs = rows // part
    for start, stop in ((0, (slabs + 1) // 2), ((slabs + 1) // 2, slabs)):
        for at in range(start, stop):
            slab(at).wait()
        here = slice(start * part, stop * part)
        flat[here, :] = dot(x[here, :], w1[...])

        def first(at, carry, start=start):
            here = slice((start + at) * part, (start + at + 1) * part)
            act = flat[here, :]
            sig = sigmoid(act)
            flat[here, :] = act * sig
            s1[here, :] = sig * (1.0 + act * (1.0 - sig))
            return carry

        loop(stop - start, first, 0)
    pad_lines(flat, ext, rows)
    shifted(ext, cols)
    padded = padded_rows(rows)
    h1pad[...] = cols[1, LINE : LINE + padded, :]
    big = chunk_of(padded, 512)
    weights[1].wait()

    def middle(at, carry):
        base = at * big
        total = jnp.zeros((big, wm.shape[1]), F32)
        for row in range(3):
            for col in range(3):
                left = cols[col, pl.ds(base + LINE * row, big), :]
                k = 3 * row + col
                depth = left.shape[1]
                total = total + dot(left, wm[k * depth : (k + 1) * depth, :])
        ext[pl.ds(base, big), :] = total
        return carry

    loop(padded // big, middle, 0)
    unpad_lines(ext, flat, rows)
    width = w3.shape[1]
    weights[2].wait()

    def second(at, hidden_sum):
        here = slice(at * chunk, (at + 1) * chunk)
        act = flat[here, :]
        sig = sigmoid(act)
        hidden = (act * sig).astype(BF16)
        h2[here, :] = hidden
        s2[here, :] = sig * (1.0 + act * (1.0 - sig))
        return hidden_sum + fold(hidden.astype(F32))

    zeros = jnp.zeros((8, w3.shape[0]), F32)
    hidden_sum = loop(rows // chunk, second, zeros)
    hidden_sum = jnp.sum(hidden_sum, axis=0, keepdims=True)
    sums[...] = jnp.broadcast_to(hidden_sum, sums.shape)
    total = row_times(hidden_sum, w3[...])
    mean = total / rows
    means[...] = jnp.broadcast_to(mean, means.shape)
    quads = width // 256
    for quad in range(quads // 2 if split else quads):
        lanes = lanes_of(quad, spot, 1 if split else None, quads)
        centered, mats, vecs = branch_quad(h2, w3, means, lanes)
        cen[:, 256 * quad : 256 * (quad + 1)] = centered
        put_stats(stats, quad, mats, vecs, split)


def own_branch_kernel(spot, h2, w3, means, cen, stats):
    quads = w3.shape[1] // 256
    for quad in range(quads // 2):
        lanes = lanes_of(quad, spot, 0, quads)
        centered, mats, vecs = branch_quad(h2, w3, means, lanes)
        cen[:, 256 * quad : 256 * (quad + 1)] = centered
        put_stats(stats, quad, mats, vecs, True)


def identity():
    shape = (PAIR, PAIR)
    return jnp.where(
        lax.broadcasted_iota(jnp.int32, shape, 0) == lax.broadcasted_iota(jnp.int32, shape, 1),
        1.0, 0.0,
    ).astype(F32)


def per_block(square):
    row_sums = jnp.sum(square, axis=1, keepdims=True)
    top = jnp.sum(row_sums[:GROUP], axis=0, keepdims=True)
    bottom = jnp.sum(row_sums[GROUP:], axis=0, keepdims=True)
    upper = lax.broadcasted_iota(jnp.int32, (PAIR, 1), 0) < GROUP
    return jnp.where(upper, top, bottom)


def total_of(terms):
    total = terms[0][...]
    for term in terms[1:]:
        total = total + term[...]
    return total


def whiten_kernel(*refs, span, packed):
    terms, (out, keep) = refs[:-2], refs[-2:]
    given = take_pairs(total_of(terms), packed)
    eye = identity()
    blocks = spread(jnp.ones((GROUP, PAIR), F32))
    means = [sums / span for _, sums, _ in given]
    covs = [
        moments / span - outer_of(mean) * blocks + epsilon * eye
        for (moments, _, _), mean in zip(given, means)
    ]
    traces = [per_block(cov * eye) for cov in covs]
    normed = [cov / trace for cov, trace in zip(covs, traces)]
    powers = [1.5 * eye - 0.5 * norm for norm in normed]
    for at, trace in enumerate(traces):
        keep[at, 0] = normed[at]
        keep[at, 1] = eye / trace
    for sweep in range(NEWTON - 1):
        both = [exact_two(power, power, norm) for power, norm in zip(powers, normed)]
        squares, sides = zip(*both)
        for at, power in enumerate(powers):
            keep[at, 2 + 2 * sweep] = power
            keep[at, 3 + 2 * sweep] = squares[at]
        powers = [
            1.5 * power - 0.5 * exact(square, side)
            for power, square, side in zip(powers, squares, sides)
        ]
    for at, power in enumerate(powers):
        keep[at, 2 * NEWTON] = power
        out[at, :GROUP, :] = pack(power / jnp.sqrt(traces[at]))
        out[at, GROUP:, :] = vectors(means[at])


def pull_kernel(*refs, span, packed):
    terms, (keep, out) = refs[:-2], refs[-2:]
    given = take_pairs(total_of(terms), packed)
    eye = identity()
    every = range(len(given))
    normed = [keep[at, 0] for at in every]
    inverse = [per_block(keep[at, 1]) / GROUP for at in every]
    roots = [jnp.sqrt(value) for value in inverse]
    powers = [keep[at, 2 * NEWTON] for at in every]
    grads = [given[at][0] * roots[at] for at in every]
    trace_grads = [
        -0.5 * inverse[at] * roots[at] * per_block(given[at][0] * powers[at]) for at in every
    ]
    normed_grads = [jnp.zeros_like(grads[0])] * len(given)
    for sweep in reversed(range(NEWTON - 1)):
        power = [keep[at, 2 + 2 * sweep] for at in every]
        square = [keep[at, 3 + 2 * sweep] for at in every]
        turned, side = zip(*(exact_two(grads[at], normed[at], power[at]) for at in every))
        turned = [turned[at] + turned[at].T for at in every]
        turned, outer = zip(*(exact_two(turned[at], power[at], square[at]) for at in every))
        side = [exact(side[at], square[at]) for at in every]
        normed_grads = [normed_grads[at] - 0.25 * (side[at] + side[at].T) for at in every]
        inner = [exact(power[at], turned[at]) for at in every]
        grads = [
            1.5 * grads[at] - 0.25 * (outer[at] + outer[at].T + inner[at]) for at in every
        ]
    for at in every:
        normed_grad = normed_grads[at] - 0.5 * grads[at]
        trace_grad = trace_grads[at] - inverse[at] * per_block(normed_grad * normed[at])
        both = normed_grad * inverse[at] + eye * trace_grad
        bias = -exact(vectors(given[at][1] / span), (powers[at] * roots[at]).T)
        out[at, :GROUP, :] = pack(both / span)
        out[at, GROUP:, :] = vectors(bias[0:1, :], given[at][2])


def place_pairs(spot, given, pairs, split):
    if split:
        for side, shares in enumerate(given):
            for at in range(shares.shape[0]):
                half = jnp.bitwise_xor(side, spot[1])
                pairs[half * shares.shape[0] + at] = shares[at]
    else:
        pairs[...] = given[0][...]


def quad_matrix(pairs, quad):
    zero = jnp.zeros((PAIR, PAIR), F32)
    first = spread(pairs[2 * quad, :GROUP, :])
    second = spread(pairs[2 * quad + 1, :GROUP, :])
    top = jnp.concatenate([first, zero], axis=1)
    bottom = jnp.concatenate([zero, second], axis=1)
    return jnp.concatenate([top, bottom], axis=0).astype(BF16)


def row_of(pairs, quad, place):
    at = GROUP + place
    return jnp.concatenate(
        [pairs[2 * quad, at : at + 1, :], pairs[2 * quad + 1, at : at + 1, :]], axis=1
    )


def backward_kernel(spot, x, og, cen, means, gain, shares, *rest, side):
    rows, width = x.shape
    quads = width // 256
    dwb, dpre_out, stats, whites = rest
    count = quads if side is None else quads // 2
    chunk = chunk_of(rows, 128)
    aways, shifts = [], []

    def multiply(quad):
        lanes = lanes_of(quad, spot, side, quads)
        whiten = quad_matrix(shares, quad)
        aways.append(means[0:1, lanes] - row_of(shares, quad, 0))
        shifts.append(row_times(aways[-1], whiten))
        whites[quad % 2] = dot(cen[:, 256 * quad : 256 * (quad + 1)], whiten)

    multiply(0)
    for quad in range(count):
        if quad + 1 < count:
            multiply(quad + 1)
        lanes = lanes_of(quad, spot, side, quads)
        to = slice(256 * quad, 256 * (quad + 1))
        away, shift = aways[quad], shifts[quad]
        scale = gain[:, lanes]

        def step(at, carry, quad=quad, lanes=lanes, to=to, shift=shift, scale=scale):
            col_sum, gain_sum = carry
            here = slice(at * chunk, (at + 1) * chunk)
            white = whites[quad % 2, here, :] + shift
            pre = x[here, lanes].astype(F32) + scale * white
            sig = sigmoid(pre)
            dpre = og[here, lanes].astype(F32) * (sig * (1.0 + pre * (1.0 - sig)))
            dpre_out[here, to] = dpre
            dwhite = scale * dpre
            dwb[here, to] = dwhite.astype(BF16)
            return col_sum + fold(dwhite), gain_sum + fold(dpre * white)

        zero = jnp.zeros((8, 256), F32)
        col_sum, gain_sum = loop(rows // chunk, step, (zero, zero))
        col_sum = jnp.sum(col_sum, axis=0, keepdims=True)
        gain_sum = jnp.sum(gain_sum, axis=0, keepdims=True)
        square = dot_t(cen[:, to], dwb[:, to]) + rank_one(away, col_sum)
        mats, vecs = [], []
        for half in range(2):
            ch = slice(PAIR * half, PAIR * (half + 1))
            inner = square[ch, ch]
            mats.append(pack(inner + inner.T))
            vecs.append((col_sum[:, ch], gain_sum[:, ch]))
        put_stats(stats, quad, mats, vecs, side is not None)


def sides_of(count):
    return (0, 1) if count == 2 else (None,)


def own_kernel(spot, h2, *refs):
    cens, out = refs[:-1], refs[-1]
    quads = out.shape[1] // 256
    for side, cen in zip(sides_of(len(cens)), cens):
        for quad in range(cen.shape[1] // 256):
            near = slice(256 * quad, 256 * (quad + 1))
            out[:, lanes_of(quad, spot, side, quads)] = dot_t(h2[...], cen[:, near]).astype(BF16)


def turn_kernel(spot, w3, *refs):
    given, (turned, flow) = refs[:-2], refs[-2:]
    half = len(given) // 2
    quads = turned.shape[1] // 256
    for side, dwb, shares in zip(sides_of(half), given[:half], given[half:]):
        for quad in range(dwb.shape[1] // 256):
            whiten = quad_matrix(shares, quad).T
            near = slice(256 * quad, 256 * (quad + 1))
            turned[:, lanes_of(quad, spot, side, quads)] = dot(dwb[:, near], whiten).astype(BF16)
    flow[...] = dot_nt(turned[...], w3[...])


def turned_kernel(h2, turned, out):
    for quad in range(turned.shape[1] // 256):
        lanes = slice(256 * quad, 256 * (quad + 1))
        out[:, lanes] = dot_t(h2[...], turned[:, lanes])


def last_kernel(spot, flow, means, s2, w3, *rest, split):
    count = 2 if split else 1
    cens, wshares, given = (rest[count * at : count * (at + 1)] for at in range(3))
    cols, gains, spairs, bias_out, ext, flat, joint = rest[3 * count :]
    rows = flow.shape[0]
    quads = w3.shape[1] // 256
    place_pairs(spot, given, spairs, split)
    gains[...] = spairs[:, GROUP + 1, :]
    chunk = chunk_of(rows, 128)
    ext[...] = jnp.zeros_like(ext)
    low = jnp.zeros((1, w3.shape[0]), F32)
    top = 0
    total = None
    for side, cen, whitens, shares in zip(sides_of(count), cens, wshares, given):
        start = top
        for quad in range(cen.shape[1] // 256):
            lanes = lanes_of(quad, spot, side, quads)
            sym = quad_matrix(shares, quad)
            away = means[0:1, lanes] - row_of(whitens, quad, 0)
            bias = row_of(shares, quad, 0) + row_times(away, sym)
            bias_out[:, lanes] = jnp.broadcast_to(bias, (8, 256))
            last = w3[:, lanes]
            low = low + row_times(bias, last, dot_nt)
            joint[top : top + 256, :] = dot_nt(sym, last).astype(BF16)
            top += 256
        part = dot(cen[...], joint[start:top, :])
        total = part if total is None else total + part
    flat[:rows, :] = total

    def middle(at, carry):
        here = slice(at * chunk, (at + 1) * chunk)
        flat[here, :] = (flow[here, :] + flat[here, :] + low) * s2[here, :]
        return carry

    loop(rows // chunk, middle, 0)
    pad_lines(flat, ext, rows)
    shifted(ext, cols)


def finish(part, outs, spot, plan):
    if plan:
        emit_split(part, outs[0], outs[1], spot[1], plan)
    else:
        outs[0][...] = part[...]


def slope_kernel(spot, cols, wm, s1, x, dmid1, *rest, plan):
    outs, (ext, flat, part) = rest[:-3], rest[-3:]
    rows, depth = s1.shape
    padded = padded_rows(rows)
    big = chunk_of(padded, 512)

    def step(at, carry):
        base = at * big
        total = jnp.zeros((big, depth), F32)
        for row in range(3):
            for col in range(3):
                near = cols[2 - col, pl.ds(base + LINE * (2 - row), big), :]
                k = 3 * row + col
                total = total + dot_nt(near, wm[k * depth : (k + 1) * depth, :])
        ext[pl.ds(base, big), :] = total
        return carry

    loop(padded // big, step, 0)
    unpad_lines(ext, flat, rows)
    dmid1[...] = (flat[:rows, :] * s1[...]).astype(BF16)
    for quad in range(x.shape[1] // 256):
        lanes = slice(256 * quad, 256 * (quad + 1))
        part[lanes, :] = dot_t(x[:, lanes], dmid1[...])
    finish(part, outs, spot, plan)


def middle_kernel(spot, cols, h1pad, turned, own, sums, spairs, bias, *rest, plans):
    outs, (part, part_last) = rest[:-2], rest[-2:]
    padded, depth = h1pad.shape
    for row in range(3):
        for col in range(3):
            k = 3 * row + col
            near = cols[2 - col, LINE * (2 - row) : LINE * (2 - row) + padded, :]
            part[k * depth : (k + 1) * depth, :] = dot_t(h1pad[...], near)
    for quad in range(turned.shape[1] // 256):
        lanes = slice(256 * quad, 256 * (quad + 1))
        sym = quad_matrix(spairs, quad)
        part_last[:, lanes] = (
            turned[:, lanes]
            + dot(own[:, lanes], sym)
            + rank_one(sums[0:1, :], bias[0:1, lanes])
        )
    if plans:
        emit_split(part, outs[0], outs[1], spot[1], plans[0])
        emit_split(part_last, outs[0], outs[1], spot[1], plans[1])
    else:
        outs[0][...] = part[...]
        outs[1][...] = part_last[...]


def spans_step(spot, *refs, steps, extra=0):
    count = 2 * (1 + max(span[0] for spans in steps for span in spans))
    given, outs = refs[: count + extra], refs[count + extra :]
    for at, spans in enumerate(steps):
        to = 0
        for source, start, size, bit in spans:
            mine, other = half_of(given[2 * source], given[2 * source + 1], spot[bit], start, size)
            outs[2 * at][to : to + size // 2, :] = mine
            outs[2 * at + 1][to : to + size // 2, :] = other
            to += size // 2
        left = outs[2 * at].shape[0] - to
        if not left:
            continue
        if extra:
            rows = jnp.concatenate([given[-1][...]] * (outs[0].shape[1] // PAIR), axis=1)
        else:
            tail = given[0].shape[0] - left
            rows = given[0][tail:, :] + given[1][tail:, :]
        for out in outs[2 * at : 2 * at + 2]:
            out[to:, :] = rows


def close_kernel(spot, keep, given, first, middle, last, gain, *, tall, high, scale):
    total = (keep[...] + given[...]) * scale
    for half in range(2):
        lanes = slice(PAIR * half, PAIR * (half + 1))
        step = tall // 4
        for wide in range(4):
            last[pl.ds(2 * wide + half, step, 8), :] = total[step * wide : step * (wide + 1), lanes]
        middle[pl.ds(half, high, 2), :] = total[tall : tall + high, lanes]
        first[pl.ds(half, tall, 2), :] = total[tall + high : 2 * tall + high, lanes]
    size = gain.shape[1]
    each = PAIR // size
    rows = total[2 * tall + high :, :PAIR]
    device = spot[6]
    at = lax.broadcasted_iota(jnp.int32, rows.shape, 0)
    row = jnp.sum(jnp.where(at == device // each, rows, 0.0), axis=0, keepdims=True)
    mine = jnp.zeros((1, size), F32)
    for place in range(each):
        mine = jnp.where(device % each == place, row[:, place * size : (place + 1) * size], mine)
    gain[...] = mine


def input_kernel(spot, dmid1, w1, *refs):
    dpres, (out, token) = refs[:-2], refs[-2:]
    token[...] = jnp.zeros_like(token)
    quads = out.shape[1] // 256
    for side, dpre in zip(sides_of(len(dpres)), dpres):
        for quad in range(dpre.shape[1] // 256):
            lanes = lanes_of(quad, spot, side, quads)
            near = slice(256 * quad, 256 * (quad + 1))
            out[:, lanes] = (dot_nt(dmid1[...], w1[lanes, :]) + dpre[:, near]).astype(BF16)


def call(kernel, outs, args, scratch=(), scalars=0, flops=0, ties=(), far=0, room=40):
    args = tuple(args) + tuple(ties)
    specs = [pl.BlockSpec(memory_space=pltpu.SMEM)] * scalars
    specs += [pl.BlockSpec(memory_space=pl.ANY)] * far
    specs += [pl.BlockSpec(memory_space=pltpu.VMEM)] * (len(args) - scalars - len(ties) - far)
    specs += [pl.BlockSpec(memory_space=pl.ANY)] * len(ties)
    count = len(args) - len(ties)

    def body(*refs):
        kernel(*refs[:count], *refs[len(args) :])

    size = sum(a.size * a.dtype.itemsize for a in args)
    size += sum(o.size * o.dtype.itemsize for o in outs)
    return pl.pallas_call(
        body,
        out_shape=tuple(outs),
        in_specs=specs,
        out_specs=tuple(pl.BlockSpec(memory_space=pltpu.VMEM) for _ in outs),
        scratch_shapes=list(scratch),
        cost_estimate=pl.CostEstimate(flops=flops, bytes_accessed=size, transcendentals=0),
        compiler_params=pltpu.CompilerParams(vmem_limit_bytes=room * 2**20),
    )(*args)


def shape(dims, dtype=F32):
    return jax.ShapeDtypeStruct(dims, dtype)


def swap(value, axis, size, flip):
    return lax.ppermute(value, axis, [(at, at ^ flip) for at in range(size)])


def shards(inputs, out_grad, conv_first, conv_middle, conv_last, gain):
    rows, width = inputs.shape
    mid = conv_first.shape[1]
    pairs = width // PAIR
    ghosts = lax.axis_size("ghost")
    groups = lax.axis_size("group")
    devices = ghosts * groups
    span = float(rows * ghosts)
    scale = (rows * devices) ** (-0.5)
    padded = padded_rows(rows)
    ghost = lax.axis_index("ghost")
    group = lax.axis_index("group")
    bits = [ghost] + [(ghost >> bit) & 1 for bit in range(3)]
    bits += [(group >> bit) & 1 for bit in range(2)] + [group * ghosts + ghost]
    spot = jnp.stack(bits).astype(jnp.int32)
    core, across, along, near, far = 1, 2, 3, 4, 5
    split = ghosts == 8 and pairs == 8 and groups == 4
    unit = 2 * rows * width * mid

    ext = pltpu.VMEM((24 + padded + LINE + 8, mid), F32)
    flat = pltpu.VMEM((rows + LINE, mid), F32)
    cols = (3, padded + 2 * LINE, mid)
    big = (pairs, TALL, PAIR)
    half = (pairs // 2, TALL, PAIR)
    packed = (pairs // 4, TALL, PAIR)
    side_stats = shape(packed if split else big)
    side_width = width // 2 if split else width

    def collect(stats, ties):
        if not split:
            return [lax.psum(stats[0], "ghost")]
        send, total = stats
        given = swap(send, "ghost", ghosts, 1)
        (total,) = call(add_kernel, [shape(packed)], (total, given))
        given = swap(total, "ghost", ghosts, 2)
        (total,) = call(add_kernel, [shape(packed)], (total, given), ties=ties)
        return [total, swap(total, "ghost", ghosts, 4)]

    own = half if split else big
    held = own[0]
    chunks = rows // chunk_of(rows, 128)
    h1pad, s1, h2, s2, means, sums, cen, stats = call(
        functools.partial(forward_kernel, split=split),
        [shape((padded, mid), BF16), shape((rows, mid)), shape((rows, mid), BF16),
         shape((rows, mid)), shape((8, width)), shape((8, mid)), shape((rows, side_width), BF16),
         side_stats],
        (spot, *(
            pltpu.with_memory_space_constraint(value, pltpu.HBM)
            for value in (inputs, conv_first, conv_middle, conv_last)
        )),
        (pltpu.VMEM((rows, width), BF16), pltpu.VMEM(conv_first.shape, BF16),
         pltpu.VMEM(conv_middle.shape, BF16), pltpu.VMEM(conv_last.shape, BF16),
         pltpu.SemaphoreType.DMA((3 + chunks,)),
         ext, pltpu.VMEM(cols, BF16), flat),
        scalars=1, flops=5 * unit, far=4,
    )
    stats, cens = [stats], (cen,)
    if split:
        cen, keep = call(
            own_branch_kernel, [shape((rows, side_width), BF16), side_stats],
            (spot, h2, conv_last, means), scalars=1, flops=unit,
        )
        stats.append(keep)
        cens = (cen, *cens)
    (own_part,) = call(
        own_kernel, [shape((mid, width), BF16)], (spot, h2, *cens), scalars=1, flops=unit
    )
    share, kept = call(
        functools.partial(whiten_kernel, span=span, packed=split),
        [shape(own), shape((held, 2 * NEWTON + 1, PAIR, PAIR))], collect(stats, (own_part,)), flops=10**7,
    )
    whites = (pltpu.VMEM((2, rows, 256), F32),)
    shares = [share, swap(share, "ghost", ghosts, 1)] if split else [share]
    dwbs, dpres, back = [], [], []
    for side, cen, whiten in zip(sides_of(len(shares)), cens, shares):
        dwb, dpre, part = call(
            functools.partial(backward_kernel, side=side),
            [shape((rows, side_width), BF16), shape((rows, side_width)), side_stats],
            (spot, inputs, out_grad, cen, means, gain.reshape(1, width), whiten), whites,
            scalars=1, flops=2 * unit, ties=dpres,
        )
        dwbs.append(dwb)
        dpres.append(dpre)
        back.insert(0, part)
    stats = back
    turned, flow = call(
        turn_kernel, [shape((rows, width), BF16), shape((rows, mid))],
        (spot, conv_last, *dwbs, *shares), scalars=1, flops=2 * unit,
    )
    (turned_part,) = call(turned_kernel, [shape((mid, width))], (h2, turned), flops=unit)
    (pulled,) = call(
        functools.partial(pull_kernel, span=span, packed=split), [shape(own)], (*collect(stats, (flow,)), kept),
        flops=10**7, ties=(turned_part,),
    )
    given = [pulled, swap(pulled, "ghost", ghosts, 1)] if split else [pulled]

    dcols, gains, spairs, bias = call(
        functools.partial(last_kernel, split=split),
        [shape(cols, BF16), shape((pairs, PAIR)), shape(big), shape((8, width))],
        (spot, flow, means, s2, conv_last, *cens, *shares, *given),
        (ext, flat, pltpu.VMEM((width, mid), BF16)), scalars=1, flops=2 * unit,
    )
    half_rows = mid * width // 512
    orders = (
        (("ghost", 1), ("ghost", 2), ("group", 0), ("group", 1)),
        (("ghost", 2), ("group", 0), ("ghost", 1), ("group", 1)),
        (("group", 0), ("ghost", 1), ("ghost", 2), ("group", 1)),
    )
    high, tall = 9 * mid // devices, width // devices
    cut = high // 24 * 8
    middle_plan = last_plan = first_plan = None
    if split:
        middle_plan = plan_of(
            [(0, cut, orders[0]), (cut, high - cut, orders[1])], high, 1, ghosts
        )
        last_plan = plan_of(
            [(0, mid // devices, orders[0])], mid // devices, width // 256, ghosts, 9 * mid // 2
        )
        first_plan = plan_of([(0, tall, orders[2])], tall, 1, ghosts)
    middle_part = call(
        functools.partial(middle_kernel, plans=(middle_plan, last_plan) if split else None),
        [shape((9 * mid // 2 + half_rows, mid))] * 2 if split
        else [shape((9 * mid, mid)), shape((mid, width))],
        (spot, dcols, h1pad, turned_part, own_part, sums, spairs, bias),
        (pltpu.VMEM((9 * mid, mid), F32), pltpu.VMEM((mid, width), F32)),
        scalars=1, flops=3 * unit,
    )
    dmid1, *first_part = call(
        functools.partial(slope_kernel, plan=first_plan),
        [shape((rows, mid), BF16)]
        + ([shape((half_rows, mid))] * 2 if split else [shape((width, mid))]),
        (spot, dcols, conv_middle, s1, inputs),
        (ext, flat, pltpu.VMEM((width, mid), F32)), scalars=1, flops=4 * unit,
    )
    portion = width // devices
    if not split:
        input_grad, _ = call(
            input_kernel, [shape((rows, width), BF16), shape((8, PAIR))],
            (spot, dmid1, conv_first, *dpres), scalars=1, flops=unit,
        )
        grads = [
            lax.psum_scatter(
                (part[0] * scale).reshape(-1), ("group", "ghost"), scatter_dimension=0, tiled=True
            )
            for part in (first_part, middle_part, middle_part[1:])
        ]
        gain_grad = lax.dynamic_slice_in_dim(
            lax.psum(gains.reshape(-1) * scale, "group"), (group * ghosts + ghost) * portion, portion
        )
        return (input_grad, *grads, gain_grad)

    def move(parts, ways):
        result = []
        for at, (axis, flip) in enumerate(ways):
            result.append(parts[2 * at])
            result.append(swap(parts[2 * at + 1], axis, groups if axis == "group" else ghosts, flip))
        return result

    def run(steps, given, extra=(), more=0, ties=()):
        outs = []
        for at, spans in enumerate(steps):
            height = sum(span[2] for span in spans) // 2 + (more if at == 0 else 0)
            outs += [shape((height, mid))] * 2
        return call(
            functools.partial(spans_step, steps=steps, extra=len(extra)), outs,
            (spot, *given, *extra), scalars=1, ties=ties,
        )

    core_way, x_way, y_way = (("ghost", 1 << bit) for bit in range(3))
    near_way, far_way = ("group", 1), ("group", 2)
    given = move(middle_part, (core_way,))
    first_given = move(first_part, (core_way,))
    pieces = devices // 2
    a_low, a_high, b_all = half_rows, pieces * cut, pieces * (high - cut)
    parts = run(
        (((0, a_high + b_all, a_low, across), (0, 0, a_high, across)),
         ((0, a_high, b_all, along),)), given,
    )
    given = move(parts, (x_way, y_way))
    parts = run((((0, 0, half_rows, near),),), first_given, ties=(parts[0],))
    given += move(parts, (near_way,))
    input_grad, token = call(
        input_kernel, [shape((rows, width), BF16), shape((8, PAIR))],
        (spot, dmid1, conv_first, *dpres), scalars=1, flops=unit, ties=(parts[0],),
    )
    a_low, a_high, b_all, c_all = a_low // 2, a_high // 2, b_all // 2, half_rows // 2
    parts = run(
        (((0, 0, a_low, along), (0, a_low, a_high, along)), ((1, 0, b_all, near),),
         ((2, 0, c_all, across),)), given, ties=(token,),
    )
    given = move(parts, (y_way, near_way, x_way))
    a_low, a_high, b_all, c_all = a_low // 2, a_high // 2, b_all // 2, c_all // 2
    parts = run(
        (((0, 0, a_low, near), (0, a_low, a_high, near)), ((1, 0, b_all, across),),
         ((2, 0, c_all, along),)), given, extra=(gains,), more=8,
    )
    given = move(parts, (near_way, x_way, y_way))
    a_low, a_high, b_all, c_all = a_low // 2, a_high // 2, b_all // 2, c_all // 2
    parts = run(
        (((0, 0, a_low, far), (0, a_low, a_high, far), (1, 0, b_all, far), (2, 0, c_all, far)),),
        given, more=8,
    )
    given = move(parts, (far_way,))
    first_grad, middle_grad, last_grad, gain_grad = call(
        functools.partial(close_kernel, tall=tall, high=high, scale=scale),
        [shape((2 * tall, PAIR)), shape((2 * high, PAIR)), shape((2 * tall, PAIR)),
         shape((1, portion))],
        (spot, *given), scalars=1,
    )
    return (
        input_grad, first_grad.reshape(-1), middle_grad.reshape(-1), last_grad.reshape(-1),
        gain_grad.reshape(-1),
    )


def solution(mesh):
    in_specs = (P(("group", "ghost"), None), P(("group", "ghost"), None), P(), P(), P(), P())
    out_specs = (
        P(("group", "ghost"), None),
        P(("group", "ghost")),
        P(("group", "ghost")),
        P(("group", "ghost")),
        P(("group", "ghost")),
    )
    return jax.shard_map(shards, mesh=mesh, in_specs=in_specs, out_specs=out_specs, check_vma=False)
```
